32 devices in a mesh: dp: 4 (over y, core), seq: 8 (over z, x).
Axes of the slice: x: 2, y: 2, z: 4, core: 2. Of those that a mesh axis runs over, the one named last changes fastest.
Arguments:
- frames_x: bfloat16 [32, 128, 1152], P(('dp', 'seq')), may hold values from -6 to 6
- grad_y: bfloat16 [32, 128, 1152], P(('dp', 'seq')), may hold values from -6 to 6
- clip_ids: int32 [4, 8], P('dp'), may hold values from 0 to 3, never falling along the last dimension, each value on 1 to 4 neighbouring positions
- clip_patches: int32 [4, 4], P('dp'), may hold values from 32 to 128, as said below
- clip_step: int32 [4, 4], P('dp'), may hold values from 0 to 15
- mod_table: float32 [16, 3456], replicated, may hold values from -3 to 3
- w_qkv: bfloat16 [1152, 3456], P('seq'), may hold values from -2 to 2
- w_out: bfloat16 [1152, 1152], P('seq'), may hold values from -0.1875 to 0.1875
Outputs:
- out_y: bfloat16 [32, 128, 1152], P(('dp', 'seq'))
- grad_x: bfloat16 [32, 128, 1152], P(('dp', 'seq'))
- grad_w_out: float32 [1152, 1152], P('seq', 'dp')
The draws below stay inside these ranges and needn't reach their ends.
Inputs may be any that keep to these rules, and one draw needn't show every extreme that they name: `clip_patches`: in every group some clip uses all 128 patch slots. `clip_ids`: frame slots of a group are numbered by clip and never fall; every clip from 0 to 3 holds 1 to 4 frames, one clip exactly 4.
All inputs are finite; a program needn't handle non-finite values.
Results may differ from the reference program's by a relative error of at most 0.0085.
The reference program's roundings to bfloat16 on the way count: a program that leaves them out, or rounds other values in their place, can miss the bound.
Values may be sent and summed in bfloat16 or wider, within the bound.
No kernel may reach another device: no remote copies, remote signals or barrier semaphores. Data moves between devices by JAX's collectives and lax.ppermute only.
A program may use at most 128 MiB of HBM per device.

```python
import math
import jax
import jax.numpy as jnp
import numpy as np
from jax import lax

D = 1152
HEADS = 16
CLIPS = 4
STEPS = 16
GROUPS = 4
FRAMES = 8
PATCHES = 128
TOTAL_FRAMES = 32


def draw_clip_patches(key, part):
    key = jax.random.fold_in(key, 11)
    key_counts, key_full = jax.random.split(key)
    counts = jax.random.randint(key_counts, (GROUPS, CLIPS), PATCHES // 4, PATCHES + 1)
    chosen = jax.random.randint(key_full, (GROUPS, 1), 0, CLIPS)
    filled = jnp.where(jnp.arange(CLIPS)[None, :] == chosen, PATCHES, counts)
    return filled.astype(jnp.int32)


def draw_w_qkv(key, part):
    key = jax.random.fold_in(key, 23)
    sample = jnp.clip(jax.random.normal(key, (D, 3 * D), jnp.float32), -6.0, 6.0) / math.sqrt(D)
    return sample.astype(jnp.bfloat16)


def plant(drawn, own_key, smallest, top_value):
    spot = [jax.random.randint(jax.random.fold_in(own_key, axis), (), 0, length) for axis, length in enumerate(drawn.shape)]
    longest = drawn.shape.index(max(drawn.shape))
    neighbour = spot[:longest] + [(spot[longest] + 1) % drawn.shape[longest]] + spot[longest + 1:]
    return drawn.at[tuple(spot)].set(smallest).at[tuple(neighbour)].set(top_value)


def strengthened(entries, own_key, source, target, blocks, factor):
    owner, partner = [(jnp.arange(entries.shape[axis_at]) // (entries.shape[axis_at] // blocks)).reshape([-1 if axis == axis_at else 1 for axis in range(entries.ndim)]) for axis_at in (source, target)]
    chosen = jax.random.permutation(own_key, blocks)[partner]
    strong = (owner == chosen) | (owner == (partner + blocks // 2) % blocks)
    return jnp.where(strong, factor * entries, entries)


def block_scale(key, extent, cuts, smallest, top_value):
    def one(dim, parts):
        heights = jax.random.uniform(jax.random.fold_in(jax.random.fold_in(key, 6), dim), (parts,), jnp.float32, smallest / len(cuts), top_value / len(cuts))
        return jnp.repeat(jnp.exp(heights), extent[dim] // parts).reshape((-1,) + (1,) * (len(extent) - dim - 1))

    gain = one(*cuts[0])
    for cut in cuts[1:]:
        gain = gain * one(*cut)
    return gain


def split_up(amount, total, reach, slope):
    portions = [(1 << 20) // math.isqrt(standing ** slope) + 1 for standing in range(2, amount + 1)]
    rest, holding = total - reach - (amount - 1), [1] * (amount - 1)
    while rest > 0:
        free = [i for i in range(amount - 1) if holding[i] < reach]
        whole, left = sum([portions[i] for i in free]), rest
        for i in free:
            addition = min(reach - holding[i], max(1, left * portions[i] // whole), rest)
            holding[i] = holding[i] + addition
            rest = rest - addition
    return np.array([reach] + holding)


def uneven(rng, amount, total, limit, skew):
    if amount == 2:
        one = jax.random.randint(rng, (), max(1, total - limit), min(limit, total - 1) + 1)
        return jnp.stack([one, total - one])
    lengths = jnp.asarray(split_up(amount, total, limit, skew), jnp.int32)
    pairs = (amount - 1) // 2
    donor, receiver = lengths[1:1 + 2 * pairs:2], lengths[2:2 + 2 * pairs:2]
    slack = jnp.minimum(donor - 1, limit - receiver)
    passed = jax.random.randint(jax.random.fold_in(rng, 1), (pairs,), 0, 1 << 20) % (slack + 1)
    lengths = lengths.at[1:1 + 2 * pairs:2].set(donor - passed).at[2:2 + 2 * pairs:2].set(receiver + passed)
    return lengths[jax.random.permutation(jax.random.fold_in(rng, 2), amount)]


def gaussian(key, dims, scale, reach, cuts=(), dtype=jnp.bfloat16):
    loudness = block_scale(key, dims, cuts, -0.22, 0.18) if cuts else 1.0
    values = jax.random.normal(key, dims, jnp.float32) * scale * loudness
    return jnp.minimum(jnp.maximum(values, -reach), reach).astype(dtype)


def gaussian_with(stream_key, extent, width, bound, shards, heavy, kind=jnp.bfloat16):
    values = width * jax.random.normal(stream_key, extent, jnp.float32)
    if shards:
        values = values * block_scale(stream_key, extent, shards, -0.22, 0.18)
    return jnp.clip(strengthened(values, jax.random.fold_in(stream_key, 3), *heavy), -bound, bound).astype(kind)


def setup_inputs(seed: int = 0) -> dict:
    key_of = jax.random.split(jax.random.key(seed), 9)
    return {
        "frames_x": gaussian(key_of[0], (TOTAL_FRAMES, PATCHES, D), 1.0, 6.0, ((0, 32),)),
        "grad_y": gaussian_with(key_of[1], (TOTAL_FRAMES, PATCHES, D), 1.0, 6.0, ((0, 32),), (0, 2, 32, 2.75)),
        "clip_ids": jax.vmap(lambda own: jnp.searchsorted(jnp.cumsum(uneven(own, CLIPS, FRAMES, FRAMES // 2, 1)), jnp.arange(FRAMES), side="right"))(jax.random.split(key_of[2], GROUPS)).reshape((GROUPS, FRAMES)).astype(jnp.int32),
        "clip_patches": draw_clip_patches(jax.random.fold_in(key_of[8], 71), 0),
        "clip_step": plant(jax.random.randint(key_of[4], (GROUPS, CLIPS), 0, STEPS), jax.random.fold_in(key_of[4], 1), 0, STEPS - 1).astype(jnp.int32),
        "mod_table": gaussian(key_of[5], (STEPS, 3 * D), 0.5, 3.0, (), jnp.float32),
        "w_qkv": draw_w_qkv(jax.random.fold_in(key_of[8], 71), 0),
        "w_out": gaussian(key_of[7], (D, D), D ** -0.5, 0.1875, ((0, 8),)),
    }


def normalize(inputs):
    values = inputs.astype(jnp.float32)
    centred = values - lax.optimization_barrier(jnp.mean(values, axis=-1, keepdims=True))
    inv_sigma = lax.rsqrt(lax.optimization_barrier(jnp.mean(centred * centred, axis=-1, keepdims=True)) + 1e-06)
    return (centred * inv_sigma, inv_sigma)

def split_heads(triple, num_heads):
    frames_all, columns, three_width = triple.shape
    head_size = three_width // 3 // num_heads
    pieces = triple.astype(jnp.float32).reshape(frames_all, columns, 3, num_heads, head_size)
    return (pieces[:, :, 0], pieces[:, :, 1], pieces[:, :, 2], head_size)

def attend_forward(triple, clip_rows, frame_patch, patch_start, num_heads):
    frames_all, columns, three_width = triple.shape
    queries, key_heads, values, head_size = split_heads(triple, num_heads)
    scores = jnp.einsum('fphe,gphe->phfg', queries, key_heads) / math.sqrt(head_size)
    position = patch_start + jnp.arange(columns)
    is_valid = position[None, :] < frame_patch[:, None]
    same_clip = clip_rows[:, None] == clip_rows[None, :]
    diag_mask = jnp.arange(frames_all)[:, None] == jnp.arange(frames_all)[None, :]
    allowed = same_clip[None] & (jnp.transpose(is_valid)[:, None, :] | diag_mask[None])
    scores = jnp.where(allowed[:, None], scores, -jnp.inf)
    largest = lax.optimization_barrier(jnp.max(scores, axis=-1, keepdims=True))
    exponent = jnp.exp(scores - largest)
    weights = exponent / lax.optimization_barrier(jnp.sum(exponent, axis=-1, keepdims=True))
    weights_low = weights.astype(jnp.bfloat16)
    output = jnp.einsum('phfg,gphe->fphe', weights_low.astype(jnp.float32), values)
    output = output.astype(jnp.bfloat16).reshape(frames_all, columns, three_width // 3)
    return (output, weights, weights_low)

def attend_backward(triple, weights, weights_low, grad_out, num_heads):
    frames_all, columns, three_width = triple.shape
    queries, key_heads, values, head_size = split_heads(triple, num_heads)
    grad_heads = grad_out.astype(jnp.float32).reshape(frames_all, columns, num_heads, head_size)
    grad_weights = jnp.einsum('fphe,gphe->phfg', grad_heads, values)
    grad_values = jnp.einsum('phfg,fphe->gphe', weights_low.astype(jnp.float32), grad_heads).astype(jnp.bfloat16)
    inner = lax.optimization_barrier(jnp.sum(weights * grad_weights, axis=-1, keepdims=True))
    grad_scores = (weights * (grad_weights - inner) / math.sqrt(head_size)).astype(jnp.bfloat16)
    grad_scores = grad_scores.astype(jnp.float32)
    grad_queries = jnp.einsum('phfg,gphe->fphe', grad_scores, key_heads).astype(jnp.bfloat16)
    grad_keys = jnp.einsum('phfg,fphe->gphe', grad_scores, queries).astype(jnp.bfloat16)
    stacked = jnp.stack([grad_queries, grad_keys, grad_values], axis=2)
    return stacked.reshape(frames_all, columns, three_width)

def group_pass(frames_x, grad_y, clip_rows, patch_row, step_row, mod_table, w_qkv, w_out):
    model_width = frames_x.shape[-1]
    frame_step = step_row[clip_rows]
    frame_patch = patch_row[clip_rows]
    modulate = mod_table[frame_step]
    shift_mod = modulate[:, :model_width][:, None, :]
    scale_mod = modulate[:, model_width:2 * model_width][:, None, :]
    gate_mod = modulate[:, 2 * model_width:][:, None, :]
    normed, inv_sigma = normalize(frames_x)
    hidden = (normed * (1.0 + scale_mod) + shift_mod).astype(jnp.bfloat16)
    triple = jnp.dot(hidden.reshape(-1, model_width), w_qkv, preferred_element_type=jnp.float32)
    triple = triple.astype(jnp.bfloat16).reshape(FRAMES, PATCHES, 3 * model_width)
    attended, weights, weights_low = attend_forward(triple, clip_rows, frame_patch, 0, HEADS)
    flat_attended = attended.reshape(-1, model_width)
    projected = jnp.dot(flat_attended, w_out, preferred_element_type=jnp.float32).astype(jnp.bfloat16)
    projected = projected.reshape(FRAMES, PATCHES, model_width)
    is_valid = jnp.arange(PATCHES)[None, :] < frame_patch[:, None]
    factor = jnp.where(is_valid[:, :, None], gate_mod, jnp.float32(0.0))
    out_y = (frames_x.astype(jnp.float32) + factor * projected.astype(jnp.float32)).astype(jnp.bfloat16)
    grad_proj = (factor * grad_y.astype(jnp.float32)).astype(jnp.bfloat16)
    flat_grad = grad_proj.reshape(-1, model_width)
    grad_w = jnp.dot(flat_attended.T, flat_grad, preferred_element_type=jnp.float32)
    grad_attn = jnp.dot(flat_grad, w_out.T, preferred_element_type=jnp.float32).astype(jnp.bfloat16)
    grad_attn = grad_attn.reshape(FRAMES, PATCHES, model_width)
    grad_triple = attend_backward(triple, weights, weights_low, grad_attn, HEADS)
    grad_hidden = jnp.dot(grad_triple.reshape(-1, 3 * model_width), w_qkv.T, preferred_element_type=jnp.float32)
    grad_hidden = grad_hidden.astype(jnp.bfloat16).reshape(FRAMES, PATCHES, model_width)
    grad_norm = grad_hidden.astype(jnp.float32) * (1.0 + scale_mod)
    first_mean = lax.optimization_barrier(jnp.mean(grad_norm, axis=-1, keepdims=True))
    second_mean = lax.optimization_barrier(jnp.mean(grad_norm * normed, axis=-1, keepdims=True))
    grad_x = grad_y.astype(jnp.float32) + inv_sigma * (grad_norm - first_mean - normed * second_mean)
    return (out_y, grad_x.astype(jnp.bfloat16), grad_w)

def reference(frames_x, grad_y, clip_ids, clip_patches, clip_step, mod_table, w_qkv, w_out):
    shaped_x = frames_x.reshape(GROUPS, FRAMES, PATCHES, D)
    shaped_grad = grad_y.reshape(GROUPS, FRAMES, PATCHES, D)

    def one_group(inputs):
        return group_pass(inputs[0], inputs[1], inputs[2], inputs[3], inputs[4], mod_table, w_qkv, w_out)
    out_y, grad_x, grad_w = lax.map(one_group, (shaped_x, shaped_grad, clip_ids, clip_patches, clip_step))
    grad_scale = 1.0 / math.sqrt(GROUPS * FRAMES * PATCHES)
    grad_w_out = lax.optimization_barrier(jnp.sum(grad_w, axis=0)) * jnp.float32(grad_scale)
    return (out_y.reshape(TOTAL_FRAMES, PATCHES, D), grad_x.reshape(TOTAL_FRAMES, PATCHES, D), grad_w_out)
```

```python
import functools
import math

import jax
import jax.numpy as jnp
from jax import lax
from jax.experimental import pallas as pl
from jax.experimental.pallas import tpu as pltpu
from jax.sharding import Mesh, PartitionSpec as P

HEADS = 16
CORES = 2
AXES = ("y", "c", "z", "x")
BLOCK = 16
VMEM_LIMIT = 56 * 1024 * 1024
BF16 = jnp.bfloat16
F32 = jnp.float32


def dot(left, right):
    return jnp.dot(left, right, preferred_element_type=F32)


def dot_t(left, right):
    return lax.dot_general(left, right, (((1,), (1,)), ((), ())), preferred_element_type=F32)


def t_dot(left, right):
    return lax.dot_general(left, right, (((0,), (0,)), ((), ())), preferred_element_type=F32)


def normalize(values):
    centred = values - jnp.mean(values, axis=-1, keepdims=True)
    inv_sigma = lax.rsqrt(jnp.mean(centred * centred, axis=-1, keepdims=True) + 1e-06)
    return centred * inv_sigma, inv_sigma


class Layout:
    def __init__(self, mesh):
        groups, seq = mesh.shape["dp"], mesh.shape["seq"]
        self.nc = CORES
        self.ny = groups // CORES
        self.nz = groups
        self.nx = seq // self.nz
        self.chips = self.ny * self.nx
        self.frames = seq

    def linear(self, y, c, z, x):
        return ((y * self.nc + c) * self.nz + z) * self.nx + x

    def perm(self, move):
        pairs = []
        for y in range(self.ny):
            for c in range(self.nc):
                for z in range(self.nz):
                    for x in range(self.nx):
                        pairs.append((self.linear(y, c, z, x), self.linear(*move(y, c, z, x))))
        return pairs

    def to_plane(self, k):
        return self.perm(lambda y, c, z, x: (z % self.ny, (z // self.ny) ^ k, c * self.ny + y, x))

    def from_plane(self, k):
        return [(target, source) for source, target in self.to_plane(k)]

    def swap(self, ky=0, kc=0, kz=0, kx=0):
        return self.perm(lambda y, c, z, x: (y ^ ky, c ^ kc, z ^ kz, x ^ kx))

    def chip_of(self, k):
        return k // self.nx, k % self.nx

    def slots(self):
        return [(k, j) for k in range(self.chips) for j in range(self.nc)]


def slot_scalars(lay, pos_ref, info_ref, slot):
    k, j = slot
    ky, kx = lay.chip_of(k)
    z_frame = (pos_ref[1] ^ j) * lay.ny + (pos_ref[0] ^ ky)
    frame = z_frame * lay.nx + (pos_ref[3] ^ kx)
    clip = info_ref[frame]
    clips = (info_ref.shape[0] - lay.frames) // 2
    return clip, info_ref[lay.frames + clip], info_ref[lay.frames + clips + clip]


def table_row(mod_ref, step, part, width):
    return mod_ref[pl.ds(step, 1), part * width : (part + 1) * width]


def allowed_pairs(lay, pos_ref, info_ref, patch_base):
    rows = lay.frames * BLOCK
    row_slot = lax.broadcasted_iota(jnp.int32, (rows, 1), 0) // BLOCK
    col_slot = lax.broadcasted_iota(jnp.int32, (1, rows), 1) // BLOCK
    row_clip = jnp.zeros((rows, 1), jnp.int32)
    col_clip = jnp.zeros((1, rows), jnp.int32)
    col_limit = jnp.zeros((1, rows), jnp.int32)
    for t, slot in enumerate(lay.slots()):
        clip, limit, _ = slot_scalars(lay, pos_ref, info_ref, slot)
        row_clip = jnp.where(row_slot == t, clip, row_clip)
        col_clip = jnp.where(col_slot == t, clip, col_clip)
        col_limit = jnp.where(col_slot == t, limit, col_limit)
    row_patch = lax.broadcasted_iota(jnp.int32, (rows, 1), 0) % BLOCK
    col_patch = lax.broadcasted_iota(jnp.int32, (1, rows), 1) % BLOCK
    row_key = row_clip * BLOCK + row_patch
    col_key = col_clip * BLOCK + col_patch
    col_valid = (patch_base + col_patch < col_limit).astype(jnp.int32)
    row_index = lax.broadcasted_iota(jnp.int32, (rows, rows), 0)
    col_index = lax.broadcasted_iota(jnp.int32, (rows, rows), 1)
    return (row_key == col_key) & ((col_valid > 0) | (row_index == col_index))


def head_mask(values, head, head_size):
    lane = lax.broadcasted_iota(jnp.int32, (1, values.shape[1]), 1)
    inside = (lane >= head * head_size) & (lane < (head + 1) * head_size)
    return jnp.where(inside, values, jnp.zeros_like(values))


def softmax(scores, allowed):
    scores = jnp.where(allowed, scores, -jnp.inf)
    exponent = jnp.exp(scores - jnp.max(scores, axis=-1, keepdims=True))
    return exponent / jnp.sum(exponent, axis=-1, keepdims=True)


def fill_weights(lay, pos_ref, w_refs, w_scr):
    halves = w_scr.shape[0]
    rows = w_refs[0].shape[0]
    for h in range(halves):
        half = (pos_ref[1] ^ h) if halves > 1 else 0
        for k in range(lay.nz):
            start = pl.multiple_of((pos_ref[2] ^ k) * rows, 16)
            w_scr[half, pl.ds(start, rows), :] = w_refs[h * lay.nz + k][...]


def forward_kernel(lay, halves, half_heads, pos_ref, info_ref, *refs):
    x_refs, refs = refs[: lay.frames], refs[lay.frames :]
    w_refs, refs = refs[: halves * lay.nz], refs[halves * lay.nz :]
    mod_ref, q_ref, k_ref, v_ref, *refs = refs
    att_refs, (w_scr, hid_scr) = refs[: lay.chips], refs[lay.chips :]
    width = hid_scr.shape[1]
    cols = w_scr.shape[2] // 3
    head_size = cols // half_heads
    patches = q_ref.shape[2] * pl.num_programs(0)

    @pl.when(pl.program_id(0) == 0)
    def _():
        fill_weights(lay, pos_ref, w_refs, w_scr)

    for t, slot in enumerate(lay.slots()):
        _, _, step = slot_scalars(lay, pos_ref, info_ref, slot)
        normed, _ = normalize(x_refs[t][...].astype(F32))
        shift, scale = table_row(mod_ref, step, 0, width), table_row(mod_ref, step, 1, width)
        hid_scr[t * BLOCK : (t + 1) * BLOCK, :] = (normed * (1.0 + scale) + shift).astype(BF16)

    patch_base = pos_ref[1] * patches + pl.program_id(0) * BLOCK
    allowed = allowed_pairs(lay, pos_ref, info_ref, patch_base)
    outputs = []
    for h in range(halves):
        triple = dot(hid_scr[...], w_scr[h])
        queries = triple[:, :cols].astype(BF16)
        keys = triple[:, cols : 2 * cols].astype(BF16)
        values = triple[:, 2 * cols :].astype(BF16)
        q_ref[h] = queries.reshape(q_ref.shape[1:])
        k_ref[h] = keys.reshape(k_ref.shape[1:])
        v_ref[h] = values.reshape(v_ref.shape[1:])
        output = jnp.zeros(queries.shape, F32)
        for head in range(half_heads):
            scores = dot_t(head_mask(queries, head, head_size), keys) * (1.0 / math.sqrt(head_size))
            weights = softmax(scores, allowed).astype(BF16)
            output = output + dot(weights, head_mask(values, head, head_size))
        outputs.append(output)
    attended = jnp.concatenate(outputs, axis=1) if halves > 1 else outputs[0]
    attended = attended.astype(BF16).reshape(lay.frames, BLOCK, attended.shape[1])
    for k in range(lay.chips):
        att_refs[k][...] = attended[k * lay.nc : (k + 1) * lay.nc]


def backward_kernel(lay, halves, half_heads, pos_ref, info_ref, *refs):
    g_refs, refs = refs[: lay.frames], refs[lay.frames :]
    w_refs, refs = refs[: halves * lay.nz], refs[halves * lay.nz :]
    mod_ref, wo_ref, q_ref, k_ref, v_ref, *refs = refs
    att_refs, refs = refs[: lay.chips], refs[lay.chips :]
    gh_refs, refs = refs[: lay.chips], refs[lay.chips :]
    gw_ref, w_scr, gp_scr, acc_scr = refs
    width = gp_scr.shape[1]
    cols = w_scr.shape[2] // 3
    head_size = cols // half_heads
    patches = q_ref.shape[2] * pl.num_programs(0)
    rows = gp_scr.shape[0]

    @pl.when(pl.program_id(0) == 0)
    def _():
        fill_weights(lay, pos_ref, w_refs, w_scr)
        acc_scr[...] = jnp.zeros_like(acc_scr)

    patch_base = pos_ref[1] * patches + pl.program_id(0) * BLOCK
    patch = patch_base + lax.broadcasted_iota(jnp.int32, (BLOCK, 1), 0)
    for t, slot in enumerate(lay.slots()):
        _, limit, step = slot_scalars(lay, pos_ref, info_ref, slot)
        factor = jnp.where(patch < limit, table_row(mod_ref, step, 2, width), 0.0)
        grad_proj = factor * g_refs[t][...].astype(F32)
        gp_scr[t * BLOCK : (t + 1) * BLOCK, :] = grad_proj.astype(BF16)

    attended = jnp.concatenate([ref[...] for ref in att_refs], axis=0).reshape(rows, -1)
    acc_scr[...] += t_dot(attended, gp_scr[...])
    grad_attn = dot_t(gp_scr[...], wo_ref[0])

    allowed = allowed_pairs(lay, pos_ref, info_ref, patch_base)
    scaling = 1.0 / math.sqrt(head_size)
    total = jnp.zeros((rows, width), F32)
    for h in range(halves):
        queries = q_ref[h].reshape(rows, cols)
        keys = k_ref[h].reshape(rows, cols)
        values = v_ref[h].reshape(rows, cols)
        grad_out = grad_attn[:, h * cols : (h + 1) * cols].astype(BF16)
        grad_queries = jnp.zeros((rows, cols), F32)
        grad_keys = jnp.zeros((rows, cols), F32)
        grad_values = jnp.zeros((rows, cols), F32)
        for head in range(half_heads):
            q_head = head_mask(queries, head, head_size)
            g_head = head_mask(grad_out, head, head_size)
            weights = softmax(dot_t(q_head, keys) * scaling, allowed)
            grad_weights = dot_t(g_head, values)
            grad_values = grad_values + t_dot(weights.astype(BF16), g_head)
            inner = jnp.sum(weights * grad_weights, axis=-1, keepdims=True)
            grad_scores = (weights * (grad_weights - inner) * scaling).astype(BF16)
            grad_queries = grad_queries + dot(grad_scores, head_mask(keys, head, head_size))
            grad_keys = grad_keys + t_dot(grad_scores, q_head)
        grad_triple = jnp.concatenate([grad_queries, grad_keys, grad_values], axis=1).astype(BF16)
        total = total + dot_t(grad_triple, w_scr[h])
    total = total.reshape(lay.frames, BLOCK, width)
    for k in range(lay.chips):
        gh_refs[k][...] = total[k * lay.nc : (k + 1) * lay.nc].astype(gh_refs[k].dtype)

    @pl.when(pl.program_id(0) == pl.num_programs(0) - 1)
    def _():
        part = gw_ref.shape[2]
        for d in range(gw_ref.shape[0]):
            gw_ref[d] = acc_scr[:, d * part : (d + 1) * part]


def output_kernel(lay, pos_ref, info_ref, *refs):
    x_refs, refs = refs[: lay.nc], refs[lay.nc :]
    att_refs, refs = refs[: lay.chips], refs[lay.chips :]
    wo_ref, mod_ref, *out_refs = refs
    _, patches, width = att_refs[0].shape
    own_chip = pos_ref[0] * lay.nx + pos_ref[3]
    model = x_refs[0].shape[1]
    total = jnp.zeros((lay.nc * patches, model), F32)
    for k in range(lay.chips):
        total = total + dot(att_refs[k][...].reshape(lay.nc * patches, width), wo_ref[own_chip ^ k])
    patch = pos_ref[1] * patches + lax.broadcasted_iota(jnp.int32, (patches, 1), 0)
    for j in range(lay.nc):
        _, limit, step = slot_scalars(lay, pos_ref, info_ref, (0, j))
        factor = jnp.where(patch < limit, table_row(mod_ref, step, 2, model), 0.0)
        projected = total[j * patches : (j + 1) * patches].astype(BF16).astype(F32)
        out_refs[j][...] = (x_refs[j][...].astype(F32) + factor * projected).astype(BF16)


def input_grad_kernel(lay, pos_ref, info_ref, *refs):
    x_refs, refs = refs[: lay.nc], refs[lay.nc :]
    g_refs, refs = refs[: lay.nc], refs[lay.nc :]
    gh_refs, refs = refs[: lay.chips], refs[lay.chips :]
    mod_ref, *out_refs = refs
    model = x_refs[0].shape[1]
    for j in range(lay.nc):
        _, _, step = slot_scalars(lay, pos_ref, info_ref, (0, j))
        grad_hidden = gh_refs[0][j]
        for k in range(1, lay.chips):
            grad_hidden = grad_hidden + gh_refs[k][j].astype(F32)
        grad_hidden = grad_hidden.astype(BF16).astype(F32)
        normed, inv_sigma = normalize(x_refs[j][...].astype(F32))
        grad_norm = grad_hidden * (1.0 + table_row(mod_ref, step, 1, model))
        first_mean = jnp.mean(grad_norm, axis=-1, keepdims=True)
        second_mean = jnp.mean(grad_norm * normed, axis=-1, keepdims=True)
        grad_x = g_refs[j][...].astype(F32) + inv_sigma * (
            grad_norm - first_mean - normed * second_mean
        )
        out_refs[j][...] = grad_x.astype(BF16)


def whole_spec(shape):
    return pl.BlockSpec(shape, lambda *_: (0,) * len(shape))


def params():
    return pltpu.CompilerParams(vmem_limit_bytes=VMEM_LIMIT)


def struct(shape, dtype=BF16):
    return jax.ShapeDtypeStruct(shape, dtype)


def pieces_of(lay, own, indices, axis_swap, count):
    return [own] + [lax.ppermute(own, AXES, axis_swap(k)) for k in range(1, count)]


def local(lay, frames_x, grad_y, clip_ids, clip_patches, clip_step, mod_table, w_qkv, w_out):
    y, c, z, x = (lax.axis_index(name) for name in AXES)
    _, patches, model = frames_x.shape
    half = patches // lay.nc
    chips, nc, nx, ny, nz = lay.chips, lay.nc, lay.nx, lay.ny, lay.nz
    chip_heads = HEADS // chips
    head_size = model // HEADS
    halves = 2 if chip_heads % 2 == 0 else 1
    half_heads = chip_heads // halves
    cols = half_heads * head_size
    chip_width = chip_heads * head_size
    rows = w_qkv.shape[0]
    blocks = half // BLOCK

    def to_plane(frame):
        own_half = z // ny
        return [
            lax.ppermute(
                lax.dynamic_slice_in_dim(frame[0], (own_half ^ k) * half, half),
                AXES,
                lay.to_plane(k),
            )
            for k in range(nc)
        ]

    def from_plane(parts):
        own_half = z // ny
        got = [lax.ppermute(part, AXES, lay.from_plane(k)) for k, part in enumerate(parts)]
        first = jnp.where(own_half == 0, got[0], got[1])
        second = jnp.where(own_half == 0, got[1], got[0])
        return jnp.concatenate([first, second], axis=0)[None]

    def chip_swap(k):
        ky, kx = lay.chip_of(k)
        return lay.swap(ky=ky, kx=kx)

    def over_chips(parts):
        return list(parts) + [
            lax.ppermute(part, AXES, chip_swap(k)) for k in range(1, chips) for part in parts
        ]

    info = jnp.concatenate([clip_ids[0], clip_patches[0], clip_step[0]])[None]
    info = lax.ppermute(info, AXES, lay.to_plane(0))[0]
    pos = jnp.stack([y, c, z, x]).astype(jnp.int32)
    x_own = to_plane(frames_x)
    x_all = over_chips(x_own)

    split = w_qkv.reshape(rows, 3, chips, halves, cols)
    mine = c if halves > 1 else 0

    def columns_of(chip):
        part = lax.dynamic_index_in_dim(split, chip, axis=2, keepdims=False)
        return lax.dynamic_index_in_dim(part, mine, axis=2, keepdims=False).reshape(rows, 3 * cols)

    by_x = [columns_of(y * nx + x)] + [
        lax.ppermute(columns_of(y * nx + (x ^ kx)), AXES, lay.swap(kx=kx)) for kx in range(1, nx)
    ]
    stacked = jnp.stack(by_x)
    ordered = [
        lax.dynamic_index_in_dim(stacked, x ^ i, axis=0, keepdims=False) for i in range(nx)
    ]
    w_own = jnp.concatenate(ordered, axis=0)
    w_pieces = [w_own] + [lax.ppermute(w_own, AXES, lay.swap(kz=kz)) for kz in range(1, nz)]
    if halves > 1:
        w_pieces = w_pieces + [lax.ppermute(piece, AXES, lay.swap(kc=1)) for piece in w_pieces]

    groups = ny * nc
    quarter = model // groups
    wo = lax.dynamic_slice_in_dim(w_out, (y * nc + c) * quarter, quarter, axis=1)
    wo = lax.all_gather(wo, ("z", "x"), axis=0, tiled=True)
    wo = lax.all_gather(wo, ("y", "c"), axis=1, tiled=True)
    wo = wo.reshape(chips, chip_width, model)

    g_own = to_plane(grad_y)
    g_all = over_chips(g_own)

    frame_spec = pl.BlockSpec((BLOCK, model), lambda i, *_: (i, 0))
    triple_spec = pl.BlockSpec((halves, lay.frames, BLOCK, cols), lambda i, *_: (0, 0, i, 0))
    att_spec = pl.BlockSpec((nc, BLOCK, chip_width), lambda i, *_: (0, i, 0))
    gh_spec = pl.BlockSpec((nc, BLOCK, model), lambda i, *_: (0, i, 0))
    w_specs = [whole_spec(piece.shape) for piece in w_pieces]
    w_scratch = pltpu.VMEM((halves, model, 3 * cols), BF16)
    triple_shape = struct((halves, lay.frames, half, cols))
    tokens = lay.frames * BLOCK

    queries, keys, values, *att = pl.pallas_call(
        functools.partial(forward_kernel, lay, halves, half_heads),
        grid_spec=pltpu.PrefetchScalarGridSpec(
            num_scalar_prefetch=2,
            grid=(blocks,),
            in_specs=[frame_spec] * lay.frames + w_specs + [whole_spec(mod_table.shape)],
            out_specs=[triple_spec] * 3 + [att_spec] * chips,
            scratch_shapes=[w_scratch, pltpu.VMEM((tokens, model), BF16)],
        ),
        out_shape=[triple_shape] * 3 + [struct((nc, half, chip_width))] * chips,
        compiler_params=params(),
        name="forward",
    )(pos, info, *x_all, *w_pieces, mod_table)

    att_own = [att[0]] + [
        lax.ppermute(att[k], AXES, chip_swap(k)) for k in range(1, chips)
    ]

    *partial_sums, grad_w = pl.pallas_call(
        functools.partial(backward_kernel, lay, halves, half_heads),
        grid_spec=pltpu.PrefetchScalarGridSpec(
            num_scalar_prefetch=2,
            grid=(blocks,),
            in_specs=[frame_spec] * lay.frames
            + w_specs
            + [
                whole_spec(mod_table.shape),
                pl.BlockSpec(
                    (1, chip_width, model), lambda i, pos_ref, _: (pos_ref[0] * nx + pos_ref[3], 0, 0)
                ),
            ]
            + [triple_spec] * 3
            + [att_spec] * chips,
            out_specs=[gh_spec] * chips + [whole_spec((groups, chip_width, quarter))],
            scratch_shapes=[
                w_scratch,
                pltpu.VMEM((tokens, model), BF16),
                pltpu.VMEM((chip_width, model), F32),
            ],
        ),
        out_shape=[struct((nc, half, model), F32)]
        + [struct((nc, half, model))] * (chips - 1)
        + [struct((groups, chip_width, quarter), F32)],
        compiler_params=params(),
        name="backward",
    )(pos, info, *g_all, *w_pieces, mod_table, wo, queries, keys, values, *att)

    gh_own = [partial_sums[0]] + [
        lax.ppermute(partial_sums[k], AXES, chip_swap(k)) for k in range(1, chips)
    ]

    flat_spec = whole_spec((half, model))
    out_parts = pl.pallas_call(
        functools.partial(output_kernel, lay),
        grid_spec=pltpu.PrefetchScalarGridSpec(
            num_scalar_prefetch=2,
            grid=(1,),
            in_specs=[flat_spec] * nc
            + [whole_spec((nc, half, chip_width))] * chips
            + [whole_spec(wo.shape), whole_spec(mod_table.shape)],
            out_specs=[flat_spec] * nc,
        ),
        out_shape=[struct((half, model))] * nc,
        compiler_params=params(),
        name="output",
    )(pos, info, *x_own, *att_own, wo, mod_table)
    out_y = from_plane(out_parts)

    grad_parts = pl.pallas_call(
        functools.partial(input_grad_kernel, lay),
        grid_spec=pltpu.PrefetchScalarGridSpec(
            num_scalar_prefetch=2,
            grid=(blocks,),
            in_specs=[frame_spec] * (2 * nc) + [gh_spec] * chips + [whole_spec(mod_table.shape)],
            out_specs=[frame_spec] * nc,
        ),
        out_shape=[struct((half, model))] * nc,
        compiler_params=params(),
        name="input_grad",
    )(pos, info, *x_own, *g_own, *gh_own, mod_table)
    grad_x = from_plane(grad_parts)

    grad_w = grad_w.reshape(ny, nc, chip_width, quarter)
    kept = lax.dynamic_index_in_dim(grad_w, c, axis=1, keepdims=False)
    sent = lax.dynamic_index_in_dim(grad_w, 1 - c, axis=1, keepdims=False)
    grad_w = kept + lax.ppermute(sent, AXES, lay.swap(kc=1))
    by_y = [lax.dynamic_index_in_dim(grad_w, y, axis=0, keepdims=False)] + [
        lax.ppermute(
            lax.dynamic_index_in_dim(grad_w, y ^ ky, axis=0, keepdims=False), AXES, lay.swap(ky=ky)
        )
        for ky in range(1, ny)
    ]
    by_y = jnp.stack(by_y).reshape(ny, nc, rows, quarter)
    if nx == nc:
        kept = lax.dynamic_index_in_dim(by_y, x, axis=1, keepdims=False)
        sent = lax.dynamic_index_in_dim(by_y, 1 - x, axis=1, keepdims=False)
        got = lax.ppermute(sent, AXES, lay.swap(kx=1))
        both = jnp.stack([kept, got], axis=1)
        pick = lambda m: m ^ x
    else:
        both = lax.all_gather(by_y, "x", axis=1, tiled=False)
        both = both.reshape(ny, nc, nx, rows, quarter)
        both = lax.dynamic_index_in_dim(both, x, axis=2, keepdims=False)
        pick = lambda m: m

    def for_plane(target):
        source_y, m = target // nc, target % nc
        return both[y ^ source_y, pick(m)]

    total = for_plane(z)
    for kz in range(1, nz):
        total = total + lax.ppermute(for_plane(z ^ kz), AXES, lay.swap(kz=kz))
    grad_w_out = total * jnp.float32(1.0 / math.sqrt(groups * lay.frames * patches))
    return out_y, grad_x, grad_w_out


def solution(mesh):
    lay = Layout(mesh)
    grid = Mesh(mesh.devices.reshape(lay.ny, lay.nc, lay.nz, lay.nx), AXES)
    rows, cols = ("z", "x"), ("y", "c")
    frame = P(AXES, None, None)
    group = P(cols, None)
    return jax.shard_map(
        functools.partial(local, lay),
        mesh=grid,
        in_specs=(frame, frame, group, group, group, P(), P(rows, None), P(rows, None)),
        out_specs=(frame, frame, P(rows, cols)),
        check_vma=False,
    )
```

```python
import functools
import math

import jax
import jax.numpy as jnp
from jax import lax
from jax.experimental import pallas as pl
from jax.experimental.pallas import tpu as pltpu
from jax.sharding import Mesh, PartitionSpec as P

HEADS = 16
CORES = 2
AXES = ("y", "c", "z", "x")
BLOCK = 16
VMEM_LIMIT = 56 * 1024 * 1024
BF16 = jnp.bfloat16
F32 = jnp.float32


def dot(left, right):
    return jnp.dot(left, right, preferred_element_type=F32)


def dot_t(left, right):
    return lax.dot_general(left, right, (((1,), (1,)), ((), ())), preferred_element_type=F32)


def t_dot(left, right):
    return lax.dot_general(left, right, (((0,), (0,)), ((), ())), preferred_element_type=F32)


def normalize(values):
    centred = values - jnp.mean(values, axis=-1, keepdims=True)
    inv_sigma = lax.rsqrt(jnp.mean(centred * centred, axis=-1, keepdims=True) + 1e-06)
    return centred * inv_sigma, inv_sigma


class Layout:
    def __init__(self, mesh):
        groups, seq = mesh.shape["dp"], mesh.shape["seq"]
        self.nc = CORES
        self.ny = groups // CORES
        self.nz = groups
        self.nx = seq // self.nz
        self.chips = self.ny * self.nx
        self.frames = seq

    def linear(self, y, c, z, x):
        return ((y * self.nc + c) * self.nz + z) * self.nx + x

    def perm(self, move):
        pairs = []
        for y in range(self.ny):
            for c in range(self.nc):
                for z in range(self.nz):
                    for x in range(self.nx):
                        pairs.append((self.linear(y, c, z, x), self.linear(*move(y, c, z, x))))
        return pairs

    def to_plane(self, k):
        return self.perm(lambda y, c, z, x: (z % self.ny, (z // self.ny) ^ k, c * self.ny + y, x))

    def from_plane(self, k):
        return [(target, source) for source, target in self.to_plane(k)]

    def swap(self, ky=0, kc=0, kz=0, kx=0):
        return self.perm(lambda y, c, z, x: (y ^ ky, c ^ kc, z ^ kz, x ^ kx))

    def rows_to_chip(self):
        def move(y, c, z, x):
            s = z * self.nx + x
            chip, core = s // self.nc, s % self.nc
            return chip // self.nx, core, c * self.ny + y, chip % self.nx

        return self.perm(move)

    def to_owner(self, j):
        def move(y, c, z, x):
            s = self.nc * (y * self.nx + x) + c
            d = z ^ j
            return d // self.nc, d % self.nc, s // self.nx, s % self.nx

        return self.perm(move)

    def chip_of(self, k):
        return k // self.nx, k % self.nx

    def slots(self):
        return [(k, j) for k in range(self.chips) for j in range(self.nc)]


def slot_scalars(lay, pos_ref, info_ref, slot):
    k, j = slot
    ky, kx = lay.chip_of(k)
    z_frame = (pos_ref[1] ^ j) * lay.ny + (pos_ref[0] ^ ky)
    frame = z_frame * lay.nx + (pos_ref[3] ^ kx)
    clip = info_ref[frame]
    clips = (info_ref.shape[0] - lay.frames) // 2
    return clip, info_ref[lay.frames + clip], info_ref[lay.frames + clips + clip]


def table_row(mod_ref, step, part, width):
    return mod_ref[pl.ds(step, 1), part * width : (part + 1) * width]


def allowed_pairs(lay, pos_ref, info_ref, patch_base):
    rows = lay.frames * BLOCK
    row_slot = lax.broadcasted_iota(jnp.int32, (rows, 1), 0) // BLOCK
    col_slot = lax.broadcasted_iota(jnp.int32, (1, rows), 1) // BLOCK
    row_clip = jnp.zeros((rows, 1), jnp.int32)
    row_limit = jnp.zeros((rows, 1), jnp.int32)
    col_clip = jnp.zeros((1, rows), jnp.int32)
    for t, slot in enumerate(lay.slots()):
        clip, limit, _ = slot_scalars(lay, pos_ref, info_ref, slot)
        row_clip = jnp.where(row_slot == t, clip, row_clip)
        row_limit = jnp.where(row_slot == t, limit, row_limit)
        col_clip = jnp.where(col_slot == t, clip, col_clip)
    row_patch = lax.broadcasted_iota(jnp.int32, (rows, 1), 0) % BLOCK
    col_patch = lax.broadcasted_iota(jnp.int32, (1, rows), 1) % BLOCK
    row_key = row_clip * BLOCK + row_patch
    col_key = col_clip * BLOCK + col_patch
    row_valid = (patch_base + row_patch < row_limit).astype(jnp.int32)
    row_index = lax.broadcasted_iota(jnp.int32, (rows, rows), 0)
    col_index = lax.broadcasted_iota(jnp.int32, (rows, rows), 1)
    return (row_key == col_key) & ((row_valid > 0) | (row_index == col_index))


def head_mask(values, head, head_size):
    lane = lax.broadcasted_iota(jnp.int32, (1, values.shape[1]), 1)
    inside = (lane >= head * head_size) & (lane < (head + 1) * head_size)
    return jnp.where(inside, values, jnp.zeros_like(values))


def softmax(scores, allowed):
    scores = jnp.where(allowed, scores, -jnp.inf)
    exponent = jnp.exp(scores - jnp.max(scores, axis=0, keepdims=True))
    return exponent / jnp.sum(exponent, axis=0, keepdims=True)


def patch_blocks(array, block):
    part = array[:, block * BLOCK : (block + 1) * BLOCK, :]
    return part.reshape(part.shape[0] * BLOCK, part.shape[2])


def pick_kernel(lay, halves, cols, pos_ref, w_ref, *out_refs):
    model = w_ref.shape[1] // 3
    for k, out_ref in enumerate(out_refs):
        chip = pos_ref[0] * lay.nx + (pos_ref[3] ^ k)
        want = chip * halves + (pos_ref[1] if halves > 1 else 0)
        for v in range(lay.chips * halves):

            @pl.when(want == v)
            def _(v=v, out_ref=out_ref):
                parts = [
                    w_ref[:, p * model + v * cols : p * model + (v + 1) * cols].astype(F32)
                    for p in range(3)
                ]
                out_ref[...] = jnp.concatenate(parts, axis=1).astype(BF16)


def forward_kernel(lay, halves, half_heads, pos_ref, info_ref, *refs):
    x_refs, refs = refs[: lay.frames], refs[lay.frames :]
    w_refs, refs = refs[:halves], refs[halves:]
    mod_ref, q_ref, k_ref, v_ref, *refs = refs
    att_refs, (hid_scr,) = refs[: lay.chips], refs[lay.chips :]
    model = hid_scr.shape[1]
    cols = w_refs[0].shape[1] // 3
    head_size = cols // half_heads
    step_patches = x_refs[0].shape[0]
    patches = step_patches * pl.num_programs(0)

    for t, slot in enumerate(lay.slots()):
        _, _, step = slot_scalars(lay, pos_ref, info_ref, slot)
        normed, _ = normalize(x_refs[t][...].astype(F32))
        shift, scale = table_row(mod_ref, step, 0, model), table_row(mod_ref, step, 1, model)
        hid_scr[t * step_patches : (t + 1) * step_patches, :] = (
            normed * (1.0 + scale) + shift
        ).astype(BF16)

    for h in range(halves):
        triple = dot(hid_scr[...], w_refs[h][...])
        for n, ref in enumerate((q_ref, k_ref, v_ref)):
            ref[h] = triple[:, n * cols : (n + 1) * cols].astype(BF16).reshape(ref.shape[1:])

    for b in range(step_patches // BLOCK):
        patch_base = pos_ref[1] * patches + pl.program_id(0) * step_patches + b * BLOCK
        allowed = allowed_pairs(lay, pos_ref, info_ref, patch_base)
        outputs = []
        for h in range(halves):
            queries, keys, values = (patch_blocks(ref[h], b) for ref in (q_ref, k_ref, v_ref))
            output = jnp.zeros(queries.shape, F32)
            for head in range(half_heads):
                scores = dot_t(head_mask(keys, head, head_size), queries)
                weights = softmax(scores * (1.0 / math.sqrt(head_size)), allowed).astype(BF16)
                output = output + t_dot(weights, head_mask(values, head, head_size))
            outputs.append(output)
        if halves > 1:
            first = jnp.where(pos_ref[1] == 0, outputs[0], outputs[1])
            second = jnp.where(pos_ref[1] == 0, outputs[1], outputs[0])
            outputs = [jnp.concatenate([first, second], axis=1)]
        attended = outputs[0].astype(BF16).reshape(lay.frames, BLOCK, halves * cols)
        for k in range(lay.chips):
            att_refs[k][:, b * BLOCK : (b + 1) * BLOCK, :] = attended[k * lay.nc : (k + 1) * lay.nc]


def projection_grad_kernel(lay, halves, pos_ref, info_ref, *refs):
    g_refs, refs = refs[: lay.frames], refs[lay.frames :]
    att_refs, refs = refs[: lay.chips], refs[lay.chips :]
    wo_refs, refs = refs[: lay.nc], refs[lay.nc :]
    mod_ref, ga_ref, kept_ref, sent_ref, gp_scr, wo_scr, acc_scr = refs
    rows, model = gp_scr.shape
    step_patches = g_refs[0].shape[0]
    patches = step_patches * pl.num_programs(0)
    width = att_refs[0].shape[2]
    block_rows = width // lay.nc
    is_first = pos_ref[1] == 0

    @pl.when(pl.program_id(0) == 0)
    def _():
        acc_scr[...] = jnp.zeros_like(acc_scr)
        own, other = wo_refs[0][...].astype(F32), wo_refs[1][...].astype(F32)
        both = [jnp.where(is_first, own, other), jnp.where(is_first, other, own)]
        wo_scr[...] = jnp.concatenate(both, axis=0).astype(BF16)

    patch_base = pos_ref[1] * patches + pl.program_id(0) * step_patches
    patch = patch_base + lax.broadcasted_iota(jnp.int32, (step_patches, 1), 0)
    for t, slot in enumerate(lay.slots()):
        _, limit, step = slot_scalars(lay, pos_ref, info_ref, slot)
        factor = jnp.where(patch < limit, table_row(mod_ref, step, 2, model), 0.0)
        grad_proj = factor * g_refs[t][...].astype(F32)
        gp_scr[t * step_patches : (t + 1) * step_patches, :] = grad_proj.astype(BF16)

    attended = jnp.concatenate([ref[...] for ref in att_refs], axis=0).reshape(rows, width)
    acc_scr[...] += t_dot(attended, gp_scr[...])
    grad_attn = dot_t(gp_scr[...], wo_scr[...])
    part = width // halves
    for h in range(halves):
        ga_ref[h] = grad_attn[:, h * part : (h + 1) * part].astype(BF16).reshape(ga_ref.shape[1:])

    @pl.when(pl.program_id(0) == pl.num_programs(0) - 1)
    def _():
        first, second = acc_scr[:block_rows, :], acc_scr[block_rows:, :]
        kept_ref[...] = jnp.where(is_first, first, second)
        sent_ref[...] = jnp.where(is_first, second, first)


def spread_kernel(lay, pos_ref, kept_ref, got_ref, *refs):
    out_refs, scr = refs[:-1], refs[-1]
    total = kept_ref[...] + got_ref[...]
    part = scr.shape[2]
    for d in range(scr.shape[0]):
        scr[d] = total[:, d * part : (d + 1) * part]
    for j, ref in enumerate(out_refs):
        ref[...] = scr[pos_ref[2] ^ j]


def backward_kernel(lay, halves, half_heads, pos_ref, info_ref, *refs):
    w_refs, refs = refs[:halves], refs[halves:]
    q_ref, k_ref, v_ref, ga_ref, *refs = refs
    gh_refs, (gt_scr,) = refs[: lay.chips], refs[lay.chips :]
    _, frames, step_patches, cols = q_ref.shape
    model = w_refs[0].shape[0]
    head_size = cols // half_heads
    patches = step_patches * pl.num_programs(0)
    scaling = 1.0 / math.sqrt(head_size)

    for b in range(step_patches // BLOCK):
        patch_base = pos_ref[1] * patches + pl.program_id(0) * step_patches + b * BLOCK
        allowed = allowed_pairs(lay, pos_ref, info_ref, patch_base)
        for h in range(halves):
            queries, keys, values = (patch_blocks(ref[h], b) for ref in (q_ref, k_ref, v_ref))
            grad_out = patch_blocks(ga_ref[(pos_ref[1] ^ h) if halves > 1 else 0], b)
            grad_queries = jnp.zeros(queries.shape, F32)
            grad_keys = jnp.zeros(queries.shape, F32)
            grad_values = jnp.zeros(queries.shape, F32)
            for head in range(half_heads):
                k_head = head_mask(keys, head, head_size)
                g_head = head_mask(grad_out, head, head_size)
                weights = softmax(dot_t(k_head, queries) * scaling, allowed)
                grad_weights = dot_t(values, g_head)
                grad_values = grad_values + dot(weights.astype(BF16), g_head)
                inner = jnp.sum(weights * grad_weights, axis=0, keepdims=True)
                grad_scores = (weights * (grad_weights - inner) * scaling).astype(BF16)
                grad_queries = grad_queries + t_dot(grad_scores, k_head)
                grad_keys = grad_keys + dot(grad_scores, head_mask(queries, head, head_size))
            grads = jnp.concatenate([grad_queries, grad_keys, grad_values], axis=1).astype(BF16)
            gt_scr[h, :, b * BLOCK : (b + 1) * BLOCK, :] = grads.reshape(frames, BLOCK, 3 * cols)

    rows = lay.nc * step_patches
    for k in range(lay.chips):
        total = jnp.zeros((rows, model), F32)
        for h in range(halves):
            part = gt_scr[h, k * lay.nc : (k + 1) * lay.nc].reshape(rows, 3 * cols)
            total = total + dot_t(part, w_refs[h][...])
        gh_refs[k][...] = total.reshape(gh_refs[k].shape).astype(gh_refs[k].dtype)


def output_kernel(lay, pos_ref, info_ref, *refs):
    x_refs, refs = refs[: lay.nc], refs[lay.nc :]
    att_refs, refs = refs[: lay.chips], refs[lay.chips :]
    wo_ref, mod_ref, *out_refs = refs
    _, patches, width = att_refs[0].shape
    own_chip = pos_ref[0] * lay.nx + pos_ref[3]
    model = x_refs[0].shape[1]
    total = jnp.zeros((lay.nc * patches, model), F32)
    for k in range(lay.chips):
        total = total + dot(att_refs[k][...].reshape(lay.nc * patches, width), wo_ref[own_chip ^ k])
    patch = pos_ref[1] * patches + lax.broadcasted_iota(jnp.int32, (patches, 1), 0)
    for j in range(lay.nc):
        _, limit, step = slot_scalars(lay, pos_ref, info_ref, (0, j))
        factor = jnp.where(patch < limit, table_row(mod_ref, step, 2, model), 0.0)
        projected = total[j * patches : (j + 1) * patches].astype(BF16).astype(F32)
        out_refs[j][...] = (x_refs[j][...].astype(F32) + factor * projected).astype(BF16)


def input_grad_kernel(lay, pos_ref, info_ref, *refs):
    x_refs, refs = refs[: lay.nc], refs[lay.nc :]
    g_refs, refs = refs[: lay.nc], refs[lay.nc :]
    gh_refs, refs = refs[: lay.chips], refs[lay.chips :]
    mod_ref, *out_refs = refs
    model = x_refs[0].shape[1]
    for j in range(lay.nc):
        _, _, step = slot_scalars(lay, pos_ref, info_ref, (0, j))
        grad_hidden = gh_refs[0][j]
        for k in range(1, lay.chips):
            grad_hidden = grad_hidden + gh_refs[k][j].astype(F32)
        grad_hidden = grad_hidden.astype(BF16).astype(F32)
        normed, inv_sigma = normalize(x_refs[j][...].astype(F32))
        grad_norm = grad_hidden * (1.0 + table_row(mod_ref, step, 1, model))
        first_mean = jnp.mean(grad_norm, axis=-1, keepdims=True)
        second_mean = jnp.mean(grad_norm * normed, axis=-1, keepdims=True)
        grad_x = g_refs[j][...].astype(F32) + inv_sigma * (
            grad_norm - first_mean - normed * second_mean
        )
        out_refs[j][...] = grad_x.astype(BF16)


def whole_spec(shape):
    return pl.BlockSpec(shape, lambda *_: (0,) * len(shape))


def struct(shape, dtype=BF16):
    return jax.ShapeDtypeStruct(shape, dtype)


def local(lay, frames_x, grad_y, clip_ids, clip_patches, clip_step, mod_table, w_qkv, w_out):
    y, c, z, x = (lax.axis_index(name) for name in AXES)
    _, patches, model = frames_x.shape
    half = patches // lay.nc
    chips, nc, nx = lay.chips, lay.nc, lay.nx
    chip_heads = HEADS // chips
    head_size = model // HEADS
    halves = 2 if chip_heads % 2 == 0 else 1
    half_heads = chip_heads // halves
    cols = half_heads * head_size
    chip_width = chip_heads * head_size
    rows = w_qkv.shape[0]
    groups = lay.nz
    quarter = model // groups
    step_patches = max(BLOCK, min(half, 512 // lay.frames))
    steps = half // step_patches
    tokens = lay.frames * step_patches

    def call(kernel, name, in_specs, out_specs, out_shape, scratch=(), grid=(1,), prefetch=2):
        return pl.pallas_call(
            kernel,
            grid_spec=pltpu.PrefetchScalarGridSpec(
                num_scalar_prefetch=prefetch,
                grid=grid,
                in_specs=in_specs,
                out_specs=out_specs,
                scratch_shapes=list(scratch),
            ),
            out_shape=out_shape,
            compiler_params=pltpu.CompilerParams(vmem_limit_bytes=VMEM_LIMIT),
            name=name,
        )

    def chip_swap(k):
        ky, kx = lay.chip_of(k)
        return lay.swap(ky=ky, kx=kx)

    def over_chips(parts):
        own = [parts[0]]
        return own + [lax.ppermute(parts[k], AXES, chip_swap(k)) for k in range(1, chips)]

    def from_plane(parts):
        got = [lax.ppermute(part, AXES, lay.from_plane(k)) for k, part in enumerate(parts)]
        first = jnp.where(z // lay.ny == 0, got[0], got[1])
        second = jnp.where(z // lay.ny == 0, got[1], got[0])
        return jnp.concatenate([first, second], axis=0)[None]

    info = jnp.concatenate([clip_ids[0], clip_patches[0], clip_step[0]])[None]
    info = lax.ppermute(info, AXES, lay.to_plane(0))[0]
    pos = jnp.stack([y, c, z, x]).astype(jnp.int32)
    own = []
    for k in range(nc):
        start = ((z // lay.ny) ^ k) * half
        pair = [lax.dynamic_slice_in_dim(frame[0], start, half) for frame in (frames_x, grad_y)]
        own.append(lax.ppermute(jnp.concatenate(pair, axis=0), AXES, lay.to_plane(k)))
    by_slot = [over_chips([part] * chips) for part in own]
    frames = [by_slot[j][k] for k, j in lay.slots()]

    picked = call(
        functools.partial(pick_kernel, lay, halves, cols),
        "pick",
        [whole_spec(w_qkv.shape)],
        [whole_spec((rows, 3 * cols))] * nx,
        [struct((rows, 3 * cols))] * nx,
        prefetch=1,
    )(pos, w_qkv)
    by_x = [picked[0]] + [
        lax.ppermute(picked[kx], AXES, lay.swap(kx=kx)) for kx in range(1, nx)
    ]
    if nx == 2:
        ordered = [jnp.where(x == i, by_x[0], by_x[1]) for i in range(nx)]
    else:
        stacked = jnp.stack(by_x)
        ordered = [lax.dynamic_index_in_dim(stacked, x ^ i, 0, keepdims=False) for i in range(nx)]
    w_own = lax.all_gather(jnp.concatenate(ordered, axis=0), "z", axis=0, tiled=True)
    w_halves = [w_own]
    if halves > 1:
        w_halves.append(lax.ppermute(w_own, AXES, lay.swap(kc=1)))

    wo_own = lax.ppermute(w_out, AXES, lay.rows_to_chip())
    wo_rows = [wo_own, lax.ppermute(wo_own, AXES, lay.swap(kc=1))]
    late_w_out, _ = lax.optimization_barrier((w_out, w_own))
    wo = lax.all_gather(late_w_out, ("z", "x"), axis=0, tiled=True)
    wo = wo.reshape(chips, chip_width, model)

    x_spec = pl.BlockSpec((step_patches, model), lambda i, *_: (i, 0))
    g_spec = pl.BlockSpec((step_patches, model), lambda i, *_: (steps + i, 0))
    triple_spec = pl.BlockSpec((halves, lay.frames, step_patches, cols), lambda i, *_: (0, 0, i, 0))
    att_spec = pl.BlockSpec((nc, step_patches, chip_width), lambda i, *_: (0, i, 0))
    gh_spec = pl.BlockSpec((nc, step_patches, model), lambda i, *_: (0, i, 0))
    w_specs = [whole_spec((model, 3 * cols))] * halves
    mod_spec = whole_spec(mod_table.shape)
    triple_shape = struct((halves, lay.frames, half, cols))

    queries, keys, values, *att = call(
        functools.partial(forward_kernel, lay, halves, half_heads),
        "forward",
        [x_spec] * lay.frames + w_specs + [mod_spec],
        [triple_spec] * 3 + [att_spec] * chips,
        [triple_shape] * 3 + [struct((nc, half, chip_width))] * chips,
        [pltpu.VMEM((tokens, model), BF16)],
        (steps,),
    )(pos, info, *frames, *w_halves, mod_table)

    grad_attn, kept, sent = call(
        functools.partial(projection_grad_kernel, lay, halves),
        "projection_grad",
        [g_spec] * lay.frames + [att_spec] * chips + [whole_spec(w_out.shape)] * nc + [mod_spec],
        [triple_spec] + [whole_spec((rows, model))] * 2,
        [triple_shape] + [struct((rows, model), F32)] * 2,
        [
            pltpu.VMEM((tokens, model), BF16),
            pltpu.VMEM((chip_width, model), BF16),
            pltpu.VMEM((chip_width, model), F32),
        ],
        (steps,),
    )(pos, info, *frames, *att, *wo_rows, mod_table)
    got = lax.ppermute(sent, AXES, lay.swap(kc=1))
    att_own = over_chips(att)

    partial_sums = call(
        functools.partial(backward_kernel, lay, halves, half_heads),
        "backward",
        w_specs + [triple_spec] * 4,
        [gh_spec] * chips,
        [struct((nc, half, model), F32)] + [struct((nc, half, model))] * (chips - 1),
        [pltpu.VMEM((halves, lay.frames, step_patches, 3 * cols), BF16)],
        (steps,),
    )(pos, info, *w_halves, queries, keys, values, grad_attn)
    gh_own = over_chips(partial_sums)

    pieces = call(
        functools.partial(spread_kernel, lay),
        "spread",
        [whole_spec((rows, model))] * 2,
        [whole_spec((rows, quarter))] * groups,
        [struct((rows, quarter), F32)] * groups,
        [pltpu.VMEM((groups, rows, quarter), F32)],
        prefetch=1,
    )(pos, kept, got)
    pieces = [lax.ppermute(piece, AXES, lay.to_owner(j)) for j, piece in enumerate(pieces)]
    grad_w_out = sum(pieces[1:], pieces[0]) * jnp.float32(
        1.0 / math.sqrt(groups * lay.frames * patches)
    )

    def half_spec(start):
        return pl.BlockSpec((half, model), lambda *_: (start, 0))

    out_parts = call(
        functools.partial(output_kernel, lay),
        "output",
        [half_spec(0)] * nc
        + [whole_spec((nc, half, chip_width))] * chips
        + [whole_spec(wo.shape), mod_spec],
        [half_spec(0)] * nc,
        [struct((half, model))] * nc,
    )(pos, info, *own, *att_own, wo, mod_table)
    out_y = from_plane(out_parts)

    grad_parts = call(
        functools.partial(input_grad_kernel, lay),
        "input_grad",
        [x_spec] * nc + [g_spec] * nc + [gh_spec] * chips + [mod_spec],
        [x_spec] * nc,
        [struct((half, model))] * nc,
        grid=(steps,),
    )(pos, info, *own, *own, *gh_own, mod_table)
    grad_x = from_plane(grad_parts)
    return out_y, grad_x, grad_w_out


def solution(mesh):
    lay = Layout(mesh)
    grid = Mesh(mesh.devices.reshape(lay.ny, lay.nc, lay.nz, lay.nx), AXES)
    rows, cols = ("z", "x"), ("y", "c")
    frame = P(AXES, None, None)
    group = P(cols, None)
    return jax.shard_map(
        functools.partial(local, lay),
        mesh=grid,
        in_specs=(frame, frame, group, group, group, P(), P(rows, None), P(rows, None)),
        out_specs=(frame, frame, P(rows, cols)),
        check_vma=False,
    )
```

```python
import functools
import math

import jax
import jax.numpy as jnp
from jax import lax
from jax.experimental import pallas as pl
from jax.experimental.pallas import tpu as pltpu
from jax.sharding import Mesh, PartitionSpec as P

HEADS = 16
CORES = 2
AXES = ("y", "c", "z", "x")
BLOCK = 16
VMEM_LIMIT = 56 * 1024 * 1024
BF16 = jnp.bfloat16
F32 = jnp.float32


def dot(left, right):
    return jnp.dot(left, right, preferred_element_type=F32)


def dot_t(left, right):
    return lax.dot_general(left, right, (((1,), (1,)), ((), ())), preferred_element_type=F32)


def t_dot(left, right):
    return lax.dot_general(left, right, (((0,), (0,)), ((), ())), preferred_element_type=F32)


def normalize(values):
    centred = values - jnp.mean(values, axis=-1, keepdims=True)
    inv_sigma = lax.rsqrt(jnp.mean(centred * centred, axis=-1, keepdims=True) + 1e-06)
    return centred * inv_sigma, inv_sigma


class Layout:
    def __init__(self, mesh):
        groups, seq = mesh.shape["dp"], mesh.shape["seq"]
        self.nc = CORES
        self.ny = groups // CORES
        self.nz = groups
        self.nx = seq // self.nz
        self.chips = self.ny * self.nx
        self.frames = seq
        self.chip_heads = HEADS // self.chips
        self.halves = 2 if self.chip_heads % 2 == 0 else 1
        self.half_heads = self.chip_heads // self.halves

    def linear(self, y, c, z, x):
        return ((y * self.nc + c) * self.nz + z) * self.nx + x

    def perm(self, move):
        pairs = []
        for y in range(self.ny):
            for c in range(self.nc):
                for z in range(self.nz):
                    for x in range(self.nx):
                        pairs.append((self.linear(y, c, z, x), self.linear(*move(y, c, z, x))))
        return pairs

    def to_plane(self, k):
        return self.perm(lambda y, c, z, x: (z % self.ny, (z // self.ny) ^ k, c * self.ny + y, x))

    def from_plane(self, k):
        return [(target, source) for source, target in self.to_plane(k)]

    def swap(self, ky=0, kc=0, kz=0, kx=0):
        return self.perm(lambda y, c, z, x: (y ^ ky, c ^ kc, z ^ kz, x ^ kx))

    def row_block(self, y, x, i):
        if self.halves > 1:
            return (i * self.ny + y) * self.nx + x
        return self.nc * (y * self.nx + x) + i

    def rows_to_chip(self):
        reader = {
            self.row_block(y, x, i): (y, x, i)
            for y in range(self.ny)
            for x in range(self.nx)
            for i in range(self.nc)
        }

        def move(y, c, z, x):
            chip_y, chip_x, i = reader[z * self.nx + x]
            return chip_y, i, c * self.ny + y, chip_x

        return self.perm(move)

    def to_owner(self, j):
        def move(y, c, z, x):
            s = self.row_block(y, x, c)
            d = z ^ j
            return d // self.nc, d % self.nc, s // self.nx, s % self.nx

        return self.perm(move)

    def chip_of(self, k):
        return k // self.nx, k % self.nx

    def slots(self):
        return [(k, j) for k in range(self.chips) for j in range(self.nc)]


def slot_scalars(lay, pos_ref, info_ref, slot):
    k, j = slot
    ky, kx = lay.chip_of(k)
    z_frame = (pos_ref[1] ^ j) * lay.ny + (pos_ref[0] ^ ky)
    frame = z_frame * lay.nx + (pos_ref[3] ^ kx)
    clip = info_ref[frame]
    clips = (info_ref.shape[0] - lay.frames) // 2
    return clip, info_ref[lay.frames + clip], info_ref[lay.frames + clips + clip]


def table_row(mod_ref, step, part, width):
    return mod_ref[pl.ds(step, 1), part * width : (part + 1) * width]


def allowed_pairs(lay, pos_ref, info_ref, patch_base):
    rows = lay.frames * BLOCK
    row_slot = lax.broadcasted_iota(jnp.int32, (rows, 1), 0) // BLOCK
    col_slot = lax.broadcasted_iota(jnp.int32, (1, rows), 1) // BLOCK
    row_clip = jnp.zeros((rows, 1), jnp.int32)
    row_limit = jnp.zeros((rows, 1), jnp.int32)
    col_clip = jnp.zeros((1, rows), jnp.int32)
    for t, slot in enumerate(lay.slots()):
        clip, limit, _ = slot_scalars(lay, pos_ref, info_ref, slot)
        row_clip = jnp.where(row_slot == t, clip, row_clip)
        row_limit = jnp.where(row_slot == t, limit, row_limit)
        col_clip = jnp.where(col_slot == t, clip, col_clip)
    row_patch = lax.broadcasted_iota(jnp.int32, (rows, 1), 0) % BLOCK
    col_patch = lax.broadcasted_iota(jnp.int32, (1, rows), 1) % BLOCK
    row_key = row_clip * BLOCK + row_patch
    col_key = col_clip * BLOCK + col_patch
    row_valid = (patch_base + row_patch < row_limit).astype(jnp.int32)
    row_index = lax.broadcasted_iota(jnp.int32, (rows, rows), 0)
    col_index = lax.broadcasted_iota(jnp.int32, (rows, rows), 1)
    return (row_key == col_key) & ((row_valid > 0) | (row_index == col_index))


def head_mask(values, head, head_size):
    lane = lax.broadcasted_iota(jnp.int32, (1, values.shape[1]), 1)
    inside = (lane >= head * head_size) & (lane < (head + 1) * head_size)
    return jnp.where(inside, values, jnp.zeros_like(values))


def patch_blocks(array, block):
    part = array[:, block * BLOCK : (block + 1) * BLOCK, :]
    return part.reshape(part.shape[0] * BLOCK, part.shape[2])


def pick_kernel(lay, cols, pos_ref, w_ref, *out_refs):
    model = w_ref.shape[1] // 3
    for k, out_ref in enumerate(out_refs):
        chip_x = pos_ref[3] ^ k
        if lay.halves > 1:
            want = lay.row_block(pos_ref[0], chip_x, pos_ref[1])
        else:
            want = pos_ref[0] * lay.nx + chip_x
        for v in range(lay.chips * lay.halves):

            @pl.when(want == v)
            def _(v=v, out_ref=out_ref):
                parts = [
                    w_ref[:, p * model + v * cols : p * model + (v + 1) * cols].astype(F32)
                    for p in range(3)
                ]
                out_ref[...] = jnp.concatenate(parts, axis=1).astype(BF16)


def fill_weights(lay, pos_ref, w_refs, w_scr):
    rows = w_refs[0].shape[0]
    for h in range(lay.halves):
        for k in range(lay.nz):
            start = pl.multiple_of((pos_ref[2] ^ k) * rows, 16)
            w_scr[h, pl.ds(start, rows), :] = w_refs[h * lay.nz + k][...]


def heads_stacked(lay, values):
    head_size = values.shape[1] // lay.half_heads
    parts = [head_mask(values, head, head_size) for head in range(lay.half_heads)]
    return jnp.concatenate(parts, axis=0) if len(parts) > 1 else parts[0]


def beside(lay, weights):
    return jnp.concatenate([weights[head] for head in range(lay.half_heads)], axis=1)


def attention_weights(lay, keys_stacked, queries, allowed, scaling):
    scores = dot_t(keys_stacked, queries) * scaling
    scores = jnp.where(allowed, scores.reshape((lay.half_heads,) + allowed.shape), -jnp.inf)
    exponent = jnp.exp(scores - jnp.max(scores, axis=1, keepdims=True))
    return exponent / jnp.sum(exponent, axis=1, keepdims=True)


def forward_kernel(lay, pos_ref, info_ref, *refs):
    x_refs, refs = refs[: lay.frames], refs[lay.frames :]
    w_refs, refs = refs[: lay.halves * lay.nz], refs[lay.halves * lay.nz :]
    mod_ref, q_ref, k_ref, v_ref, att_ref, w_scr, hid_scr = refs
    model = hid_scr.shape[1]
    cols = w_scr.shape[2] // 3
    scaling = 1.0 / math.sqrt(cols // lay.half_heads)
    step_patches = x_refs[0].shape[0]
    patches = step_patches * pl.num_programs(0)

    @pl.when(pl.program_id(0) == 0)
    def _():
        fill_weights(lay, pos_ref, w_refs, w_scr)

    for t, slot in enumerate(lay.slots()):
        _, _, step = slot_scalars(lay, pos_ref, info_ref, slot)
        normed, _ = normalize(x_refs[t][...].astype(F32))
        shift, scale = table_row(mod_ref, step, 0, model), table_row(mod_ref, step, 1, model)
        hid_scr[t * step_patches : (t + 1) * step_patches, :] = (
            normed * (1.0 + scale) + shift
        ).astype(BF16)

    for h in range(lay.halves):
        triple = dot(hid_scr[...], w_scr[h])
        for n, ref in enumerate((q_ref, k_ref, v_ref)):
            ref[h] = triple[:, n * cols : (n + 1) * cols].astype(BF16).reshape(ref.shape[1:])

    for b in range(step_patches // BLOCK):
        patch_base = pos_ref[1] * patches + pl.program_id(0) * step_patches + b * BLOCK
        allowed = allowed_pairs(lay, pos_ref, info_ref, patch_base)
        outputs = []
        for h in range(lay.halves):
            queries, keys, values = (patch_blocks(ref[h], b) for ref in (q_ref, k_ref, v_ref))
            weights = attention_weights(lay, heads_stacked(lay, keys), queries, allowed, scaling)
            weights = weights.astype(BF16).reshape(-1, allowed.shape[1])
            outputs.append(t_dot(weights, heads_stacked(lay, values)))
        if lay.halves > 1:
            first = jnp.where(pos_ref[1] == 0, outputs[0], outputs[1])
            second = jnp.where(pos_ref[1] == 0, outputs[1], outputs[0])
            outputs = [jnp.concatenate([first, second], axis=1)]
        attended = outputs[0].astype(BF16)
        att_ref[:, b * BLOCK : (b + 1) * BLOCK, :] = attended.reshape(lay.frames, BLOCK, -1)


def weight_grad_kernel(lay, pos_ref, info_ref, *refs):
    g_refs, refs = refs[: lay.frames], refs[lay.frames :]
    att_ref, mod_ref, gp_ref, kept_ref, sent_ref, acc_scr = refs
    _, step_patches, model = gp_ref.shape
    tokens = lay.frames * step_patches
    patches = step_patches * pl.num_programs(0)
    groups, block_rows, part = kept_ref.shape
    is_first = pos_ref[1] == 0

    @pl.when(pl.program_id(0) == 0)
    def _():
        acc_scr[...] = jnp.zeros_like(acc_scr)

    patch_base = pos_ref[1] * patches + pl.program_id(0) * step_patches
    patch = patch_base + lax.broadcasted_iota(jnp.int32, (step_patches, 1), 0)
    for t, slot in enumerate(lay.slots()):
        _, limit, step = slot_scalars(lay, pos_ref, info_ref, slot)
        factor = jnp.where(patch < limit, table_row(mod_ref, step, 2, model), 0.0)
        gp_ref[t] = (factor * g_refs[t][...].astype(F32)).astype(BF16)

    attended = att_ref[...].reshape(tokens, -1)
    acc_scr[...] += t_dot(attended, gp_ref[...].reshape(tokens, model))

    @pl.when(pl.program_id(0) == pl.num_programs(0) - 1)
    def _():
        first, second = acc_scr[:block_rows, :], acc_scr[block_rows:, :]
        kept = jnp.where(is_first, first, second)
        sent = jnp.where(is_first, second, first)
        for d in range(groups):
            kept_ref[pos_ref[2] ^ d] = kept[:, d * part : (d + 1) * part]
            sent_ref[pos_ref[2] ^ d] = sent[:, d * part : (d + 1) * part]


def projection_kernel(lay, pos_ref, gp_ref, att_ref, *refs):
    wo_refs, refs = refs[: lay.nc], refs[lay.nc :]
    ga_ref, *refs = refs
    pr_refs, (wo_scr,) = refs[: lay.chips], refs[lay.chips :]
    _, step_patches, model = gp_ref.shape
    tokens = lay.frames * step_patches
    is_first = pos_ref[1] == 0

    @pl.when(pl.program_id(0) == 0)
    def _():
        own, other = wo_refs[0][...].astype(F32), wo_refs[1][...].astype(F32)
        both = [jnp.where(is_first, own, other), jnp.where(is_first, other, own)]
        wo_scr[...] = jnp.concatenate(both, axis=0).astype(BF16)

    grad_attn = dot_t(gp_ref[...].reshape(tokens, model), wo_scr[...])
    part = wo_scr.shape[0] // lay.halves
    for h in range(lay.halves):
        ga_ref[h] = grad_attn[:, h * part : (h + 1) * part].astype(BF16).reshape(ga_ref.shape[1:])
    attended = att_ref[...].reshape(tokens, -1)
    projected = dot(attended, wo_scr[...]).reshape(lay.chips, lay.nc, step_patches, model)
    for k in range(lay.chips):
        pr_refs[k][...] = projected[k].astype(pr_refs[k].dtype)


def backward_kernel(lay, pos_ref, info_ref, *refs):
    w_refs, refs = refs[: lay.halves * lay.nz], refs[lay.halves * lay.nz :]
    q_ref, k_ref, v_ref, ga_ref, *refs = refs
    gh_refs, (w_scr, gt_scr) = refs[: lay.chips], refs[lay.chips :]
    _, frames, step_patches, cols = q_ref.shape
    model = w_scr.shape[1]
    patches = step_patches * pl.num_programs(0)
    scaling = 1.0 / math.sqrt(cols // lay.half_heads)

    @pl.when(pl.program_id(0) == 0)
    def _():
        fill_weights(lay, pos_ref, w_refs, w_scr)

    for b in range(step_patches // BLOCK):
        patch_base = pos_ref[1] * patches + pl.program_id(0) * step_patches + b * BLOCK
        allowed = allowed_pairs(lay, pos_ref, info_ref, patch_base)
        for h in range(lay.halves):
            queries, keys, values = (patch_blocks(ref[h], b) for ref in (q_ref, k_ref, v_ref))
            grad_out = patch_blocks(ga_ref[(pos_ref[1] ^ h) if lay.halves > 1 else 0], b)
            keys = heads_stacked(lay, keys)
            weights = attention_weights(lay, keys, queries, allowed, scaling)
            grad_weights = dot_t(heads_stacked(lay, values), grad_out).reshape(weights.shape)
            grad_values = dot(beside(lay, weights.astype(BF16)), heads_stacked(lay, grad_out))
            inner = jnp.sum(weights * grad_weights, axis=1, keepdims=True)
            grad_scores = (weights * (grad_weights - inner) * scaling).astype(BF16)
            grad_queries = t_dot(grad_scores.reshape(-1, grad_scores.shape[2]), keys)
            grad_keys = dot(beside(lay, grad_scores), heads_stacked(lay, queries))
            grads = jnp.concatenate([grad_queries, grad_keys, grad_values], axis=1).astype(BF16)
            gt_scr[h, :, b * BLOCK : (b + 1) * BLOCK, :] = grads.reshape(frames, BLOCK, 3 * cols)

    rows = lay.nc * step_patches
    for k in range(lay.chips):
        total = jnp.zeros((rows, model), F32)
        for h in range(lay.halves):
            part = gt_scr[h, k * lay.nc : (k + 1) * lay.nc].reshape(rows, 3 * cols)
            total = total + dot_t(part, w_scr[h])
        gh_refs[k][...] = total.reshape(gh_refs[k].shape).astype(gh_refs[k].dtype)


def output_kernel(lay, pos_ref, info_ref, *refs):
    x_refs, refs = refs[: lay.nc], refs[lay.nc :]
    pr_refs, refs = refs[: lay.chips], refs[lay.chips :]
    mod_ref, *out_refs = refs
    step_patches, model = x_refs[0].shape
    patches = step_patches * pl.num_programs(0)
    patch_base = pos_ref[1] * patches + pl.program_id(0) * step_patches
    patch = patch_base + lax.broadcasted_iota(jnp.int32, (step_patches, 1), 0)
    for j in range(lay.nc):
        _, limit, step = slot_scalars(lay, pos_ref, info_ref, (0, j))
        factor = jnp.where(patch < limit, table_row(mod_ref, step, 2, model), 0.0)
        projected = pr_refs[0][j]
        for k in range(1, lay.chips):
            projected = projected + pr_refs[k][j].astype(F32)
        projected = projected.astype(BF16).astype(F32)
        out_refs[j][...] = (x_refs[j][...].astype(F32) + factor * projected).astype(BF16)


def input_grad_kernel(lay, pos_ref, info_ref, *refs):
    x_refs, refs = refs[: lay.nc], refs[lay.nc :]
    g_refs, refs = refs[: lay.nc], refs[lay.nc :]
    gh_refs, refs = refs[: lay.chips], refs[lay.chips :]
    mod_ref, *out_refs = refs
    model = x_refs[0].shape[1]
    for j in range(lay.nc):
        _, _, step = slot_scalars(lay, pos_ref, info_ref, (0, j))
        grad_hidden = gh_refs[0][j]
        for k in range(1, lay.chips):
            grad_hidden = grad_hidden + gh_refs[k][j].astype(F32)
        grad_hidden = grad_hidden.astype(BF16).astype(F32)
        normed, inv_sigma = normalize(x_refs[j][...].astype(F32))
        grad_norm = grad_hidden * (1.0 + table_row(mod_ref, step, 1, model))
        first_mean = jnp.mean(grad_norm, axis=-1, keepdims=True)
        second_mean = jnp.mean(grad_norm * normed, axis=-1, keepdims=True)
        grad_x = g_refs[j][...].astype(F32) + inv_sigma * (
            grad_norm - first_mean - normed * second_mean
        )
        out_refs[j][...] = grad_x.astype(BF16)


def whole_spec(shape):
    return pl.BlockSpec(shape, lambda *_: (0,) * len(shape))


def struct(shape, dtype=BF16):
    return jax.ShapeDtypeStruct(shape, dtype)


def local(lay, frames_x, grad_y, clip_ids, clip_patches, clip_step, mod_table, w_qkv, w_out):
    y, c, z, x = (lax.axis_index(name) for name in AXES)
    _, patches, model = frames_x.shape
    half = patches // lay.nc
    chips, nc, nx = lay.chips, lay.nc, lay.nx
    head_size = model // HEADS
    halves = lay.halves
    cols = lay.half_heads * head_size
    chip_width = lay.chip_heads * head_size
    rows = w_qkv.shape[0]
    groups = lay.nz
    quarter = model // groups
    step_patches = max(BLOCK, min(half, 512 // lay.frames))
    steps = half // step_patches
    tokens = lay.frames * step_patches

    def call(kernel, name, in_specs, out_specs, out_shape, scratch=(), grid=(1,), prefetch=2):
        return pl.pallas_call(
            kernel,
            grid_spec=pltpu.PrefetchScalarGridSpec(
                num_scalar_prefetch=prefetch,
                grid=grid,
                in_specs=in_specs,
                out_specs=out_specs,
                scratch_shapes=list(scratch),
            ),
            out_shape=out_shape,
            compiler_params=pltpu.CompilerParams(vmem_limit_bytes=VMEM_LIMIT),
            name=name,
        )

    def chip_swap(k):
        ky, kx = lay.chip_of(k)
        return lay.swap(ky=ky, kx=kx)

    def over_chips(parts):
        own = [parts[0]]
        return own + [lax.ppermute(parts[k], AXES, chip_swap(k)) for k in range(1, chips)]

    def from_plane(parts):
        got = [lax.ppermute(part, AXES, lay.from_plane(k)) for k, part in enumerate(parts)]
        first = jnp.where(z // lay.ny == 0, got[0], got[1])
        second = jnp.where(z // lay.ny == 0, got[1], got[0])
        return jnp.concatenate([first, second], axis=0)[None]

    info = jnp.concatenate([clip_ids[0], clip_patches[0], clip_step[0]])[None]
    info = lax.ppermute(info, AXES, lay.to_plane(0))[0]
    pos = jnp.stack([y, c, z, x]).astype(jnp.int32)
    own = []
    for k in range(nc):
        start = ((z // lay.ny) ^ k) * half
        pair = [lax.dynamic_slice_in_dim(frame[0], start, half) for frame in (frames_x, grad_y)]
        own.append(lax.ppermute(jnp.concatenate(pair, axis=0), AXES, lay.to_plane(k)))
    by_slot = [over_chips([part] * chips) for part in own]
    frames = [by_slot[j][k] for k, j in lay.slots()]

    picked = call(
        functools.partial(pick_kernel, lay, cols),
        "pick",
        [whole_spec(w_qkv.shape)],
        [whole_spec((rows, 3 * cols))] * nx,
        [struct((rows, 3 * cols))] * nx,
        prefetch=1,
    )(pos, w_qkv)
    by_x = [picked[0]] + [
        lax.ppermute(picked[kx], AXES, lay.swap(kx=kx)) for kx in range(1, nx)
    ]
    if nx == 2:
        ordered = [jnp.where(x == i, by_x[0], by_x[1]) for i in range(nx)]
    else:
        stacked = jnp.stack(by_x)
        ordered = [lax.dynamic_index_in_dim(stacked, x ^ i, 0, keepdims=False) for i in range(nx)]
    w_own = jnp.concatenate(ordered, axis=0)
    w_pieces = [w_own] + [lax.ppermute(w_own, AXES, lay.swap(kz=kz)) for kz in range(1, lay.nz)]
    if halves > 1:
        w_pieces += [lax.ppermute(piece, AXES, lay.swap(kc=1)) for piece in w_pieces]

    wo_own = lax.ppermute(w_out, AXES, lay.rows_to_chip())
    wo_rows = [wo_own, lax.ppermute(wo_own, AXES, lay.swap(kc=1))]

    x_spec = pl.BlockSpec((step_patches, model), lambda i, *_: (i, 0))
    g_spec = pl.BlockSpec((step_patches, model), lambda i, *_: (steps + i, 0))
    triple_spec = pl.BlockSpec((halves, lay.frames, step_patches, cols), lambda i, *_: (0, 0, i, 0))
    att_spec = pl.BlockSpec((lay.frames, step_patches, chip_width), lambda i, *_: (0, i, 0))
    gp_spec = pl.BlockSpec((lay.frames, step_patches, model), lambda i, *_: (0, i, 0))
    part_spec = pl.BlockSpec((nc, step_patches, model), lambda i, *_: (0, i, 0))
    w_specs = [whole_spec(piece.shape) for piece in w_pieces]
    w_scratch = pltpu.VMEM((halves, model, 3 * cols), BF16)
    mod_spec = whole_spec(mod_table.shape)
    triple_shape = struct((halves, lay.frames, half, cols))
    part_shapes = [struct((nc, half, model), F32)] + [struct((nc, half, model))] * (chips - 1)

    queries, keys, values, attended = call(
        functools.partial(forward_kernel, lay),
        "forward",
        [x_spec] * lay.frames + w_specs + [mod_spec],
        [triple_spec] * 3 + [att_spec],
        [triple_shape] * 3 + [struct((lay.frames, half, chip_width))],
        [w_scratch, pltpu.VMEM((tokens, model), BF16)],
        (steps,),
    )(pos, info, *frames, *w_pieces, mod_table)

    piece_shape = (groups, rows, quarter)
    grad_proj, kept, sent = call(
        functools.partial(weight_grad_kernel, lay),
        "weight_grad",
        [g_spec] * lay.frames + [att_spec, mod_spec],
        [gp_spec] + [whole_spec(piece_shape)] * 2,
        [struct((lay.frames, half, model))] + [struct(piece_shape, F32)] * 2,
        [pltpu.VMEM((chip_width, model), F32)],
        (steps,),
    )(pos, info, *frames, attended, mod_table)
    got = lax.ppermute(sent, AXES, lay.swap(kc=1))

    grad_attn, *projected = call(
        functools.partial(projection_kernel, lay),
        "projection",
        [gp_spec, att_spec] + [whole_spec(w_out.shape)] * nc,
        [triple_spec] + [part_spec] * chips,
        [triple_shape] + part_shapes,
        [pltpu.VMEM((chip_width, model), BF16)],
        (steps,),
        prefetch=1,
    )(pos, grad_proj, attended, *wo_rows)

    pieces = [kept[j] + got[j] for j in range(groups)]
    grad_attn, *pieces = lax.optimization_barrier((grad_attn, *pieces))
    pieces = [lax.ppermute(piece, AXES, lay.to_owner(j)) for j, piece in enumerate(pieces)]
    grad_w_out = sum(pieces[1:], pieces[0]) * jnp.float32(
        1.0 / math.sqrt(groups * lay.frames * patches)
    )
    projected = over_chips(projected)

    partial_sums = call(
        functools.partial(backward_kernel, lay),
        "backward",
        w_specs + [triple_spec] * 4,
        [part_spec] * chips,
        part_shapes,
        [w_scratch, pltpu.VMEM((halves, lay.frames, step_patches, 3 * cols), BF16)],
        (steps,),
    )(pos, info, *w_pieces, queries, keys, values, grad_attn)
    grad_hidden = over_chips(partial_sums)

    out_parts = call(
        functools.partial(output_kernel, lay),
        "output",
        [x_spec] * nc + [part_spec] * chips + [mod_spec],
        [x_spec] * nc,
        [struct((half, model))] * nc,
        grid=(steps,),
    )(pos, info, *own, *projected, mod_table)
    out_y = from_plane(out_parts)

    grad_parts = call(
        functools.partial(input_grad_kernel, lay),
        "input_grad",
        [x_spec] * nc + [g_spec] * nc + [part_spec] * chips + [mod_spec],
        [x_spec] * nc,
        [struct((half, model))] * nc,
        grid=(steps,),
    )(pos, info, *own, *own, *grad_hidden, mod_table)
    grad_x = from_plane(grad_parts)
    return out_y, grad_x, grad_w_out


def solution(mesh):
    lay = Layout(mesh)
    grid = Mesh(mesh.devices.reshape(lay.ny, lay.nc, lay.nz, lay.nx), AXES)
    rows, cols = ("z", "x"), ("y", "c")
    frame = P(AXES, None, None)
    group = P(cols, None)
    return jax.shard_map(
        functools.partial(local, lay),
        mesh=grid,
        in_specs=(frame, frame, group, group, group, P(), P(rows, None), P(rows, None)),
        out_specs=(frame, frame, P(rows, cols)),
        check_vma=False,
    )
```

```python
import functools
import math

import jax
import jax.numpy as jnp
from jax import lax
from jax.experimental import pallas as pl
from jax.experimental.pallas import tpu as pltpu
from jax.sharding import Mesh, PartitionSpec as P

HEADS = 16
CORES = 2
AXES = ("y", "c", "z", "x")
BLOCK = 16
VMEM_LIMIT = 56 * 1024 * 1024
BF16 = jnp.bfloat16
F32 = jnp.float32


def dot(left, right):
    return jnp.dot(left, right, preferred_element_type=F32)


def dot_t(left, right):
    return lax.dot_general(left, right, (((1,), (1,)), ((), ())), preferred_element_type=F32)


def t_dot(left, right):
    return lax.dot_general(left, right, (((0,), (0,)), ((), ())), preferred_element_type=F32)


def normalize(values):
    centred = values - jnp.mean(values, axis=-1, keepdims=True)
    inv_sigma = lax.rsqrt(jnp.mean(centred * centred, axis=-1, keepdims=True) + 1e-06)
    return centred * inv_sigma, inv_sigma


class Layout:
    def __init__(self, mesh):
        groups, seq = mesh.shape["dp"], mesh.shape["seq"]
        self.nc = CORES
        self.ny = groups // CORES
        self.nz = groups
        self.nx = seq // self.nz
        self.chips = self.ny * self.nx
        self.frames = seq
        self.chip_heads = HEADS // self.chips
        self.halves = 2 if self.chip_heads % 2 == 0 else 1
        self.half_heads = self.chip_heads // self.halves

    def linear(self, y, c, z, x):
        return ((y * self.nc + c) * self.nz + z) * self.nx + x

    def perm(self, move):
        pairs = []
        for y in range(self.ny):
            for c in range(self.nc):
                for z in range(self.nz):
                    for x in range(self.nx):
                        pairs.append((self.linear(y, c, z, x), self.linear(*move(y, c, z, x))))
        return pairs

    def to_plane(self, k):
        return self.perm(lambda y, c, z, x: (z % self.ny, (z // self.ny) ^ k, c * self.ny + y, x))

    def from_plane(self, k):
        return [(target, source) for source, target in self.to_plane(k)]

    def swap(self, ky=0, kc=0, kz=0, kx=0):
        return self.perm(lambda y, c, z, x: (y ^ ky, c ^ kc, z ^ kz, x ^ kx))

    def row_block(self, y, x, i):
        if self.halves > 1:
            return (i * self.ny + y) * self.nx + x
        return self.nc * (y * self.nx + x) + i

    def rows_to_chip(self):
        reader = {
            self.row_block(y, x, i): (y, x, i)
            for y in range(self.ny)
            for x in range(self.nx)
            for i in range(self.nc)
        }

        def move(y, c, z, x):
            chip_y, chip_x, i = reader[z * self.nx + x]
            return chip_y, i, c * self.ny + y, chip_x

        return self.perm(move)

    def to_owner(self):
        def move(y, c, z, x):
            s = self.row_block(y, x, c)
            return z // self.nc, z % self.nc, s // self.nx, s % self.nx

        return self.perm(move)

    def chip_of(self, k):
        return k // self.nx, k % self.nx

    def bits(self, count):
        return [1 << b for b in range(count.bit_length() - 1)]

    def chip_bits(self, j):
        bits = self.bits(self.chips)
        return bits if j % 2 == 0 else bits[::-1]

    def doubled(self, bits):
        held = [0]
        for bit in bits:
            held = held + [k ^ bit for k in held]
        return held

    def halved(self, bit):
        return [k for k in range(self.chips) if not k & bit]

    def slots(self):
        return [(k, j) for k in range(self.chips) for j in range(self.nc)]


def slot_scalars(lay, pos_ref, info_ref, slot):
    k, j = slot
    ky, kx = lay.chip_of(k)
    z_frame = (pos_ref[1] ^ j) * lay.ny + (pos_ref[0] ^ ky)
    frame = z_frame * lay.nx + (pos_ref[3] ^ kx)
    clip = info_ref[frame]
    clips = (info_ref.shape[0] - lay.frames) // 2
    return clip, info_ref[lay.frames + clip], info_ref[lay.frames + clips + clip]


def table_row(mod_ref, step, part, width):
    return mod_ref[pl.ds(step, 1), part * width : (part + 1) * width]


def allowed_pairs(lay, pos_ref, info_ref, patch_base):
    rows = lay.frames * BLOCK
    row_slot = lax.broadcasted_iota(jnp.int32, (rows, 1), 0) // BLOCK
    col_slot = lax.broadcasted_iota(jnp.int32, (1, rows), 1) // BLOCK
    row_clip = jnp.zeros((rows, 1), jnp.int32)
    row_limit = jnp.zeros((rows, 1), jnp.int32)
    col_clip = jnp.zeros((1, rows), jnp.int32)
    for t, slot in enumerate(lay.slots()):
        clip, limit, _ = slot_scalars(lay, pos_ref, info_ref, slot)
        row_clip = jnp.where(row_slot == t, clip, row_clip)
        row_limit = jnp.where(row_slot == t, limit, row_limit)
        col_clip = jnp.where(col_slot == t, clip, col_clip)
    row_patch = lax.broadcasted_iota(jnp.int32, (rows, 1), 0) % BLOCK
    col_patch = lax.broadcasted_iota(jnp.int32, (1, rows), 1) % BLOCK
    row_key = row_clip * BLOCK + row_patch
    col_key = col_clip * BLOCK + col_patch
    row_valid = (patch_base + row_patch < row_limit).astype(jnp.int32)
    row_index = lax.broadcasted_iota(jnp.int32, (rows, rows), 0)
    col_index = lax.broadcasted_iota(jnp.int32, (rows, rows), 1)
    return (row_key == col_key) & ((row_valid > 0) | (row_index == col_index))


def head_mask(values, head, head_size):
    lane = lax.broadcasted_iota(jnp.int32, (1, values.shape[1]), 1)
    inside = (lane >= head * head_size) & (lane < (head + 1) * head_size)
    return jnp.where(inside, values, jnp.zeros_like(values))


def patch_blocks(array, block):
    part = array[:, block * BLOCK : (block + 1) * BLOCK, :]
    return part.reshape(part.shape[0] * BLOCK, part.shape[2])


def pick_kernel(lay, cols, pos_ref, w_ref, *out_refs):
    model = w_ref.shape[1] // 3
    for k, out_ref in enumerate(out_refs):
        chip_x = pos_ref[3] ^ k
        if lay.halves > 1:
            want = lay.row_block(pos_ref[0], chip_x, pos_ref[1])
        else:
            want = pos_ref[0] * lay.nx + chip_x
        for v in range(lay.chips * lay.halves):

            @pl.when(want == v)
            def _(v=v, out_ref=out_ref):
                parts = [
                    w_ref[:, p * model + v * cols : p * model + (v + 1) * cols].astype(F32)
                    for p in range(3)
                ]
                out_ref[...] = jnp.concatenate(parts, axis=1).astype(BF16)


def fill_weights(lay, pos_ref, w_refs, w_scr):
    rows = w_scr.shape[1] // lay.nz
    order = lay.doubled(lay.bits(lay.nz)[::-1])
    for h in range(lay.halves):
        for n, k in enumerate(order):
            ref, place = w_refs[2 * h + (2 * n) // lay.nz], n % (lay.nz // 2)
            start = pl.multiple_of((pos_ref[2] ^ k) * rows, 16)
            w_scr[h, pl.ds(start, rows), :] = ref[place]


def heads_stacked(lay, values):
    head_size = values.shape[1] // lay.half_heads
    parts = [head_mask(values, head, head_size) for head in range(lay.half_heads)]
    return jnp.concatenate(parts, axis=0) if len(parts) > 1 else parts[0]


def beside(lay, weights):
    return jnp.concatenate([weights[head] for head in range(lay.half_heads)], axis=1)


def attention_weights(lay, keys_stacked, queries, allowed, scaling):
    scores = dot_t(keys_stacked, queries) * scaling
    scores = jnp.where(allowed, scores.reshape((lay.half_heads,) + allowed.shape), -jnp.inf)
    exponent = jnp.exp(scores - jnp.max(scores, axis=1, keepdims=True))
    return exponent * (1.0 / jnp.sum(exponent, axis=1, keepdims=True))


def prepare_kernel(lay, pos_ref, info_ref, *refs):
    pair_refs, (mod_ref, hid_ref, gp_ref) = refs[: 2 * lay.nc], refs[2 * lay.nc :]
    _, step_patches, model = hid_ref.shape
    patches = step_patches * pl.num_programs(0)
    patch_base = pos_ref[1] * patches + pl.program_id(0) * step_patches
    patch = patch_base + lax.broadcasted_iota(jnp.int32, (step_patches, 1), 0)
    for t, (k, j) in enumerate(lay.slots()):
        _, limit, step = slot_scalars(lay, pos_ref, info_ref, (k, j))
        n = lay.doubled(lay.chip_bits(j)).index(k)
        ref, place = pair_refs[2 * j + (2 * n) // lay.chips], n % (lay.chips // 2)
        normed, _ = normalize(ref[place, 0].astype(F32))
        shift, scale = table_row(mod_ref, step, 0, model), table_row(mod_ref, step, 1, model)
        hid_ref[t] = (normed * (1.0 + scale) + shift).astype(BF16)
        factor = jnp.where(patch < limit, table_row(mod_ref, step, 2, model), 0.0)
        gp_ref[t] = (factor * ref[place, 1].astype(F32)).astype(BF16)


def forward_kernel(lay, pos_ref, info_ref, hid_ref, *refs):
    w_refs, refs = refs[: 2 * lay.halves], refs[2 * lay.halves :]
    q_ref, k_ref, v_ref, att_ref, w_scr = refs
    _, step_patches, model = hid_ref.shape
    cols = w_scr.shape[2] // 3
    scaling = 1.0 / math.sqrt(cols // lay.half_heads)
    patches = step_patches * pl.num_programs(0)

    @pl.when(pl.program_id(0) == 0)
    def _():
        fill_weights(lay, pos_ref, w_refs, w_scr)

    hidden = hid_ref[...].reshape(lay.frames * step_patches, model)
    for h in range(lay.halves):
        triple = dot(hidden, w_scr[h])
        for n, ref in enumerate((q_ref, k_ref, v_ref)):
            ref[h] = triple[:, n * cols : (n + 1) * cols].astype(BF16).reshape(ref.shape[1:])

    for b in range(step_patches // BLOCK):
        patch_base = pos_ref[1] * patches + pl.program_id(0) * step_patches + b * BLOCK
        allowed = allowed_pairs(lay, pos_ref, info_ref, patch_base)
        outputs = []
        for h in range(lay.halves):
            queries, keys, values = (patch_blocks(ref[h], b) for ref in (q_ref, k_ref, v_ref))
            weights = attention_weights(lay, heads_stacked(lay, keys), queries, allowed, scaling)
            weights = weights.astype(BF16).reshape(-1, allowed.shape[1])
            outputs.append(t_dot(weights, heads_stacked(lay, values)))
        if lay.halves > 1:
            first = jnp.where(pos_ref[1] == 0, outputs[0], outputs[1])
            second = jnp.where(pos_ref[1] == 0, outputs[1], outputs[0])
            outputs = [jnp.concatenate([first, second], axis=1)]
        attended = outputs[0].astype(BF16)
        att_ref[:, b * BLOCK : (b + 1) * BLOCK, :] = attended.reshape(lay.frames, BLOCK, -1)


def weight_grad_kernel(lay, pos_ref, gp_ref, att_ref, kept_ref, sent_ref, acc_scr):
    _, step_patches, model = gp_ref.shape
    tokens = lay.frames * step_patches
    groups, block_rows, part = kept_ref.shape
    is_first = pos_ref[1] == 0

    @pl.when(pl.program_id(0) == 0)
    def _():
        acc_scr[...] = jnp.zeros_like(acc_scr)

    attended = att_ref[...].reshape(tokens, -1)
    acc_scr[...] += t_dot(attended, gp_ref[...].reshape(tokens, model))

    @pl.when(pl.program_id(0) == pl.num_programs(0) - 1)
    def _():
        first, second = acc_scr[:block_rows, :], acc_scr[block_rows:, :]
        kept = jnp.where(is_first, first, second)
        sent = jnp.where(is_first, second, first)
        for d in range(groups):
            kept_ref[d] = kept[:, d * part : (d + 1) * part]
            sent_ref[d] = sent[:, d * part : (d + 1) * part]


def projection_kernel(lay, pos_ref, gp_ref, att_ref, *refs):
    wo_refs, refs = refs[: lay.nc], refs[lay.nc :]
    ga_ref, own_ref, sent_ref, wo_scr = refs
    own_chip = pos_ref[0] * lay.nx + pos_ref[3]
    _, step_patches, model = gp_ref.shape
    tokens = lay.frames * step_patches
    is_first = pos_ref[1] == 0

    @pl.when(pl.program_id(0) == 0)
    def _():
        own, other = wo_refs[0][...].astype(F32), wo_refs[1][...].astype(F32)
        both = [jnp.where(is_first, own, other), jnp.where(is_first, other, own)]
        wo_scr[...] = jnp.concatenate(both, axis=0).astype(BF16)

    grad_attn = dot_t(gp_ref[...].reshape(tokens, model), wo_scr[...])
    part = wo_scr.shape[0] // lay.halves
    for h in range(lay.halves):
        ga_ref[h] = grad_attn[:, h * part : (h + 1) * part].astype(BF16).reshape(ga_ref.shape[1:])
    attended = att_ref[...].reshape(tokens, -1)
    projected = dot(attended, wo_scr[...]).reshape(lay.chips, lay.nc, step_patches, model)
    own_ref[...] = projected[0]
    for k in range(lay.chips):
        sent_ref[own_chip ^ k] = projected[k].astype(BF16)


def backward_kernel(lay, pos_ref, info_ref, *refs):
    w_refs, refs = refs[: 2 * lay.halves], refs[2 * lay.halves :]
    q_ref, k_ref, v_ref, ga_ref, *refs = refs
    kept_refs, refs = refs[: lay.nc], refs[lay.nc :]
    sent_refs, (w_scr, gt_scr) = refs[: lay.nc], refs[lay.nc :]
    _, frames, step_patches, cols = q_ref.shape
    model = w_scr.shape[1]
    patches = step_patches * pl.num_programs(0)
    scaling = 1.0 / math.sqrt(cols // lay.half_heads)

    @pl.when(pl.program_id(0) == 0)
    def _():
        fill_weights(lay, pos_ref, w_refs, w_scr)

    for b in range(step_patches // BLOCK):
        patch_base = pos_ref[1] * patches + pl.program_id(0) * step_patches + b * BLOCK
        allowed = allowed_pairs(lay, pos_ref, info_ref, patch_base)
        for h in range(lay.halves):
            queries, keys, values = (patch_blocks(ref[h], b) for ref in (q_ref, k_ref, v_ref))
            grad_out = patch_blocks(ga_ref[(pos_ref[1] ^ h) if lay.halves > 1 else 0], b)
            keys = heads_stacked(lay, keys)
            weights = attention_weights(lay, keys, queries, allowed, scaling)
            grad_weights = dot_t(heads_stacked(lay, values), grad_out).reshape(weights.shape)
            grad_values = dot(beside(lay, weights.astype(BF16)), heads_stacked(lay, grad_out))
            inner = jnp.sum(weights * grad_weights, axis=1, keepdims=True)
            grad_scores = (weights * (grad_weights - inner) * scaling).astype(BF16)
            grad_queries = t_dot(grad_scores.reshape(-1, grad_scores.shape[2]), keys)
            grad_keys = dot(beside(lay, grad_scores), heads_stacked(lay, queries))
            grads = jnp.concatenate([grad_queries, grad_keys, grad_values], axis=1).astype(BF16)
            gt_scr[h, :, b * BLOCK : (b + 1) * BLOCK, :] = grads.reshape(frames, BLOCK, 3 * cols)

    rows = lay.nc * step_patches
    for k in range(lay.chips):
        total = jnp.zeros((rows, model), F32)
        for h in range(lay.halves):
            part = gt_scr[h, k * lay.nc : (k + 1) * lay.nc].reshape(rows, 3 * cols)
            total = total + dot_t(part, w_scr[h])
        total = total.reshape(lay.nc, step_patches, model)
        for j in range(lay.nc):
            first = lay.chip_bits(j)[0]
            place = lay.halved(first).index(k & ~first)
            if k & first:
                sent_refs[j][place] = total[j].astype(BF16)
            else:
                kept_refs[j][place] = total[j]


def output_kernel(lay, pos_ref, info_ref, *refs):
    pair_refs, refs = refs[: lay.nc], refs[lay.nc :]
    own_ref, got_ref, refs = refs[0], refs[1], refs[2:]
    kept_refs, refs = refs[: lay.nc], refs[lay.nc :]
    add_refs, refs = refs[: lay.nc], refs[lay.nc :]
    mod_ref, *refs = refs
    out_refs, sum_refs = refs[: lay.nc], refs[lay.nc :]
    own_chip = pos_ref[0] * lay.nx + pos_ref[3]
    step_patches, model = out_refs[0].shape
    patches = step_patches * pl.num_programs(0)
    patch_base = pos_ref[1] * patches + pl.program_id(0) * step_patches
    patch = patch_base + lax.broadcasted_iota(jnp.int32, (step_patches, 1), 0)
    for j in range(lay.nc):
        _, limit, step = slot_scalars(lay, pos_ref, info_ref, (0, j))
        factor = jnp.where(patch < limit, table_row(mod_ref, step, 2, model), 0.0)
        projected = own_ref[j]
        for k in range(1, lay.chips):
            projected = projected + got_ref[own_chip ^ k, j].astype(F32)
        projected = projected.astype(BF16).astype(F32)
        out_refs[j][...] = (pair_refs[j][0, 0].astype(F32) + factor * projected).astype(BF16)
        sum_refs[j][...] = (kept_refs[j][1] + add_refs[j][1].astype(F32)).astype(BF16)


def input_grad_kernel(lay, pos_ref, info_ref, *refs):
    pair_refs, refs = refs[: lay.nc], refs[lay.nc :]
    kept_refs, refs = refs[: lay.nc], refs[lay.nc :]
    add_refs, refs = refs[: lay.nc], refs[lay.nc :]
    last_refs, refs = refs[: lay.nc], refs[lay.nc :]
    mod_ref, *out_refs = refs
    model = out_refs[0].shape[1]
    for j in range(lay.nc):
        _, _, step = slot_scalars(lay, pos_ref, info_ref, (0, j))
        grad_hidden = kept_refs[j][0] + add_refs[j][0].astype(F32)
        grad_hidden = grad_hidden + last_refs[j][...].astype(F32)
        grad_hidden = grad_hidden.astype(BF16).astype(F32)
        normed, inv_sigma = normalize(pair_refs[j][0, 0].astype(F32))
        grad_norm = grad_hidden * (1.0 + table_row(mod_ref, step, 1, model))
        first_mean = jnp.mean(grad_norm, axis=-1, keepdims=True)
        second_mean = jnp.mean(grad_norm * normed, axis=-1, keepdims=True)
        grad_x = pair_refs[j][0, 1].astype(F32) + inv_sigma * (
            grad_norm - first_mean - normed * second_mean
        )
        out_refs[j][...] = grad_x.astype(BF16)


def whole_spec(shape):
    return pl.BlockSpec(shape, lambda *_: (0,) * len(shape))


def struct(shape, dtype=BF16):
    return jax.ShapeDtypeStruct(shape, dtype)


def local(lay, frames_x, grad_y, clip_ids, clip_patches, clip_step, mod_table, w_qkv, w_out):
    y, c, z, x = (lax.axis_index(name) for name in AXES)
    _, patches, model = frames_x.shape
    half = patches // lay.nc
    chips, nc, nx = lay.chips, lay.nc, lay.nx
    head_size = model // HEADS
    halves = lay.halves
    cols = lay.half_heads * head_size
    chip_width = lay.chip_heads * head_size
    rows = w_qkv.shape[0]
    groups = lay.nz
    quarter = model // groups
    step_patches = max(BLOCK, min(half, 512 // lay.frames))
    steps = half // step_patches
    tokens = lay.frames * step_patches

    def call(kernel, name, cost, in_specs, out_specs, out_shape, scratch=(), grid=(1,), prefetch=2):
        return pl.pallas_call(
            kernel,
            grid_spec=pltpu.PrefetchScalarGridSpec(
                num_scalar_prefetch=prefetch,
                grid=grid,
                in_specs=in_specs,
                out_specs=out_specs,
                scratch_shapes=list(scratch),
            ),
            out_shape=out_shape,
            compiler_params=pltpu.CompilerParams(vmem_limit_bytes=VMEM_LIMIT),
            cost_estimate=pl.CostEstimate(
                flops=cost * tokens * steps, bytes_accessed=4 * model * tokens, transcendentals=0
            ),
            name=name,
        )

    def chip_swap(k):
        ky, kx = lay.chip_of(k)
        return lay.swap(ky=ky, kx=kx)

    def doubling(held, bits, swap):
        for bit in bits[:-1]:
            held = jnp.concatenate([held, lax.ppermute(held, AXES, swap(bit))], axis=0)
        return [held, lax.ppermute(held, AXES, swap(bits[-1]))]

    def over_chips(parts):
        own = [parts[0]]
        return own + [lax.ppermute(parts[k], AXES, chip_swap(k)) for k in range(1, chips)]

    def from_plane(parts):
        got = [lax.ppermute(part, AXES, lay.from_plane(k)) for k, part in enumerate(parts)]
        first = jnp.where(z // lay.ny == 0, got[0], got[1])
        second = jnp.where(z // lay.ny == 0, got[1], got[0])
        return jnp.concatenate([first, second], axis=0)[None]

    info = jnp.concatenate([clip_ids[0], clip_patches[0], clip_step[0]])[None]
    info = lax.ppermute(info, AXES, lay.to_plane(0))[0]
    pos = jnp.stack([y, c, z, x]).astype(jnp.int32)
    own = []
    for k in range(nc):
        start = ((z // lay.ny) ^ k) * half
        pair = [lax.dynamic_slice_in_dim(frame, start, half, axis=1) for frame in (frames_x, grad_y)]
        own.append(lax.ppermute(jnp.stack(pair, axis=1), AXES, lay.to_plane(k)))
    pairs = []
    for j in range(nc):
        pairs += doubling(own[j], lay.chip_bits(j), chip_swap)

    picked = call(
        functools.partial(pick_kernel, lay, cols),
        "pick",
        2 * model * 1000,
        [whole_spec(w_qkv.shape)],
        [whole_spec((rows, 3 * cols))] * nx,
        [struct((rows, 3 * cols))] * nx,
        prefetch=1,
    )(pos, w_qkv)
    by_x = [picked[0]] + [
        lax.ppermute(picked[kx], AXES, lay.swap(kx=kx)) for kx in range(1, nx)
    ]
    if nx == 2:
        ordered = [jnp.where(x == i, by_x[0], by_x[1]) for i in range(nx)]
    else:
        stacked = jnp.stack(by_x)
        ordered = [lax.dynamic_index_in_dim(stacked, x ^ i, 0, keepdims=False) for i in range(nx)]
    w_own = jnp.concatenate(ordered, axis=0)[None]
    w_pieces = doubling(w_own, lay.bits(lay.nz)[::-1], lambda kz: lay.swap(kz=kz))
    if halves > 1:
        w_pieces += [lax.ppermute(piece, AXES, lay.swap(kc=1)) for piece in w_pieces]

    late_w_out, _ = lax.optimization_barrier((w_out, w_pieces[:2]))
    wo_own = lax.ppermute(late_w_out, AXES, lay.rows_to_chip())
    wo_rows = [wo_own, lax.ppermute(wo_own, AXES, lay.swap(kc=1))]

    x_spec = pl.BlockSpec((step_patches, model), lambda i, *_: (i, 0))

    def pair_spec(count):
        return pl.BlockSpec((count, 2, step_patches, model), lambda i, *_: (0, 0, i, 0))

    triple_spec = pl.BlockSpec((halves, lay.frames, step_patches, cols), lambda i, *_: (0, 0, i, 0))
    att_spec = pl.BlockSpec((lay.frames, step_patches, chip_width), lambda i, *_: (0, i, 0))
    gp_spec = pl.BlockSpec((lay.frames, step_patches, model), lambda i, *_: (0, i, 0))
    part_spec = pl.BlockSpec((nc, step_patches, model), lambda i, *_: (0, i, 0))
    w_specs = [whole_spec(piece.shape) for piece in w_pieces]
    w_scratch = pltpu.VMEM((halves, model, 3 * cols), BF16)
    mod_spec = whole_spec(mod_table.shape)
    triple_shape = struct((halves, lay.frames, half, cols))

    hidden, grad_proj = call(
        functools.partial(prepare_kernel, lay),
        "prepare",
        3 * model * 1000,
        [pair_spec(chips // 2)] * (2 * nc) + [mod_spec],
        [gp_spec] * 2,
        [struct((lay.frames, half, model))] * 2,
        grid=(steps,),
    )(pos, info, *pairs, mod_table)

    queries, keys, values, attended = call(
        functools.partial(forward_kernel, lay),
        "forward",
        8 * model * 1000,
        [gp_spec] + w_specs,
        [triple_spec] * 3 + [att_spec],
        [triple_shape] * 3 + [struct((lay.frames, half, chip_width))],
        [w_scratch],
        (steps,),
    )(pos, info, hidden, *w_pieces)

    piece_shape = (groups, rows, quarter)
    kept, sent = call(
        functools.partial(weight_grad_kernel, lay),
        "weight_grad",
        4 * model * 1000,
        [gp_spec, att_spec],
        [whole_spec(piece_shape)] * 2,
        [struct(piece_shape, F32)] * 2,
        [pltpu.VMEM((chip_width, model), F32)],
        (steps,),
        prefetch=1,
    )(pos, grad_proj, attended)
    got = lax.ppermute(sent, AXES, lay.swap(kc=1))

    grad_attn, projected, sent = call(
        functools.partial(projection_kernel, lay),
        "projection",
        4 * model * 1000,
        [gp_spec, att_spec] + [whole_spec(w_out.shape)] * nc,
        [
            triple_spec,
            part_spec,
            pl.BlockSpec((chips, nc, step_patches, model), lambda i, *_: (0, 0, i, 0)),
        ],
        [triple_shape, struct((nc, half, model), F32), struct((chips, nc, half, model))],
        [pltpu.VMEM((chip_width, model), BF16)],
        (steps,),
        prefetch=1,
    )(pos, grad_proj, attended, *wo_rows)
    others = lax.all_to_all(sent, ("y", "x"), split_axis=0, concat_axis=0, tiled=True)

    cut = kept + got
    grad_attn, cut = lax.optimization_barrier((grad_attn, cut))
    cut = lax.all_to_all(cut, "z", split_axis=0, concat_axis=0, tiled=True)
    grad_w_out = lax.ppermute(jnp.sum(cut, axis=0), AXES, lay.to_owner()) * jnp.float32(
        1.0 / math.sqrt(groups * lay.frames * patches)
    )

    def side_spec(count):
        return pl.BlockSpec((count, step_patches, model), lambda i, *_: (0, i, 0))

    side = chips // 2
    sums = call(
        functools.partial(backward_kernel, lay),
        "backward",
        10 * model * 1000,
        w_specs + [triple_spec] * 4,
        [side_spec(side)] * (2 * nc),
        [struct((side, half, model), F32)] * nc + [struct((side, half, model))] * nc,
        [w_scratch, pltpu.VMEM((halves, lay.frames, step_patches, 3 * cols), BF16)],
        (steps,),
    )(pos, info, *w_pieces, queries, keys, values, grad_attn)
    held, added = list(sums[:nc]), []
    for j in range(nc):
        bits = lay.chip_bits(j)
        keys_held = lay.halved(bits[0])
        added.append(lax.ppermute(sums[nc + j], AXES, chip_swap(bits[0])))
        for bit in bits[1:-1]:
            total = held[j] + added[j].astype(F32)
            out_at = [n for n, k in enumerate(keys_held) if k & bit]
            in_at = [n for n, k in enumerate(keys_held) if not k & bit]
            out_part = jnp.stack([total[n] for n in out_at]).astype(BF16)
            held[j] = jnp.stack([total[n] for n in in_at])
            added[j] = lax.ppermute(out_part, AXES, chip_swap(bit))
            keys_held = [keys_held[n] for n in in_at]

    *out_parts, last0, last1 = call(
        functools.partial(output_kernel, lay),
        "output",
        3 * model * 1000,
        [pair_spec(1)] * nc
        + [part_spec, pl.BlockSpec((chips, nc, step_patches, model), lambda i, *_: (0, 0, i, 0))]
        + [side_spec(2)] * (2 * nc)
        + [mod_spec],
        [x_spec] * (2 * nc),
        [struct((half, model))] * (2 * nc),
        grid=(steps,),
    )(pos, info, *own, projected, others, *held, *added, mod_table)
    last = [
        lax.ppermute(part, AXES, chip_swap(lay.chip_bits(j)[-1]))
        for j, part in enumerate((last0, last1))
    ]
    out_y = from_plane(out_parts)

    grad_parts = call(
        functools.partial(input_grad_kernel, lay),
        "input_grad",
        3 * model * 1000,
        [pair_spec(1)] * nc + [side_spec(1)] * (2 * nc) + [x_spec] * nc + [mod_spec],
        [x_spec] * nc,
        [struct((half, model))] * nc,
        grid=(steps,),
    )(pos, info, *own, *held, *added, *last, mod_table)
    grad_x = from_plane(grad_parts)
    return out_y, grad_x, grad_w_out


def solution(mesh):
    lay = Layout(mesh)
    grid = Mesh(mesh.devices.reshape(lay.ny, lay.nc, lay.nz, lay.nx), AXES)
    rows, cols = ("z", "x"), ("y", "c")
    frame = P(AXES, None, None)
    group = P(cols, None)
    return jax.shard_map(
        functools.partial(local, lay),
        mesh=grid,
        in_specs=(frame, frame, group, group, group, P(), P(rows, None), P(rows, None)),
        out_specs=(frame, frame, P(rows, cols)),
        check_vma=False,
    )
```

```python
import functools
import math

import jax
import jax.numpy as jnp
from jax import lax
from jax.experimental import pallas as pl
from jax.experimental.pallas import tpu as pltpu
from jax.sharding import Mesh, PartitionSpec as P

HEADS = 16
CORES = 2
AXES = ("y", "c", "z", "x")
BLOCK = 16
VMEM_LIMIT = 56 * 1024 * 1024
BF16 = jnp.bfloat16
F32 = jnp.float32


def dot(left, right):
    return jnp.dot(left, right, preferred_element_type=F32)


def dot_t(left, right):
    return lax.dot_general(left, right, (((1,), (1,)), ((), ())), preferred_element_type=F32)


def t_dot(left, right):
    return lax.dot_general(left, right, (((0,), (0,)), ((), ())), preferred_element_type=F32)


def normalize(values):
    centred = values - jnp.mean(values, axis=-1, keepdims=True)
    inv_sigma = lax.rsqrt(jnp.mean(centred * centred, axis=-1, keepdims=True) + 1e-06)
    return centred * inv_sigma, inv_sigma


class Layout:
    def __init__(self, mesh):
        groups, seq = mesh.shape["dp"], mesh.shape["seq"]
        self.nc = CORES
        self.ny = groups // CORES
        self.nz = groups
        self.nx = seq // self.nz
        self.chips = self.ny * self.nx
        self.frames = seq
        self.chip_heads = HEADS // self.chips
        self.halves = 2 if self.chip_heads % 2 == 0 else 1
        self.half_heads = self.chip_heads // self.halves

    def linear(self, y, c, z, x):
        return ((y * self.nc + c) * self.nz + z) * self.nx + x

    def perm(self, move):
        pairs = []
        for y in range(self.ny):
            for c in range(self.nc):
                for z in range(self.nz):
                    for x in range(self.nx):
                        pairs.append((self.linear(y, c, z, x), self.linear(*move(y, c, z, x))))
        return pairs

    def to_plane(self, k):
        return self.perm(
            lambda y, c, z, x: ((z % self.ny) ^ c, (z // self.ny) ^ k, c * self.ny + y, x)
        )

    def to_plane_from_neighbour(self, k):
        def move(y, c, z, x):
            y = y ^ 1
            return (z % self.ny) ^ c, (z // self.ny) ^ k, c * self.ny + y, x

        return self.perm(move)

    def from_plane(self, k):
        return [(target, source) for source, target in self.to_plane(k)]

    def swap(self, ky=0, kc=0, kz=0, kx=0):
        return self.perm(lambda y, c, z, x: (y ^ ky, c ^ kc, z ^ kz, x ^ kx))

    def row_block(self, y, x, i):
        if self.halves > 1:
            return (i * self.ny + y) * self.nx + x
        return self.nc * (y * self.nx + x) + i

    def rows_to_chip(self):
        reader = {
            self.row_block(y, x, i): (y, x, i)
            for y in range(self.ny)
            for x in range(self.nx)
            for i in range(self.nc)
        }

        def move(y, c, z, x):
            chip_y, chip_x, i = reader[z * self.nx + x]
            return chip_y, i, c * self.ny + (y ^ (z & 1)), chip_x

        return self.perm(move)

    def to_owner(self):
        def move(y, c, z, x):
            s = self.row_block(y, x, c)
            return z // self.nc, z % self.nc, s // self.nx, s % self.nx

        return self.perm(move)

    def chip_of(self, k):
        return k // self.nx, k % self.nx

    def bits(self, count):
        return [1 << b for b in range(count.bit_length() - 1)]

    def chip_bits(self, j):
        bits = self.bits(self.chips)
        return bits if j % 2 == 0 else bits[::-1]

    def doubled(self, bits):
        held = [0]
        for bit in bits:
            held = held + [k ^ bit for k in held]
        return held

    def halved(self, bit):
        return [k for k in range(self.chips) if not k & bit]

    def slots(self):
        return [(k, j) for k in range(self.chips) for j in range(self.nc)]


def slot_scalars(lay, pos_ref, info_ref, slot):
    k, j = slot
    ky, kx = lay.chip_of(k)
    z_frame = (pos_ref[1] ^ j) * lay.ny + (pos_ref[0] ^ ky ^ (pos_ref[2] // lay.ny))
    frame = z_frame * lay.nx + (pos_ref[3] ^ kx)
    clip = info_ref[frame]
    clips = (info_ref.shape[0] - lay.frames) // 2
    return clip, info_ref[lay.frames + clip], info_ref[lay.frames + clips + clip]


def table_row(mod_ref, step, part, width):
    return mod_ref[pl.ds(step, 1), part * width : (part + 1) * width]


def allowed_pairs(lay, pos_ref, info_ref, patch_base):
    rows = lay.frames * BLOCK
    row_slot = lax.broadcasted_iota(jnp.int32, (rows, 1), 0) // BLOCK
    col_slot = lax.broadcasted_iota(jnp.int32, (1, rows), 1) // BLOCK
    row_clip = jnp.zeros((rows, 1), jnp.int32)
    row_limit = jnp.zeros((rows, 1), jnp.int32)
    col_clip = jnp.zeros((1, rows), jnp.int32)
    for t, slot in enumerate(lay.slots()):
        clip, limit, _ = slot_scalars(lay, pos_ref, info_ref, slot)
        row_clip = jnp.where(row_slot == t, clip, row_clip)
        row_limit = jnp.where(row_slot == t, limit, row_limit)
        col_clip = jnp.where(col_slot == t, clip, col_clip)
    row_patch = lax.broadcasted_iota(jnp.int32, (rows, 1), 0) % BLOCK
    col_patch = lax.broadcasted_iota(jnp.int32, (1, rows), 1) % BLOCK
    row_key = row_clip * BLOCK + row_patch
    col_key = col_clip * BLOCK + col_patch
    row_valid = (patch_base + row_patch < row_limit).astype(jnp.int32)
    row_index = lax.broadcasted_iota(jnp.int32, (rows, rows), 0)
    col_index = lax.broadcasted_iota(jnp.int32, (rows, rows), 1)
    return (row_key == col_key) & ((row_valid > 0) | (row_index == col_index))


def head_mask(values, head, head_size):
    lane = lax.broadcasted_iota(jnp.int32, (1, values.shape[1]), 1)
    inside = (lane >= head * head_size) & (lane < (head + 1) * head_size)
    return jnp.where(inside, values, jnp.zeros_like(values))


def patch_blocks(array, block):
    part = array[:, block * BLOCK : (block + 1) * BLOCK, :]
    return part.reshape(part.shape[0] * BLOCK, part.shape[2])


def pick_kernel(lay, cols, pos_ref, w_ref, *out_refs):
    model = w_ref.shape[1] // 3
    for k, out_ref in enumerate(out_refs):
        chip_x = pos_ref[3] ^ k
        if lay.halves > 1:
            want = lay.row_block(pos_ref[0], chip_x, pos_ref[1])
        else:
            want = pos_ref[0] * lay.nx + chip_x
        for v in range(lay.chips * lay.halves):

            @pl.when(want == v)
            def _(v=v, out_ref=out_ref):
                parts = [
                    w_ref[:, p * model + v * cols : p * model + (v + 1) * cols]
                    for p in range(3)
                ]
                out_ref[...] = jnp.concatenate(parts, axis=1)


def fill_weights(lay, pos_ref, w_refs, w_scr):
    order = lay.doubled(lay.bits(lay.nz)[::-1])
    block = w_scr.shape[1] // lay.nz
    rows, width = w_refs[0].shape[1], w_scr.shape[2]
    for h in range(lay.halves):
        for n, k in enumerate(order):
            ref, place = w_refs[2 * h + (2 * n) // lay.nz], n % (lay.nz // 2)
            for m in range(block // rows):
                start = pl.multiple_of((pos_ref[2] ^ k) * block + m * rows, 16)
                w_scr[h, pl.ds(start, rows), :] = ref[place, :, m * width : (m + 1) * width]


def heads_stacked(lay, values):
    head_size = values.shape[1] // lay.half_heads
    parts = [head_mask(values, head, head_size) for head in range(lay.half_heads)]
    return jnp.concatenate(parts, axis=0) if len(parts) > 1 else parts[0]


def beside(lay, weights):
    return jnp.concatenate([weights[head] for head in range(lay.half_heads)], axis=1)


def attention_weights(lay, keys_stacked, queries, allowed, scaling):
    scores = dot_t(keys_stacked, queries) * scaling
    scores = jnp.where(allowed, scores.reshape((lay.half_heads,) + allowed.shape), -jnp.inf)
    exponent = jnp.exp(scores - jnp.max(scores, axis=1, keepdims=True))
    return exponent * (1.0 / jnp.sum(exponent, axis=1, keepdims=True))


def prepare_kernel(lay, pos_ref, info_ref, *refs):
    pair_refs, (mod_ref, hid_ref, gp_ref) = refs[: 2 * lay.nc], refs[2 * lay.nc :]
    _, step_patches, model = hid_ref.shape
    patches = step_patches * pl.num_programs(0)
    patch_base = pos_ref[1] * patches + pl.program_id(0) * step_patches
    patch = patch_base + lax.broadcasted_iota(jnp.int32, (step_patches, 1), 0)
    for t, (k, j) in enumerate(lay.slots()):
        _, limit, step = slot_scalars(lay, pos_ref, info_ref, (k, j))
        n = lay.doubled(lay.chip_bits(j)).index(k)
        ref, place = pair_refs[2 * j + (2 * n) // lay.chips], n % (lay.chips // 2)
        normed, _ = normalize(ref[place, 0].astype(F32))
        shift, scale = table_row(mod_ref, step, 0, model), table_row(mod_ref, step, 1, model)
        hid_ref[t] = (normed * (1.0 + scale) + shift).astype(BF16)
        factor = jnp.where(patch < limit, table_row(mod_ref, step, 2, model), 0.0)
        gp_ref[t] = (factor * ref[place, 1].astype(F32)).astype(BF16)


def forward_kernel(lay, pos_ref, info_ref, hid_ref, *refs):
    w_refs, refs = refs[: 2 * lay.halves], refs[2 * lay.halves :]
    q_ref, k_ref, v_ref, att_ref, w_scr = refs
    _, step_patches, model = hid_ref.shape
    cols = w_scr.shape[2] // 3
    scaling = 1.0 / math.sqrt(cols // lay.half_heads)
    patches = step_patches * pl.num_programs(0)

    @pl.when(pl.program_id(0) == 0)
    def _():
        fill_weights(lay, pos_ref, w_refs, w_scr)

    hidden = hid_ref[...].reshape(lay.frames * step_patches, model)
    for h in range(lay.halves):
        triple = dot(hidden, w_scr[h])
        for n, ref in enumerate((q_ref, k_ref, v_ref)):
            ref[h] = triple[:, n * cols : (n + 1) * cols].astype(BF16).reshape(ref.shape[1:])

    for b in range(step_patches // BLOCK):
        patch_base = pos_ref[1] * patches + pl.program_id(0) * step_patches + b * BLOCK
        allowed = allowed_pairs(lay, pos_ref, info_ref, patch_base)
        outputs = []
        for h in range(lay.halves):
            queries, keys, values = (patch_blocks(ref[h], b) for ref in (q_ref, k_ref, v_ref))
            weights = attention_weights(lay, heads_stacked(lay, keys), queries, allowed, scaling)
            weights = weights.astype(BF16).reshape(-1, allowed.shape[1])
            outputs.append(t_dot(weights, heads_stacked(lay, values)))
        if lay.halves > 1:
            first = jnp.where(pos_ref[1] == 0, outputs[0], outputs[1])
            second = jnp.where(pos_ref[1] == 0, outputs[1], outputs[0])
            outputs = [jnp.concatenate([first, second], axis=1)]
        attended = outputs[0].astype(BF16)
        att_ref[:, b * BLOCK : (b + 1) * BLOCK, :] = attended.reshape(lay.frames, BLOCK, -1)


def weight_grad_kernel(lay, pos_ref, gp_ref, att_ref, kept_ref, sent_ref, acc_scr, cut_scr):
    _, step_patches, model = gp_ref.shape
    tokens = lay.frames * step_patches
    groups, chunk_rows, chunk_width = kept_ref.shape
    block_rows, part = acc_scr.shape[0] // lay.nc, model // groups
    fold = chunk_width // part
    order = lay.doubled(lay.bits(lay.nz)[::-1])
    is_first = pos_ref[1] == 0

    @pl.when(pl.program_id(0) == 0)
    def _():
        acc_scr[...] = jnp.zeros_like(acc_scr)

    attended = att_ref[...].reshape(tokens, -1)
    acc_scr[...] += t_dot(attended, gp_ref[...].reshape(tokens, model))

    @pl.when(pl.program_id(0) == pl.num_programs(0) - 1)
    def _():
        first, second = acc_scr[:block_rows, :], acc_scr[block_rows:, :]
        kept = jnp.where(is_first, first, second)
        sent = jnp.where(is_first, second, first)
        for ref, rows in ((kept_ref, kept), (sent_ref, sent)):
            for d in range(groups):
                chunk = [
                    rows[m * chunk_rows : (m + 1) * chunk_rows, d * part : (d + 1) * part]
                    for m in range(fold)
                ]
                cut_scr[d] = jnp.concatenate(chunk, axis=1) if fold > 1 else chunk[0]
            for n, k in enumerate(order):
                ref[n] = cut_scr[pos_ref[2] ^ k]


def projection_kernel(lay, pos_ref, gp_ref, att_ref, *refs):
    wo_refs, refs = refs[: lay.nc], refs[lay.nc :]
    ga_ref, *refs = refs
    pr_refs, (wo_scr,) = refs[: lay.chips], refs[lay.chips :]
    _, step_patches, model = gp_ref.shape
    tokens = lay.frames * step_patches
    is_first = pos_ref[1] == 0

    @pl.when(pl.program_id(0) == 0)
    def _():
        own, other = wo_refs[0][...].astype(F32), wo_refs[1][...].astype(F32)
        both = [jnp.where(is_first, own, other), jnp.where(is_first, other, own)]
        wo_scr[...] = jnp.concatenate(both, axis=0).astype(BF16)

    grad_attn = dot_t(gp_ref[...].reshape(tokens, model), wo_scr[...])
    part = wo_scr.shape[0] // lay.halves
    for h in range(lay.halves):
        ga_ref[h] = grad_attn[:, h * part : (h + 1) * part].astype(BF16).reshape(ga_ref.shape[1:])
    attended = att_ref[...].reshape(tokens, -1)
    projected = dot(attended, wo_scr[...]).reshape(lay.chips, lay.nc, step_patches, model)
    for k in range(lay.chips):
        pr_refs[k][...] = projected[k].astype(pr_refs[k].dtype)


def backward_kernel(lay, pos_ref, info_ref, *refs):
    w_refs, refs = refs[: 2 * lay.halves], refs[2 * lay.halves :]
    q_ref, k_ref, v_ref, ga_ref, *refs = refs
    kept_refs, refs = refs[: lay.nc], refs[lay.nc :]
    sent_refs, (w_scr, gt_scr) = refs[: lay.nc], refs[lay.nc :]
    _, frames, step_patches, cols = q_ref.shape
    model = w_scr.shape[1]
    patches = step_patches * pl.num_programs(0)
    scaling = 1.0 / math.sqrt(cols // lay.half_heads)

    @pl.when(pl.program_id(0) == 0)
    def _():
        fill_weights(lay, pos_ref, w_refs, w_scr)

    for b in range(step_patches // BLOCK):
        patch_base = pos_ref[1] * patches + pl.program_id(0) * step_patches + b * BLOCK
        allowed = allowed_pairs(lay, pos_ref, info_ref, patch_base)
        for h in range(lay.halves):
            queries, keys, values = (patch_blocks(ref[h], b) for ref in (q_ref, k_ref, v_ref))
            grad_out = patch_blocks(ga_ref[(pos_ref[1] ^ h) if lay.halves > 1 else 0], b)
            keys = heads_stacked(lay, keys)
            weights = attention_weights(lay, keys, queries, allowed, scaling)
            grad_weights = dot_t(heads_stacked(lay, values), grad_out).reshape(weights.shape)
            grad_values = dot(beside(lay, weights.astype(BF16)), heads_stacked(lay, grad_out))
            inner = jnp.sum(weights * grad_weights, axis=1, keepdims=True)
            grad_scores = (weights * (grad_weights - inner) * scaling).astype(BF16)
            grad_queries = t_dot(grad_scores.reshape(-1, grad_scores.shape[2]), keys)
            grad_keys = dot(beside(lay, grad_scores), heads_stacked(lay, queries))
            grads = jnp.concatenate([grad_queries, grad_keys, grad_values], axis=1).astype(BF16)
            gt_scr[h, :, b * BLOCK : (b + 1) * BLOCK, :] = grads.reshape(frames, BLOCK, 3 * cols)

    rows = lay.nc * step_patches
    for k in range(lay.chips):
        total = jnp.zeros((rows, model), F32)
        for h in range(lay.halves):
            part = gt_scr[h, k * lay.nc : (k + 1) * lay.nc].reshape(rows, 3 * cols)
            total = total + dot_t(part, w_scr[h])
        total = total.reshape(lay.nc, step_patches, model)
        for j in range(lay.nc):
            first = lay.chip_bits(j)[0]
            place = lay.halved(first).index(k & ~first)
            if k & first:
                sent_refs[j][place] = total[j].astype(BF16)
            else:
                kept_refs[j][place] = total[j]


def output_kernel(lay, pos_ref, info_ref, *refs):
    pair_refs, refs = refs[: lay.nc], refs[lay.nc :]
    pr_refs, refs = refs[: lay.chips], refs[lay.chips :]
    kept_refs, refs = refs[: lay.nc], refs[lay.nc :]
    add_refs, refs = refs[: lay.nc], refs[lay.nc :]
    mod_ref, *refs = refs
    out_refs, sum_refs = refs[: lay.nc], refs[lay.nc :]
    step_patches, model = out_refs[0].shape
    patches = step_patches * pl.num_programs(0)
    patch_base = pos_ref[1] * patches + pl.program_id(0) * step_patches
    patch = patch_base + lax.broadcasted_iota(jnp.int32, (step_patches, 1), 0)
    for j in range(lay.nc):
        _, limit, step = slot_scalars(lay, pos_ref, info_ref, (0, j))
        factor = jnp.where(patch < limit, table_row(mod_ref, step, 2, model), 0.0)
        projected = pr_refs[0][j]
        for k in range(1, lay.chips):
            projected = projected + pr_refs[k][j].astype(F32)
        projected = projected.astype(BF16).astype(F32)
        out_refs[j][...] = (pair_refs[j][0, 0].astype(F32) + factor * projected).astype(BF16)
        sum_refs[j][...] = (kept_refs[j][1] + add_refs[j][1].astype(F32)).astype(BF16)


def input_grad_kernel(lay, pos_ref, info_ref, *refs):
    pair_refs, refs = refs[: lay.nc], refs[lay.nc :]
    kept_refs, refs = refs[: lay.nc], refs[lay.nc :]
    add_refs, refs = refs[: lay.nc], refs[lay.nc :]
    last_refs, refs = refs[: lay.nc], refs[lay.nc :]
    mod_ref, *out_refs = refs
    model = out_refs[0].shape[1]
    for j in range(lay.nc):
        _, _, step = slot_scalars(lay, pos_ref, info_ref, (0, j))
        grad_hidden = kept_refs[j][0] + add_refs[j][0].astype(F32)
        grad_hidden = grad_hidden + last_refs[j][...].astype(F32)
        grad_hidden = grad_hidden.astype(BF16).astype(F32)
        normed, inv_sigma = normalize(pair_refs[j][0, 0].astype(F32))
        grad_norm = grad_hidden * (1.0 + table_row(mod_ref, step, 1, model))
        first_mean = jnp.mean(grad_norm, axis=-1, keepdims=True)
        second_mean = jnp.mean(grad_norm * normed, axis=-1, keepdims=True)
        grad_x = pair_refs[j][0, 1].astype(F32) + inv_sigma * (
            grad_norm - first_mean - normed * second_mean
        )
        out_refs[j][...] = grad_x.astype(BF16)


def whole_spec(shape):
    return pl.BlockSpec(shape, lambda *_: (0,) * len(shape))


def struct(shape, dtype=BF16):
    return jax.ShapeDtypeStruct(shape, dtype)


def local(lay, frames_x, grad_y, clip_ids, clip_patches, clip_step, mod_table, w_qkv, w_out):
    y, c, z, x = (lax.axis_index(name) for name in AXES)
    _, patches, model = frames_x.shape
    half = patches // lay.nc
    chips, nc, nx = lay.chips, lay.nc, lay.nx
    head_size = model // HEADS
    halves = lay.halves
    cols = lay.half_heads * head_size
    chip_width = lay.chip_heads * head_size
    rows = w_qkv.shape[0]
    groups = lay.nz
    quarter = model // groups
    step_patches = max(BLOCK, min(half, 512 // lay.frames))
    steps = half // step_patches
    tokens = lay.frames * step_patches

    def call(kernel, name, cost, in_specs, out_specs, out_shape, scratch=(), grid=(1,), prefetch=2):
        return pl.pallas_call(
            kernel,
            grid_spec=pltpu.PrefetchScalarGridSpec(
                num_scalar_prefetch=prefetch,
                grid=grid,
                in_specs=in_specs,
                out_specs=out_specs,
                scratch_shapes=list(scratch),
            ),
            out_shape=out_shape,
            compiler_params=pltpu.CompilerParams(vmem_limit_bytes=VMEM_LIMIT),
            cost_estimate=pl.CostEstimate(
                flops=cost * tokens * steps, bytes_accessed=4 * model * tokens, transcendentals=0
            ),
            name=name,
        )

    def chip_swap(k):
        ky, kx = lay.chip_of(k)
        return lay.swap(ky=ky, kx=kx)

    def doubling(held, bits, swap):
        for bit in bits[:-1]:
            held = jnp.concatenate([held, lax.ppermute(held, AXES, swap(bit))], axis=0)
        return [held, lax.ppermute(held, AXES, swap(bits[-1]))]

    def from_plane(parts):
        got = [lax.ppermute(part, AXES, lay.from_plane(k)) for k, part in enumerate(parts)]
        first = jnp.where(z // lay.ny == 0, got[0], got[1])
        second = jnp.where(z // lay.ny == 0, got[1], got[0])
        return jnp.concatenate([first, second], axis=0)[None]

    info = jnp.concatenate([clip_ids[0], clip_patches[0], clip_step[0]])[None]
    info = lax.ppermute(info, AXES, lay.to_plane(0))[0]
    pos = jnp.stack([y, c, z, x]).astype(jnp.int32)
    own = []
    for k in range(nc):
        start = ((z // lay.ny) ^ k) * half
        pair = [lax.dynamic_slice_in_dim(frame, start, half, axis=1) for frame in (frames_x, grad_y)]
        pair = jnp.stack(pair, axis=1)
        if k == 0:
            own.append(lax.ppermute(pair, AXES, lay.to_plane(k)))
        else:
            pair = lax.ppermute(pair, AXES, lay.swap(ky=1))
            own.append(lax.ppermute(pair, AXES, lay.to_plane_from_neighbour(k)))
    own[0], info = lax.optimization_barrier((own[0], info))
    pairs = []
    for j in range(nc):
        pairs += doubling(own[j], lay.chip_bits(j), chip_swap)

    picked = call(
        functools.partial(pick_kernel, lay, cols),
        "pick",
        2 * model * 1000,
        [whole_spec(w_qkv.shape)],
        [whole_spec((rows, 3 * cols))] * nx,
        [struct((rows, 3 * cols))] * nx,
        prefetch=1,
    )(pos, w_qkv)
    by_x = [picked[0]] + [
        lax.ppermute(picked[kx], AXES, lay.swap(kx=kx)) for kx in range(1, nx)
    ]
    if nx == 2:
        ordered = [jnp.where(x == i, by_x[0], by_x[1]) for i in range(nx)]
    else:
        stacked = jnp.stack(by_x)
        ordered = [lax.dynamic_index_in_dim(stacked, x ^ i, 0, keepdims=False) for i in range(nx)]
    w_own = jnp.concatenate(ordered, axis=1 if rows % 16 == 0 else 0)[None]
    w_pieces = doubling(w_own, lay.bits(lay.nz)[::-1], lambda kz: lay.swap(kz=kz))
    if halves > 1:
        w_pieces += [lax.ppermute(piece, AXES, lay.swap(kc=1)) for piece in w_pieces]

    late_w_out, _ = lax.optimization_barrier((w_out, w_pieces[:2]))
    wo_own = lax.ppermute(late_w_out, AXES, lay.rows_to_chip())
    wo_rows = [wo_own, lax.ppermute(wo_own, AXES, lay.swap(kc=1))]

    x_spec = pl.BlockSpec((step_patches, model), lambda i, *_: (i, 0))

    def pair_spec(count):
        return pl.BlockSpec((count, 2, step_patches, model), lambda i, *_: (0, 0, i, 0))

    triple_spec = pl.BlockSpec((halves, lay.frames, step_patches, cols), lambda i, *_: (0, 0, i, 0))
    att_spec = pl.BlockSpec((lay.frames, step_patches, chip_width), lambda i, *_: (0, i, 0))
    gp_spec = pl.BlockSpec((lay.frames, step_patches, model), lambda i, *_: (0, i, 0))
    part_spec = pl.BlockSpec((nc, step_patches, model), lambda i, *_: (0, i, 0))
    w_specs = [whole_spec(piece.shape) for piece in w_pieces]
    w_scratch = pltpu.VMEM((halves, model, 3 * cols), BF16)
    mod_spec = whole_spec(mod_table.shape)
    triple_shape = struct((halves, lay.frames, half, cols))

    hidden, grad_proj = call(
        functools.partial(prepare_kernel, lay),
        "prepare",
        3 * model * 1000,
        [pair_spec(chips // 2)] * (2 * nc) + [mod_spec],
        [gp_spec] * 2,
        [struct((lay.frames, half, model))] * 2,
        grid=(steps,),
    )(pos, info, *pairs, mod_table)

    queries, keys, values, attended = call(
        functools.partial(forward_kernel, lay),
        "forward",
        8 * model * 1000,
        [gp_spec] + w_specs,
        [triple_spec] * 3 + [att_spec],
        [triple_shape] * 3 + [struct((lay.frames, half, chip_width))],
        [w_scratch],
        (steps,),
    )(pos, info, hidden, *w_pieces)

    fold = 3 if rows % 24 == 0 else 1
    piece_shape = (groups, rows // fold, quarter * fold)
    kept, sent = call(
        functools.partial(weight_grad_kernel, lay),
        "weight_grad",
        4 * model * 1000,
        [gp_spec, att_spec],
        [whole_spec(piece_shape)] * 2,
        [struct(piece_shape, F32)] * 2,
        [pltpu.VMEM((chip_width, model), F32), pltpu.VMEM(piece_shape, F32)],
        (steps,),
        prefetch=1,
    )(pos, grad_proj, attended)
    got = lax.ppermute(sent, AXES, lay.swap(kc=1))

    grad_attn, *projected = call(
        functools.partial(projection_kernel, lay),
        "projection",
        4 * model * 1000,
        [gp_spec, att_spec] + [whole_spec(w_out.shape)] * nc,
        [triple_spec] + [part_spec] * chips,
        [triple_shape, struct((nc, half, model), F32)] + [struct((nc, half, model))] * (chips - 1),
        [pltpu.VMEM((chip_width, model), BF16)],
        (steps,),
        prefetch=1,
    )(pos, grad_proj, attended, *wo_rows)
    projected = [projected[0]] + [
        lax.ppermute(projected[k], AXES, chip_swap(k)) for k in range(1, chips)
    ]

    middle = groups // 2
    cut, away = kept[:middle] + got[:middle], kept[middle:] + got[middle:]
    grad_attn, cut, away = lax.optimization_barrier((grad_attn, cut, away))
    first_away = lax.ppermute(away, AXES, lay.swap(kz=1))

    def side_spec(count):
        return pl.BlockSpec((count, step_patches, model), lambda i, *_: (0, i, 0))

    side = chips // 2
    sums = call(
        functools.partial(backward_kernel, lay),
        "backward",
        10 * model * 1000,
        w_specs + [triple_spec] * 4,
        [side_spec(side)] * (2 * nc),
        [struct((side, half, model), F32)] * nc + [struct((side, half, model))] * nc,
        [w_scratch, pltpu.VMEM((halves, lay.frames, step_patches, 3 * cols), BF16)],
        (steps,),
    )(pos, info, *w_pieces, queries, keys, values, grad_attn)
    sums, first_away, projected = lax.optimization_barrier((sums, first_away, projected))
    cut = cut + first_away
    for bit in lay.bits(lay.nz)[1:]:
        middle = middle // 2
        cut = cut[:middle] + lax.ppermute(cut[middle:], AXES, lay.swap(kz=bit))
    projected, cut = lax.optimization_barrier((projected, cut))
    grad_w = lax.ppermute(cut[0], AXES, lay.to_owner())
    grad_w = jnp.concatenate(
        [grad_w[:, m * quarter : (m + 1) * quarter] for m in range(fold)], axis=0
    )
    grad_w_out = grad_w * jnp.float32(1.0 / math.sqrt(groups * lay.frames * patches))

    held, added = list(sums[:nc]), []
    for j in range(nc):
        bits = lay.chip_bits(j)
        keys_held = lay.halved(bits[0])
        added.append(lax.ppermute(sums[nc + j], AXES, chip_swap(bits[0])))
        for bit in bits[1:-1]:
            total = held[j] + added[j].astype(F32)
            out_at = [n for n, k in enumerate(keys_held) if k & bit]
            in_at = [n for n, k in enumerate(keys_held) if not k & bit]
            out_part = jnp.stack([total[n] for n in out_at]).astype(BF16)
            held[j] = jnp.stack([total[n] for n in in_at])
            added[j] = lax.ppermute(out_part, AXES, chip_swap(bit))
            keys_held = [keys_held[n] for n in in_at]

    *out_parts, last0, last1 = call(
        functools.partial(output_kernel, lay),
        "output",
        3 * model * 1000,
        [pair_spec(1)] * nc
        + [part_spec] * chips
        + [side_spec(2)] * (2 * nc)
        + [mod_spec],
        [x_spec] * (2 * nc),
        [struct((half, model))] * (2 * nc),
        grid=(steps,),
    )(pos, info, *own, *projected, *held, *added, mod_table)
    last = [
        lax.ppermute(part, AXES, chip_swap(lay.chip_bits(j)[-1]))
        for j, part in enumerate((last0, last1))
    ]
    out_y = from_plane(out_parts)

    grad_parts = call(
        functools.partial(input_grad_kernel, lay),
        "input_grad",
        3 * model * 1000,
        [pair_spec(1)] * nc + [side_spec(1)] * (2 * nc) + [x_spec] * nc + [mod_spec],
        [x_spec] * nc,
        [struct((half, model))] * nc,
        grid=(steps,),
    )(pos, info, *own, *held, *added, *last, mod_table)
    grad_x = from_plane(grad_parts)
    return out_y, grad_x, grad_w_out


def solution(mesh):
    lay = Layout(mesh)
    grid = Mesh(mesh.devices.reshape(lay.ny, lay.nc, lay.nz, lay.nx), AXES)
    rows, cols = ("z", "x"), ("y", "c")
    frame = P(AXES, None, None)
    group = P(cols, None)
    return jax.shard_map(
        functools.partial(local, lay),
        mesh=grid,
        in_specs=(frame, frame, group, group, group, P(), P(rows, None), P(rows, None)),
        out_specs=(frame, frame, P(rows, cols)),
        check_vma=False,
    )
```

```python
import functools
import math

import jax
import jax.numpy as jnp
from jax import lax
from jax.experimental import pallas as pl
from jax.experimental.pallas import tpu as pltpu
from jax.sharding import Mesh, PartitionSpec as P

HEADS = 16
CORES = 2
AXES = ("y", "c", "z", "x")
BLOCK = 16
VMEM_LIMIT = 56 * 1024 * 1024
BF16 = jnp.bfloat16
F32 = jnp.float32


def dot(left, right):
    return jnp.dot(left, right, preferred_element_type=F32)


def dot_t(left, right):
    return lax.dot_general(left, right, (((1,), (1,)), ((), ())), preferred_element_type=F32)


def t_dot(left, right):
    return lax.dot_general(left, right, (((0,), (0,)), ((), ())), preferred_element_type=F32)


def normalize(values):
    centred = values - jnp.mean(values, axis=-1, keepdims=True)
    inv_sigma = lax.rsqrt(jnp.mean(centred * centred, axis=-1, keepdims=True) + 1e-06)
    return centred * inv_sigma, inv_sigma


class Layout:
    def __init__(self, mesh):
        groups, seq = mesh.shape["dp"], mesh.shape["seq"]
        self.nc = CORES
        self.ny = groups // CORES
        self.nz = groups
        self.nx = seq // self.nz
        self.chips = self.ny * self.nx
        self.frames = seq
        self.chip_heads = HEADS // self.chips
        self.halves = 2 if self.chip_heads % 2 == 0 else 1
        self.half_heads = self.chip_heads // self.halves

    def linear(self, y, c, z, x):
        return ((y * self.nc + c) * self.nz + z) * self.nx + x

    def perm(self, move):
        pairs = []
        for y in range(self.ny):
            for c in range(self.nc):
                for z in range(self.nz):
                    for x in range(self.nx):
                        pairs.append((self.linear(y, c, z, x), self.linear(*move(y, c, z, x))))
        return pairs

    def to_plane(self, k):
        return self.perm(
            lambda y, c, z, x: ((z % self.ny) ^ c, (z // self.ny) ^ k, c * self.ny + y, x)
        )

    def from_plane(self, k):
        return [(target, source) for source, target in self.to_plane(k)]

    def swap(self, ky=0, kc=0, kz=0, kx=0):
        return self.perm(lambda y, c, z, x: (y ^ ky, c ^ kc, z ^ kz, x ^ kx))

    def row_block(self, y, x, i):
        if self.halves > 1:
            return (i * self.ny + y) * self.nx + x
        return self.nc * (y * self.nx + x) + i

    def rows_to_chip(self):
        reader = {
            self.row_block(y, x, i): (y, x, i)
            for y in range(self.ny)
            for x in range(self.nx)
            for i in range(self.nc)
        }

        def move(y, c, z, x):
            chip_y, chip_x, i = reader[z * self.nx + x]
            return chip_y, i, c * self.ny + (y ^ (z & 1)), chip_x

        return self.perm(move)

    def to_owner(self):
        def move(y, c, z, x):
            s = self.row_block(y, x, c)
            return z // self.nc, z % self.nc, s // self.nx, s % self.nx

        return self.perm(move)

    def chip_of(self, k):
        return k // self.nx, k % self.nx

    def bits(self, count):
        return [1 << b for b in range(count.bit_length() - 1)]

    def chip_bits(self, j):
        bits = self.bits(self.chips)
        return bits if j % 2 == 0 else bits[::-1]

    def doubled(self, bits):
        held = [0]
        for bit in bits:
            held = held + [k ^ bit for k in held]
        return held

    def slots(self):
        return [(k, j) for k in range(self.chips) for j in range(self.nc)]


def slot_scalars(lay, pos_ref, info_ref, slot):
    k, j = slot
    ky, kx = lay.chip_of(k)
    z_frame = (pos_ref[1] ^ j) * lay.ny + (pos_ref[0] ^ ky ^ (pos_ref[2] // lay.ny))
    frame = z_frame * lay.nx + (pos_ref[3] ^ kx)
    clip = info_ref[frame]
    clips = (info_ref.shape[0] - lay.frames) // 2
    return clip, info_ref[lay.frames + clip], info_ref[lay.frames + clips + clip]


def table_row(mod_ref, step, part, width):
    return mod_ref[pl.ds(step, 1), part * width : (part + 1) * width]


def allowed_pairs(lay, pos_ref, info_ref, patch_base):
    rows = lay.frames * BLOCK
    row_slot = lax.broadcasted_iota(jnp.int32, (rows, 1), 0) // BLOCK
    col_slot = lax.broadcasted_iota(jnp.int32, (1, rows), 1) // BLOCK
    row_clip = jnp.zeros((rows, 1), jnp.int32)
    row_limit = jnp.zeros((rows, 1), jnp.int32)
    col_clip = jnp.zeros((1, rows), jnp.int32)
    for t, slot in enumerate(lay.slots()):
        clip, limit, _ = slot_scalars(lay, pos_ref, info_ref, slot)
        row_clip = jnp.where(row_slot == t, clip, row_clip)
        row_limit = jnp.where(row_slot == t, limit, row_limit)
        col_clip = jnp.where(col_slot == t, clip, col_clip)
    row_patch = lax.broadcasted_iota(jnp.int32, (rows, 1), 0) % BLOCK
    col_patch = lax.broadcasted_iota(jnp.int32, (1, rows), 1) % BLOCK
    row_key = row_clip * BLOCK + row_patch
    col_key = col_clip * BLOCK + col_patch
    row_valid = (patch_base + row_patch < row_limit).astype(jnp.int32)
    row_index = lax.broadcasted_iota(jnp.int32, (rows, rows), 0)
    col_index = lax.broadcasted_iota(jnp.int32, (rows, rows), 1)
    return (row_key == col_key) & ((row_valid > 0) | (row_index == col_index))


def head_mask(values, head, head_size):
    lane = lax.broadcasted_iota(jnp.int32, (1, values.shape[1]), 1)
    inside = (lane >= head * head_size) & (lane < (head + 1) * head_size)
    return jnp.where(inside, values, jnp.zeros_like(values))


def patch_blocks(array, block):
    part = array[:, block * BLOCK : (block + 1) * BLOCK, :]
    return part.reshape(part.shape[0] * BLOCK, part.shape[2])


def pick_kernel(lay, cols, pos_ref, w_ref, *out_refs):
    model = w_ref.shape[1] // 3
    for k, out_ref in enumerate(out_refs):
        chip_x = pos_ref[3] ^ k
        if lay.halves > 1:
            want = lay.row_block(pos_ref[0], chip_x, pos_ref[1])
        else:
            want = pos_ref[0] * lay.nx + chip_x
        for v in range(lay.chips * lay.halves):

            @pl.when(want == v)
            def _(v=v, out_ref=out_ref):
                parts = [
                    w_ref[:, p * model + v * cols : p * model + (v + 1) * cols]
                    for p in range(3)
                ]
                out_ref[...] = jnp.concatenate(parts, axis=1)


def fill_weights(lay, pos_ref, w_refs, w_scr):
    order = lay.doubled(lay.bits(lay.nz)[::-1])
    block = w_scr.shape[1] // lay.nz
    rows, width = w_refs[0].shape[1], w_scr.shape[2]
    for h in range(lay.halves):
        for n, k in enumerate(order):
            ref, place = w_refs[2 * h + (2 * n) // lay.nz], n % (lay.nz // 2)
            for m in range(block // rows):
                start = pl.multiple_of((pos_ref[2] ^ k) * block + m * rows, 16)
                w_scr[h, pl.ds(start, rows), :] = ref[place, :, m * width : (m + 1) * width]


def heads_stacked(lay, values):
    head_size = values.shape[1] // lay.half_heads
    parts = [head_mask(values, head, head_size) for head in range(lay.half_heads)]
    return jnp.concatenate(parts, axis=0) if len(parts) > 1 else parts[0]


def beside(lay, weights):
    return jnp.concatenate([weights[head] for head in range(lay.half_heads)], axis=1)


def attention_weights(lay, keys_stacked, queries, allowed, scaling):
    scores = dot_t(keys_stacked, queries) * scaling
    scores = jnp.where(allowed, scores.reshape((lay.half_heads,) + allowed.shape), -jnp.inf)
    exponent = jnp.exp(scores - jnp.max(scores, axis=1, keepdims=True))
    return exponent * (1.0 / jnp.sum(exponent, axis=1, keepdims=True))


def prepare_kernel(lay, pos_ref, info_ref, *refs):
    pair_refs, (mod_ref, hid_ref, gp_ref) = refs[: 2 * lay.nc], refs[2 * lay.nc :]
    _, step_patches, model = hid_ref.shape
    patches = step_patches * pl.num_programs(0)
    patch_base = pos_ref[1] * patches + pl.program_id(0) * step_patches
    patch = patch_base + lax.broadcasted_iota(jnp.int32, (step_patches, 1), 0)
    for t, (k, j) in enumerate(lay.slots()):
        _, limit, step = slot_scalars(lay, pos_ref, info_ref, (k, j))
        n = lay.doubled(lay.chip_bits(j)).index(k)
        ref, place = pair_refs[2 * j + (2 * n) // lay.chips], n % (lay.chips // 2)
        normed, _ = normalize(ref[place, 0].astype(F32))
        shift, scale = table_row(mod_ref, step, 0, model), table_row(mod_ref, step, 1, model)
        hid_ref[t] = (normed * (1.0 + scale) + shift).astype(BF16)
        factor = jnp.where(patch < limit, table_row(mod_ref, step, 2, model), 0.0)
        gp_ref[t] = (factor * ref[place, 1].astype(F32)).astype(BF16)


def forward_kernel(lay, pos_ref, info_ref, hid_ref, gp_ref, *refs):
    w_refs, refs = refs[: 2 * lay.halves], refs[2 * lay.halves :]
    wo_refs, refs = refs[: lay.nc], refs[lay.nc :]
    q_ref, k_ref, v_ref, ga_ref, kept_ref, sent_ref, *refs = refs
    pr_refs, (w_scr, att_scr, wo_scr, acc_scr, cut_scr) = refs[: lay.chips], refs[lay.chips :]
    _, step_patches, model = hid_ref.shape
    tokens = lay.frames * step_patches
    cols = w_scr.shape[2] // 3
    scaling = 1.0 / math.sqrt(cols // lay.half_heads)
    patches = step_patches * pl.num_programs(0)
    is_first = pos_ref[1] == 0

    @pl.when(pl.program_id(0) == 0)
    def _():
        fill_weights(lay, pos_ref, w_refs, w_scr)
        own, other = wo_refs[0][...].astype(F32), wo_refs[1][...].astype(F32)
        both = [jnp.where(is_first, own, other), jnp.where(is_first, other, own)]
        wo_scr[...] = jnp.concatenate(both, axis=0).astype(BF16)
        acc_scr[...] = jnp.zeros_like(acc_scr)

    hidden = hid_ref[...].reshape(lay.frames * step_patches, model)
    for h in range(lay.halves):
        triple = dot(hidden, w_scr[h])
        for n, ref in enumerate((q_ref, k_ref, v_ref)):
            ref[h] = triple[:, n * cols : (n + 1) * cols].astype(BF16).reshape(ref.shape[1:])

    for b in range(step_patches // BLOCK):
        patch_base = pos_ref[1] * patches + pl.program_id(0) * step_patches + b * BLOCK
        allowed = allowed_pairs(lay, pos_ref, info_ref, patch_base)
        outputs = []
        for h in range(lay.halves):
            queries, keys, values = (patch_blocks(ref[h], b) for ref in (q_ref, k_ref, v_ref))
            weights = attention_weights(lay, heads_stacked(lay, keys), queries, allowed, scaling)
            weights = weights.astype(BF16).reshape(-1, allowed.shape[1])
            outputs.append(t_dot(weights, heads_stacked(lay, values)))
        if lay.halves > 1:
            first = jnp.where(pos_ref[1] == 0, outputs[0], outputs[1])
            second = jnp.where(pos_ref[1] == 0, outputs[1], outputs[0])
            outputs = [jnp.concatenate([first, second], axis=1)]
        attended = outputs[0].astype(BF16)
        att_scr[:, b * BLOCK : (b + 1) * BLOCK, :] = attended.reshape(lay.frames, BLOCK, -1)

    attended = att_scr[...].reshape(tokens, -1)
    grad_proj = gp_ref[...].reshape(tokens, model)
    acc_scr[...] += t_dot(attended, grad_proj)
    grad_attn = dot_t(grad_proj, wo_scr[...])
    part = wo_scr.shape[0] // lay.halves
    for h in range(lay.halves):
        ga_ref[h] = grad_attn[:, h * part : (h + 1) * part].astype(BF16).reshape(ga_ref.shape[1:])
    projected = dot(attended, wo_scr[...]).reshape(lay.chips, lay.nc, step_patches, model)
    for k in range(lay.chips):
        pr_refs[k][...] = projected[k].astype(pr_refs[k].dtype)

    @pl.when(pl.program_id(0) == pl.num_programs(0) - 1)
    def _():
        groups, chunk_rows, chunk_width = kept_ref.shape
        block_rows, part = acc_scr.shape[0] // lay.nc, model // groups
        order = lay.doubled(lay.bits(lay.nz)[::-1])
        first, second = acc_scr[:block_rows, :], acc_scr[block_rows:, :]
        kept = jnp.where(is_first, first, second)
        sent = jnp.where(is_first, second, first)
        for ref, rows in ((kept_ref, kept), (sent_ref, sent)):
            for d in range(groups):
                chunk = [
                    rows[m * chunk_rows : (m + 1) * chunk_rows, d * part : (d + 1) * part]
                    for m in range(chunk_width // part)
                ]
                cut_scr[d] = jnp.concatenate(chunk, axis=1) if len(chunk) > 1 else chunk[0]
            for n, k in enumerate(order):
                ref[n] = cut_scr[pos_ref[2] ^ k]


def backward_kernel(lay, pos_ref, info_ref, *refs):
    w_refs, refs = refs[: 2 * lay.halves], refs[2 * lay.halves :]
    q_ref, k_ref, v_ref, ga_ref, *refs = refs
    gh_refs, (w_scr, gt_scr) = refs[: lay.chips], refs[lay.chips :]
    _, frames, step_patches, cols = q_ref.shape
    model = w_scr.shape[1]
    patches = step_patches * pl.num_programs(0)
    scaling = 1.0 / math.sqrt(cols // lay.half_heads)

    @pl.when(pl.program_id(0) == 0)
    def _():
        fill_weights(lay, pos_ref, w_refs, w_scr)

    for b in range(step_patches // BLOCK):
        patch_base = pos_ref[1] * patches + pl.program_id(0) * step_patches + b * BLOCK
        allowed = allowed_pairs(lay, pos_ref, info_ref, patch_base)
        for h in range(lay.halves):
            queries, keys, values = (patch_blocks(ref[h], b) for ref in (q_ref, k_ref, v_ref))
            grad_out = patch_blocks(ga_ref[(pos_ref[1] ^ h) if lay.halves > 1 else 0], b)
            keys = heads_stacked(lay, keys)
            weights = attention_weights(lay, keys, queries, allowed, scaling)
            grad_weights = dot_t(heads_stacked(lay, values), grad_out).reshape(weights.shape)
            grad_values = dot(beside(lay, weights.astype(BF16)), heads_stacked(lay, grad_out))
            inner = jnp.sum(weights * grad_weights, axis=1, keepdims=True)
            grad_scores = (weights * (grad_weights - inner) * scaling).astype(BF16)
            grad_queries = t_dot(grad_scores.reshape(-1, grad_scores.shape[2]), keys)
            grad_keys = dot(beside(lay, grad_scores), heads_stacked(lay, queries))
            grads = jnp.concatenate([grad_queries, grad_keys, grad_values], axis=1).astype(BF16)
            gt_scr[h, :, b * BLOCK : (b + 1) * BLOCK, :] = grads.reshape(frames, BLOCK, 3 * cols)

    rows = lay.nc * step_patches
    for k in range(lay.chips):
        total = jnp.zeros((rows, model), F32)
        for h in range(lay.halves):
            part = gt_scr[h, k * lay.nc : (k + 1) * lay.nc].reshape(rows, 3 * cols)
            total = total + dot_t(part, w_scr[h])
        gh_refs[k][...] = total.reshape(gh_refs[k].shape).astype(gh_refs[k].dtype)


def output_kernel(lay, pos_ref, info_ref, *refs):
    pair_refs, refs = refs[: lay.nc], refs[lay.nc :]
    pr_refs, refs = refs[: lay.chips], refs[lay.chips :]
    mod_ref, *out_refs = refs
    step_patches, model = out_refs[0].shape
    patches = step_patches * pl.num_programs(0)
    patch_base = pos_ref[1] * patches + pl.program_id(0) * step_patches
    patch = patch_base + lax.broadcasted_iota(jnp.int32, (step_patches, 1), 0)
    for j in range(lay.nc):
        _, limit, step = slot_scalars(lay, pos_ref, info_ref, (0, j))
        factor = jnp.where(patch < limit, table_row(mod_ref, step, 2, model), 0.0)
        projected = pr_refs[0][j]
        for k in range(1, lay.chips):
            projected = projected + pr_refs[k][j].astype(F32)
        projected = projected.astype(BF16).astype(F32)
        out_refs[j][...] = (pair_refs[j][0, 0].astype(F32) + factor * projected).astype(BF16)


def input_grad_kernel(lay, pos_ref, info_ref, *refs):
    pair_refs, refs = refs[: lay.nc], refs[lay.nc :]
    gh_refs, refs = refs[: lay.chips], refs[lay.chips :]
    mod_ref, *out_refs = refs
    model = out_refs[0].shape[1]
    for j in range(lay.nc):
        _, _, step = slot_scalars(lay, pos_ref, info_ref, (0, j))
        grad_hidden = gh_refs[0][j]
        for k in range(1, lay.chips):
            grad_hidden = grad_hidden + gh_refs[k][j].astype(F32)
        grad_hidden = grad_hidden.astype(BF16).astype(F32)
        normed, inv_sigma = normalize(pair_refs[j][0, 0].astype(F32))
        grad_norm = grad_hidden * (1.0 + table_row(mod_ref, step, 1, model))
        first_mean = jnp.mean(grad_norm, axis=-1, keepdims=True)
        second_mean = jnp.mean(grad_norm * normed, axis=-1, keepdims=True)
        grad_x = pair_refs[j][0, 1].astype(F32) + inv_sigma * (
            grad_norm - first_mean - normed * second_mean
        )
        out_refs[j][...] = grad_x.astype(BF16)


def whole_spec(shape):
    return pl.BlockSpec(shape, lambda *_: (0,) * len(shape))


def struct(shape, dtype=BF16):
    return jax.ShapeDtypeStruct(shape, dtype)


def local(lay, frames_x, grad_y, clip_ids, clip_patches, clip_step, mod_table, w_qkv, w_out):
    y, c, z, x = (lax.axis_index(name) for name in AXES)
    _, patches, model = frames_x.shape
    half = patches // lay.nc
    chips, nc, nx = lay.chips, lay.nc, lay.nx
    head_size = model // HEADS
    halves = lay.halves
    cols = lay.half_heads * head_size
    chip_width = lay.chip_heads * head_size
    rows = w_qkv.shape[0]
    groups = lay.nz
    quarter = model // groups
    step_patches = max(BLOCK, min(half, 512 // lay.frames))
    steps = half // step_patches
    tokens = lay.frames * step_patches

    def call(kernel, name, cost, in_specs, out_specs, out_shape, scratch=(), grid=(1,), prefetch=2):
        return pl.pallas_call(
            kernel,
            grid_spec=pltpu.PrefetchScalarGridSpec(
                num_scalar_prefetch=prefetch,
                grid=grid,
                in_specs=in_specs,
                out_specs=out_specs,
                scratch_shapes=list(scratch),
            ),
            out_shape=out_shape,
            compiler_params=pltpu.CompilerParams(vmem_limit_bytes=VMEM_LIMIT),
            cost_estimate=pl.CostEstimate(
                flops=cost * tokens * steps, bytes_accessed=4 * model * tokens, transcendentals=0
            ),
            name=name,
        )

    def chip_swap(k):
        ky, kx = lay.chip_of(k)
        return lay.swap(ky=ky, kx=kx)

    def doubling(held, bits, swap, after=()):
        for bit in bits[:-1]:
            held = jnp.concatenate([held, lax.ppermute(held, AXES, swap(bit))], axis=0)
        held, _ = lax.optimization_barrier((held, after))
        return [held, lax.ppermute(held, AXES, swap(bits[-1]))]

    def over_chips(parts):
        got = [lax.ppermute(parts[k], AXES, chip_swap(k)) for k in range(1, chips)]
        return [parts[0]] + got

    def from_plane(parts):
        got = [lax.ppermute(part, AXES, lay.from_plane(k)) for k, part in enumerate(parts)]
        first = jnp.where(z // lay.ny == 0, got[0], got[1])
        second = jnp.where(z // lay.ny == 0, got[1], got[0])
        return jnp.concatenate([first, second], axis=0)[None]

    info = jnp.concatenate([clip_ids[0], clip_patches[0], clip_step[0]])[None]
    info = lax.ppermute(info, AXES, lay.to_plane(0))[0]
    pos = jnp.stack([y, c, z, x]).astype(jnp.int32)
    own = []
    for k in range(nc):
        start = ((z // lay.ny) ^ k) * half
        pair = [lax.dynamic_slice_in_dim(frame, start, half, axis=1) for frame in (frames_x, grad_y)]
        pair = jnp.stack(pair, axis=1)
        if k == 0:
            pair, info = lax.optimization_barrier((pair, info))
        own.append(lax.ppermute(pair, AXES, lay.to_plane(k)))
    pairs = []
    for j in range(nc):
        pairs += doubling(own[j], lay.chip_bits(j), chip_swap)

    picked = call(
        functools.partial(pick_kernel, lay, cols),
        "pick",
        2 * model * 1000,
        [whole_spec(w_qkv.shape)],
        [whole_spec((rows, 3 * cols))] * nx,
        [struct((rows, 3 * cols))] * nx,
        prefetch=1,
    )(pos, w_qkv)
    by_x = [picked[0]] + [
        lax.ppermute(picked[kx], AXES, lay.swap(kx=kx)) for kx in range(1, nx)
    ]
    if nx == 2:
        ordered = [jnp.where(x == i, by_x[0], by_x[1]) for i in range(nx)]
    else:
        stacked = jnp.stack(by_x)
        ordered = [lax.dynamic_index_in_dim(stacked, x ^ i, 0, keepdims=False) for i in range(nx)]
    w_own = jnp.concatenate(ordered, axis=1 if rows % 16 == 0 else 0)[None]
    w_pieces = doubling(w_own, lay.bits(lay.nz)[::-1], lambda kz: lay.swap(kz=kz), pairs[::2])
    if halves > 1:
        w_pieces += [lax.ppermute(piece, AXES, lay.swap(kc=1)) for piece in w_pieces]

    late_w_out, _ = lax.optimization_barrier((w_out, w_pieces[:2]))
    wo_own = lax.ppermute(late_w_out, AXES, lay.rows_to_chip())

    def spread(count, width, patches_at_once):
        return pl.BlockSpec((count, patches_at_once, width), lambda i, *_: (0, i, 0))

    def pair_spec(count, patches_at_once):
        return pl.BlockSpec((count, 2, patches_at_once, model), lambda i, *_: (0, 0, i, 0))

    few = max(BLOCK, step_patches // 2)
    few_steps = half // few
    x_spec = pl.BlockSpec((few, model), lambda i, *_: (i, 0))
    triple_spec = pl.BlockSpec((halves, lay.frames, step_patches, cols), lambda i, *_: (0, 0, i, 0))
    w_specs = [whole_spec(piece.shape) for piece in w_pieces]
    w_scratch = pltpu.VMEM((halves, model, 3 * cols), BF16)
    mod_spec = whole_spec(mod_table.shape)
    triple_shape = struct((halves, lay.frames, half, cols))
    part_specs = [spread(nc, model, step_patches)] * chips
    part_shapes = [struct((nc, half, model), F32)] + [struct((nc, half, model))] * (chips - 1)

    hidden, grad_proj = call(
        functools.partial(prepare_kernel, lay),
        "prepare",
        3 * model * 1000,
        [pair_spec(chips // 2, few)] * (2 * nc) + [mod_spec],
        [spread(lay.frames, model, few)] * 2,
        [struct((lay.frames, half, model))] * 2,
        grid=(few_steps,),
    )(pos, info, *pairs, mod_table)
    wo_own, _ = lax.optimization_barrier((wo_own, hidden))
    wo_rows = [wo_own, lax.ppermute(wo_own, AXES, lay.swap(kc=1))]

    fold = 3 if rows % 24 == 0 else 1
    piece_shape = (groups, rows // fold, quarter * fold)
    queries, keys, values, grad_attn, kept, sent, *projected = call(
        functools.partial(forward_kernel, lay),
        "forward",
        14 * model * 1000,
        [spread(lay.frames, model, step_patches)] * 2
        + w_specs
        + [whole_spec(w_out.shape)] * nc,
        [triple_spec] * 4 + [whole_spec(piece_shape)] * 2 + part_specs,
        [triple_shape] * 4 + [struct(piece_shape, F32)] * 2 + part_shapes,
        [
            w_scratch,
            pltpu.VMEM((lay.frames, step_patches, chip_width), BF16),
            pltpu.VMEM((chip_width, model), BF16),
            pltpu.VMEM((chip_width, model), F32),
            pltpu.VMEM(piece_shape, F32),
        ],
        (steps,),
    )(pos, info, hidden, grad_proj, *w_pieces, *wo_rows)
    got = lax.ppermute(sent, AXES, lay.swap(kc=1))
    projected = over_chips(projected)

    middle = groups // 2
    cut, away = kept[:middle] + got[:middle], kept[middle:] + got[middle:]
    grad_attn, cut, away = lax.optimization_barrier((grad_attn, cut, away))
    first_away = lax.ppermute(away, AXES, lay.swap(kz=1))

    sums = call(
        functools.partial(backward_kernel, lay),
        "backward",
        10 * model * 1000,
        w_specs + [triple_spec] * 4,
        part_specs,
        part_shapes,
        [w_scratch, pltpu.VMEM((halves, lay.frames, step_patches, 3 * cols), BF16)],
        (steps,),
    )(pos, info, *w_pieces, queries, keys, values, grad_attn)
    sums, first_away, projected = lax.optimization_barrier((sums, first_away, projected))
    grad_hidden = over_chips(sums)
    projected, _ = lax.optimization_barrier((projected, grad_hidden[1]))

    out_parts = call(
        functools.partial(output_kernel, lay),
        "output",
        3 * model * 1000,
        [pair_spec(1, few)] * nc + [spread(nc, model, few)] * chips + [mod_spec],
        [x_spec] * nc,
        [struct((half, model))] * nc,
        grid=(few_steps,),
    )(pos, info, *own, *projected, mod_table)

    cut = cut + first_away
    for bit in lay.bits(lay.nz)[1:]:
        middle = middle // 2
        away = lax.ppermute(cut[middle:], AXES, lay.swap(kz=bit))
        away, _ = lax.optimization_barrier((away, out_parts))
        cut = cut[:middle] + away
    grad_w = lax.ppermute(cut[0], AXES, lay.to_owner())
    grad_w = jnp.concatenate(
        [grad_w[:, m * quarter : (m + 1) * quarter] for m in range(fold)], axis=0
    )
    grad_w_out = grad_w * jnp.float32(1.0 / math.sqrt(groups * lay.frames * patches))

    out_y = from_plane(out_parts)

    grad_parts = call(
        functools.partial(input_grad_kernel, lay),
        "input_grad",
        3 * model * 1000,
        [pair_spec(1, few)] * nc + [spread(nc, model, few)] * chips + [mod_spec],
        [x_spec] * nc,
        [struct((half, model))] * nc,
        grid=(few_steps,),
    )(pos, info, *own, *grad_hidden, mod_table)
    grad_x = from_plane(grad_parts)
    return out_y, grad_x, grad_w_out


def solution(mesh):
    lay = Layout(mesh)
    grid = Mesh(mesh.devices.reshape(lay.ny, lay.nc, lay.nz, lay.nx), AXES)
    rows, cols = ("z", "x"), ("y", "c")
    frame = P(AXES, None, None)
    group = P(cols, None)
    return jax.shard_map(
        functools.partial(local, lay),
        mesh=grid,
        in_specs=(frame, frame, group, group, group, P(), P(rows, None), P(rows, None)),
        out_specs=(frame, frame, P(rows, cols)),
        check_vma=False,
    )
```

```python
import functools
import math

import jax
import jax.numpy as jnp
from jax import lax
from jax.experimental import pallas as pl
from jax.experimental.pallas import tpu as pltpu
from jax.sharding import Mesh, PartitionSpec as P

HEADS = 16
CORES = 2
AXES = ("y", "c", "z", "x")
BLOCK = 16
VMEM_LIMIT = 56 * 1024 * 1024
BF16 = jnp.bfloat16
F32 = jnp.float32


def dot(left, right):
    return jnp.dot(left, right, preferred_element_type=F32)


def dot_t(left, right):
    return lax.dot_general(left, right, (((1,), (1,)), ((), ())), preferred_element_type=F32)


def t_dot(left, right):
    return lax.dot_general(left, right, (((0,), (0,)), ((), ())), preferred_element_type=F32)


def normalize(values):
    centred = values - jnp.mean(values, axis=-1, keepdims=True)
    inv_sigma = lax.rsqrt(jnp.mean(centred * centred, axis=-1, keepdims=True) + 1e-06)
    return centred * inv_sigma, inv_sigma


class Layout:
    def __init__(self, mesh):
        groups, seq = mesh.shape["dp"], mesh.shape["seq"]
        self.nc = CORES
        self.ny = groups // CORES
        self.nz = groups
        self.nx = seq // self.nz
        self.chips = self.ny * self.nx
        self.frames = seq
        self.chip_heads = HEADS // self.chips
        self.halves = 2 if self.chip_heads % 2 == 0 else 1
        self.half_heads = self.chip_heads // self.halves

    def linear(self, y, c, z, x):
        return ((y * self.nc + c) * self.nz + z) * self.nx + x

    def perm(self, move):
        pairs = []
        for y in range(self.ny):
            for c in range(self.nc):
                for z in range(self.nz):
                    for x in range(self.nx):
                        pairs.append((self.linear(y, c, z, x), self.linear(*move(y, c, z, x))))
        return pairs

    def to_plane(self, k):
        return self.perm(
            lambda y, c, z, x: ((z % self.ny) ^ c, (z // self.ny) ^ k, c * self.ny + y, x)
        )

    def from_plane(self, k):
        return [(target, source) for source, target in self.to_plane(k)]

    def swap(self, ky=0, kc=0, kz=0, kx=0):
        return self.perm(lambda y, c, z, x: (y ^ ky, c ^ kc, z ^ kz, x ^ kx))

    def row_block(self, y, x, i):
        if self.halves > 1:
            return (i * self.ny + y) * self.nx + x
        return self.nc * (y * self.nx + x) + i

    def rows_to_chip(self):
        reader = {
            self.row_block(y, x, i): (y, x, i)
            for y in range(self.ny)
            for x in range(self.nx)
            for i in range(self.nc)
        }

        def move(y, c, z, x):
            chip_y, chip_x, i = reader[z * self.nx + x]
            return chip_y, i, c * self.ny + (y ^ (z & 1)), chip_x

        return self.perm(move)

    def to_owner(self):
        def move(y, c, z, x):
            s = self.row_block(y, x, c)
            return z // self.nc, z % self.nc, s // self.nx, s % self.nx

        return self.perm(move)

    def chip_of(self, k):
        return k // self.nx, k % self.nx

    def bits(self, count):
        return [1 << b for b in range(count.bit_length() - 1)]

    def chip_bits(self, j):
        bits = self.bits(self.chips)
        return bits if j % 2 == 0 else bits[::-1]

    def doubled(self, bits):
        held = [0]
        for bit in bits:
            held = held + [k ^ bit for k in held]
        return held

    def slots(self):
        return [(k, j) for k in range(self.chips) for j in range(self.nc)]


def slot_scalars(lay, pos_ref, info_ref, slot):
    k, j = slot
    ky, kx = lay.chip_of(k)
    z_frame = (pos_ref[1] ^ j) * lay.ny + (pos_ref[0] ^ ky ^ (pos_ref[2] // lay.ny))
    frame = z_frame * lay.nx + (pos_ref[3] ^ kx)
    clip = info_ref[frame]
    clips = (info_ref.shape[0] - lay.frames) // 2
    return clip, info_ref[lay.frames + clip], info_ref[lay.frames + clips + clip]


def table_row(mod_ref, step, part, width):
    return mod_ref[pl.ds(step, 1), part * width : (part + 1) * width]


def allowed_pairs(lay, pos_ref, info_ref, patch_base):
    rows = lay.frames * BLOCK
    row_slot = lax.broadcasted_iota(jnp.int32, (rows, 1), 0) // BLOCK
    col_slot = lax.broadcasted_iota(jnp.int32, (1, rows), 1) // BLOCK
    row_clip = jnp.zeros((rows, 1), jnp.int32)
    row_limit = jnp.zeros((rows, 1), jnp.int32)
    col_clip = jnp.zeros((1, rows), jnp.int32)
    for t, slot in enumerate(lay.slots()):
        clip, limit, _ = slot_scalars(lay, pos_ref, info_ref, slot)
        row_clip = jnp.where(row_slot == t, clip, row_clip)
        row_limit = jnp.where(row_slot == t, limit, row_limit)
        col_clip = jnp.where(col_slot == t, clip, col_clip)
    row_patch = lax.broadcasted_iota(jnp.int32, (rows, 1), 0) % BLOCK
    col_patch = lax.broadcasted_iota(jnp.int32, (1, rows), 1) % BLOCK
    row_key = row_clip * BLOCK + row_patch
    col_key = col_clip * BLOCK + col_patch
    row_valid = (patch_base + row_patch < row_limit).astype(jnp.int32)
    row_index = lax.broadcasted_iota(jnp.int32, (rows, rows), 0)
    col_index = lax.broadcasted_iota(jnp.int32, (rows, rows), 1)
    return (row_key == col_key) & ((row_valid > 0) | (row_index == col_index))


def head_mask(values, head, head_size):
    lane = lax.broadcasted_iota(jnp.int32, (1, values.shape[1]), 1)
    inside = (lane >= head * head_size) & (lane < (head + 1) * head_size)
    return jnp.where(inside, values, jnp.zeros_like(values))


def patch_blocks(array, block):
    part = array[:, block * BLOCK : (block + 1) * BLOCK, :]
    return part.reshape(part.shape[0] * BLOCK, part.shape[2])


def start_kernel(lay, cols, pos_ref, x_ref, g_ref, w_ref, *refs):
    pair_refs, out_refs = refs[: lay.nc], refs[lay.nc :]
    half = x_ref.shape[1] // lay.nc
    for k, ref in enumerate(pair_refs):
        first = pl.multiple_of(((pos_ref[2] // lay.ny) ^ k) * half, 16)
        ref[0, 0] = x_ref[0, pl.ds(first, half), :]
        ref[0, 1] = g_ref[0, pl.ds(first, half), :]
    model = w_ref.shape[1] // 3
    for k, out_ref in enumerate(out_refs):
        chip_x = pos_ref[3] ^ k
        if lay.halves > 1:
            want = lay.row_block(pos_ref[0], chip_x, pos_ref[1])
        else:
            want = pos_ref[0] * lay.nx + chip_x
        for v in range(lay.chips * lay.halves):

            @pl.when(want == v)
            def _(v=v, out_ref=out_ref):
                parts = [
                    w_ref[:, p * model + v * cols : p * model + (v + 1) * cols]
                    for p in range(3)
                ]
                out_ref[...] = jnp.concatenate(parts, axis=1)


def fill_weights(lay, pos_ref, w_refs, w_scr):
    block = w_scr.shape[1] // lay.nz
    rows, width = w_refs[0].shape[0], w_scr.shape[2]
    for h in range(lay.halves):
        for k in range(lay.nz):
            ref = w_refs[h * lay.nz + k]
            for m in range(block // rows):
                start = pl.multiple_of((pos_ref[2] ^ k) * block + m * rows, 16)
                w_scr[h, pl.ds(start, rows), :] = ref[:, m * width : (m + 1) * width]


def heads_stacked(lay, values):
    head_size = values.shape[1] // lay.half_heads
    parts = [head_mask(values, head, head_size) for head in range(lay.half_heads)]
    return jnp.concatenate(parts, axis=0) if len(parts) > 1 else parts[0]


def beside(lay, weights):
    return jnp.concatenate([weights[head] for head in range(lay.half_heads)], axis=1)


def attention_weights(lay, keys_stacked, queries, allowed, scaling):
    scores = dot_t(keys_stacked, queries) * scaling
    scores = jnp.where(allowed, scores.reshape((lay.half_heads,) + allowed.shape), -jnp.inf)
    exponent = jnp.exp(scores - jnp.max(scores, axis=1, keepdims=True))
    return exponent * (1.0 / jnp.sum(exponent, axis=1, keepdims=True))


def prepare_kernel(lay, pos_ref, info_ref, *refs):
    pair_refs, (mod_ref, hid_ref, gp_ref) = refs[: 2 * lay.nc], refs[2 * lay.nc :]
    _, step_patches, model = hid_ref.shape
    patches = step_patches * pl.num_programs(0)
    patch_base = pos_ref[1] * patches + pl.program_id(0) * step_patches
    patch = patch_base + lax.broadcasted_iota(jnp.int32, (step_patches, 1), 0)
    for t, (k, j) in enumerate(lay.slots()):
        _, limit, step = slot_scalars(lay, pos_ref, info_ref, (k, j))
        n = lay.doubled(lay.chip_bits(j)).index(k)
        ref, place = pair_refs[2 * j + (2 * n) // lay.chips], n % (lay.chips // 2)
        normed, _ = normalize(ref[place, 0].astype(F32))
        shift, scale = table_row(mod_ref, step, 0, model), table_row(mod_ref, step, 1, model)
        hid_ref[t] = (normed * (1.0 + scale) + shift).astype(BF16)
        factor = jnp.where(patch < limit, table_row(mod_ref, step, 2, model), 0.0)
        gp_ref[t] = (factor * ref[place, 1].astype(F32)).astype(BF16)


def forward_kernel(lay, pos_ref, info_ref, hid_ref, gp_ref, *refs):
    w_refs, refs = refs[: lay.halves * lay.nz], refs[lay.halves * lay.nz :]
    wo_refs, refs = refs[: lay.nc], refs[lay.nc :]
    q_ref, k_ref, v_ref, ga_ref, kept_ref, sent_ref, *refs = refs
    pr_refs, (w_scr, att_scr, wo_scr, acc_scr, cut_scr) = refs[: lay.chips], refs[lay.chips :]
    _, step_patches, model = hid_ref.shape
    tokens = lay.frames * step_patches
    cols = w_scr.shape[2] // 3
    scaling = 1.0 / math.sqrt(cols // lay.half_heads)
    patches = step_patches * pl.num_programs(0)
    is_first = pos_ref[1] == 0

    @pl.when(pl.program_id(0) == 0)
    def _():
        fill_weights(lay, pos_ref, w_refs, w_scr)
        own, other = wo_refs[0][...].astype(F32), wo_refs[1][...].astype(F32)
        both = [jnp.where(is_first, own, other), jnp.where(is_first, other, own)]
        wo_scr[...] = jnp.concatenate(both, axis=0).astype(BF16)
        acc_scr[...] = jnp.zeros_like(acc_scr)

    hidden = hid_ref[...].reshape(lay.frames * step_patches, model)
    for h in range(lay.halves):
        triple = dot(hidden, w_scr[h])
        for n, ref in enumerate((q_ref, k_ref, v_ref)):
            ref[h] = triple[:, n * cols : (n + 1) * cols].astype(BF16).reshape(ref.shape[1:])

    for b in range(step_patches // BLOCK):
        patch_base = pos_ref[1] * patches + pl.program_id(0) * step_patches + b * BLOCK
        allowed = allowed_pairs(lay, pos_ref, info_ref, patch_base)
        outputs = []
        for h in range(lay.halves):
            queries, keys, values = (patch_blocks(ref[h], b) for ref in (q_ref, k_ref, v_ref))
            weights = attention_weights(lay, heads_stacked(lay, keys), queries, allowed, scaling)
            weights = weights.astype(BF16).reshape(-1, allowed.shape[1])
            outputs.append(t_dot(weights, heads_stacked(lay, values)))
        if lay.halves > 1:
            first = jnp.where(pos_ref[1] == 0, outputs[0], outputs[1])
            second = jnp.where(pos_ref[1] == 0, outputs[1], outputs[0])
            outputs = [jnp.concatenate([first, second], axis=1)]
        attended = outputs[0].astype(BF16)
        att_scr[:, b * BLOCK : (b + 1) * BLOCK, :] = attended.reshape(lay.frames, BLOCK, -1)

    attended = att_scr[...].reshape(tokens, -1)
    grad_proj = gp_ref[...].reshape(tokens, model)
    acc_scr[...] += t_dot(attended, grad_proj)
    grad_attn = dot_t(grad_proj, wo_scr[...])
    part = wo_scr.shape[0] // lay.halves
    for h in range(lay.halves):
        ga_ref[h] = grad_attn[:, h * part : (h + 1) * part].astype(BF16).reshape(ga_ref.shape[1:])
    projected = dot(attended, wo_scr[...]).reshape(lay.chips, lay.nc, step_patches, model)
    for k in range(lay.chips):
        pr_refs[k][...] = projected[k].astype(pr_refs[k].dtype)

    @pl.when(pl.program_id(0) == pl.num_programs(0) - 1)
    def _():
        groups, chunk_rows, chunk_width = kept_ref.shape
        block_rows, part = acc_scr.shape[0] // lay.nc, model // groups
        order = lay.doubled(lay.bits(lay.nz)[::-1])
        first, second = acc_scr[:block_rows, :], acc_scr[block_rows:, :]
        kept = jnp.where(is_first, first, second)
        sent = jnp.where(is_first, second, first)
        for ref, rows in ((kept_ref, kept), (sent_ref, sent)):
            for d in range(groups):
                chunk = [
                    rows[m * chunk_rows : (m + 1) * chunk_rows, d * part : (d + 1) * part]
                    for m in range(chunk_width // part)
                ]
                cut_scr[d] = jnp.concatenate(chunk, axis=1) if len(chunk) > 1 else chunk[0]
            for n, k in enumerate(order):
                ref[n] = cut_scr[pos_ref[2] ^ k]


def backward_kernel(lay, pos_ref, info_ref, *refs):
    w_refs, refs = refs[: lay.halves * lay.nz], refs[lay.halves * lay.nz :]
    q_ref, k_ref, v_ref, ga_ref, *refs = refs
    gh_refs, (w_scr, gt_scr) = refs[: lay.chips], refs[lay.chips :]
    _, frames, step_patches, cols = q_ref.shape
    model = w_scr.shape[1]
    patches = step_patches * pl.num_programs(0)
    scaling = 1.0 / math.sqrt(cols // lay.half_heads)

    @pl.when(pl.program_id(0) == 0)
    def _():
        fill_weights(lay, pos_ref, w_refs, w_scr)

    for b in range(step_patches // BLOCK):
        patch_base = pos_ref[1] * patches + pl.program_id(0) * step_patches + b * BLOCK
        allowed = allowed_pairs(lay, pos_ref, info_ref, patch_base)
        for h in range(lay.halves):
            queries, keys, values = (patch_blocks(ref[h], b) for ref in (q_ref, k_ref, v_ref))
            grad_out = patch_blocks(ga_ref[(pos_ref[1] ^ h) if lay.halves > 1 else 0], b)
            keys = heads_stacked(lay, keys)
            weights = attention_weights(lay, keys, queries, allowed, scaling)
            grad_weights = dot_t(heads_stacked(lay, values), grad_out).reshape(weights.shape)
            grad_values = dot(beside(lay, weights.astype(BF16)), heads_stacked(lay, grad_out))
            inner = jnp.sum(weights * grad_weights, axis=1, keepdims=True)
            grad_scores = (weights * (grad_weights - inner) * scaling).astype(BF16)
            grad_queries = t_dot(grad_scores.reshape(-1, grad_scores.shape[2]), keys)
            grad_keys = dot(beside(lay, grad_scores), heads_stacked(lay, queries))
            grads = jnp.concatenate([grad_queries, grad_keys, grad_values], axis=1).astype(BF16)
            gt_scr[h, :, b * BLOCK : (b + 1) * BLOCK, :] = grads.reshape(frames, BLOCK, 3 * cols)

    rows = lay.nc * step_patches
    for k in range(lay.chips):
        total = jnp.zeros((rows, model), F32)
        for h in range(lay.halves):
            part = gt_scr[h, k * lay.nc : (k + 1) * lay.nc].reshape(rows, 3 * cols)
            total = total + dot_t(part, w_scr[h])
        gh_refs[k][...] = total.reshape(gh_refs[k].shape).astype(gh_refs[k].dtype)


def output_kernel(lay, pos_ref, info_ref, *refs):
    pair_refs, refs = refs[: lay.nc], refs[lay.nc :]
    pr_refs, refs = refs[: lay.chips], refs[lay.chips :]
    mod_ref, *out_refs = refs
    step_patches, model = out_refs[0].shape
    patches = step_patches * pl.num_programs(0)
    patch_base = pos_ref[1] * patches + pl.program_id(0) * step_patches
    patch = patch_base + lax.broadcasted_iota(jnp.int32, (step_patches, 1), 0)
    for j in range(lay.nc):
        _, limit, step = slot_scalars(lay, pos_ref, info_ref, (0, j))
        factor = jnp.where(patch < limit, table_row(mod_ref, step, 2, model), 0.0)
        projected = pr_refs[0][j]
        for k in range(1, lay.chips):
            projected = projected + pr_refs[k][j].astype(F32)
        projected = projected.astype(BF16).astype(F32)
        out_refs[j][...] = (pair_refs[j][0, 0].astype(F32) + factor * projected).astype(BF16)


def input_grad_kernel(lay, pos_ref, info_ref, *refs):
    pair_refs, refs = refs[: lay.nc], refs[lay.nc :]
    gh_refs, refs = refs[: lay.chips], refs[lay.chips :]
    mod_ref, *out_refs = refs
    model = out_refs[0].shape[1]
    for j in range(lay.nc):
        _, _, step = slot_scalars(lay, pos_ref, info_ref, (0, j))
        grad_hidden = gh_refs[0][j]
        for k in range(1, lay.chips):
            grad_hidden = grad_hidden + gh_refs[k][j].astype(F32)
        grad_hidden = grad_hidden.astype(BF16).astype(F32)
        normed, inv_sigma = normalize(pair_refs[j][0, 0].astype(F32))
        grad_norm = grad_hidden * (1.0 + table_row(mod_ref, step, 1, model))
        first_mean = jnp.mean(grad_norm, axis=-1, keepdims=True)
        second_mean = jnp.mean(grad_norm * normed, axis=-1, keepdims=True)
        grad_x = pair_refs[j][0, 1].astype(F32) + inv_sigma * (
            grad_norm - first_mean - normed * second_mean
        )
        out_refs[j][...] = grad_x.astype(BF16)


def whole_spec(shape):
    return pl.BlockSpec(shape, lambda *_: (0,) * len(shape))


def struct(shape, dtype=BF16):
    return jax.ShapeDtypeStruct(shape, dtype)


def local(lay, frames_x, grad_y, clip_ids, clip_patches, clip_step, mod_table, w_qkv, w_out):
    y, c, z, x = (lax.axis_index(name) for name in AXES)
    _, patches, model = frames_x.shape
    half = patches // lay.nc
    chips, nc, nx = lay.chips, lay.nc, lay.nx
    head_size = model // HEADS
    halves = lay.halves
    cols = lay.half_heads * head_size
    chip_width = lay.chip_heads * head_size
    rows = w_qkv.shape[0]
    groups = lay.nz
    quarter = model // groups
    step_patches = max(BLOCK, min(half, 512 // lay.frames))
    steps = half // step_patches
    tokens = lay.frames * step_patches

    def call(kernel, name, cost, in_specs, out_specs, out_shape, scratch=(), grid=(1,), prefetch=2):
        return pl.pallas_call(
            kernel,
            grid_spec=pltpu.PrefetchScalarGridSpec(
                num_scalar_prefetch=prefetch,
                grid=grid,
                in_specs=in_specs,
                out_specs=out_specs,
                scratch_shapes=list(scratch),
            ),
            out_shape=out_shape,
            compiler_params=pltpu.CompilerParams(vmem_limit_bytes=VMEM_LIMIT),
            cost_estimate=pl.CostEstimate(
                flops=cost * tokens * steps, bytes_accessed=4 * model * tokens, transcendentals=0
            ),
            name=name,
        )

    def chip_swap(k):
        ky, kx = lay.chip_of(k)
        return lay.swap(ky=ky, kx=kx)

    def doubling(held, bits, swap, after):
        for bit in bits[:-1]:
            held = jnp.concatenate([held, lax.ppermute(held, AXES, swap(bit))], axis=0)
        held, _ = lax.optimization_barrier((held, after))
        return [held, lax.ppermute(held, AXES, swap(bits[-1]))]

    def over_chips(parts):
        got = [lax.ppermute(parts[k], AXES, chip_swap(k)) for k in range(1, chips)]
        return [parts[0]] + got

    def from_plane(parts):
        got = [lax.ppermute(part, AXES, lay.from_plane(k)) for k, part in enumerate(parts)]
        first = jnp.where(z // lay.ny == 0, got[0], got[1])
        second = jnp.where(z // lay.ny == 0, got[1], got[0])
        return jnp.concatenate([first, second], axis=0)[None]

    info = jnp.concatenate([clip_ids[0], clip_patches[0], clip_step[0]])[None]
    by_core = jnp.concatenate([info, lax.ppermute(info, AXES, lay.swap(kc=1))], axis=0)
    info = [by_core] + [
        lax.ppermute(by_core, AXES, lay.swap(ky=ky)) for ky in range(1, lay.ny)
    ]
    group_y, group_c = z % lay.ny, z // lay.ny
    info = sum(
        jnp.where((y ^ ky == group_y) & (c ^ kc == group_c), info[ky][kc], 0)
        for ky in range(lay.ny)
        for kc in range(nc)
    )
    pos = jnp.stack([y, c, z, x]).astype(jnp.int32)
    pair_shape = (1, 2, half, model)
    outputs = call(
        functools.partial(start_kernel, lay, cols),
        "start",
        2 * model * 1000,
        [whole_spec(frames_x.shape)] * 2 + [whole_spec(w_qkv.shape)],
        [whole_spec(pair_shape)] * nc + [whole_spec((rows, 3 * cols))] * nx,
        [struct(pair_shape)] * nc + [struct((rows, 3 * cols))] * nx,
        prefetch=1,
    )(pos, frames_x, grad_y, w_qkv)
    pairs, picked = outputs[:nc], outputs[nc:]
    own = [lax.ppermute(pair, AXES, lay.to_plane(k)) for k, pair in enumerate(pairs)]
    by_x = [picked[0]] + [
        lax.ppermute(picked[kx], AXES, lay.swap(kx=kx)) for kx in range(1, nx)
    ]
    if nx == 2:
        ordered = [jnp.where(x == i, by_x[0], by_x[1]) for i in range(nx)]
    else:
        stacked = jnp.stack(by_x)
        ordered = [lax.dynamic_index_in_dim(stacked, x ^ i, 0, keepdims=False) for i in range(nx)]
    w_own = jnp.concatenate(ordered, axis=1 if rows % 16 == 0 else 0)
    own[0], _ = lax.optimization_barrier((own[0], w_own))
    w_pieces = {0: w_own}
    for bit in lay.bits(lay.nz):
        w_pieces[bit] = lax.ppermute(w_own, AXES, lay.swap(kz=bit))
    early = [w_pieces[bit] for bit in lay.bits(lay.nz)]
    for k in range(1, lay.nz):
        if k not in w_pieces:
            bit = k & -k
            w_pieces[k] = lax.ppermute(w_pieces[k ^ bit], AXES, lay.swap(kz=bit))
    w_pieces = [w_pieces[k] for k in range(lay.nz)]
    late = w_pieces[-1]
    if halves > 1:
        w_pieces += [lax.ppermute(piece, AXES, lay.swap(kc=1)) for piece in w_pieces]

    pairs = []
    for j in range(nc):
        pairs += doubling(own[j], lay.chip_bits(j), chip_swap, early if j else info)
    pairs, _ = lax.optimization_barrier((pairs, [late] + w_pieces[lay.nz : -1]))

    late_w_out, _ = lax.optimization_barrier((w_out, own))
    wo_own = lax.ppermute(late_w_out, AXES, lay.rows_to_chip())

    def spread(count, width, patches_at_once):
        return pl.BlockSpec((count, patches_at_once, width), lambda i, *_: (0, i, 0))

    def pair_spec(count, patches_at_once):
        return pl.BlockSpec((count, 2, patches_at_once, model), lambda i, *_: (0, 0, i, 0))

    few = max(BLOCK, step_patches // 2)
    few_steps = half // few
    x_spec = pl.BlockSpec((few, model), lambda i, *_: (i, 0))
    triple_spec = pl.BlockSpec((halves, lay.frames, step_patches, cols), lambda i, *_: (0, 0, i, 0))
    w_specs = [whole_spec(piece.shape) for piece in w_pieces]
    w_scratch = pltpu.VMEM((halves, model, 3 * cols), BF16)
    mod_spec = whole_spec(mod_table.shape)
    triple_shape = struct((halves, lay.frames, half, cols))
    part_specs = [spread(nc, model, step_patches)] * chips
    part_shapes = [struct((nc, half, model), F32)] + [struct((nc, half, model))] * (chips - 1)

    hidden, grad_proj = call(
        functools.partial(prepare_kernel, lay),
        "prepare",
        3 * model * 1000,
        [pair_spec(chips // 2, few)] * (2 * nc) + [mod_spec],
        [spread(lay.frames, model, few)] * 2,
        [struct((lay.frames, half, model))] * 2,
        grid=(few_steps,),
    )(pos, info, *pairs, mod_table)
    wo_own, _ = lax.optimization_barrier((wo_own, hidden))
    wo_rows = [wo_own, lax.ppermute(wo_own, AXES, lay.swap(kc=1))]

    fold = 3 if rows % 24 == 0 else 1
    piece_shape = (groups, rows // fold, quarter * fold)
    queries, keys, values, grad_attn, kept, sent, *projected = call(
        functools.partial(forward_kernel, lay),
        "forward",
        14 * model * 1000,
        [spread(lay.frames, model, step_patches)] * 2
        + w_specs
        + [whole_spec(w_out.shape)] * nc,
        [triple_spec] * 4 + [whole_spec(piece_shape)] * 2 + part_specs,
        [triple_shape] * 4 + [struct(piece_shape, F32)] * 2 + part_shapes,
        [
            w_scratch,
            pltpu.VMEM((lay.frames, step_patches, chip_width), BF16),
            pltpu.VMEM((chip_width, model), BF16),
            pltpu.VMEM((chip_width, model), F32),
            pltpu.VMEM(piece_shape, F32),
        ],
        (steps,),
    )(pos, info, hidden, grad_proj, *w_pieces, *wo_rows)
    got = lax.ppermute(sent, AXES, lay.swap(kc=1))
    projected = over_chips(projected)

    middle = groups // 2
    cut, away = kept[:middle] + got[:middle], kept[middle:] + got[middle:]
    grad_attn, cut, away = lax.optimization_barrier((grad_attn, cut, away))
    first_away = lax.ppermute(away, AXES, lay.swap(kz=1))

    sums = call(
        functools.partial(backward_kernel, lay),
        "backward",
        10 * model * 1000,
        w_specs + [triple_spec] * 4,
        part_specs,
        part_shapes,
        [w_scratch, pltpu.VMEM((halves, lay.frames, step_patches, 3 * cols), BF16)],
        (steps,),
    )(pos, info, *w_pieces, queries, keys, values, grad_attn)
    sums, first_away, projected = lax.optimization_barrier((sums, first_away, projected))
    grad_hidden = over_chips(sums)

    projected, _ = lax.optimization_barrier((projected, grad_hidden[1]))
    out_parts = call(
        functools.partial(output_kernel, lay),
        "output",
        3 * model * 1000,
        [pair_spec(1, few)] * nc + [spread(nc, model, few)] * chips + [mod_spec],
        [x_spec] * nc,
        [struct((half, model))] * nc,
        grid=(few_steps,),
    )(pos, info, *own, *projected, mod_table)

    cut = cut + first_away
    for bit in lay.bits(lay.nz)[1:]:
        middle = middle // 2
        cut = cut[:middle] + lax.ppermute(cut[middle:], AXES, lay.swap(kz=bit))


    grad_parts = call(
        functools.partial(input_grad_kernel, lay),
        "input_grad",
        3 * model * 1000,
        [pair_spec(1, few)] * nc + [spread(nc, model, few)] * chips + [mod_spec],
        [x_spec] * nc,
        [struct((half, model))] * nc,
        grid=(few_steps,),
    )(pos, info, *own, *grad_hidden, mod_table)
    grad_x = from_plane(grad_parts)
    out_parts, _ = lax.optimization_barrier((out_parts, grad_parts))
    out_y = from_plane(out_parts)

    cut, _ = lax.optimization_barrier((cut, grad_parts))
    grad_w = lax.ppermute(cut[0], AXES, lay.to_owner())
    grad_w = jnp.concatenate(
        [grad_w[:, m * quarter : (m + 1) * quarter] for m in range(fold)], axis=0
    )
    grad_w_out = grad_w * jnp.float32(1.0 / math.sqrt(groups * lay.frames * patches))
    return out_y, grad_x, grad_w_out


def solution(mesh):
    lay = Layout(mesh)
    grid = Mesh(mesh.devices.reshape(lay.ny, lay.nc, lay.nz, lay.nx), AXES)
    rows, cols = ("z", "x"), ("y", "c")
    frame = P(AXES, None, None)
    group = P(cols, None)
    return jax.shard_map(
        functools.partial(local, lay),
        mesh=grid,
        in_specs=(frame, frame, group, group, group, P(), P(rows, None), P(rows, None)),
        out_specs=(frame, frame, P(rows, cols)),
        check_vma=False,
    )
```

```python
import functools
import math

import jax
import jax.numpy as jnp
from jax import lax
from jax.experimental import pallas as pl
from jax.experimental.pallas import tpu as pltpu
from jax.sharding import Mesh, PartitionSpec as P

HEADS = 16
CORES = 2
AXES = ("y", "c", "z", "x")
BLOCK = 16
VMEM_LIMIT = 56 * 1024 * 1024
BF16 = jnp.bfloat16
F32 = jnp.float32


def dot(left, right):
    return jnp.dot(left, right, preferred_element_type=F32)


def dot_t(left, right):
    return lax.dot_general(left, right, (((1,), (1,)), ((), ())), preferred_element_type=F32)


def t_dot(left, right):
    return lax.dot_general(left, right, (((0,), (0,)), ((), ())), preferred_element_type=F32)


def normalize(values):
    centred = values - jnp.mean(values, axis=-1, keepdims=True)
    inv_sigma = lax.rsqrt(jnp.mean(centred * centred, axis=-1, keepdims=True) + 1e-06)
    return centred * inv_sigma, inv_sigma


class Layout:
    def __init__(self, mesh):
        groups, seq = mesh.shape["dp"], mesh.shape["seq"]
        self.nc = CORES
        self.ny = groups // CORES
        self.nz = groups
        self.nx = seq // self.nz
        self.chips = self.ny * self.nx
        self.frames = seq
        self.chip_heads = HEADS // self.chips
        self.halves = 2 if self.chip_heads % 2 == 0 else 1
        self.half_heads = self.chip_heads // self.halves

    def linear(self, y, c, z, x):
        return ((y * self.nc + c) * self.nz + z) * self.nx + x

    def perm(self, move):
        pairs = []
        for y in range(self.ny):
            for c in range(self.nc):
                for z in range(self.nz):
                    for x in range(self.nx):
                        pairs.append((self.linear(y, c, z, x), self.linear(*move(y, c, z, x))))
        return pairs

    def to_plane(self, k):
        return self.perm(
            lambda y, c, z, x: ((z % self.ny) ^ c, (z // self.ny) ^ k, c * self.ny + y, x)
        )

    def from_plane(self, k):
        return [(target, source) for source, target in self.to_plane(k)]

    def swap(self, ky=0, kc=0, kz=0, kx=0):
        return self.perm(lambda y, c, z, x: (y ^ ky, c ^ kc, z ^ kz, x ^ kx))

    def row_block(self, y, x, i):
        if self.halves > 1:
            return (i * self.ny + y) * self.nx + x
        return self.nc * (y * self.nx + x) + i

    def rows_to_chip(self):
        reader = {
            self.row_block(y, x, i): (y, x, i)
            for y in range(self.ny)
            for x in range(self.nx)
            for i in range(self.nc)
        }

        def move(y, c, z, x):
            chip_y, chip_x, i = reader[z * self.nx + x]
            return chip_y, i, c * self.ny + (y ^ (z & 1)), chip_x

        return self.perm(move)

    def to_owner(self):
        def move(y, c, z, x):
            s = self.row_block(y, x, c)
            return z // self.nc, z % self.nc, s // self.nx, s % self.nx

        return self.perm(move)

    def chip_of(self, k):
        return k // self.nx, k % self.nx

    def bits(self, count):
        return [1 << b for b in range(count.bit_length() - 1)]

    def chip_bits(self, j):
        bits = self.bits(self.chips)
        return bits if j % 2 == 0 else bits[::-1]

    def doubled(self, bits):
        held = [0]
        for bit in bits:
            held = held + [k ^ bit for k in held]
        return held

    def slots(self):
        return [(k, j) for k in range(self.chips) for j in range(self.nc)]


def slot_scalars(lay, pos_ref, info_ref, slot):
    k, j = slot
    ky, kx = lay.chip_of(k)
    z_frame = (pos_ref[1] ^ j) * lay.ny + (pos_ref[0] ^ ky ^ (pos_ref[2] // lay.ny))
    frame = z_frame * lay.nx + (pos_ref[3] ^ kx)
    clip = info_ref[frame]
    clips = (info_ref.shape[0] - lay.frames) // 2
    return clip, info_ref[lay.frames + clip], info_ref[lay.frames + clips + clip]


def table_row(mod_ref, step, part, width):
    return mod_ref[pl.ds(step, 1), part * width : (part + 1) * width]


def allowed_pairs(lay, pos_ref, info_ref, patch_base):
    rows = lay.frames * BLOCK
    row_slot = lax.broadcasted_iota(jnp.int32, (rows, 1), 0) // BLOCK
    col_slot = lax.broadcasted_iota(jnp.int32, (1, rows), 1) // BLOCK
    row_clip = jnp.zeros((rows, 1), jnp.int32)
    row_limit = jnp.zeros((rows, 1), jnp.int32)
    col_clip = jnp.zeros((1, rows), jnp.int32)
    for t, slot in enumerate(lay.slots()):
        clip, limit, _ = slot_scalars(lay, pos_ref, info_ref, slot)
        row_clip = jnp.where(row_slot == t, clip, row_clip)
        row_limit = jnp.where(row_slot == t, limit, row_limit)
        col_clip = jnp.where(col_slot == t, clip, col_clip)
    row_patch = lax.broadcasted_iota(jnp.int32, (rows, 1), 0) % BLOCK
    col_patch = lax.broadcasted_iota(jnp.int32, (1, rows), 1) % BLOCK
    row_key = row_clip * BLOCK + row_patch
    col_key = col_clip * BLOCK + col_patch
    row_valid = (patch_base + row_patch < row_limit).astype(jnp.int32)
    row_index = lax.broadcasted_iota(jnp.int32, (rows, rows), 0)
    col_index = lax.broadcasted_iota(jnp.int32, (rows, rows), 1)
    return (row_key == col_key) & ((row_valid > 0) | (row_index == col_index))


def head_mask(values, head, head_size):
    lane = lax.broadcasted_iota(jnp.int32, (1, values.shape[1]), 1)
    inside = (lane >= head * head_size) & (lane < (head + 1) * head_size)
    return jnp.where(inside, values, jnp.zeros_like(values))


def patch_blocks(array, block):
    part = array[:, block * BLOCK : (block + 1) * BLOCK, :]
    return part.reshape(part.shape[0] * BLOCK, part.shape[2])


def start_kernel(lay, cols, pos_ref, x_ref, g_ref, w_ref, *refs):
    pair_refs, out_refs = refs[: lay.nc], refs[lay.nc :]
    half = x_ref.shape[1] // lay.nc
    for k, ref in enumerate(pair_refs):
        first = pl.multiple_of(((pos_ref[2] // lay.ny) ^ k) * half, 16)
        ref[0, 0] = x_ref[0, pl.ds(first, half), :]
        ref[0, 1] = g_ref[0, pl.ds(first, half), :]
    model = w_ref.shape[1] // 3
    for k, out_ref in enumerate(out_refs):
        chip_x = pos_ref[3] ^ k
        if lay.halves > 1:
            want = lay.row_block(pos_ref[0], chip_x, pos_ref[1])
        else:
            want = pos_ref[0] * lay.nx + chip_x
        for v in range(lay.chips * lay.halves):

            @pl.when(want == v)
            def _(v=v, out_ref=out_ref):
                parts = [
                    w_ref[:, p * model + v * cols : p * model + (v + 1) * cols]
                    for p in range(3)
                ]
                out_ref[...] = jnp.concatenate(parts, axis=1)


def fill_weights(lay, pos_ref, w_refs, w_scr):
    block = w_scr.shape[1] // lay.nz
    rows, width = w_refs[0].shape[0], w_scr.shape[2]
    for h in range(lay.halves):
        for k in range(lay.nz):
            ref = w_refs[h * lay.nz + k]
            for m in range(block // rows):
                start = pl.multiple_of((pos_ref[2] ^ k) * block + m * rows, 16)
                w_scr[h, pl.ds(start, rows), :] = ref[:, m * width : (m + 1) * width]


def heads_stacked(lay, values):
    head_size = values.shape[1] // lay.half_heads
    parts = [head_mask(values, head, head_size) for head in range(lay.half_heads)]
    return jnp.concatenate(parts, axis=0) if len(parts) > 1 else parts[0]


def beside(lay, weights):
    return jnp.concatenate([weights[head] for head in range(lay.half_heads)], axis=1)


def attention_weights(lay, keys_stacked, queries, allowed, scaling):
    scores = dot_t(keys_stacked, queries) * scaling
    scores = jnp.where(allowed, scores.reshape((lay.half_heads,) + allowed.shape), -jnp.inf)
    exponent = jnp.exp(scores - jnp.max(scores, axis=1, keepdims=True))
    return exponent * (1.0 / jnp.sum(exponent, axis=1, keepdims=True))


def prepare_kernel(lay, pos_ref, info_ref, *refs):
    pair_refs, (mod_ref, hid_ref, gp_ref) = refs[: 2 * lay.nc], refs[2 * lay.nc :]
    _, step_patches, model = hid_ref.shape
    patches = step_patches * pl.num_programs(0)
    patch_base = pos_ref[1] * patches + pl.program_id(0) * step_patches
    patch = patch_base + lax.broadcasted_iota(jnp.int32, (step_patches, 1), 0)
    for t, (k, j) in enumerate(lay.slots()):
        _, limit, step = slot_scalars(lay, pos_ref, info_ref, (k, j))
        n = lay.doubled(lay.chip_bits(j)).index(k)
        ref, place = pair_refs[2 * j + (2 * n) // lay.chips], n % (lay.chips // 2)
        normed, _ = normalize(ref[place, 0].astype(F32))
        shift, scale = table_row(mod_ref, step, 0, model), table_row(mod_ref, step, 1, model)
        hid_ref[t] = (normed * (1.0 + scale) + shift).astype(BF16)
        factor = jnp.where(patch < limit, table_row(mod_ref, step, 2, model), 0.0)
        gp_ref[t] = (factor * ref[place, 1].astype(F32)).astype(BF16)


def forward_kernel(lay, pos_ref, info_ref, hid_ref, gp_ref, *refs):
    w_refs, refs = refs[: lay.halves * lay.nz], refs[lay.halves * lay.nz :]
    wo_refs, refs = refs[: lay.nc], refs[lay.nc :]
    q_ref, k_ref, v_ref, ga_ref, kept_ref, sent_ref, *refs = refs
    pr_refs, (w_scr, att_scr, wo_scr, acc_scr, cut_scr) = refs[: lay.chips], refs[lay.chips :]
    _, step_patches, model = hid_ref.shape
    tokens = lay.frames * step_patches
    cols = w_scr.shape[2] // 3
    scaling = 1.0 / math.sqrt(cols // lay.half_heads)
    patches = step_patches * pl.num_programs(0)
    is_first = pos_ref[1] == 0

    @pl.when(pl.program_id(0) == 0)
    def _():
        fill_weights(lay, pos_ref, w_refs, w_scr)
        own, other = wo_refs[0][...].astype(F32), wo_refs[1][...].astype(F32)
        both = [jnp.where(is_first, own, other), jnp.where(is_first, other, own)]
        wo_scr[...] = jnp.concatenate(both, axis=0).astype(BF16)
        acc_scr[...] = jnp.zeros_like(acc_scr)

    hidden = hid_ref[...].reshape(lay.frames * step_patches, model)
    for h in range(lay.halves):
        triple = dot(hidden, w_scr[h])
        for n, ref in enumerate((q_ref, k_ref, v_ref)):
            ref[h] = triple[:, n * cols : (n + 1) * cols].astype(BF16).reshape(ref.shape[1:])

    for b in range(step_patches // BLOCK):
        patch_base = pos_ref[1] * patches + pl.program_id(0) * step_patches + b * BLOCK
        allowed = allowed_pairs(lay, pos_ref, info_ref, patch_base)
        outputs = []
        for h in range(lay.halves):
            queries, keys, values = (patch_blocks(ref[h], b) for ref in (q_ref, k_ref, v_ref))
            weights = attention_weights(lay, heads_stacked(lay, keys), queries, allowed, scaling)
            weights = weights.astype(BF16).reshape(-1, allowed.shape[1])
            outputs.append(t_dot(weights, heads_stacked(lay, values)))
        if lay.halves > 1:
            first = jnp.where(pos_ref[1] == 0, outputs[0], outputs[1])
            second = jnp.where(pos_ref[1] == 0, outputs[1], outputs[0])
            outputs = [jnp.concatenate([first, second], axis=1)]
        attended = outputs[0].astype(BF16)
        att_scr[:, b * BLOCK : (b + 1) * BLOCK, :] = attended.reshape(lay.frames, BLOCK, -1)

    attended = att_scr[...].reshape(tokens, -1)
    grad_proj = gp_ref[...].reshape(tokens, model)
    acc_scr[...] += t_dot(attended, grad_proj)
    grad_attn = dot_t(grad_proj, wo_scr[...])
    part = wo_scr.shape[0] // lay.halves
    for h in range(lay.halves):
        ga_ref[h] = grad_attn[:, h * part : (h + 1) * part].astype(BF16).reshape(ga_ref.shape[1:])
    projected = dot(attended, wo_scr[...]).reshape(lay.chips, lay.nc, step_patches, model)
    for k in range(lay.chips):
        pr_refs[k][...] = projected[k].astype(pr_refs[k].dtype)

    @pl.when(pl.program_id(0) == pl.num_programs(0) - 1)
    def _():
        groups, chunk_rows, chunk_width = kept_ref.shape
        block_rows, part = acc_scr.shape[0] // lay.nc, model // groups
        order = lay.doubled(lay.bits(lay.nz)[::-1])
        first, second = acc_scr[:block_rows, :], acc_scr[block_rows:, :]
        kept = jnp.where(is_first, first, second)
        sent = jnp.where(is_first, second, first)
        for ref, rows in ((kept_ref, kept), (sent_ref, sent)):
            for d in range(groups):
                chunk = [
                    rows[m * chunk_rows : (m + 1) * chunk_rows, d * part : (d + 1) * part]
                    for m in range(chunk_width // part)
                ]
                cut_scr[d] = jnp.concatenate(chunk, axis=1) if len(chunk) > 1 else chunk[0]
            for n, k in enumerate(order):
                ref[n] = cut_scr[pos_ref[2] ^ k]


def backward_kernel(lay, pos_ref, info_ref, *refs):
    w_refs, refs = refs[: lay.halves * lay.nz], refs[lay.halves * lay.nz :]
    q_ref, k_ref, v_ref, ga_ref, *refs = refs
    gh_refs, (w_scr, gt_scr) = refs[: lay.chips], refs[lay.chips :]
    _, frames, step_patches, cols = q_ref.shape
    model = w_scr.shape[1]
    patches = step_patches * pl.num_programs(0)
    scaling = 1.0 / math.sqrt(cols // lay.half_heads)

    @pl.when(pl.program_id(0) == 0)
    def _():
        fill_weights(lay, pos_ref, w_refs, w_scr)

    for b in range(step_patches // BLOCK):
        patch_base = pos_ref[1] * patches + pl.program_id(0) * step_patches + b * BLOCK
        allowed = allowed_pairs(lay, pos_ref, info_ref, patch_base)
        for h in range(lay.halves):
            queries, keys, values = (patch_blocks(ref[h], b) for ref in (q_ref, k_ref, v_ref))
            grad_out = patch_blocks(ga_ref[(pos_ref[1] ^ h) if lay.halves > 1 else 0], b)
            keys = heads_stacked(lay, keys)
            weights = attention_weights(lay, keys, queries, allowed, scaling)
            grad_weights = dot_t(heads_stacked(lay, values), grad_out).reshape(weights.shape)
            grad_values = dot(beside(lay, weights.astype(BF16)), heads_stacked(lay, grad_out))
            inner = jnp.sum(weights * grad_weights, axis=1, keepdims=True)
            grad_scores = (weights * (grad_weights - inner) * scaling).astype(BF16)
            grad_queries = t_dot(grad_scores.reshape(-1, grad_scores.shape[2]), keys)
            grad_keys = dot(beside(lay, grad_scores), heads_stacked(lay, queries))
            grads = jnp.concatenate([grad_queries, grad_keys, grad_values], axis=1).astype(BF16)
            gt_scr[h, :, b * BLOCK : (b + 1) * BLOCK, :] = grads.reshape(frames, BLOCK, 3 * cols)

    rows = lay.nc * step_patches
    for k in range(lay.chips):
        total = jnp.zeros((rows, model), F32)
        for h in range(lay.halves):
            part = gt_scr[h, k * lay.nc : (k + 1) * lay.nc].reshape(rows, 3 * cols)
            total = total + dot_t(part, w_scr[h])
        gh_refs[k][...] = total.reshape(gh_refs[k].shape).astype(gh_refs[k].dtype)


def output_kernel(lay, pos_ref, info_ref, *refs):
    pair_refs, refs = refs[: lay.nc], refs[lay.nc :]
    pr_refs, refs = refs[: lay.chips], refs[lay.chips :]
    mod_ref, *out_refs = refs
    step_patches, model = out_refs[0].shape
    patches = step_patches * pl.num_programs(0)
    patch_base = pos_ref[1] * patches + pl.program_id(0) * step_patches
    patch = patch_base + lax.broadcasted_iota(jnp.int32, (step_patches, 1), 0)
    for j in range(lay.nc):
        _, limit, step = slot_scalars(lay, pos_ref, info_ref, (0, j))
        factor = jnp.where(patch < limit, table_row(mod_ref, step, 2, model), 0.0)
        projected = pr_refs[0][j]
        for k in range(1, lay.chips):
            projected = projected + pr_refs[k][j].astype(F32)
        projected = projected.astype(BF16).astype(F32)
        out_refs[j][...] = (pair_refs[j][0, 0].astype(F32) + factor * projected).astype(BF16)


def input_grad_kernel(lay, pos_ref, info_ref, *refs):
    pair_refs, refs = refs[: lay.nc], refs[lay.nc :]
    gh_refs, refs = refs[: lay.chips], refs[lay.chips :]
    mod_ref, *out_refs = refs
    model = out_refs[0].shape[1]
    for j in range(lay.nc):
        _, _, step = slot_scalars(lay, pos_ref, info_ref, (0, j))
        grad_hidden = gh_refs[0][j]
        for k in range(1, lay.chips):
            grad_hidden = grad_hidden + gh_refs[k][j].astype(F32)
        grad_hidden = grad_hidden.astype(BF16).astype(F32)
        normed, inv_sigma = normalize(pair_refs[j][0, 0].astype(F32))
        grad_norm = grad_hidden * (1.0 + table_row(mod_ref, step, 1, model))
        first_mean = jnp.mean(grad_norm, axis=-1, keepdims=True)
        second_mean = jnp.mean(grad_norm * normed, axis=-1, keepdims=True)
        grad_x = pair_refs[j][0, 1].astype(F32) + inv_sigma * (
            grad_norm - first_mean - normed * second_mean
        )
        out_refs[j][...] = grad_x.astype(BF16)


def whole_spec(shape):
    return pl.BlockSpec(shape, lambda *_: (0,) * len(shape))


def struct(shape, dtype=BF16):
    return jax.ShapeDtypeStruct(shape, dtype)


def local(lay, frames_x, grad_y, clip_ids, clip_patches, clip_step, mod_table, w_qkv, w_out):
    y, c, z, x = (lax.axis_index(name) for name in AXES)
    _, patches, model = frames_x.shape
    half = patches // lay.nc
    chips, nc, nx = lay.chips, lay.nc, lay.nx
    head_size = model // HEADS
    halves = lay.halves
    cols = lay.half_heads * head_size
    chip_width = lay.chip_heads * head_size
    rows = w_qkv.shape[0]
    groups = lay.nz
    quarter = model // groups
    step_patches = max(BLOCK, min(half, 512 // lay.frames))
    steps = half // step_patches
    tokens = lay.frames * step_patches

    def call(kernel, name, cost, in_specs, out_specs, out_shape, scratch=(), grid=(1,), prefetch=2):
        return pl.pallas_call(
            kernel,
            grid_spec=pltpu.PrefetchScalarGridSpec(
                num_scalar_prefetch=prefetch,
                grid=grid,
                in_specs=in_specs,
                out_specs=out_specs,
                scratch_shapes=list(scratch),
            ),
            out_shape=out_shape,
            compiler_params=pltpu.CompilerParams(vmem_limit_bytes=VMEM_LIMIT),
            cost_estimate=pl.CostEstimate(
                flops=cost * tokens * steps, bytes_accessed=4 * model * tokens, transcendentals=0
            ),
            name=name,
        )

    def chip_swap(k):
        ky, kx = lay.chip_of(k)
        return lay.swap(ky=ky, kx=kx)

    def doubling(held, bits, swap, after):
        for bit in bits[:-1]:
            held = jnp.concatenate([held, lax.ppermute(held, AXES, swap(bit))], axis=0)
        held, _ = lax.optimization_barrier((held, after))
        return [held, lax.ppermute(held, AXES, swap(bits[-1]))]

    def over_chips(parts):
        got = [lax.ppermute(parts[k], AXES, chip_swap(k)) for k in range(1, chips)]
        return [parts[0]] + got

    def from_plane(parts):
        got = [lax.ppermute(part, AXES, lay.from_plane(k)) for k, part in enumerate(parts)]
        first = jnp.where(z // lay.ny == 0, got[0], got[1])
        second = jnp.where(z // lay.ny == 0, got[1], got[0])
        return jnp.concatenate([first, second], axis=0)[None]

    info = jnp.concatenate([clip_ids[0], clip_patches[0], clip_step[0]])[None]
    by_core = jnp.concatenate([info, lax.ppermute(info, AXES, lay.swap(kc=1))], axis=0)
    info = [by_core] + [
        lax.ppermute(by_core, AXES, lay.swap(ky=ky)) for ky in range(1, lay.ny)
    ]
    group_y, group_c = z % lay.ny, z // lay.ny
    info = sum(
        jnp.where((y ^ ky == group_y) & (c ^ kc == group_c), info[ky][kc], 0)
        for ky in range(lay.ny)
        for kc in range(nc)
    )
    pos = jnp.stack([y, c, z, x]).astype(jnp.int32)
    pair_shape = (1, 2, half, model)
    outputs = call(
        functools.partial(start_kernel, lay, cols),
        "start",
        2 * model * 1000,
        [whole_spec(frames_x.shape)] * 2 + [whole_spec(w_qkv.shape)],
        [whole_spec(pair_shape)] * nc + [whole_spec((rows, 3 * cols))] * nx,
        [struct(pair_shape)] * nc + [struct((rows, 3 * cols))] * nx,
        prefetch=1,
    )(pos, frames_x, grad_y, w_qkv)
    pairs, picked = outputs[:nc], outputs[nc:]
    own = [lax.ppermute(pair, AXES, lay.to_plane(k)) for k, pair in enumerate(pairs)]
    by_x = [picked[0]] + [
        lax.ppermute(picked[kx], AXES, lay.swap(kx=kx)) for kx in range(1, nx)
    ]
    if nx == 2:
        ordered = [jnp.where(x == i, by_x[0], by_x[1]) for i in range(nx)]
    else:
        stacked = jnp.stack(by_x)
        ordered = [lax.dynamic_index_in_dim(stacked, x ^ i, 0, keepdims=False) for i in range(nx)]
    w_own = jnp.concatenate(ordered, axis=1 if rows % 16 == 0 else 0)
    own[0], _ = lax.optimization_barrier((own[0], w_own))
    w_pieces = {0: w_own}
    for bit in lay.bits(lay.nz):
        w_pieces[bit] = lax.ppermute(w_own, AXES, lay.swap(kz=bit))
    early = [w_pieces[bit] for bit in lay.bits(lay.nz)]
    for k in range(1, lay.nz):
        if k not in w_pieces:
            bit = k & -k
            w_pieces[k] = lax.ppermute(w_pieces[k ^ bit], AXES, lay.swap(kz=bit))
    w_pieces = [w_pieces[k] for k in range(lay.nz)]
    late = w_pieces[-1]
    if halves > 1:
        w_pieces += [lax.ppermute(piece, AXES, lay.swap(kc=1)) for piece in w_pieces]

    late_w_out, _ = lax.optimization_barrier((w_out, own))
    wo_own = lax.ppermute(late_w_out, AXES, lay.rows_to_chip())

    pairs = []
    for j in range(nc):
        pairs += doubling(own[j], lay.chip_bits(j), chip_swap, info)
    pairs, _ = lax.optimization_barrier((pairs, [late, wo_own] + w_pieces[lay.nz : -1]))


    def spread(count, width, patches_at_once):
        return pl.BlockSpec((count, patches_at_once, width), lambda i, *_: (0, i, 0))

    def pair_spec(count, patches_at_once):
        return pl.BlockSpec((count, 2, patches_at_once, model), lambda i, *_: (0, 0, i, 0))

    few = max(BLOCK, step_patches // 2)
    few_steps = half // few
    x_spec = pl.BlockSpec((few, model), lambda i, *_: (i, 0))
    triple_spec = pl.BlockSpec((halves, lay.frames, step_patches, cols), lambda i, *_: (0, 0, i, 0))
    w_specs = [whole_spec(piece.shape) for piece in w_pieces]
    w_scratch = pltpu.VMEM((halves, model, 3 * cols), BF16)
    mod_spec = whole_spec(mod_table.shape)
    triple_shape = struct((halves, lay.frames, half, cols))
    part_specs = [spread(nc, model, step_patches)] * chips
    part_shapes = [struct((nc, half, model), F32)] + [struct((nc, half, model))] * (chips - 1)

    hidden, grad_proj = call(
        functools.partial(prepare_kernel, lay),
        "prepare",
        3 * model * 1000,
        [pair_spec(chips // 2, few)] * (2 * nc) + [mod_spec],
        [spread(lay.frames, model, few)] * 2,
        [struct((lay.frames, half, model))] * 2,
        grid=(few_steps,),
    )(pos, info, *pairs, mod_table)
    wo_rows = [wo_own, lax.ppermute(wo_own, AXES, lay.swap(kc=1))]

    fold = 3 if rows % 24 == 0 else 1
    piece_shape = (groups, rows // fold, quarter * fold)
    queries, keys, values, grad_attn, kept, sent, *projected = call(
        functools.partial(forward_kernel, lay),
        "forward",
        14 * model * 1000,
        [spread(lay.frames, model, step_patches)] * 2
        + w_specs
        + [whole_spec(w_out.shape)] * nc,
        [triple_spec] * 4 + [whole_spec(piece_shape)] * 2 + part_specs,
        [triple_shape] * 4 + [struct(piece_shape, F32)] * 2 + part_shapes,
        [
            w_scratch,
            pltpu.VMEM((lay.frames, step_patches, chip_width), BF16),
            pltpu.VMEM((chip_width, model), BF16),
            pltpu.VMEM((chip_width, model), F32),
            pltpu.VMEM(piece_shape, F32),
        ],
        (steps,),
    )(pos, info, hidden, grad_proj, *w_pieces, *wo_rows)
    got = lax.ppermute(sent, AXES, lay.swap(kc=1))
    projected = over_chips(projected)

    middle = groups // 2
    cut, away = kept[:middle] + got[:middle], kept[middle:] + got[middle:]
    grad_attn, cut, away = lax.optimization_barrier((grad_attn, cut, away))
    first_away = lax.ppermute(away, AXES, lay.swap(kz=1))

    sums = call(
        functools.partial(backward_kernel, lay),
        "backward",
        10 * model * 1000,
        w_specs + [triple_spec] * 4,
        part_specs,
        part_shapes,
        [w_scratch, pltpu.VMEM((halves, lay.frames, step_patches, 3 * cols), BF16)],
        (steps,),
    )(pos, info, *w_pieces, queries, keys, values, grad_attn)
    sums, first_away, projected = lax.optimization_barrier((sums, first_away, projected))
    grad_hidden = over_chips(sums)

    projected, _ = lax.optimization_barrier((projected, grad_hidden[1]))
    out_parts = call(
        functools.partial(output_kernel, lay),
        "output",
        3 * model * 1000,
        [pair_spec(1, few)] * nc + [spread(nc, model, few)] * chips + [mod_spec],
        [x_spec] * nc,
        [struct((half, model))] * nc,
        grid=(few_steps,),
    )(pos, info, *own, *projected, mod_table)

    cut = cut + first_away
    for bit in lay.bits(lay.nz)[1:]:
        middle = middle // 2
        away = lax.ppermute(cut[middle:], AXES, lay.swap(kz=bit))
        away, _ = lax.optimization_barrier((away, out_parts))
        cut = cut[:middle] + away
    out_y = from_plane(out_parts)


    grad_parts = call(
        functools.partial(input_grad_kernel, lay),
        "input_grad",
        3 * model * 1000,
        [pair_spec(1, few)] * nc + [spread(nc, model, few)] * chips + [mod_spec],
        [x_spec] * nc,
        [struct((half, model))] * nc,
        grid=(few_steps,),
    )(pos, info, *own, *grad_hidden, mod_table)
    grad_x = from_plane(grad_parts)

    cut, _ = lax.optimization_barrier((cut, grad_parts))
    grad_w = lax.ppermute(cut[0], AXES, lay.to_owner())
    grad_w = jnp.concatenate(
        [grad_w[:, m * quarter : (m + 1) * quarter] for m in range(fold)], axis=0
    )
    grad_w_out = grad_w * jnp.float32(1.0 / math.sqrt(groups * lay.frames * patches))
    return out_y, grad_x, grad_w_out


def solution(mesh):
    lay = Layout(mesh)
    grid = Mesh(mesh.devices.reshape(lay.ny, lay.nc, lay.nz, lay.nx), AXES)
    rows, cols = ("z", "x"), ("y", "c")
    frame = P(AXES, None, None)
    group = P(cols, None)
    return jax.shard_map(
        functools.partial(local, lay),
        mesh=grid,
        in_specs=(frame, frame, group, group, group, P(), P(rows, None), P(rows, None)),
        out_specs=(frame, frame, P(rows, cols)),
        check_vma=False,
    )
```

```python
import functools
import math

import jax
import jax.numpy as jnp
from jax import lax
from jax.experimental import pallas as pl
from jax.experimental.pallas import tpu as pltpu
from jax.sharding import Mesh, PartitionSpec as P

HEADS = 16
CORES = 2
AXES = ("y", "c", "z", "x")
BLOCK = 16
VMEM_LIMIT = 56 * 1024 * 1024
BF16 = jnp.bfloat16
F32 = jnp.float32


def dot(left, right):
    return jnp.dot(left, right, preferred_element_type=F32)


def dot_t(left, right):
    return lax.dot_general(left, right, (((1,), (1,)), ((), ())), preferred_element_type=F32)


def t_dot(left, right):
    return lax.dot_general(left, right, (((0,), (0,)), ((), ())), preferred_element_type=F32)


def normalize(values):
    centred = values - jnp.mean(values, axis=-1, keepdims=True)
    inv_sigma = lax.rsqrt(jnp.mean(centred * centred, axis=-1, keepdims=True) + 1e-06)
    return centred * inv_sigma, inv_sigma


class Layout:
    def __init__(self, mesh):
        groups, seq = mesh.shape["dp"], mesh.shape["seq"]
        self.nc = CORES
        self.ny = groups // CORES
        self.nz = groups
        self.nx = seq // self.nz
        self.chips = self.ny * self.nx
        self.frames = seq
        self.chip_heads = HEADS // self.chips
        self.halves = 2 if self.chip_heads % 2 == 0 else 1
        self.half_heads = self.chip_heads // self.halves

    def linear(self, y, c, z, x):
        return ((y * self.nc + c) * self.nz + z) * self.nx + x

    def perm(self, move):
        pairs = []
        for y in range(self.ny):
            for c in range(self.nc):
                for z in range(self.nz):
                    for x in range(self.nx):
                        pairs.append((self.linear(y, c, z, x), self.linear(*move(y, c, z, x))))
        return pairs

    def to_plane(self, k):
        def move(y, c, z, x):
            half = (z // self.ny) ^ k
            plane = ((y // self.nc) * self.nc + c) * self.nc + half
            return (z % self.ny) ^ c, y % self.nc, plane, x

        return self.perm(move)

    def unit(self, c, z):
        return (z // (self.nc * self.nc)) * self.nc + c, (z // self.nc) % self.nc, z % self.nc

    def from_plane(self, k):
        return [(target, source) for source, target in self.to_plane(k)]

    def swap(self, ky=0, kc=0, kz=0, kx=0):
        return self.perm(lambda y, c, z, x: (y ^ ky, c ^ kc, z ^ kz, x ^ kx))

    def row_block(self, y, x, i):
        if self.halves > 1:
            return (i * self.ny + y) * self.nx + x
        return self.nc * (y * self.nx + x) + i

    def rows_to_chip(self):
        reader = {
            self.row_block(y, x, i): (y, x, i)
            for y in range(self.ny)
            for x in range(self.nx)
            for i in range(self.nc)
        }

        def move(y, c, z, x):
            chip_y, chip_x, i = reader[z * self.nx + x]
            return chip_y, i, c * self.ny + (y ^ (z & 1)), chip_x

        return self.perm(move)

    def to_owner(self):
        def move(y, c, z, x):
            s = self.row_block(y, x, c)
            return z // self.nc, z % self.nc, s // self.nx, s % self.nx

        return self.perm(move)

    def chip_of(self, k):
        return k // self.nx, k % self.nx

    def bits(self, count):
        return [1 << b for b in range(count.bit_length() - 1)]

    def chip_bits(self, j):
        bits = self.bits(self.chips)
        return bits if j % 2 == 0 else bits[::-1]

    def doubled(self, bits):
        held = [0]
        for bit in bits:
            held = held + [k ^ bit for k in held]
        return held

    def slots(self):
        return [(k, j) for k in range(self.chips) for j in range(self.nc)]


def slot_scalars(lay, pos_ref, info_ref, slot):
    k, j = slot
    ky, kx = lay.chip_of(k)
    _, group_c, half = lay.unit(pos_ref[1], pos_ref[2])
    z_frame = (half ^ j) * lay.ny + (pos_ref[0] ^ ky ^ group_c)
    frame = z_frame * lay.nx + (pos_ref[3] ^ kx)
    clip = info_ref[frame]
    clips = (info_ref.shape[0] - lay.frames) // 2
    return clip, info_ref[lay.frames + clip], info_ref[lay.frames + clips + clip]


def table_row(mod_ref, step, part, width):
    return mod_ref[pl.ds(step, 1), part * width : (part + 1) * width]


def allowed_pairs(lay, pos_ref, info_ref, patch_base):
    rows = lay.frames * BLOCK
    row_slot = lax.broadcasted_iota(jnp.int32, (rows, 1), 0) // BLOCK
    col_slot = lax.broadcasted_iota(jnp.int32, (1, rows), 1) // BLOCK
    row_clip = jnp.zeros((rows, 1), jnp.int32)
    row_limit = jnp.zeros((rows, 1), jnp.int32)
    col_clip = jnp.zeros((1, rows), jnp.int32)
    for t, slot in enumerate(lay.slots()):
        clip, limit, _ = slot_scalars(lay, pos_ref, info_ref, slot)
        row_clip = jnp.where(row_slot == t, clip, row_clip)
        row_limit = jnp.where(row_slot == t, limit, row_limit)
        col_clip = jnp.where(col_slot == t, clip, col_clip)
    row_patch = lax.broadcasted_iota(jnp.int32, (rows, 1), 0) % BLOCK
    col_patch = lax.broadcasted_iota(jnp.int32, (1, rows), 1) % BLOCK
    row_key = row_clip * BLOCK + row_patch
    col_key = col_clip * BLOCK + col_patch
    row_valid = (patch_base + row_patch < row_limit).astype(jnp.int32)
    row_index = lax.broadcasted_iota(jnp.int32, (rows, rows), 0)
    col_index = lax.broadcasted_iota(jnp.int32, (rows, rows), 1)
    return (row_key == col_key) & ((row_valid > 0) | (row_index == col_index))


def head_mask(values, head, head_size):
    lane = lax.broadcasted_iota(jnp.int32, (1, values.shape[1]), 1)
    inside = (lane >= head * head_size) & (lane < (head + 1) * head_size)
    return jnp.where(inside, values, jnp.zeros_like(values))


def patch_blocks(array, block):
    part = array[:, block * BLOCK : (block + 1) * BLOCK, :]
    return part.reshape(part.shape[0] * BLOCK, part.shape[2])


def start_kernel(lay, cols, pos_ref, x_ref, g_ref, w_ref, *refs):
    pair_refs, out_refs = refs[: lay.nc], refs[lay.nc :]
    half = x_ref.shape[1] // lay.nc
    for k, ref in enumerate(pair_refs):
        first = pl.multiple_of(((pos_ref[2] // lay.ny) ^ k) * half, 16)
        ref[0, 0] = x_ref[0, pl.ds(first, half), :]
        ref[0, 1] = g_ref[0, pl.ds(first, half), :]
    model = w_ref.shape[1] // 3
    for k, out_ref in enumerate(out_refs):
        chip_x = pos_ref[3] ^ k
        if lay.halves > 1:
            want = lay.row_block(pos_ref[0], chip_x, pos_ref[1])
        else:
            want = pos_ref[0] * lay.nx + chip_x
        for v in range(lay.chips * lay.halves):

            @pl.when(want == v)
            def _(v=v, out_ref=out_ref):
                parts = [
                    w_ref[:, p * model + v * cols : p * model + (v + 1) * cols]
                    for p in range(3)
                ]
                out_ref[...] = jnp.concatenate(parts, axis=1)


def fill_weights(lay, pos_ref, w_refs, w_scr):
    block = w_scr.shape[1] // lay.nz
    rows, width = w_refs[0].shape[0], w_scr.shape[2]
    for h in range(lay.halves):
        for k in range(lay.nz):
            ref = w_refs[h * lay.nz + k]
            for m in range(block // rows):
                start = pl.multiple_of((pos_ref[2] ^ k) * block + m * rows, 16)
                w_scr[h, pl.ds(start, rows), :] = ref[:, m * width : (m + 1) * width]


def heads_stacked(lay, values):
    head_size = values.shape[1] // lay.half_heads
    parts = [head_mask(values, head, head_size) for head in range(lay.half_heads)]
    return jnp.concatenate(parts, axis=0) if len(parts) > 1 else parts[0]


def beside(lay, weights):
    return jnp.concatenate([weights[head] for head in range(lay.half_heads)], axis=1)


def attention_weights(lay, keys_stacked, queries, allowed, scaling):
    scores = dot_t(keys_stacked, queries) * scaling
    scores = jnp.where(allowed, scores.reshape((lay.half_heads,) + allowed.shape), -jnp.inf)
    exponent = jnp.exp(scores - jnp.max(scores, axis=1, keepdims=True))
    return exponent * (1.0 / jnp.sum(exponent, axis=1, keepdims=True))


def prepare_kernel(lay, pos_ref, info_ref, *refs):
    pair_refs, (mod_ref, hid_ref, gp_ref) = refs[: 2 * lay.nc], refs[2 * lay.nc :]
    _, step_patches, model = hid_ref.shape
    patches = step_patches * pl.num_programs(0)
    patch_base = lay.unit(pos_ref[1], pos_ref[2])[2] * patches + pl.program_id(0) * step_patches
    patch = patch_base + lax.broadcasted_iota(jnp.int32, (step_patches, 1), 0)
    for t, (k, j) in enumerate(lay.slots()):
        _, limit, step = slot_scalars(lay, pos_ref, info_ref, (k, j))
        n = lay.doubled(lay.chip_bits(j)).index(k)
        ref, place = pair_refs[2 * j + (2 * n) // lay.chips], n % (lay.chips // 2)
        normed, _ = normalize(ref[place, 0].astype(F32))
        shift, scale = table_row(mod_ref, step, 0, model), table_row(mod_ref, step, 1, model)
        hid_ref[t] = (normed * (1.0 + scale) + shift).astype(BF16)
        factor = jnp.where(patch < limit, table_row(mod_ref, step, 2, model), 0.0)
        gp_ref[t] = (factor * ref[place, 1].astype(F32)).astype(BF16)


def forward_kernel(lay, pos_ref, info_ref, hid_ref, gp_ref, *refs):
    w_refs, refs = refs[: lay.halves * lay.nz], refs[lay.halves * lay.nz :]
    wo_refs, refs = refs[: lay.nc], refs[lay.nc :]
    q_ref, k_ref, v_ref, ga_ref, kept_ref, sent_ref, *refs = refs
    pr_refs, (w_scr, att_scr, wo_scr, acc_scr, cut_scr) = refs[: lay.chips], refs[lay.chips :]
    _, step_patches, model = hid_ref.shape
    tokens = lay.frames * step_patches
    cols = w_scr.shape[2] // 3
    scaling = 1.0 / math.sqrt(cols // lay.half_heads)
    patches = step_patches * pl.num_programs(0)
    is_first = pos_ref[1] == 0

    @pl.when(pl.program_id(0) == 0)
    def _():
        fill_weights(lay, pos_ref, w_refs, w_scr)
        own, other = wo_refs[0][...].astype(F32), wo_refs[1][...].astype(F32)
        both = [jnp.where(is_first, own, other), jnp.where(is_first, other, own)]
        wo_scr[...] = jnp.concatenate(both, axis=0).astype(BF16)
        acc_scr[...] = jnp.zeros_like(acc_scr)

    hidden = hid_ref[...].reshape(lay.frames * step_patches, model)
    for h in range(lay.halves):
        triple = dot(hidden, w_scr[h])
        for n, ref in enumerate((q_ref, k_ref, v_ref)):
            ref[h] = triple[:, n * cols : (n + 1) * cols].astype(BF16).reshape(ref.shape[1:])

    for b in range(step_patches // BLOCK):
        patch_base = lay.unit(pos_ref[1], pos_ref[2])[2] * patches + pl.program_id(0) * step_patches + b * BLOCK
        allowed = allowed_pairs(lay, pos_ref, info_ref, patch_base)
        outputs = []
        for h in range(lay.halves):
            queries, keys, values = (patch_blocks(ref[h], b) for ref in (q_ref, k_ref, v_ref))
            weights = attention_weights(lay, heads_stacked(lay, keys), queries, allowed, scaling)
            weights = weights.astype(BF16).reshape(-1, allowed.shape[1])
            outputs.append(t_dot(weights, heads_stacked(lay, values)))
        if lay.halves > 1:
            first = jnp.where(pos_ref[1] == 0, outputs[0], outputs[1])
            second = jnp.where(pos_ref[1] == 0, outputs[1], outputs[0])
            outputs = [jnp.concatenate([first, second], axis=1)]
        attended = outputs[0].astype(BF16)
        att_scr[:, b * BLOCK : (b + 1) * BLOCK, :] = attended.reshape(lay.frames, BLOCK, -1)

    attended = att_scr[...].reshape(tokens, -1)
    grad_proj = gp_ref[...].reshape(tokens, model)
    acc_scr[...] += t_dot(attended, grad_proj)
    grad_attn = dot_t(grad_proj, wo_scr[...])
    part = wo_scr.shape[0] // lay.halves
    for h in range(lay.halves):
        ga_ref[h] = grad_attn[:, h * part : (h + 1) * part].astype(BF16).reshape(ga_ref.shape[1:])
    projected = dot(attended, wo_scr[...]).reshape(lay.chips, lay.nc, step_patches, model)
    for k in range(lay.chips):
        pr_refs[k][...] = projected[k].astype(pr_refs[k].dtype)

    @pl.when(pl.program_id(0) == pl.num_programs(0) - 1)
    def _():
        groups, chunk_rows, chunk_width = kept_ref.shape
        block_rows, part = acc_scr.shape[0] // lay.nc, model // groups
        order = lay.doubled(lay.bits(lay.nz)[::-1])
        first, second = acc_scr[:block_rows, :], acc_scr[block_rows:, :]
        kept = jnp.where(is_first, first, second)
        sent = jnp.where(is_first, second, first)
        for ref, rows in ((kept_ref, kept), (sent_ref, sent)):
            for d in range(groups):
                chunk = [
                    rows[m * chunk_rows : (m + 1) * chunk_rows, d * part : (d + 1) * part]
                    for m in range(chunk_width // part)
                ]
                cut_scr[d] = jnp.concatenate(chunk, axis=1) if len(chunk) > 1 else chunk[0]
            for n, k in enumerate(order):
                ref[n] = cut_scr[pos_ref[2] ^ k]


def backward_kernel(lay, pos_ref, info_ref, *refs):
    w_refs, refs = refs[: lay.halves * lay.nz], refs[lay.halves * lay.nz :]
    q_ref, k_ref, v_ref, ga_ref, *refs = refs
    gh_refs, (w_scr, gt_scr) = refs[: lay.chips], refs[lay.chips :]
    _, frames, step_patches, cols = q_ref.shape
    model = w_scr.shape[1]
    patches = step_patches * pl.num_programs(0)
    scaling = 1.0 / math.sqrt(cols // lay.half_heads)

    @pl.when(pl.program_id(0) == 0)
    def _():
        fill_weights(lay, pos_ref, w_refs, w_scr)

    for b in range(step_patches // BLOCK):
        patch_base = lay.unit(pos_ref[1], pos_ref[2])[2] * patches + pl.program_id(0) * step_patches + b * BLOCK
        allowed = allowed_pairs(lay, pos_ref, info_ref, patch_base)
        for h in range(lay.halves):
            queries, keys, values = (patch_blocks(ref[h], b) for ref in (q_ref, k_ref, v_ref))
            grad_out = patch_blocks(ga_ref[(pos_ref[1] ^ h) if lay.halves > 1 else 0], b)
            keys = heads_stacked(lay, keys)
            weights = attention_weights(lay, keys, queries, allowed, scaling)
            grad_weights = dot_t(heads_stacked(lay, values), grad_out).reshape(weights.shape)
            grad_values = dot(beside(lay, weights.astype(BF16)), heads_stacked(lay, grad_out))
            inner = jnp.sum(weights * grad_weights, axis=1, keepdims=True)
            grad_scores = (weights * (grad_weights - inner) * scaling).astype(BF16)
            grad_queries = t_dot(grad_scores.reshape(-1, grad_scores.shape[2]), keys)
            grad_keys = dot(beside(lay, grad_scores), heads_stacked(lay, queries))
            grads = jnp.concatenate([grad_queries, grad_keys, grad_values], axis=1).astype(BF16)
            gt_scr[h, :, b * BLOCK : (b + 1) * BLOCK, :] = grads.reshape(frames, BLOCK, 3 * cols)

    rows = lay.nc * step_patches
    for k in range(lay.chips):
        total = jnp.zeros((rows, model), F32)
        for h in range(lay.halves):
            part = gt_scr[h, k * lay.nc : (k + 1) * lay.nc].reshape(rows, 3 * cols)
            total = total + dot_t(part, w_scr[h])
        gh_refs[k][...] = total.reshape(gh_refs[k].shape).astype(gh_refs[k].dtype)


def output_kernel(lay, pos_ref, info_ref, *refs):
    pair_refs, refs = refs[: lay.nc], refs[lay.nc :]
    pr_refs, refs = refs[: lay.chips], refs[lay.chips :]
    mod_ref, *out_refs = refs
    step_patches, model = out_refs[0].shape
    patches = step_patches * pl.num_programs(0)
    patch_base = lay.unit(pos_ref[1], pos_ref[2])[2] * patches + pl.program_id(0) * step_patches
    patch = patch_base + lax.broadcasted_iota(jnp.int32, (step_patches, 1), 0)
    for j in range(lay.nc):
        _, limit, step = slot_scalars(lay, pos_ref, info_ref, (0, j))
        factor = jnp.where(patch < limit, table_row(mod_ref, step, 2, model), 0.0)
        projected = pr_refs[0][j]
        for k in range(1, lay.chips):
            projected = projected + pr_refs[k][j].astype(F32)
        projected = projected.astype(BF16).astype(F32)
        out_refs[j][...] = (pair_refs[j][0, 0].astype(F32) + factor * projected).astype(BF16)


def input_grad_kernel(lay, pos_ref, info_ref, *refs):
    pair_refs, refs = refs[: lay.nc], refs[lay.nc :]
    gh_refs, refs = refs[: lay.chips], refs[lay.chips :]
    mod_ref, *out_refs = refs
    model = out_refs[0].shape[1]
    for j in range(lay.nc):
        _, _, step = slot_scalars(lay, pos_ref, info_ref, (0, j))
        grad_hidden = gh_refs[0][j]
        for k in range(1, lay.chips):
            grad_hidden = grad_hidden + gh_refs[k][j].astype(F32)
        grad_hidden = grad_hidden.astype(BF16).astype(F32)
        normed, inv_sigma = normalize(pair_refs[j][0, 0].astype(F32))
        grad_norm = grad_hidden * (1.0 + table_row(mod_ref, step, 1, model))
        first_mean = jnp.mean(grad_norm, axis=-1, keepdims=True)
        second_mean = jnp.mean(grad_norm * normed, axis=-1, keepdims=True)
        grad_x = pair_refs[j][0, 1].astype(F32) + inv_sigma * (
            grad_norm - first_mean - normed * second_mean
        )
        out_refs[j][...] = grad_x.astype(BF16)


def whole_spec(shape):
    return pl.BlockSpec(shape, lambda *_: (0,) * len(shape))


def struct(shape, dtype=BF16):
    return jax.ShapeDtypeStruct(shape, dtype)


def local(lay, frames_x, grad_y, clip_ids, clip_patches, clip_step, mod_table, w_qkv, w_out):
    y, c, z, x = (lax.axis_index(name) for name in AXES)
    _, patches, model = frames_x.shape
    half = patches // lay.nc
    chips, nc, nx = lay.chips, lay.nc, lay.nx
    head_size = model // HEADS
    halves = lay.halves
    cols = lay.half_heads * head_size
    chip_width = lay.chip_heads * head_size
    rows = w_qkv.shape[0]
    groups = lay.nz
    quarter = model // groups
    step_patches = max(BLOCK, min(half, 512 // lay.frames))
    steps = half // step_patches
    tokens = lay.frames * step_patches

    def call(kernel, name, cost, in_specs, out_specs, out_shape, scratch=(), grid=(1,), prefetch=2):
        return pl.pallas_call(
            kernel,
            grid_spec=pltpu.PrefetchScalarGridSpec(
                num_scalar_prefetch=prefetch,
                grid=grid,
                in_specs=in_specs,
                out_specs=out_specs,
                scratch_shapes=list(scratch),
            ),
            out_shape=out_shape,
            compiler_params=pltpu.CompilerParams(vmem_limit_bytes=VMEM_LIMIT),
            cost_estimate=pl.CostEstimate(
                flops=cost * tokens * steps, bytes_accessed=4 * model * tokens, transcendentals=0
            ),
            name=name,
        )

    def chip_swap(k):
        ky, kx = lay.chip_of(k)
        return lay.swap(ky=ky, kx=kx)

    def doubling(held, bits, swap, after):
        for bit in bits[:-1]:
            held = jnp.concatenate([held, lax.ppermute(held, AXES, swap(bit))], axis=0)
        held, _ = lax.optimization_barrier((held, after))
        return [held, lax.ppermute(held, AXES, swap(bits[-1]))]

    def over_chips(parts):
        got = [lax.ppermute(parts[k], AXES, chip_swap(k)) for k in range(1, chips)]
        return [parts[0]] + got

    def from_plane(parts):
        got = [lax.ppermute(part, AXES, lay.from_plane(k)) for k, part in enumerate(parts)]
        first = jnp.where(z // lay.ny == 0, got[0], got[1])
        second = jnp.where(z // lay.ny == 0, got[1], got[0])
        return jnp.concatenate([first, second], axis=0)[None]

    info = jnp.concatenate([clip_ids[0], clip_patches[0], clip_step[0]])[None]
    by_core = jnp.concatenate([info, lax.ppermute(info, AXES, lay.swap(kc=1))], axis=0)
    info = [by_core] + [
        lax.ppermute(by_core, AXES, lay.swap(ky=ky)) for ky in range(1, lay.ny)
    ]
    group_y, group_c, _ = lay.unit(c, z)
    info = sum(
        jnp.where((y ^ ky == group_y) & (c ^ kc == group_c), info[ky][kc], 0)
        for ky in range(lay.ny)
        for kc in range(nc)
    )
    pos = jnp.stack([y, c, z, x]).astype(jnp.int32)
    pair_shape = (1, 2, half, model)
    outputs = call(
        functools.partial(start_kernel, lay, cols),
        "start",
        2 * model * 1000,
        [whole_spec(frames_x.shape)] * 2 + [whole_spec(w_qkv.shape)],
        [whole_spec(pair_shape)] * nc + [whole_spec((rows, 3 * cols))] * nx,
        [struct(pair_shape)] * nc + [struct((rows, 3 * cols))] * nx,
        prefetch=1,
    )(pos, frames_x, grad_y, w_qkv)
    pairs, picked = outputs[:nc], outputs[nc:]
    own = [lax.ppermute(pair, AXES, lay.to_plane(k)) for k, pair in enumerate(pairs)]
    by_x = [picked[0]] + [
        lax.ppermute(picked[kx], AXES, lay.swap(kx=kx)) for kx in range(1, nx)
    ]
    if nx == 2:
        ordered = [jnp.where(x == i, by_x[0], by_x[1]) for i in range(nx)]
    else:
        stacked = jnp.stack(by_x)
        ordered = [lax.dynamic_index_in_dim(stacked, x ^ i, 0, keepdims=False) for i in range(nx)]
    w_own = jnp.concatenate(ordered, axis=1 if rows % 16 == 0 else 0)
    own[0], _ = lax.optimization_barrier((own[0], w_own))
    w_pieces = {0: w_own}
    for bit in lay.bits(lay.nz):
        w_pieces[bit] = lax.ppermute(w_own, AXES, lay.swap(kz=bit))
    for k in range(1, lay.nz):
        if k not in w_pieces:
            bit = k & -k
            w_pieces[k] = lax.ppermute(w_pieces[k ^ bit], AXES, lay.swap(kz=bit))
    w_pieces = [w_pieces[k] for k in range(lay.nz)]
    if halves > 1:
        w_pieces += [lax.ppermute(piece, AXES, lay.swap(kc=1)) for piece in w_pieces[:-1]]

    late_w_out, _ = lax.optimization_barrier((w_out, own))
    wo_own = lax.ppermute(late_w_out, AXES, lay.rows_to_chip())

    pairs = []
    for j in range(nc):
        pairs += doubling(own[j], lay.chip_bits(j), chip_swap, info)
    pairs, _ = lax.optimization_barrier((pairs, w_pieces[lay.nz :]))


    def spread(count, width, patches_at_once):
        return pl.BlockSpec((count, patches_at_once, width), lambda i, *_: (0, i, 0))

    def pair_spec(count, patches_at_once):
        return pl.BlockSpec((count, 2, patches_at_once, model), lambda i, *_: (0, 0, i, 0))

    few = max(BLOCK, step_patches // 2)
    few_steps = half // few
    x_spec = pl.BlockSpec((few, model), lambda i, *_: (i, 0))
    triple_spec = pl.BlockSpec((halves, lay.frames, step_patches, cols), lambda i, *_: (0, 0, i, 0))
    w_specs = [whole_spec(w_own.shape)] * (halves * lay.nz)
    w_scratch = pltpu.VMEM((halves, model, 3 * cols), BF16)
    mod_spec = whole_spec(mod_table.shape)
    triple_shape = struct((halves, lay.frames, half, cols))
    part_specs = [spread(nc, model, step_patches)] * chips
    part_shapes = [struct((nc, half, model), F32)] + [struct((nc, half, model))] * (chips - 1)

    hidden, grad_proj = call(
        functools.partial(prepare_kernel, lay),
        "prepare",
        3 * model * 1000,
        [pair_spec(chips // 2, few)] * (2 * nc) + [mod_spec],
        [spread(lay.frames, model, few)] * 2,
        [struct((lay.frames, half, model))] * 2,
        grid=(few_steps,),
    )(pos, info, *pairs, mod_table)
    wo_own, w_last, _ = lax.optimization_barrier((wo_own, w_pieces[lay.nz - 1], hidden))
    wo_rows = [wo_own, lax.ppermute(wo_own, AXES, lay.swap(kc=1))]
    w_pieces[lay.nz - 1] = w_last
    if halves > 1:
        w_pieces.append(lax.ppermute(w_last, AXES, lay.swap(kc=1)))

    fold = 3 if rows % 24 == 0 else 1
    piece_shape = (groups, rows // fold, quarter * fold)
    queries, keys, values, grad_attn, kept, sent, *projected = call(
        functools.partial(forward_kernel, lay),
        "forward",
        14 * model * 1000,
        [spread(lay.frames, model, step_patches)] * 2
        + w_specs
        + [whole_spec(w_out.shape)] * nc,
        [triple_spec] * 4 + [whole_spec(piece_shape)] * 2 + part_specs,
        [triple_shape] * 4 + [struct(piece_shape, F32)] * 2 + part_shapes,
        [
            w_scratch,
            pltpu.VMEM((lay.frames, step_patches, chip_width), BF16),
            pltpu.VMEM((chip_width, model), BF16),
            pltpu.VMEM((chip_width, model), F32),
            pltpu.VMEM(piece_shape, F32),
        ],
        (steps,),
    )(pos, info, hidden, grad_proj, *w_pieces, *wo_rows)
    got = lax.ppermute(sent, AXES, lay.swap(kc=1))
    projected = over_chips(projected)

    middle = groups // 2
    cut, away = kept[:middle] + got[:middle], kept[middle:] + got[middle:]
    grad_attn, cut, away = lax.optimization_barrier((grad_attn, cut, away))
    first_away = lax.ppermute(away, AXES, lay.swap(kz=1))

    sums = call(
        functools.partial(backward_kernel, lay),
        "backward",
        10 * model * 1000,
        w_specs + [triple_spec] * 4,
        part_specs,
        part_shapes,
        [w_scratch, pltpu.VMEM((halves, lay.frames, step_patches, 3 * cols), BF16)],
        (steps,),
    )(pos, info, *w_pieces, queries, keys, values, grad_attn)
    sums, first_away, projected = lax.optimization_barrier((sums, first_away, projected))
    grad_hidden = over_chips(sums)

    projected, _ = lax.optimization_barrier((projected, grad_hidden[1]))
    out_parts = call(
        functools.partial(output_kernel, lay),
        "output",
        3 * model * 1000,
        [pair_spec(1, few)] * nc + [spread(nc, model, few)] * chips + [mod_spec],
        [x_spec] * nc,
        [struct((half, model))] * nc,
        grid=(few_steps,),
    )(pos, info, *own, *projected, mod_table)

    cut = cut + first_away
    for bit in lay.bits(lay.nz)[1:]:
        middle = middle // 2
        away = lax.ppermute(cut[middle:], AXES, lay.swap(kz=bit))
        away, _ = lax.optimization_barrier((away, out_parts))
        cut = cut[:middle] + away
    out_y = from_plane(out_parts)


    grad_parts = call(
        functools.partial(input_grad_kernel, lay),
        "input_grad",
        3 * model * 1000,
        [pair_spec(1, few)] * nc + [spread(nc, model, few)] * chips + [mod_spec],
        [x_spec] * nc,
        [struct((half, model))] * nc,
        grid=(few_steps,),
    )(pos, info, *own, *grad_hidden, mod_table)
    grad_x = from_plane(grad_parts)

    cut, _ = lax.optimization_barrier((cut, grad_parts))
    grad_w = lax.ppermute(cut[0], AXES, lay.to_owner())
    grad_w = jnp.concatenate(
        [grad_w[:, m * quarter : (m + 1) * quarter] for m in range(fold)], axis=0
    )
    grad_w_out = grad_w * jnp.float32(1.0 / math.sqrt(groups * lay.frames * patches))
    return out_y, grad_x, grad_w_out


def solution(mesh):
    lay = Layout(mesh)
    grid = Mesh(mesh.devices.reshape(lay.ny, lay.nc, lay.nz, lay.nx), AXES)
    rows, cols = ("z", "x"), ("y", "c")
    frame = P(AXES, None, None)
    group = P(cols, None)
    return jax.shard_map(
        functools.partial(local, lay),
        mesh=grid,
        in_specs=(frame, frame, group, group, group, P(), P(rows, None), P(rows, None)),
        out_specs=(frame, frame, P(rows, cols)),
        check_vma=False,
    )
```

```python
import functools
import math

import jax
import jax.numpy as jnp
from jax import lax
from jax.experimental import pallas as pl
from jax.experimental.pallas import tpu as pltpu
from jax.sharding import Mesh, PartitionSpec as P

HEADS = 16
CORES = 2
AXES = ("y", "c", "z", "x")
BLOCK = 16
VMEM_LIMIT = 56 * 1024 * 1024
BF16 = jnp.bfloat16
F32 = jnp.float32


def dot(left, right):
    return jnp.dot(left, right, preferred_element_type=F32)


def dot_t(left, right):
    return lax.dot_general(left, right, (((1,), (1,)), ((), ())), preferred_element_type=F32)


def t_dot(left, right):
    return lax.dot_general(left, right, (((0,), (0,)), ((), ())), preferred_element_type=F32)


def normalize(values):
    centred = values - jnp.mean(values, axis=-1, keepdims=True)
    inv_sigma = lax.rsqrt(jnp.mean(centred * centred, axis=-1, keepdims=True) + 1e-06)
    return centred * inv_sigma, inv_sigma


class Layout:
    def __init__(self, mesh):
        groups, seq = mesh.shape["dp"], mesh.shape["seq"]
        self.nc = CORES
        self.ny = groups // CORES
        self.nz = groups
        self.nx = seq // self.nz
        self.chips = self.ny * self.nx
        self.frames = seq
        self.chip_heads = HEADS // self.chips
        self.halves = 2 if self.chip_heads % 2 == 0 else 1
        self.half_heads = self.chip_heads // self.halves

    def linear(self, y, c, z, x):
        return ((y * self.nc + c) * self.nz + z) * self.nx + x

    def perm(self, move):
        pairs = []
        for y in range(self.ny):
            for c in range(self.nc):
                for z in range(self.nz):
                    for x in range(self.nx):
                        pairs.append((self.linear(y, c, z, x), self.linear(*move(y, c, z, x))))
        return pairs

    def to_plane(self, k):
        def move(y, c, z, x):
            half = (z // self.ny) ^ k
            plane = ((y // self.nc) * self.nc + c) * self.nc + half
            return (z % self.ny) ^ c, y % self.nc, plane, x

        return self.perm(move)

    def unit(self, c, z):
        return (z // (self.nc * self.nc)) * self.nc + c, (z // self.nc) % self.nc, z % self.nc

    def from_plane(self, k):
        return [(target, source) for source, target in self.to_plane(k)]

    def swap(self, ky=0, kc=0, kz=0, kx=0):
        return self.perm(lambda y, c, z, x: (y ^ ky, c ^ kc, z ^ kz, x ^ kx))

    def row_block(self, y, x, i):
        if self.halves > 1:
            return (i * self.ny + y) * self.nx + x
        return self.nc * (y * self.nx + x) + i

    def rows_to_chip(self):
        reader = {
            self.row_block(y, x, i): (y, x, i)
            for y in range(self.ny)
            for x in range(self.nx)
            for i in range(self.nc)
        }

        def move(y, c, z, x):
            chip_y, chip_x, i = reader[z * self.nx + x]
            return chip_y, i, c * self.ny + (y ^ (z & 1)), chip_x

        return self.perm(move)

    def to_owner(self):
        def move(y, c, z, x):
            s = self.row_block(y, x, c)
            return z // self.nc, z % self.nc, s // self.nx, s % self.nx

        return self.perm(move)

    def chip_of(self, k):
        return k // self.nx, k % self.nx

    def bits(self, count):
        return [1 << b for b in range(count.bit_length() - 1)]

    def chip_bits(self, j):
        bits = self.bits(self.chips)
        return bits if j % 2 == 0 else bits[::-1]

    def doubled(self, bits):
        held = [0]
        for bit in bits:
            held = held + [k ^ bit for k in held]
        return held

    def slots(self):
        return [(k, j) for k in range(self.chips) for j in range(self.nc)]


def slot_scalars(lay, pos_ref, info_ref, slot):
    k, j = slot
    ky, kx = lay.chip_of(k)
    _, group_c, half = lay.unit(pos_ref[1], pos_ref[2])
    z_frame = (half ^ j) * lay.ny + (pos_ref[0] ^ ky ^ group_c)
    frame = z_frame * lay.nx + (pos_ref[3] ^ kx)
    clip = info_ref[frame]
    clips = (info_ref.shape[0] - lay.frames) // 2
    return clip, info_ref[lay.frames + clip], info_ref[lay.frames + clips + clip]


def table_row(mod_ref, step, part, width):
    return mod_ref[pl.ds(step, 1), part * width : (part + 1) * width]


def allowed_pairs(lay, pos_ref, info_ref, patch_base):
    rows = lay.frames * BLOCK
    row_slot = lax.broadcasted_iota(jnp.int32, (rows, 1), 0) // BLOCK
    col_slot = lax.broadcasted_iota(jnp.int32, (1, rows), 1) // BLOCK
    row_clip = jnp.zeros((rows, 1), jnp.int32)
    row_limit = jnp.zeros((rows, 1), jnp.int32)
    col_clip = jnp.zeros((1, rows), jnp.int32)
    for t, slot in enumerate(lay.slots()):
        clip, limit, _ = slot_scalars(lay, pos_ref, info_ref, slot)
        row_clip = jnp.where(row_slot == t, clip, row_clip)
        row_limit = jnp.where(row_slot == t, limit, row_limit)
        col_clip = jnp.where(col_slot == t, clip, col_clip)
    row_patch = lax.broadcasted_iota(jnp.int32, (rows, 1), 0) % BLOCK
    col_patch = lax.broadcasted_iota(jnp.int32, (1, rows), 1) % BLOCK
    row_key = row_clip * BLOCK + row_patch
    col_key = col_clip * BLOCK + col_patch
    row_valid = (patch_base + row_patch < row_limit).astype(jnp.int32)
    row_index = lax.broadcasted_iota(jnp.int32, (rows, rows), 0)
    col_index = lax.broadcasted_iota(jnp.int32, (rows, rows), 1)
    return (row_key == col_key) & ((row_valid > 0) | (row_index == col_index))


def head_mask(values, head, head_size):
    lane = lax.broadcasted_iota(jnp.int32, (1, values.shape[1]), 1)
    inside = (lane >= head * head_size) & (lane < (head + 1) * head_size)
    return jnp.where(inside, values, jnp.zeros_like(values))


def patch_blocks(array, block):
    part = array[:, block * BLOCK : (block + 1) * BLOCK, :]
    return part.reshape(part.shape[0] * BLOCK, part.shape[2])


def start_kernel(lay, cols, pos_ref, x_ref, g_ref, w_ref, *refs):
    pair_refs, out_refs = refs[: lay.nc], refs[lay.nc :]
    half = x_ref.shape[1] // lay.nc
    for k, ref in enumerate(pair_refs):
        first = pl.multiple_of(((pos_ref[2] // lay.ny) ^ k) * half, 16)
        ref[0, 0] = x_ref[0, pl.ds(first, half), :]
        ref[0, 1] = g_ref[0, pl.ds(first, half), :]
    model = w_ref.shape[1] // 3
    for k, out_ref in enumerate(out_refs):
        chip_x = pos_ref[3] ^ k
        if lay.halves > 1:
            want = lay.row_block(pos_ref[0], chip_x, pos_ref[1])
        else:
            want = pos_ref[0] * lay.nx + chip_x
        for v in range(lay.chips * lay.halves):

            @pl.when(want == v)
            def _(v=v, out_ref=out_ref):
                parts = [
                    w_ref[:, p * model + v * cols : p * model + (v + 1) * cols]
                    for p in range(3)
                ]
                out_ref[...] = jnp.concatenate(parts, axis=1)


def fill_weights(lay, pos_ref, w_refs, w_scr):
    order = lay.doubled(lay.bits(lay.nz)[::-1])
    block = w_scr.shape[1] // lay.nz
    rows, width = w_refs[0].shape[1], w_scr.shape[2]
    for h in range(lay.halves):
        for n, k in enumerate(order):
            ref, place = w_refs[2 * h + (2 * n) // lay.nz], n % (lay.nz // 2)
            for m in range(block // rows):
                start = pl.multiple_of((pos_ref[2] ^ k) * block + m * rows, 16)
                w_scr[h, pl.ds(start, rows), :] = ref[place, :, m * width : (m + 1) * width]


def heads_stacked(lay, values):
    head_size = values.shape[1] // lay.half_heads
    parts = [head_mask(values, head, head_size) for head in range(lay.half_heads)]
    return jnp.concatenate(parts, axis=0) if len(parts) > 1 else parts[0]


def beside(lay, weights):
    return jnp.concatenate([weights[head] for head in range(lay.half_heads)], axis=1)


def attention_weights(lay, keys_stacked, queries, allowed, scaling):
    scores = dot_t(keys_stacked, queries) * scaling
    scores = jnp.where(allowed, scores.reshape((lay.half_heads,) + allowed.shape), -jnp.inf)
    exponent = jnp.exp(scores - jnp.max(scores, axis=1, keepdims=True))
    return exponent * (1.0 / jnp.sum(exponent, axis=1, keepdims=True))


def prepare_kernel(lay, pos_ref, info_ref, *refs):
    pair_refs, (mod_ref, hid_ref, gp_ref) = refs[: 2 * lay.nc], refs[2 * lay.nc :]
    _, step_patches, model = hid_ref.shape
    patches = step_patches * pl.num_programs(0)
    patch_base = lay.unit(pos_ref[1], pos_ref[2])[2] * patches + pl.program_id(0) * step_patches
    patch = patch_base + lax.broadcasted_iota(jnp.int32, (step_patches, 1), 0)
    for t, (k, j) in enumerate(lay.slots()):
        _, limit, step = slot_scalars(lay, pos_ref, info_ref, (k, j))
        n = lay.doubled(lay.chip_bits(j)).index(k)
        ref, place = pair_refs[2 * j + (2 * n) // lay.chips], n % (lay.chips // 2)
        normed, _ = normalize(ref[place, 0].astype(F32))
        shift, scale = table_row(mod_ref, step, 0, model), table_row(mod_ref, step, 1, model)
        hid_ref[t] = (normed * (1.0 + scale) + shift).astype(BF16)
        factor = jnp.where(patch < limit, table_row(mod_ref, step, 2, model), 0.0)
        gp_ref[t] = (factor * ref[place, 1].astype(F32)).astype(BF16)


def forward_kernel(lay, pos_ref, info_ref, hid_ref, gp_ref, *refs):
    w_refs, refs = refs[: 2 * lay.halves], refs[2 * lay.halves :]
    wo_refs, refs = refs[: lay.nc], refs[lay.nc :]
    q_ref, k_ref, v_ref, ga_ref, kept_ref, sent_ref, *refs = refs
    pr_refs, (w_scr, att_scr, wo_scr, acc_scr, cut_scr) = refs[: lay.chips], refs[lay.chips :]
    _, step_patches, model = hid_ref.shape
    tokens = lay.frames * step_patches
    cols = w_scr.shape[2] // 3
    scaling = 1.0 / math.sqrt(cols // lay.half_heads)
    patches = step_patches * pl.num_programs(0)
    is_first = pos_ref[1] == 0

    @pl.when(pl.program_id(0) == 0)
    def _():
        fill_weights(lay, pos_ref, w_refs, w_scr)
        own, other = wo_refs[0][...].astype(F32), wo_refs[1][...].astype(F32)
        both = [jnp.where(is_first, own, other), jnp.where(is_first, other, own)]
        wo_scr[...] = jnp.concatenate(both, axis=0).astype(BF16)
        acc_scr[...] = jnp.zeros_like(acc_scr)

    hidden = hid_ref[...].reshape(lay.frames * step_patches, model)
    for h in range(lay.halves):
        triple = dot(hidden, w_scr[h])
        for n, ref in enumerate((q_ref, k_ref, v_ref)):
            ref[h] = triple[:, n * cols : (n + 1) * cols].astype(BF16).reshape(ref.shape[1:])

    for b in range(step_patches // BLOCK):
        patch_base = lay.unit(pos_ref[1], pos_ref[2])[2] * patches + pl.program_id(0) * step_patches + b * BLOCK
        allowed = allowed_pairs(lay, pos_ref, info_ref, patch_base)
        outputs = []
        for h in range(lay.halves):
            queries, keys, values = (patch_blocks(ref[h], b) for ref in (q_ref, k_ref, v_ref))
            weights = attention_weights(lay, heads_stacked(lay, keys), queries, allowed, scaling)
            weights = weights.astype(BF16).reshape(-1, allowed.shape[1])
            outputs.append(t_dot(weights, heads_stacked(lay, values)))
        if lay.halves > 1:
            first = jnp.where(pos_ref[1] == 0, outputs[0], outputs[1])
            second = jnp.where(pos_ref[1] == 0, outputs[1], outputs[0])
            outputs = [jnp.concatenate([first, second], axis=1)]
        attended = outputs[0].astype(BF16)
        att_scr[:, b * BLOCK : (b + 1) * BLOCK, :] = attended.reshape(lay.frames, BLOCK, -1)

    attended = att_scr[...].reshape(tokens, -1)
    grad_proj = gp_ref[...].reshape(tokens, model)
    acc_scr[...] += t_dot(attended, grad_proj)
    grad_attn = dot_t(grad_proj, wo_scr[...])
    part = wo_scr.shape[0] // lay.halves
    for h in range(lay.halves):
        ga_ref[h] = grad_attn[:, h * part : (h + 1) * part].astype(BF16).reshape(ga_ref.shape[1:])
    projected = dot(attended, wo_scr[...]).reshape(lay.chips, lay.nc, step_patches, model)
    for k in range(lay.chips):
        pr_refs[k][...] = projected[k].astype(pr_refs[k].dtype)

    @pl.when(pl.program_id(0) == pl.num_programs(0) - 1)
    def _():
        groups, chunk_rows, chunk_width = kept_ref.shape
        block_rows, part = acc_scr.shape[0] // lay.nc, model // groups
        order = lay.doubled(lay.bits(lay.nz)[::-1])
        first, second = acc_scr[:block_rows, :], acc_scr[block_rows:, :]
        kept = jnp.where(is_first, first, second)
        sent = jnp.where(is_first, second, first)
        for ref, rows in ((kept_ref, kept), (sent_ref, sent)):
            for d in range(groups):
                chunk = [
                    rows[m * chunk_rows : (m + 1) * chunk_rows, d * part : (d + 1) * part]
                    for m in range(chunk_width // part)
                ]
                cut_scr[d] = jnp.concatenate(chunk, axis=1) if len(chunk) > 1 else chunk[0]
            for n, k in enumerate(order):
                ref[n] = cut_scr[pos_ref[2] ^ k]


def backward_kernel(lay, pos_ref, info_ref, *refs):
    w_refs, refs = refs[: 2 * lay.halves], refs[2 * lay.halves :]
    q_ref, k_ref, v_ref, ga_ref, *refs = refs
    gh_refs, (w_scr, gt_scr) = refs[: lay.chips], refs[lay.chips :]
    _, frames, step_patches, cols = q_ref.shape
    model = w_scr.shape[1]
    patches = step_patches * pl.num_programs(0)
    scaling = 1.0 / math.sqrt(cols // lay.half_heads)

    @pl.when(pl.program_id(0) == 0)
    def _():
        fill_weights(lay, pos_ref, w_refs, w_scr)

    for b in range(step_patches // BLOCK):
        patch_base = lay.unit(pos_ref[1], pos_ref[2])[2] * patches + pl.program_id(0) * step_patches + b * BLOCK
        allowed = allowed_pairs(lay, pos_ref, info_ref, patch_base)
        for h in range(lay.halves):
            queries, keys, values = (patch_blocks(ref[h], b) for ref in (q_ref, k_ref, v_ref))
            grad_out = patch_blocks(ga_ref[(pos_ref[1] ^ h) if lay.halves > 1 else 0], b)
            keys = heads_stacked(lay, keys)
            weights = attention_weights(lay, keys, queries, allowed, scaling)
            grad_weights = dot_t(heads_stacked(lay, values), grad_out).reshape(weights.shape)
            grad_values = dot(beside(lay, weights.astype(BF16)), heads_stacked(lay, grad_out))
            inner = jnp.sum(weights * grad_weights, axis=1, keepdims=True)
            grad_scores = (weights * (grad_weights - inner) * scaling).astype(BF16)
            grad_queries = t_dot(grad_scores.reshape(-1, grad_scores.shape[2]), keys)
            grad_keys = dot(beside(lay, grad_scores), heads_stacked(lay, queries))
            grads = jnp.concatenate([grad_queries, grad_keys, grad_values], axis=1).astype(BF16)
            gt_scr[h, :, b * BLOCK : (b + 1) * BLOCK, :] = grads.reshape(frames, BLOCK, 3 * cols)

    rows = lay.nc * step_patches
    for k in range(lay.chips):
        total = jnp.zeros((rows, model), F32)
        for h in range(lay.halves):
            part = gt_scr[h, k * lay.nc : (k + 1) * lay.nc].reshape(rows, 3 * cols)
            total = total + dot_t(part, w_scr[h])
        gh_refs[k][...] = total.reshape(gh_refs[k].shape).astype(gh_refs[k].dtype)


def output_kernel(lay, pos_ref, info_ref, *refs):
    pair_refs, refs = refs[: lay.nc], refs[lay.nc :]
    pr_refs, refs = refs[: lay.chips], refs[lay.chips :]
    gh_refs, refs = refs[: lay.chips], refs[lay.chips :]
    mod_ref, *out_refs = refs
    _, _, step_patches, model = out_refs[0].shape
    patches = step_patches * pl.num_programs(0)
    patch_base = lay.unit(pos_ref[1], pos_ref[2])[2] * patches + pl.program_id(0) * step_patches
    patch = patch_base + lax.broadcasted_iota(jnp.int32, (step_patches, 1), 0)
    for j in range(lay.nc):
        _, limit, step = slot_scalars(lay, pos_ref, info_ref, (0, j))
        values = pair_refs[j][0, 0].astype(F32)
        factor = jnp.where(patch < limit, table_row(mod_ref, step, 2, model), 0.0)
        projected, grad_hidden = pr_refs[0][j], gh_refs[0][j]
        for k in range(1, lay.chips):
            projected = projected + pr_refs[k][j].astype(F32)
            grad_hidden = grad_hidden + gh_refs[k][j].astype(F32)
        projected = projected.astype(BF16).astype(F32)
        out_refs[j][0, 0] = (values + factor * projected).astype(BF16)

        grad_hidden = grad_hidden.astype(BF16).astype(F32)
        normed, inv_sigma = normalize(values)
        grad_norm = grad_hidden * (1.0 + table_row(mod_ref, step, 1, model))
        first_mean = jnp.mean(grad_norm, axis=-1, keepdims=True)
        second_mean = jnp.mean(grad_norm * normed, axis=-1, keepdims=True)
        grad_x = pair_refs[j][0, 1].astype(F32) + inv_sigma * (
            grad_norm - first_mean - normed * second_mean
        )
        out_refs[j][0, 1] = grad_x.astype(BF16)


def whole_spec(shape):
    return pl.BlockSpec(shape, lambda *_: (0,) * len(shape))


def struct(shape, dtype=BF16):
    return jax.ShapeDtypeStruct(shape, dtype)


def local(lay, frames_x, grad_y, clip_ids, clip_patches, clip_step, mod_table, w_qkv, w_out):
    y, c, z, x = (lax.axis_index(name) for name in AXES)
    _, patches, model = frames_x.shape
    half = patches // lay.nc
    chips, nc, nx = lay.chips, lay.nc, lay.nx
    head_size = model // HEADS
    halves = lay.halves
    cols = lay.half_heads * head_size
    chip_width = lay.chip_heads * head_size
    rows = w_qkv.shape[0]
    groups = lay.nz
    quarter = model // groups
    step_patches = max(BLOCK, min(half, 512 // lay.frames))
    steps = half // step_patches
    tokens = lay.frames * step_patches

    def call(kernel, name, cost, in_specs, out_specs, out_shape, scratch=(), grid=(1,), prefetch=2):
        return pl.pallas_call(
            kernel,
            grid_spec=pltpu.PrefetchScalarGridSpec(
                num_scalar_prefetch=prefetch,
                grid=grid,
                in_specs=in_specs,
                out_specs=out_specs,
                scratch_shapes=list(scratch),
            ),
            out_shape=out_shape,
            compiler_params=pltpu.CompilerParams(vmem_limit_bytes=VMEM_LIMIT),
            cost_estimate=pl.CostEstimate(
                flops=cost * tokens * steps, bytes_accessed=4 * model * tokens, transcendentals=0
            ),
            name=name,
        )

    def chip_swap(k):
        ky, kx = lay.chip_of(k)
        return lay.swap(ky=ky, kx=kx)

    def doubling(held, bits, swap, after):
        for bit in bits[:-1]:
            held = jnp.concatenate([held, lax.ppermute(held, AXES, swap(bit))], axis=0)
        held, _ = lax.optimization_barrier((held, after))
        return [held, lax.ppermute(held, AXES, swap(bits[-1]))]

    def over_chips(parts):
        got = [lax.ppermute(parts[k], AXES, chip_swap(k)) for k in range(1, chips)]
        return [parts[0]] + got

    info = jnp.concatenate([clip_ids[0], clip_patches[0], clip_step[0]])[None]
    by_core = jnp.concatenate([info, lax.ppermute(info, AXES, lay.swap(kc=1))], axis=0)
    info = [by_core] + [
        lax.ppermute(by_core, AXES, lay.swap(ky=ky)) for ky in range(1, lay.ny)
    ]
    group_y, group_c, _ = lay.unit(c, z)
    info = sum(
        jnp.where((y ^ ky == group_y) & (c ^ kc == group_c), info[ky][kc], 0)
        for ky in range(lay.ny)
        for kc in range(nc)
    )
    pos = jnp.stack([y, c, z, x]).astype(jnp.int32)
    pair_shape = (1, 2, half, model)
    outputs = call(
        functools.partial(start_kernel, lay, cols),
        "start",
        2 * model * 1000,
        [whole_spec(frames_x.shape)] * 2 + [whole_spec(w_qkv.shape)],
        [whole_spec(pair_shape)] * nc + [whole_spec((rows, 3 * cols))] * nx,
        [struct(pair_shape)] * nc + [struct((rows, 3 * cols))] * nx,
        prefetch=1,
    )(pos, frames_x, grad_y, w_qkv)
    pairs, picked = outputs[:nc], outputs[nc:]
    own = [lax.ppermute(pair, AXES, lay.to_plane(k)) for k, pair in enumerate(pairs)]
    by_x = [picked[0]] + [
        lax.ppermute(picked[kx], AXES, lay.swap(kx=kx)) for kx in range(1, nx)
    ]
    if nx == 2:
        ordered = [jnp.where(x == i, by_x[0], by_x[1]) for i in range(nx)]
    else:
        stacked = jnp.stack(by_x)
        ordered = [lax.dynamic_index_in_dim(stacked, x ^ i, 0, keepdims=False) for i in range(nx)]
    w_own = jnp.concatenate(ordered, axis=1 if rows % 16 == 0 else 0)[None]
    own[0], _ = lax.optimization_barrier((own[0], w_own))
    w_pieces = doubling(w_own, lay.bits(lay.nz)[::-1], lambda kz: lay.swap(kz=kz), [])
    if halves > 1:
        w_pieces += [lax.ppermute(piece, AXES, lay.swap(kc=1)) for piece in w_pieces]

    late_w_out, _ = lax.optimization_barrier((w_out, own))
    wo_own = lax.ppermute(late_w_out, AXES, lay.rows_to_chip())

    pairs = []
    for j in range(nc):
        pairs += doubling(own[j], lay.chip_bits(j), chip_swap, [info, w_pieces[0]])
    pairs, _ = lax.optimization_barrier((pairs, w_pieces[2:]))


    def spread(count, width, patches_at_once):
        return pl.BlockSpec((count, patches_at_once, width), lambda i, *_: (0, i, 0))

    def pair_spec(count, patches_at_once):
        return pl.BlockSpec((count, 2, patches_at_once, model), lambda i, *_: (0, 0, i, 0))

    few = max(BLOCK, step_patches // 2)
    few_steps = half // few
    x_spec = pl.BlockSpec((few, model), lambda i, *_: (i, 0))
    triple_spec = pl.BlockSpec((halves, lay.frames, step_patches, cols), lambda i, *_: (0, 0, i, 0))
    w_specs = [whole_spec(piece.shape) for piece in w_pieces]
    w_scratch = pltpu.VMEM((halves, model, 3 * cols), BF16)
    mod_spec = whole_spec(mod_table.shape)
    triple_shape = struct((halves, lay.frames, half, cols))
    part_specs = [spread(nc, model, step_patches)] * chips
    part_shapes = [struct((nc, half, model), F32)] + [struct((nc, half, model))] * (chips - 1)

    hidden, grad_proj = call(
        functools.partial(prepare_kernel, lay),
        "prepare",
        3 * model * 1000,
        [pair_spec(chips // 2, few)] * (2 * nc) + [mod_spec],
        [spread(lay.frames, model, few)] * 2,
        [struct((lay.frames, half, model))] * 2,
        grid=(few_steps,),
    )(pos, info, *pairs, mod_table)
    wo_own, _ = lax.optimization_barrier((wo_own, hidden))
    wo_rows = [wo_own, lax.ppermute(wo_own, AXES, lay.swap(kc=1))]

    fold = 3 if rows % 24 == 0 else 1
    piece_shape = (groups, rows // fold, quarter * fold)
    queries, keys, values, grad_attn, kept, sent, *projected = call(
        functools.partial(forward_kernel, lay),
        "forward",
        14 * model * 1000,
        [spread(lay.frames, model, step_patches)] * 2
        + w_specs
        + [whole_spec(w_out.shape)] * nc,
        [triple_spec] * 4 + [whole_spec(piece_shape)] * 2 + part_specs,
        [triple_shape] * 4 + [struct(piece_shape, F32)] * 2 + part_shapes,
        [
            w_scratch,
            pltpu.VMEM((lay.frames, step_patches, chip_width), BF16),
            pltpu.VMEM((chip_width, model), BF16),
            pltpu.VMEM((chip_width, model), F32),
            pltpu.VMEM(piece_shape, F32),
        ],
        (steps,),
    )(pos, info, hidden, grad_proj, *w_pieces, *wo_rows)
    got = lax.ppermute(sent, AXES, lay.swap(kc=1))
    projected = over_chips(projected)

    middle = groups // 2
    cut, away = kept[:middle] + got[:middle], kept[middle:] + got[middle:]
    grad_attn, cut, away = lax.optimization_barrier((grad_attn, cut, away))
    first_away = lax.ppermute(away, AXES, lay.swap(kz=1))

    sums = call(
        functools.partial(backward_kernel, lay),
        "backward",
        10 * model * 1000,
        w_specs + [triple_spec] * 4,
        part_specs,
        part_shapes,
        [w_scratch, pltpu.VMEM((halves, lay.frames, step_patches, 3 * cols), BF16)],
        (steps,),
    )(pos, info, *w_pieces, queries, keys, values, grad_attn)
    sums, first_away, projected = lax.optimization_barrier((sums, first_away, projected))
    grad_hidden = over_chips(sums)

    parts = call(
        functools.partial(output_kernel, lay),
        "output",
        3 * model * 1000,
        [pair_spec(1, few)] * nc + [spread(nc, model, few)] * (2 * chips) + [mod_spec],
        [pair_spec(1, few)] * nc,
        [struct(pair_shape)] * nc,
        grid=(few_steps,),
    )(pos, info, *own, *projected, *grad_hidden, mod_table)
    got = [lax.ppermute(part, AXES, lay.from_plane(k)) for k, part in enumerate(parts)]
    is_first = z // lay.ny == 0
    out_y, grad_x = (
        jnp.concatenate(
            [
                jnp.where(is_first, got[0][:, n], got[1][:, n]),
                jnp.where(is_first, got[1][:, n], got[0][:, n]),
            ],
            axis=1,
        )
        for n in range(2)
    )

    cut = cut + first_away
    for bit in lay.bits(lay.nz)[1:]:
        middle = middle // 2
        cut = cut[:middle] + lax.ppermute(cut[middle:], AXES, lay.swap(kz=bit))
    grad_w = lax.ppermute(cut[0], AXES, lay.to_owner())
    grad_w = jnp.concatenate(
        [grad_w[:, m * quarter : (m + 1) * quarter] for m in range(fold)], axis=0
    )
    grad_w_out = grad_w * jnp.float32(1.0 / math.sqrt(groups * lay.frames * patches))
    return out_y, grad_x, grad_w_out


def solution(mesh):
    lay = Layout(mesh)
    grid = Mesh(mesh.devices.reshape(lay.ny, lay.nc, lay.nz, lay.nx), AXES)
    rows, cols = ("z", "x"), ("y", "c")
    frame = P(AXES, None, None)
    group = P(cols, None)
    return jax.shard_map(
        functools.partial(local, lay),
        mesh=grid,
        in_specs=(frame, frame, group, group, group, P(), P(rows, None), P(rows, None)),
        out_specs=(frame, frame, P(rows, cols)),
        check_vma=False,
    )
```

```python
import functools
import math

import jax
import jax.numpy as jnp
from jax import lax
from jax.experimental import pallas as pl
from jax.experimental.pallas import tpu as pltpu
from jax.sharding import Mesh, PartitionSpec as P

HEADS = 16
CORES = 2
AXES = ("y", "c", "z", "x")
BLOCK = 16
VMEM_LIMIT = 56 * 1024 * 1024
BF16 = jnp.bfloat16
F32 = jnp.float32


def dot(left, right):
    return jnp.dot(left, right, preferred_element_type=F32)


def dot_t(left, right):
    return lax.dot_general(left, right, (((1,), (1,)), ((), ())), preferred_element_type=F32)


def t_dot(left, right):
    return lax.dot_general(left, right, (((0,), (0,)), ((), ())), preferred_element_type=F32)


def normalize(values):
    centred = values - jnp.mean(values, axis=-1, keepdims=True)
    inv_sigma = lax.rsqrt(jnp.mean(centred * centred, axis=-1, keepdims=True) + 1e-06)
    return centred * inv_sigma, inv_sigma


class Layout:
    def __init__(self, mesh):
        groups, seq = mesh.shape["dp"], mesh.shape["seq"]
        self.nc = CORES
        self.ny = groups // CORES
        self.nz = groups
        self.nx = seq // self.nz
        self.chips = self.ny * self.nx
        self.frames = seq
        self.chip_heads = HEADS // self.chips
        self.halves = 2 if self.chip_heads % 2 == 0 else 1
        self.half_heads = self.chip_heads // self.halves

    def linear(self, y, c, z, x):
        return ((y * self.nc + c) * self.nz + z) * self.nx + x

    def perm(self, move):
        pairs = []
        for y in range(self.ny):
            for c in range(self.nc):
                for z in range(self.nz):
                    for x in range(self.nx):
                        pairs.append((self.linear(y, c, z, x), self.linear(*move(y, c, z, x))))
        return pairs

    def to_plane(self, k):
        def move(y, c, z, x):
            half = (z // self.ny) ^ k
            plane = ((y // self.nc) * self.nc + c) * self.nc + half
            return (z % self.ny) ^ c, y % self.nc, plane, x

        return self.perm(move)

    def unit(self, c, z):
        return (z // (self.nc * self.nc)) * self.nc + c, (z // self.nc) % self.nc, z % self.nc

    def from_plane(self, k):
        return [(target, source) for source, target in self.to_plane(k)]

    def swap(self, ky=0, kc=0, kz=0, kx=0):
        return self.perm(lambda y, c, z, x: (y ^ ky, c ^ kc, z ^ kz, x ^ kx))

    def row_block(self, y, x, i):
        if self.halves > 1:
            return (i * self.ny + y) * self.nx + x
        return self.nc * (y * self.nx + x) + i

    def rows_to_chip(self):
        reader = {
            self.row_block(y, x, i): (y, x, i)
            for y in range(self.ny)
            for x in range(self.nx)
            for i in range(self.nc)
        }

        def move(y, c, z, x):
            chip_y, chip_x, i = reader[z * self.nx + x]
            return chip_y, i, c * self.ny + (y ^ (z & 1)), chip_x

        return self.perm(move)

    def to_owner(self):
        def move(y, c, z, x):
            s = self.row_block(y, x, c)
            return z // self.nc, z % self.nc, s // self.nx, s % self.nx

        return self.perm(move)

    def chip_of(self, k):
        return k // self.nx, k % self.nx

    def bits(self, count):
        return [1 << b for b in range(count.bit_length() - 1)]

    def chip_bits(self, j):
        bits = self.bits(self.chips)
        return bits if j % 2 == 0 else bits[::-1]

    def doubled(self, bits):
        held = [0]
        for bit in bits:
            held = held + [k ^ bit for k in held]
        return held

    def slots(self):
        return [(k, j) for k in range(self.chips) for j in range(self.nc)]


def slot_scalars(lay, pos_ref, info_ref, slot):
    k, j = slot
    ky, kx = lay.chip_of(k)
    _, group_c, half = lay.unit(pos_ref[1], pos_ref[2])
    z_frame = (half ^ j) * lay.ny + (pos_ref[0] ^ ky ^ group_c)
    frame = z_frame * lay.nx + (pos_ref[3] ^ kx)
    clip = info_ref[frame]
    clips = (info_ref.shape[0] - lay.frames) // 2
    return clip, info_ref[lay.frames + clip], info_ref[lay.frames + clips + clip]


def table_row(mod_ref, step, part, width):
    return mod_ref[pl.ds(step, 1), part * width : (part + 1) * width]


def allowed_pairs(lay, pos_ref, info_ref, patch_base):
    rows = lay.frames * BLOCK
    row_slot = lax.broadcasted_iota(jnp.int32, (rows, 1), 0) // BLOCK
    col_slot = lax.broadcasted_iota(jnp.int32, (1, rows), 1) // BLOCK
    row_clip = jnp.zeros((rows, 1), jnp.int32)
    row_limit = jnp.zeros((rows, 1), jnp.int32)
    col_clip = jnp.zeros((1, rows), jnp.int32)
    for t, slot in enumerate(lay.slots()):
        clip, limit, _ = slot_scalars(lay, pos_ref, info_ref, slot)
        row_clip = jnp.where(row_slot == t, clip, row_clip)
        row_limit = jnp.where(row_slot == t, limit, row_limit)
        col_clip = jnp.where(col_slot == t, clip, col_clip)
    row_patch = lax.broadcasted_iota(jnp.int32, (rows, 1), 0) % BLOCK
    col_patch = lax.broadcasted_iota(jnp.int32, (1, rows), 1) % BLOCK
    row_key = row_clip * BLOCK + row_patch
    col_key = col_clip * BLOCK + col_patch
    row_valid = (patch_base + row_patch < row_limit).astype(jnp.int32)
    row_index = lax.broadcasted_iota(jnp.int32, (rows, rows), 0)
    col_index = lax.broadcasted_iota(jnp.int32, (rows, rows), 1)
    return (row_key == col_key) & ((row_valid > 0) | (row_index == col_index))


def head_mask(values, head, head_size):
    lane = lax.broadcasted_iota(jnp.int32, (1, values.shape[1]), 1)
    inside = (lane >= head * head_size) & (lane < (head + 1) * head_size)
    return jnp.where(inside, values, jnp.zeros_like(values))


def patch_blocks(array, block):
    part = array[:, block * BLOCK : (block + 1) * BLOCK, :]
    return part.reshape(part.shape[0] * BLOCK, part.shape[2])


def start_kernel(lay, cols, pos_ref, x_ref, g_ref, w_ref, *refs):
    pair_refs, out_refs = refs[: lay.nc], refs[lay.nc :]
    half = x_ref.shape[1] // lay.nc
    for k, ref in enumerate(pair_refs):
        first = pl.multiple_of(((pos_ref[2] // lay.ny) ^ k) * half, 16)
        ref[0, 0] = x_ref[0, pl.ds(first, half), :]
        ref[0, 1] = g_ref[0, pl.ds(first, half), :]
    model = w_ref.shape[1] // 3
    for k, out_ref in enumerate(out_refs):
        chip_x = pos_ref[3] ^ k
        if lay.halves > 1:
            want = lay.row_block(pos_ref[0], chip_x, pos_ref[1])
        else:
            want = pos_ref[0] * lay.nx + chip_x
        for v in range(lay.chips * lay.halves):

            @pl.when(want == v)
            def _(v=v, out_ref=out_ref):
                parts = [
                    w_ref[:, p * model + v * cols : p * model + (v + 1) * cols]
                    for p in range(3)
                ]
                out_ref[...] = jnp.concatenate(parts, axis=1)


def fill_weights(lay, pos_ref, w_refs, w_scr):
    order = lay.doubled(lay.bits(lay.nz)[::-1])
    block = w_scr.shape[1] // lay.nz
    rows, width = w_refs[0].shape[1], w_scr.shape[2]
    for h in range(lay.halves):
        for n, k in enumerate(order):
            ref, place = w_refs[2 * h + (2 * n) // lay.nz], n % (lay.nz // 2)
            for m in range(block // rows):
                start = pl.multiple_of((pos_ref[2] ^ k) * block + m * rows, 16)
                w_scr[h, pl.ds(start, rows), :] = ref[place, :, m * width : (m + 1) * width]


def heads_stacked(lay, values):
    head_size = values.shape[1] // lay.half_heads
    parts = [head_mask(values, head, head_size) for head in range(lay.half_heads)]
    return jnp.concatenate(parts, axis=0) if len(parts) > 1 else parts[0]


def beside(lay, weights):
    return jnp.concatenate([weights[head] for head in range(lay.half_heads)], axis=1)


def attention_weights(lay, keys_stacked, queries, allowed, scaling):
    scores = dot_t(keys_stacked, queries) * scaling
    scores = jnp.where(allowed, scores.reshape((lay.half_heads,) + allowed.shape), -jnp.inf)
    exponent = jnp.exp(scores - jnp.max(scores, axis=1, keepdims=True))
    return exponent * (1.0 / jnp.sum(exponent, axis=1, keepdims=True))


def prepare_kernel(lay, pos_ref, info_ref, *refs):
    pair_refs, (mod_ref, hid_ref, gp_ref) = refs[: 2 * lay.nc], refs[2 * lay.nc :]
    _, step_patches, model = hid_ref.shape
    patches = step_patches * pl.num_programs(0)
    patch_base = lay.unit(pos_ref[1], pos_ref[2])[2] * patches + pl.program_id(0) * step_patches
    patch = patch_base + lax.broadcasted_iota(jnp.int32, (step_patches, 1), 0)
    for t, (k, j) in enumerate(lay.slots()):
        _, limit, step = slot_scalars(lay, pos_ref, info_ref, (k, j))
        n = lay.doubled(lay.chip_bits(j)).index(k)
        ref, place = pair_refs[2 * j + (2 * n) // lay.chips], n % (lay.chips // 2)
        normed, _ = normalize(ref[place, 0].astype(F32))
        shift, scale = table_row(mod_ref, step, 0, model), table_row(mod_ref, step, 1, model)
        hid_ref[t] = (normed * (1.0 + scale) + shift).astype(BF16)
        factor = jnp.where(patch < limit, table_row(mod_ref, step, 2, model), 0.0)
        gp_ref[t] = (factor * ref[place, 1].astype(F32)).astype(BF16)


def forward_kernel(lay, pos_ref, info_ref, hid_ref, gp_ref, *refs):
    w_refs, refs = refs[: 2 * lay.halves], refs[2 * lay.halves :]
    wo_refs, refs = refs[: lay.nc], refs[lay.nc :]
    q_ref, k_ref, v_ref, ga_ref, kept_ref, sent_ref, *refs = refs
    pr_refs, (w_scr, att_scr, wo_scr, acc_scr, cut_scr) = refs[: lay.chips], refs[lay.chips :]
    _, step_patches, model = hid_ref.shape
    tokens = lay.frames * step_patches
    cols = w_scr.shape[2] // 3
    scaling = 1.0 / math.sqrt(cols // lay.half_heads)
    patches = step_patches * pl.num_programs(0)
    is_first = pos_ref[1] == 0

    @pl.when(pl.program_id(0) == 0)
    def _():
        fill_weights(lay, pos_ref, w_refs, w_scr)
        own, other = wo_refs[0][...].astype(F32), wo_refs[1][...].astype(F32)
        both = [jnp.where(is_first, own, other), jnp.where(is_first, other, own)]
        wo_scr[...] = jnp.concatenate(both, axis=0).astype(BF16)
        acc_scr[...] = jnp.zeros_like(acc_scr)

    hidden = hid_ref[...].reshape(lay.frames * step_patches, model)
    for h in range(lay.halves):
        triple = dot(hidden, w_scr[h])
        for n, ref in enumerate((q_ref, k_ref, v_ref)):
            ref[h] = triple[:, n * cols : (n + 1) * cols].astype(BF16).reshape(ref.shape[1:])

    for b in range(step_patches // BLOCK):
        patch_base = lay.unit(pos_ref[1], pos_ref[2])[2] * patches + pl.program_id(0) * step_patches + b * BLOCK
        allowed = allowed_pairs(lay, pos_ref, info_ref, patch_base)
        outputs = []
        for h in range(lay.halves):
            queries, keys, values = (patch_blocks(ref[h], b) for ref in (q_ref, k_ref, v_ref))
            weights = attention_weights(lay, heads_stacked(lay, keys), queries, allowed, scaling)
            weights = weights.astype(BF16).reshape(-1, allowed.shape[1])
            outputs.append(t_dot(weights, heads_stacked(lay, values)))
        if lay.halves > 1:
            first = jnp.where(pos_ref[1] == 0, outputs[0], outputs[1])
            second = jnp.where(pos_ref[1] == 0, outputs[1], outputs[0])
            outputs = [jnp.concatenate([first, second], axis=1)]
        attended = outputs[0].astype(BF16)
        att_scr[:, b * BLOCK : (b + 1) * BLOCK, :] = attended.reshape(lay.frames, BLOCK, -1)

    attended = att_scr[...].reshape(tokens, -1)
    grad_proj = gp_ref[...].reshape(tokens, model)
    acc_scr[...] += t_dot(attended, grad_proj)
    grad_attn = dot_t(grad_proj, wo_scr[...])
    part = wo_scr.shape[0] // lay.halves
    for h in range(lay.halves):
        ga_ref[h] = grad_attn[:, h * part : (h + 1) * part].astype(BF16).reshape(ga_ref.shape[1:])
    projected = dot(attended, wo_scr[...]).reshape(lay.chips, lay.nc, step_patches, model)
    for k in range(lay.chips):
        pr_refs[k][...] = projected[k].astype(pr_refs[k].dtype)

    @pl.when(pl.program_id(0) == pl.num_programs(0) - 1)
    def _():
        groups, chunk_rows, chunk_width = kept_ref.shape
        block_rows, part = acc_scr.shape[0] // lay.nc, model // groups
        order = lay.doubled(lay.bits(lay.nz)[::-1])
        first, second = acc_scr[:block_rows, :], acc_scr[block_rows:, :]
        kept = jnp.where(is_first, first, second)
        sent = jnp.where(is_first, second, first)
        for ref, rows in ((kept_ref, kept), (sent_ref, sent)):
            for d in range(groups):
                chunk = [
                    rows[m * chunk_rows : (m + 1) * chunk_rows, d * part : (d + 1) * part]
                    for m in range(chunk_width // part)
                ]
                cut_scr[d] = jnp.concatenate(chunk, axis=1) if len(chunk) > 1 else chunk[0]
            for n, k in enumerate(order):
                ref[n] = cut_scr[pos_ref[2] ^ k]


def backward_kernel(lay, pos_ref, info_ref, *refs):
    w_refs, refs = refs[: 2 * lay.halves], refs[2 * lay.halves :]
    q_ref, k_ref, v_ref, ga_ref, *refs = refs
    gh_refs, (w_scr, gt_scr) = refs[: lay.chips], refs[lay.chips :]
    _, frames, step_patches, cols = q_ref.shape
    model = w_scr.shape[1]
    patches = step_patches * pl.num_programs(0)
    scaling = 1.0 / math.sqrt(cols // lay.half_heads)

    @pl.when(pl.program_id(0) == 0)
    def _():
        fill_weights(lay, pos_ref, w_refs, w_scr)

    for b in range(step_patches // BLOCK):
        patch_base = lay.unit(pos_ref[1], pos_ref[2])[2] * patches + pl.program_id(0) * step_patches + b * BLOCK
        allowed = allowed_pairs(lay, pos_ref, info_ref, patch_base)
        for h in range(lay.halves):
            queries, keys, values = (patch_blocks(ref[h], b) for ref in (q_ref, k_ref, v_ref))
            grad_out = patch_blocks(ga_ref[(pos_ref[1] ^ h) if lay.halves > 1 else 0], b)
            keys = heads_stacked(lay, keys)
            weights = attention_weights(lay, keys, queries, allowed, scaling)
            grad_weights = dot_t(heads_stacked(lay, values), grad_out).reshape(weights.shape)
            grad_values = dot(beside(lay, weights.astype(BF16)), heads_stacked(lay, grad_out))
            inner = jnp.sum(weights * grad_weights, axis=1, keepdims=True)
            grad_scores = (weights * (grad_weights - inner) * scaling).astype(BF16)
            grad_queries = t_dot(grad_scores.reshape(-1, grad_scores.shape[2]), keys)
            grad_keys = dot(beside(lay, grad_scores), heads_stacked(lay, queries))
            grads = jnp.concatenate([grad_queries, grad_keys, grad_values], axis=1).astype(BF16)
            gt_scr[h, :, b * BLOCK : (b + 1) * BLOCK, :] = grads.reshape(frames, BLOCK, 3 * cols)

    rows = lay.nc * step_patches
    for k in range(lay.chips):
        total = jnp.zeros((rows, model), F32)
        for h in range(lay.halves):
            part = gt_scr[h, k * lay.nc : (k + 1) * lay.nc].reshape(rows, 3 * cols)
            total = total + dot_t(part, w_scr[h])
        gh_refs[k][...] = total.reshape(gh_refs[k].shape).astype(gh_refs[k].dtype)


def output_kernel(lay, pos_ref, info_ref, *refs):
    pair_refs, refs = refs[: lay.nc], refs[lay.nc :]
    pr_refs, refs = refs[: lay.chips], refs[lay.chips :]
    gh_refs, refs = refs[: lay.chips], refs[lay.chips :]
    mod_ref, *out_refs = refs
    _, _, step_patches, model = out_refs[0].shape
    patches = step_patches * pl.num_programs(0)
    patch_base = lay.unit(pos_ref[1], pos_ref[2])[2] * patches + pl.program_id(0) * step_patches
    patch = patch_base + lax.broadcasted_iota(jnp.int32, (step_patches, 1), 0)
    for j in range(lay.nc):
        _, limit, step = slot_scalars(lay, pos_ref, info_ref, (0, j))
        values = pair_refs[j][0, 0].astype(F32)
        factor = jnp.where(patch < limit, table_row(mod_ref, step, 2, model), 0.0)
        projected, grad_hidden = pr_refs[0][j], gh_refs[0][j]
        for k in range(1, lay.chips):
            projected = projected + pr_refs[k][j].astype(F32)
            grad_hidden = grad_hidden + gh_refs[k][j].astype(F32)
        projected = projected.astype(BF16).astype(F32)
        out_refs[j][0, 0] = (values + factor * projected).astype(BF16)

        grad_hidden = grad_hidden.astype(BF16).astype(F32)
        normed, inv_sigma = normalize(values)
        grad_norm = grad_hidden * (1.0 + table_row(mod_ref, step, 1, model))
        first_mean = jnp.mean(grad_norm, axis=-1, keepdims=True)
        second_mean = jnp.mean(grad_norm * normed, axis=-1, keepdims=True)
        grad_x = pair_refs[j][0, 1].astype(F32) + inv_sigma * (
            grad_norm - first_mean - normed * second_mean
        )
        out_refs[j][0, 1] = grad_x.astype(BF16)


def whole_spec(shape):
    return pl.BlockSpec(shape, lambda *_: (0,) * len(shape))


def struct(shape, dtype=BF16):
    return jax.ShapeDtypeStruct(shape, dtype)


def local(lay, frames_x, grad_y, clip_ids, clip_patches, clip_step, mod_table, w_qkv, w_out):
    y, c, z, x = (lax.axis_index(name) for name in AXES)
    _, patches, model = frames_x.shape
    half = patches // lay.nc
    chips, nc, nx = lay.chips, lay.nc, lay.nx
    head_size = model // HEADS
    halves = lay.halves
    cols = lay.half_heads * head_size
    chip_width = lay.chip_heads * head_size
    rows = w_qkv.shape[0]
    groups = lay.nz
    quarter = model // groups
    step_patches = max(BLOCK, min(half, 512 // lay.frames))
    steps = half // step_patches
    tokens = lay.frames * step_patches

    def call(kernel, name, cost, in_specs, out_specs, out_shape, scratch=(), grid=(1,), prefetch=2):
        return pl.pallas_call(
            kernel,
            grid_spec=pltpu.PrefetchScalarGridSpec(
                num_scalar_prefetch=prefetch,
                grid=grid,
                in_specs=in_specs,
                out_specs=out_specs,
                scratch_shapes=list(scratch),
            ),
            out_shape=out_shape,
            compiler_params=pltpu.CompilerParams(vmem_limit_bytes=VMEM_LIMIT),
            cost_estimate=pl.CostEstimate(
                flops=cost * tokens * steps, bytes_accessed=4 * model * tokens, transcendentals=0
            ),
            name=name,
        )

    def chip_swap(k):
        ky, kx = lay.chip_of(k)
        return lay.swap(ky=ky, kx=kx)

    def doubling(held, bits, swap, after, first=None):
        for bit in bits[:-1]:
            got = lax.ppermute(held, AXES, swap(bit)) if first is None else first
            held, first = jnp.concatenate([held, got], axis=0), None
        held, _ = lax.optimization_barrier((held, after))
        return [held, lax.ppermute(held, AXES, swap(bits[-1]))]

    def over_chips(parts):
        got = [lax.ppermute(parts[k], AXES, chip_swap(k)) for k in range(1, chips)]
        return [parts[0]] + got

    info = jnp.concatenate([clip_ids[0], clip_patches[0], clip_step[0]])[None]
    by_core = jnp.concatenate([info, lax.ppermute(info, AXES, lay.swap(kc=1))], axis=0)
    info = [by_core] + [
        lax.ppermute(by_core, AXES, lay.swap(ky=ky)) for ky in range(1, lay.ny)
    ]
    group_y, group_c, _ = lay.unit(c, z)
    info = sum(
        jnp.where((y ^ ky == group_y) & (c ^ kc == group_c), info[ky][kc], 0)
        for ky in range(lay.ny)
        for kc in range(nc)
    )
    pos = jnp.stack([y, c, z, x]).astype(jnp.int32)
    pair_shape = (1, 2, half, model)
    outputs = call(
        functools.partial(start_kernel, lay, cols),
        "start",
        2 * model * 1000,
        [whole_spec(frames_x.shape)] * 2 + [whole_spec(w_qkv.shape)],
        [whole_spec(pair_shape)] * nc + [whole_spec((rows, 3 * cols))] * nx,
        [struct(pair_shape)] * nc + [struct((rows, 3 * cols))] * nx,
        prefetch=1,
    )(pos, frames_x, grad_y, w_qkv)
    pairs, picked = outputs[:nc], outputs[nc:]
    own = [lax.ppermute(pair, AXES, lay.to_plane(k)) for k, pair in enumerate(pairs)]
    by_x = [picked[0]] + [
        lax.ppermute(picked[kx], AXES, lay.swap(kx=kx)) for kx in range(1, nx)
    ]
    if nx == 2:
        ordered = [jnp.where(x == i, by_x[0], by_x[1]) for i in range(nx)]
    else:
        stacked = jnp.stack(by_x)
        ordered = [lax.dynamic_index_in_dim(stacked, x ^ i, 0, keepdims=False) for i in range(nx)]
    w_own = jnp.concatenate(ordered, axis=1 if rows % 16 == 0 else 0)[None]
    first = lax.ppermute(own[0], AXES, chip_swap(lay.chip_bits(0)[0]))
    own[1], first = lax.optimization_barrier((own[1], first))
    w_own, _ = lax.optimization_barrier((w_own, own[1]))
    w_pieces = doubling(w_own, lay.bits(lay.nz)[::-1], lambda kz: lay.swap(kz=kz), [])
    late_w_out, _ = lax.optimization_barrier((w_out, own))
    wo_own = lax.ppermute(late_w_out, AXES, lay.rows_to_chip())

    pairs = []
    for j in range(nc):
        after = ([], None) if j else (info, first)
        pairs += doubling(own[j], lay.chip_bits(j), chip_swap, *after)
    pairs, _ = lax.optimization_barrier((pairs, w_pieces))


    def spread(count, width, patches_at_once):
        return pl.BlockSpec((count, patches_at_once, width), lambda i, *_: (0, i, 0))

    def pair_spec(count, patches_at_once):
        return pl.BlockSpec((count, 2, patches_at_once, model), lambda i, *_: (0, 0, i, 0))

    few = max(BLOCK, step_patches // 2)
    few_steps = half // few
    x_spec = pl.BlockSpec((few, model), lambda i, *_: (i, 0))
    triple_spec = pl.BlockSpec((halves, lay.frames, step_patches, cols), lambda i, *_: (0, 0, i, 0))
    w_specs = [whole_spec(w_pieces[0].shape)] * (2 * halves)
    w_scratch = pltpu.VMEM((halves, model, 3 * cols), BF16)
    mod_spec = whole_spec(mod_table.shape)
    triple_shape = struct((halves, lay.frames, half, cols))
    part_specs = [spread(nc, model, step_patches)] * chips
    part_shapes = [struct((nc, half, model), F32)] + [struct((nc, half, model))] * (chips - 1)

    hidden, grad_proj = call(
        functools.partial(prepare_kernel, lay),
        "prepare",
        3 * model * 1000,
        [pair_spec(chips // 2, few)] * (2 * nc) + [mod_spec],
        [spread(lay.frames, model, few)] * 2,
        [struct((lay.frames, half, model))] * 2,
        grid=(few_steps,),
    )(pos, info, *pairs, mod_table)
    wo_own, w_pieces, _ = lax.optimization_barrier((wo_own, w_pieces, hidden))
    if halves > 1:
        w_pieces += [lax.ppermute(piece, AXES, lay.swap(kc=1)) for piece in w_pieces]
    wo_rows = [wo_own, lax.ppermute(wo_own, AXES, lay.swap(kc=1))]

    fold = 3 if rows % 24 == 0 else 1
    piece_shape = (groups, rows // fold, quarter * fold)
    queries, keys, values, grad_attn, kept, sent, *projected = call(
        functools.partial(forward_kernel, lay),
        "forward",
        14 * model * 1000,
        [spread(lay.frames, model, step_patches)] * 2
        + w_specs
        + [whole_spec(w_out.shape)] * nc,
        [triple_spec] * 4 + [whole_spec(piece_shape)] * 2 + part_specs,
        [triple_shape] * 4 + [struct(piece_shape, F32)] * 2 + part_shapes,
        [
            w_scratch,
            pltpu.VMEM((lay.frames, step_patches, chip_width), BF16),
            pltpu.VMEM((chip_width, model), BF16),
            pltpu.VMEM((chip_width, model), F32),
            pltpu.VMEM(piece_shape, F32),
        ],
        (steps,),
    )(pos, info, hidden, grad_proj, *w_pieces, *wo_rows)
    got = lax.ppermute(sent, AXES, lay.swap(kc=1))
    projected = over_chips(projected)

    middle = groups // 2
    cut, away = kept[:middle] + got[:middle], kept[middle:] + got[middle:]
    grad_attn, cut, away = lax.optimization_barrier((grad_attn, cut, away))
    first_away = lax.ppermute(away, AXES, lay.swap(kz=1))

    sums = call(
        functools.partial(backward_kernel, lay),
        "backward",
        10 * model * 1000,
        w_specs + [triple_spec] * 4,
        part_specs,
        part_shapes,
        [w_scratch, pltpu.VMEM((halves, lay.frames, step_patches, 3 * cols), BF16)],
        (steps,),
    )(pos, info, *w_pieces, queries, keys, values, grad_attn)
    sums, first_away, projected = lax.optimization_barrier((sums, first_away, projected))
    grad_hidden = over_chips(sums)

    parts = call(
        functools.partial(output_kernel, lay),
        "output",
        3 * model * 1000,
        [pair_spec(1, few)] * nc + [spread(nc, model, few)] * (2 * chips) + [mod_spec],
        [pair_spec(1, few)] * nc,
        [struct(pair_shape)] * nc,
        grid=(few_steps,),
    )(pos, info, *own, *projected, *grad_hidden, mod_table)
    got = [lax.ppermute(part, AXES, lay.from_plane(k)) for k, part in enumerate(parts)]
    is_first = z // lay.ny == 0
    out_y, grad_x = (
        jnp.concatenate(
            [
                jnp.where(is_first, got[0][:, n], got[1][:, n]),
                jnp.where(is_first, got[1][:, n], got[0][:, n]),
            ],
            axis=1,
        )
        for n in range(2)
    )

    cut, _ = lax.optimization_barrier((cut + first_away, grad_hidden[1]))
    for bit in lay.bits(lay.nz)[1:]:
        middle = middle // 2
        cut = cut[:middle] + lax.ppermute(cut[middle:], AXES, lay.swap(kz=bit))
    cut, _ = lax.optimization_barrier((cut, parts))
    grad_w = lax.ppermute(cut[0], AXES, lay.to_owner())
    grad_w = jnp.concatenate(
        [grad_w[:, m * quarter : (m + 1) * quarter] for m in range(fold)], axis=0
    )
    grad_w_out = grad_w * jnp.float32(1.0 / math.sqrt(groups * lay.frames * patches))
    return out_y, grad_x, grad_w_out


def solution(mesh):
    lay = Layout(mesh)
    grid = Mesh(mesh.devices.reshape(lay.ny, lay.nc, lay.nz, lay.nx), AXES)
    rows, cols = ("z", "x"), ("y", "c")
    frame = P(AXES, None, None)
    group = P(cols, None)
    return jax.shard_map(
        functools.partial(local, lay),
        mesh=grid,
        in_specs=(frame, frame, group, group, group, P(), P(rows, None), P(rows, None)),
        out_specs=(frame, frame, P(rows, cols)),
        check_vma=False,
    )
```

```python
import functools
import math

import jax
import jax.numpy as jnp
from jax import lax
from jax.experimental import pallas as pl
from jax.experimental.pallas import tpu as pltpu
from jax.sharding import Mesh, PartitionSpec as P

HEADS = 16
CORES = 2
AXES = ("y", "c", "z", "x")
BLOCK = 16
VMEM_LIMIT = 56 * 1024 * 1024
BF16 = jnp.bfloat16
F32 = jnp.float32


def dot(left, right):
    return jnp.dot(left, right, preferred_element_type=F32)


def dot_t(left, right):
    return lax.dot_general(left, right, (((1,), (1,)), ((), ())), preferred_element_type=F32)


def t_dot(left, right):
    return lax.dot_general(left, right, (((0,), (0,)), ((), ())), preferred_element_type=F32)


def normalize(values):
    centred = values - jnp.mean(values, axis=-1, keepdims=True)
    inv_sigma = lax.rsqrt(jnp.mean(centred * centred, axis=-1, keepdims=True) + 1e-06)
    return centred * inv_sigma, inv_sigma


class Layout:
    def __init__(self, mesh):
        groups, seq = mesh.shape["dp"], mesh.shape["seq"]
        self.nc = CORES
        self.ny = groups // CORES
        self.nz = groups
        self.nx = seq // self.nz
        self.chips = self.ny * self.nx
        self.frames = seq
        self.chip_heads = HEADS // self.chips
        self.halves = 2 if self.chip_heads % 2 == 0 else 1
        self.half_heads = self.chip_heads // self.halves

    def linear(self, y, c, z, x):
        return ((y * self.nc + c) * self.nz + z) * self.nx + x

    def perm(self, move):
        pairs = []
        for y in range(self.ny):
            for c in range(self.nc):
                for z in range(self.nz):
                    for x in range(self.nx):
                        pairs.append((self.linear(y, c, z, x), self.linear(*move(y, c, z, x))))
        return pairs

    def to_plane(self, k):
        def move(y, c, z, x):
            half = (z // self.ny) ^ k
            plane = ((y // self.nc) * self.nc + c) * self.nc + half
            return (z % self.ny) ^ c, y % self.nc, plane, x

        return self.perm(move)

    def unit(self, c, z):
        return (z // (self.nc * self.nc)) * self.nc + c, (z // self.nc) % self.nc, z % self.nc

    def from_plane(self, k):
        return [(target, source) for source, target in self.to_plane(k)]

    def swap(self, ky=0, kc=0, kz=0, kx=0):
        return self.perm(lambda y, c, z, x: (y ^ ky, c ^ kc, z ^ kz, x ^ kx))

    def row_block(self, y, x, i):
        if self.halves > 1:
            return (i * self.ny + y) * self.nx + x
        return self.nc * (y * self.nx + x) + i

    def rows_to_chip(self):
        reader = {
            self.row_block(y, x, i): (y, x, i)
            for y in range(self.ny)
            for x in range(self.nx)
            for i in range(self.nc)
        }

        def move(y, c, z, x):
            chip_y, chip_x, i = reader[z * self.nx + x]
            return chip_y, i, c * self.ny + (y ^ (z & 1)), chip_x

        return self.perm(move)

    def to_owner(self):
        def move(y, c, z, x):
            s = self.row_block(y, x, c)
            return z // self.nc, z % self.nc, s // self.nx, s % self.nx

        return self.perm(move)

    def chip_of(self, k):
        return k // self.nx, k % self.nx

    def bits(self, count):
        return [1 << b for b in range(count.bit_length() - 1)]

    def chip_bits(self, j):
        bits = self.bits(self.chips)
        return bits if j % 2 == 0 else bits[::-1]

    def doubled(self, bits):
        held = [0]
        for bit in bits:
            held = held + [k ^ bit for k in held]
        return held

    def slots(self):
        return [(k, j) for k in range(self.chips) for j in range(self.nc)]


def slot_scalars(lay, pos_ref, info_ref, slot):
    k, j = slot
    ky, kx = lay.chip_of(k)
    _, group_c, half = lay.unit(pos_ref[1], pos_ref[2])
    z_frame = (half ^ j) * lay.ny + (pos_ref[0] ^ ky ^ group_c)
    frame = z_frame * lay.nx + (pos_ref[3] ^ kx)
    clip = info_ref[frame]
    clips = (info_ref.shape[0] - lay.frames) // 2
    return clip, info_ref[lay.frames + clip], info_ref[lay.frames + clips + clip]


def table_row(mod_ref, step, part, width):
    return mod_ref[pl.ds(step, 1), part * width : (part + 1) * width]


def allowed_pairs(lay, pos_ref, info_ref, patch_base):
    rows = lay.frames * BLOCK
    row_slot = lax.broadcasted_iota(jnp.int32, (rows, 1), 0) // BLOCK
    col_slot = lax.broadcasted_iota(jnp.int32, (1, rows), 1) // BLOCK
    row_clip = jnp.zeros((rows, 1), jnp.int32)
    row_limit = jnp.zeros((rows, 1), jnp.int32)
    col_clip = jnp.zeros((1, rows), jnp.int32)
    for t, slot in enumerate(lay.slots()):
        clip, limit, _ = slot_scalars(lay, pos_ref, info_ref, slot)
        row_clip = jnp.where(row_slot == t, clip, row_clip)
        row_limit = jnp.where(row_slot == t, limit, row_limit)
        col_clip = jnp.where(col_slot == t, clip, col_clip)
    row_patch = lax.broadcasted_iota(jnp.int32, (rows, 1), 0) % BLOCK
    col_patch = lax.broadcasted_iota(jnp.int32, (1, rows), 1) % BLOCK
    row_key = row_clip * BLOCK + row_patch
    col_key = col_clip * BLOCK + col_patch
    row_valid = (patch_base + row_patch < row_limit).astype(jnp.int32)
    row_index = lax.broadcasted_iota(jnp.int32, (rows, rows), 0)
    col_index = lax.broadcasted_iota(jnp.int32, (rows, rows), 1)
    return (row_key == col_key) & ((row_valid > 0) | (row_index == col_index))


def head_mask(values, head, head_size):
    lane = lax.broadcasted_iota(jnp.int32, (1, values.shape[1]), 1)
    inside = (lane >= head * head_size) & (lane < (head + 1) * head_size)
    return jnp.where(inside, values, jnp.zeros_like(values))


def patch_blocks(array, block):
    part = array[:, block * BLOCK : (block + 1) * BLOCK, :]
    return part.reshape(part.shape[0] * BLOCK, part.shape[2])


def start_kernel(lay, cols, pos_ref, x_ref, g_ref, w_ref, *refs):
    pair_refs, out_refs = refs[: lay.nc], refs[lay.nc :]
    half = x_ref.shape[1] // lay.nc
    for k, ref in enumerate(pair_refs):
        first = pl.multiple_of(((pos_ref[2] // lay.ny) ^ k) * half, 16)
        ref[0, 0] = x_ref[0, pl.ds(first, half), :]
        ref[0, 1] = g_ref[0, pl.ds(first, half), :]
    model = w_ref.shape[1] // 3
    for k, out_ref in enumerate(out_refs):
        chip_x = pos_ref[3] ^ k
        if lay.halves > 1:
            want = lay.row_block(pos_ref[0], chip_x, pos_ref[1])
        else:
            want = pos_ref[0] * lay.nx + chip_x
        for v in range(lay.chips * lay.halves):

            @pl.when(want == v)
            def _(v=v, out_ref=out_ref):
                parts = [
                    w_ref[:, p * model + v * cols : p * model + (v + 1) * cols]
                    for p in range(3)
                ]
                out_ref[...] = jnp.concatenate(parts, axis=1)


def fill_weights(lay, pos_ref, w_refs, w_scr):
    order = lay.doubled(lay.bits(lay.nz)[::-1])
    block = w_scr.shape[1] // lay.nz
    rows, width = w_refs[0].shape[1], w_scr.shape[2]
    for h in range(lay.halves):
        for n, k in enumerate(order):
            ref, place = w_refs[2 * h + (2 * n) // lay.nz], n % (lay.nz // 2)
            for m in range(block // rows):
                start = pl.multiple_of((pos_ref[2] ^ k) * block + m * rows, 16)
                w_scr[h, pl.ds(start, rows), :] = ref[place, :, m * width : (m + 1) * width]


def heads_stacked(lay, values):
    head_size = values.shape[1] // lay.half_heads
    parts = [head_mask(values, head, head_size) for head in range(lay.half_heads)]
    return jnp.concatenate(parts, axis=0) if len(parts) > 1 else parts[0]


def beside(lay, weights):
    return jnp.concatenate([weights[head] for head in range(lay.half_heads)], axis=1)


def attention_weights(lay, keys_stacked, queries, allowed, scaling):
    scores = dot_t(keys_stacked, queries) * scaling
    scores = jnp.where(allowed, scores.reshape((lay.half_heads,) + allowed.shape), -jnp.inf)
    exponent = jnp.exp(scores - jnp.max(scores, axis=1, keepdims=True))
    return exponent * (1.0 / jnp.sum(exponent, axis=1, keepdims=True))


def prepare_kernel(lay, pos_ref, info_ref, *refs):
    pair_refs, (mod_ref, hid_ref, gp_ref) = refs[: 2 * lay.nc], refs[2 * lay.nc :]
    _, step_patches, model = hid_ref.shape
    patches = step_patches * pl.num_programs(0)
    patch_base = lay.unit(pos_ref[1], pos_ref[2])[2] * patches + pl.program_id(0) * step_patches
    patch = patch_base + lax.broadcasted_iota(jnp.int32, (step_patches, 1), 0)
    for t, (k, j) in enumerate(lay.slots()):
        _, limit, step = slot_scalars(lay, pos_ref, info_ref, (k, j))
        n = lay.doubled(lay.chip_bits(j)).index(k)
        ref, place = pair_refs[2 * j + (2 * n) // lay.chips], n % (lay.chips // 2)
        normed, _ = normalize(ref[place, 0].astype(F32))
        shift, scale = table_row(mod_ref, step, 0, model), table_row(mod_ref, step, 1, model)
        hid_ref[t] = (normed * (1.0 + scale) + shift).astype(BF16)
        factor = jnp.where(patch < limit, table_row(mod_ref, step, 2, model), 0.0)
        gp_ref[t] = (factor * ref[place, 1].astype(F32)).astype(BF16)


def forward_kernel(lay, pos_ref, info_ref, hid_ref, gp_ref, *refs):
    w_refs, refs = refs[: 2 * lay.halves], refs[2 * lay.halves :]
    wo_refs, refs = refs[: lay.nc], refs[lay.nc :]
    q_ref, k_ref, v_ref, ga_ref, kept_ref, sent_ref, *refs = refs
    pr_refs, (w_scr, att_scr, wo_scr, acc_scr, cut_scr) = refs[: lay.chips], refs[lay.chips :]
    _, step_patches, model = hid_ref.shape
    tokens = lay.frames * step_patches
    cols = w_scr.shape[2] // 3
    scaling = 1.0 / math.sqrt(cols // lay.half_heads)
    patches = step_patches * pl.num_programs(0)
    is_first = pos_ref[1] == 0

    @pl.when(pl.program_id(0) == 0)
    def _():
        fill_weights(lay, pos_ref, w_refs, w_scr)
        own, other = wo_refs[0][...].astype(F32), wo_refs[1][...].astype(F32)
        both = [jnp.where(is_first, own, other), jnp.where(is_first, other, own)]
        wo_scr[...] = jnp.concatenate(both, axis=0).astype(BF16)
        acc_scr[...] = jnp.zeros_like(acc_scr)

    hidden = hid_ref[...].reshape(lay.frames * step_patches, model)
    for h in range(lay.halves):
        triple = dot(hidden, w_scr[h])
        for n, ref in enumerate((q_ref, k_ref, v_ref)):
            ref[h] = triple[:, n * cols : (n + 1) * cols].astype(BF16).reshape(ref.shape[1:])

    for b in range(step_patches // BLOCK):
        patch_base = lay.unit(pos_ref[1], pos_ref[2])[2] * patches + pl.program_id(0) * step_patches + b * BLOCK
        allowed = allowed_pairs(lay, pos_ref, info_ref, patch_base)
        outputs = []
        for h in range(lay.halves):
            queries, keys, values = (patch_blocks(ref[h], b) for ref in (q_ref, k_ref, v_ref))
            weights = attention_weights(lay, heads_stacked(lay, keys), queries, allowed, scaling)
            weights = weights.astype(BF16).reshape(-1, allowed.shape[1])
            outputs.append(t_dot(weights, heads_stacked(lay, values)))
        if lay.halves > 1:
            first = jnp.where(pos_ref[1] == 0, outputs[0], outputs[1])
            second = jnp.where(pos_ref[1] == 0, outputs[1], outputs[0])
            outputs = [jnp.concatenate([first, second], axis=1)]
        attended = outputs[0].astype(BF16)
        att_scr[:, b * BLOCK : (b + 1) * BLOCK, :] = attended.reshape(lay.frames, BLOCK, -1)

    attended = att_scr[...].reshape(tokens, -1)
    grad_proj = gp_ref[...].reshape(tokens, model)
    acc_scr[...] += t_dot(attended, grad_proj)
    grad_attn = dot_t(grad_proj, wo_scr[...])
    part = wo_scr.shape[0] // lay.halves
    for h in range(lay.halves):
        ga_ref[h] = grad_attn[:, h * part : (h + 1) * part].astype(BF16).reshape(ga_ref.shape[1:])
    projected = dot(attended, wo_scr[...]).reshape(lay.chips, lay.nc, step_patches, model)
    for k in range(lay.chips):
        pr_refs[k][...] = projected[k].astype(pr_refs[k].dtype)

    @pl.when(pl.program_id(0) == pl.num_programs(0) - 1)
    def _():
        groups, chunk_rows, chunk_width = kept_ref.shape
        block_rows, part = acc_scr.shape[0] // lay.nc, model // groups
        order = lay.doubled(lay.bits(lay.nz)[::-1])
        first, second = acc_scr[:block_rows, :], acc_scr[block_rows:, :]
        kept = jnp.where(is_first, first, second)
        sent = jnp.where(is_first, second, first)
        for ref, rows in ((kept_ref, kept), (sent_ref, sent)):
            for d in range(groups):
                chunk = [
                    rows[m * chunk_rows : (m + 1) * chunk_rows, d * part : (d + 1) * part]
                    for m in range(chunk_width // part)
                ]
                cut_scr[d] = jnp.concatenate(chunk, axis=1) if len(chunk) > 1 else chunk[0]
            for n, k in enumerate(order):
                ref[n] = cut_scr[pos_ref[2] ^ k]


def backward_kernel(lay, pos_ref, info_ref, *refs):
    w_refs, refs = refs[: 2 * lay.halves], refs[2 * lay.halves :]
    q_ref, k_ref, v_ref, ga_ref, *refs = refs
    gh_refs, (w_scr, gt_scr) = refs[: lay.chips], refs[lay.chips :]
    _, frames, step_patches, cols = q_ref.shape
    model = w_scr.shape[1]
    patches = step_patches * pl.num_programs(0)
    scaling = 1.0 / math.sqrt(cols // lay.half_heads)

    @pl.when(pl.program_id(0) == 0)
    def _():
        fill_weights(lay, pos_ref, w_refs, w_scr)

    for b in range(step_patches // BLOCK):
        patch_base = lay.unit(pos_ref[1], pos_ref[2])[2] * patches + pl.program_id(0) * step_patches + b * BLOCK
        allowed = allowed_pairs(lay, pos_ref, info_ref, patch_base)
        for h in range(lay.halves):
            queries, keys, values = (patch_blocks(ref[h], b) for ref in (q_ref, k_ref, v_ref))
            grad_out = patch_blocks(ga_ref[(pos_ref[1] ^ h) if lay.halves > 1 else 0], b)
            keys = heads_stacked(lay, keys)
            weights = attention_weights(lay, keys, queries, allowed, scaling)
            grad_weights = dot_t(heads_stacked(lay, values), grad_out).reshape(weights.shape)
            grad_values = dot(beside(lay, weights.astype(BF16)), heads_stacked(lay, grad_out))
            inner = jnp.sum(weights * grad_weights, axis=1, keepdims=True)
            grad_scores = (weights * (grad_weights - inner) * scaling).astype(BF16)
            grad_queries = t_dot(grad_scores.reshape(-1, grad_scores.shape[2]), keys)
            grad_keys = dot(beside(lay, grad_scores), heads_stacked(lay, queries))
            grads = jnp.concatenate([grad_queries, grad_keys, grad_values], axis=1).astype(BF16)
            gt_scr[h, :, b * BLOCK : (b + 1) * BLOCK, :] = grads.reshape(frames, BLOCK, 3 * cols)

    rows = lay.nc * step_patches
    for k in range(lay.chips):
        total = jnp.zeros((rows, model), F32)
        for h in range(lay.halves):
            part = gt_scr[h, k * lay.nc : (k + 1) * lay.nc].reshape(rows, 3 * cols)
            total = total + dot_t(part, w_scr[h])
        gh_refs[k][...] = total.reshape(gh_refs[k].shape).astype(gh_refs[k].dtype)


def output_kernel(lay, pos_ref, info_ref, *refs):
    pair_refs, refs = refs[: lay.nc], refs[lay.nc :]
    pr_refs, refs = refs[: lay.chips], refs[lay.chips :]
    mod_ref, *out_refs = refs
    step_patches, model = out_refs[0].shape
    patches = step_patches * pl.num_programs(0)
    patch_base = lay.unit(pos_ref[1], pos_ref[2])[2] * patches + pl.program_id(0) * step_patches
    patch = patch_base + lax.broadcasted_iota(jnp.int32, (step_patches, 1), 0)
    for j in range(lay.nc):
        _, limit, step = slot_scalars(lay, pos_ref, info_ref, (0, j))
        factor = jnp.where(patch < limit, table_row(mod_ref, step, 2, model), 0.0)
        projected = pr_refs[0][j]
        for k in range(1, lay.chips):
            projected = projected + pr_refs[k][j].astype(F32)
        projected = projected.astype(BF16).astype(F32)
        out_refs[j][...] = (pair_refs[j][0, 0].astype(F32) + factor * projected).astype(BF16)


def input_grad_kernel(lay, pos_ref, info_ref, *refs):
    pair_refs, refs = refs[: lay.nc], refs[lay.nc :]
    gh_refs, refs = refs[: lay.chips], refs[lay.chips :]
    mod_ref, *out_refs = refs
    model = out_refs[0].shape[1]
    for j in range(lay.nc):
        _, _, step = slot_scalars(lay, pos_ref, info_ref, (0, j))
        grad_hidden = gh_refs[0][j]
        for k in range(1, lay.chips):
            grad_hidden = grad_hidden + gh_refs[k][j].astype(F32)
        grad_hidden = grad_hidden.astype(BF16).astype(F32)
        normed, inv_sigma = normalize(pair_refs[j][0, 0].astype(F32))
        grad_norm = grad_hidden * (1.0 + table_row(mod_ref, step, 1, model))
        first_mean = jnp.mean(grad_norm, axis=-1, keepdims=True)
        second_mean = jnp.mean(grad_norm * normed, axis=-1, keepdims=True)
        grad_x = pair_refs[j][0, 1].astype(F32) + inv_sigma * (
            grad_norm - first_mean - normed * second_mean
        )
        out_refs[j][...] = grad_x.astype(BF16)


def whole_spec(shape):
    return pl.BlockSpec(shape, lambda *_: (0,) * len(shape))


def struct(shape, dtype=BF16):
    return jax.ShapeDtypeStruct(shape, dtype)


def local(lay, frames_x, grad_y, clip_ids, clip_patches, clip_step, mod_table, w_qkv, w_out):
    y, c, z, x = (lax.axis_index(name) for name in AXES)
    _, patches, model = frames_x.shape
    half = patches // lay.nc
    chips, nc, nx = lay.chips, lay.nc, lay.nx
    head_size = model // HEADS
    halves = lay.halves
    cols = lay.half_heads * head_size
    chip_width = lay.chip_heads * head_size
    rows = w_qkv.shape[0]
    groups = lay.nz
    quarter = model // groups
    step_patches = max(BLOCK, min(half, 512 // lay.frames))
    steps = half // step_patches
    tokens = lay.frames * step_patches

    def call(kernel, name, cost, in_specs, out_specs, out_shape, scratch=(), grid=(1,), prefetch=2):
        return pl.pallas_call(
            kernel,
            grid_spec=pltpu.PrefetchScalarGridSpec(
                num_scalar_prefetch=prefetch,
                grid=grid,
                in_specs=in_specs,
                out_specs=out_specs,
                scratch_shapes=list(scratch),
            ),
            out_shape=out_shape,
            compiler_params=pltpu.CompilerParams(vmem_limit_bytes=VMEM_LIMIT),
            cost_estimate=pl.CostEstimate(
                flops=cost * tokens * steps, bytes_accessed=4 * model * tokens, transcendentals=0
            ),
            name=name,
        )

    def chip_swap(k):
        ky, kx = lay.chip_of(k)
        return lay.swap(ky=ky, kx=kx)

    def from_plane(parts):
        got = [lax.ppermute(part, AXES, lay.from_plane(k)) for k, part in enumerate(parts)]
        first = jnp.where(z // lay.ny == 0, got[0], got[1])
        second = jnp.where(z // lay.ny == 0, got[1], got[0])
        return jnp.concatenate([first, second], axis=0)[None]

    def doubling(held, bits, swap, after, first=None):
        for bit in bits[:-1]:
            got = lax.ppermute(held, AXES, swap(bit)) if first is None else first
            held, first = jnp.concatenate([held, got], axis=0), None
        held, _ = lax.optimization_barrier((held, after))
        return [held, lax.ppermute(held, AXES, swap(bits[-1]))]

    def over_chips(parts):
        got = [lax.ppermute(parts[k], AXES, chip_swap(k)) for k in range(1, chips)]
        return [parts[0]] + got

    info = jnp.concatenate([clip_ids[0], clip_patches[0], clip_step[0]])[None]
    by_core = jnp.concatenate([info, lax.ppermute(info, AXES, lay.swap(kc=1))], axis=0)
    info = [by_core] + [
        lax.ppermute(by_core, AXES, lay.swap(ky=ky)) for ky in range(1, lay.ny)
    ]
    group_y, group_c, _ = lay.unit(c, z)
    info = sum(
        jnp.where((y ^ ky == group_y) & (c ^ kc == group_c), info[ky][kc], 0)
        for ky in range(lay.ny)
        for kc in range(nc)
    )
    pos = jnp.stack([y, c, z, x]).astype(jnp.int32)
    pair_shape = (1, 2, half, model)
    outputs = call(
        functools.partial(start_kernel, lay, cols),
        "start",
        2 * model * 1000,
        [whole_spec(frames_x.shape)] * 2 + [whole_spec(w_qkv.shape)],
        [whole_spec(pair_shape)] * nc + [whole_spec((rows, 3 * cols))] * nx,
        [struct(pair_shape)] * nc + [struct((rows, 3 * cols))] * nx,
        prefetch=1,
    )(pos, frames_x, grad_y, w_qkv)
    pairs, picked = outputs[:nc], outputs[nc:]
    own = [lax.ppermute(pair, AXES, lay.to_plane(k)) for k, pair in enumerate(pairs)]
    by_x = [picked[0]] + [
        lax.ppermute(picked[kx], AXES, lay.swap(kx=kx)) for kx in range(1, nx)
    ]
    if nx == 2:
        ordered = [jnp.where(x == i, by_x[0], by_x[1]) for i in range(nx)]
    else:
        stacked = jnp.stack(by_x)
        ordered = [lax.dynamic_index_in_dim(stacked, x ^ i, 0, keepdims=False) for i in range(nx)]
    w_own = jnp.concatenate(ordered, axis=1 if rows % 16 == 0 else 0)[None]
    first = lax.ppermute(own[0], AXES, chip_swap(lay.chip_bits(0)[0]))
    own[1], first = lax.optimization_barrier((own[1], first))
    w_own, _ = lax.optimization_barrier((w_own, own[1]))
    w_pieces = doubling(w_own, lay.bits(lay.nz)[::-1], lambda kz: lay.swap(kz=kz), [])
    late_w_out, _ = lax.optimization_barrier((w_out, own))
    wo_own = lax.ppermute(late_w_out, AXES, lay.rows_to_chip())

    pairs = []
    for j in range(nc):
        after = ([], None) if j else (info, first)
        pairs += doubling(own[j], lay.chip_bits(j), chip_swap, *after)
    pairs, w_pieces, wo_own = lax.optimization_barrier((pairs, w_pieces, wo_own))
    if halves > 1:
        w_pieces += [lax.ppermute(piece, AXES, lay.swap(kc=1)) for piece in w_pieces]
    wo_rows = [wo_own, lax.ppermute(wo_own, AXES, lay.swap(kc=1))]


    def spread(count, width, patches_at_once):
        return pl.BlockSpec((count, patches_at_once, width), lambda i, *_: (0, i, 0))

    def pair_spec(count, patches_at_once):
        return pl.BlockSpec((count, 2, patches_at_once, model), lambda i, *_: (0, 0, i, 0))

    few = max(BLOCK, step_patches // 2)
    few_steps = half // few
    x_spec = pl.BlockSpec((few, model), lambda i, *_: (i, 0))
    triple_spec = pl.BlockSpec((halves, lay.frames, step_patches, cols), lambda i, *_: (0, 0, i, 0))
    w_specs = [whole_spec(w_pieces[0].shape)] * (2 * halves)
    w_scratch = pltpu.VMEM((halves, model, 3 * cols), BF16)
    mod_spec = whole_spec(mod_table.shape)
    triple_shape = struct((halves, lay.frames, half, cols))
    part_specs = [spread(nc, model, step_patches)] * chips
    part_shapes = [struct((nc, half, model), F32)] + [struct((nc, half, model))] * (chips - 1)

    hidden, grad_proj = call(
        functools.partial(prepare_kernel, lay),
        "prepare",
        3 * model * 1000,
        [pair_spec(chips // 2, few)] * (2 * nc) + [mod_spec],
        [spread(lay.frames, model, few)] * 2,
        [struct((lay.frames, half, model))] * 2,
        grid=(few_steps,),
    )(pos, info, *pairs, mod_table)

    fold = 3 if rows % 24 == 0 else 1
    piece_shape = (groups, rows // fold, quarter * fold)
    queries, keys, values, grad_attn, kept, sent, *projected = call(
        functools.partial(forward_kernel, lay),
        "forward",
        14 * model * 1000,
        [spread(lay.frames, model, step_patches)] * 2
        + w_specs
        + [whole_spec(w_out.shape)] * nc,
        [triple_spec] * 4 + [whole_spec(piece_shape)] * 2 + part_specs,
        [triple_shape] * 4 + [struct(piece_shape, F32)] * 2 + part_shapes,
        [
            w_scratch,
            pltpu.VMEM((lay.frames, step_patches, chip_width), BF16),
            pltpu.VMEM((chip_width, model), BF16),
            pltpu.VMEM((chip_width, model), F32),
            pltpu.VMEM(piece_shape, F32),
        ],
        (steps,),
    )(pos, info, hidden, grad_proj, *w_pieces, *wo_rows)
    got = lax.ppermute(sent, AXES, lay.swap(kc=1))
    projected = over_chips(projected)

    middle = groups // 2
    cut, away = kept[:middle] + got[:middle], kept[middle:] + got[middle:]
    grad_attn, cut, away = lax.optimization_barrier((grad_attn, cut, away))
    first_away = lax.ppermute(away, AXES, lay.swap(kz=1))

    sums = call(
        functools.partial(backward_kernel, lay),
        "backward",
        10 * model * 1000,
        w_specs + [triple_spec] * 4,
        part_specs,
        part_shapes,
        [w_scratch, pltpu.VMEM((halves, lay.frames, step_patches, 3 * cols), BF16)],
        (steps,),
    )(pos, info, *w_pieces, queries, keys, values, grad_attn)
    sums, first_away, projected = lax.optimization_barrier((sums, first_away, projected))
    grad_hidden = over_chips(sums)

    out_parts = call(
        functools.partial(output_kernel, lay),
        "output",
        20 * model * 1000,
        [pair_spec(1, few)] * nc + [spread(nc, model, few)] * chips + [mod_spec],
        [x_spec] * nc,
        [struct((half, model))] * nc,
        grid=(few_steps,),
    )(pos, info, *own, *projected, mod_table)
    out_y = from_plane(out_parts)

    grad_hidden, _ = lax.optimization_barrier((grad_hidden, out_parts))
    grad_parts = call(
        functools.partial(input_grad_kernel, lay),
        "input_grad",
        3 * model * 1000,
        [pair_spec(1, few)] * nc + [spread(nc, model, few)] * chips + [mod_spec],
        [x_spec] * nc,
        [struct((half, model))] * nc,
        grid=(few_steps,),
    )(pos, info, *own, *grad_hidden, mod_table)
    grad_x = from_plane(grad_parts)

    cut, _ = lax.optimization_barrier((cut + first_away, out_parts))
    for bit in lay.bits(lay.nz)[1:]:
        middle = middle // 2
        cut = cut[:middle] + lax.ppermute(cut[middle:], AXES, lay.swap(kz=bit))
    cut, _ = lax.optimization_barrier((cut, grad_parts))
    grad_w = lax.ppermute(cut[0], AXES, lay.to_owner())
    grad_w = jnp.concatenate(
        [grad_w[:, m * quarter : (m + 1) * quarter] for m in range(fold)], axis=0
    )
    grad_w_out = grad_w * jnp.float32(1.0 / math.sqrt(groups * lay.frames * patches))
    return out_y, grad_x, grad_w_out


def solution(mesh):
    lay = Layout(mesh)
    grid = Mesh(mesh.devices.reshape(lay.ny, lay.nc, lay.nz, lay.nx), AXES)
    rows, cols = ("z", "x"), ("y", "c")
    frame = P(AXES, None, None)
    group = P(cols, None)
    return jax.shard_map(
        functools.partial(local, lay),
        mesh=grid,
        in_specs=(frame, frame, group, group, group, P(), P(rows, None), P(rows, None)),
        out_specs=(frame, frame, P(rows, cols)),
        check_vma=False,
    )
```

```python
import functools
import math

import jax
import jax.numpy as jnp
from jax import lax
from jax.experimental import pallas as pl
from jax.experimental.pallas import tpu as pltpu
from jax.sharding import Mesh, PartitionSpec as P

HEADS = 16
CORES = 2
AXES = ("y", "c", "z", "x")
BLOCK = 16
VMEM_LIMIT = 56 * 1024 * 1024
BF16 = jnp.bfloat16
F32 = jnp.float32


def dot(left, right):
    return jnp.dot(left, right, preferred_element_type=F32)


def dot_t(left, right):
    return lax.dot_general(left, right, (((1,), (1,)), ((), ())), preferred_element_type=F32)


def t_dot(left, right):
    return lax.dot_general(left, right, (((0,), (0,)), ((), ())), preferred_element_type=F32)


def normalize(values):
    centred = values - jnp.mean(values, axis=-1, keepdims=True)
    inv_sigma = lax.rsqrt(jnp.mean(centred * centred, axis=-1, keepdims=True) + 1e-06)
    return centred * inv_sigma, inv_sigma


class Layout:
    def __init__(self, mesh):
        groups, seq = mesh.shape["dp"], mesh.shape["seq"]
        self.nc = CORES
        self.ny = groups // CORES
        self.nz = groups
        self.nx = seq // self.nz
        self.chips = self.ny * self.nx
        self.frames = seq
        self.chip_heads = HEADS // self.chips
        self.halves = 2 if self.chip_heads % 2 == 0 else 1
        self.half_heads = self.chip_heads // self.halves

    def linear(self, y, c, z, x):
        return ((y * self.nc + c) * self.nz + z) * self.nx + x

    def perm(self, move):
        pairs = []
        for y in range(self.ny):
            for c in range(self.nc):
                for z in range(self.nz):
                    for x in range(self.nx):
                        pairs.append((self.linear(y, c, z, x), self.linear(*move(y, c, z, x))))
        return pairs

    def to_plane(self, k):
        def move(y, c, z, x):
            half = (z // self.ny) ^ k
            plane = ((y // self.nc) * self.nc + c) * self.nc + half
            return (z % self.ny) ^ c, y % self.nc, plane, x

        return self.perm(move)

    def unit(self, c, z):
        return (z // (self.nc * self.nc)) * self.nc + c, (z // self.nc) % self.nc, z % self.nc

    def from_plane(self, k):
        return [(target, source) for source, target in self.to_plane(k)]

    def swap(self, ky=0, kc=0, kz=0, kx=0):
        return self.perm(lambda y, c, z, x: (y ^ ky, c ^ kc, z ^ kz, x ^ kx))

    def row_block(self, y, x, i):
        if self.halves > 1:
            return (i * self.ny + y) * self.nx + x
        return self.nc * (y * self.nx + x) + i

    def rows_to_chip(self):
        reader = {
            self.row_block(y, x, i): (y, x, i)
            for y in range(self.ny)
            for x in range(self.nx)
            for i in range(self.nc)
        }

        def move(y, c, z, x):
            chip_y, chip_x, i = reader[z * self.nx + x]
            return chip_y, i, c * self.ny + (y ^ (z & 1)), chip_x

        return self.perm(move)

    def to_owner(self):
        def move(y, c, z, x):
            s = self.row_block(y, x, c)
            return z // self.nc, z % self.nc, s // self.nx, s % self.nx

        return self.perm(move)

    def chip_of(self, k):
        return k // self.nx, k % self.nx

    def bits(self, count):
        return [1 << b for b in range(count.bit_length() - 1)]

    def chip_bits(self, j):
        bits = self.bits(self.chips)
        return bits if j % 2 == 0 else bits[::-1]

    def doubled(self, bits):
        held = [0]
        for bit in bits:
            held = held + [k ^ bit for k in held]
        return held

    def slots(self):
        return [(k, j) for k in range(self.chips) for j in range(self.nc)]


def slot_scalars(lay, pos_ref, info_ref, slot):
    k, j = slot
    ky, kx = lay.chip_of(k)
    _, group_c, half = lay.unit(pos_ref[1], pos_ref[2])
    z_frame = (half ^ j) * lay.ny + (pos_ref[0] ^ ky ^ group_c)
    frame = z_frame * lay.nx + (pos_ref[3] ^ kx)
    clip = info_ref[frame]
    clips = (info_ref.shape[0] - lay.frames) // 2
    return clip, info_ref[lay.frames + clip], info_ref[lay.frames + clips + clip]


def table_row(mod_ref, step, part, width):
    return mod_ref[pl.ds(step, 1), part * width : (part + 1) * width]


def allowed_pairs(lay, pos_ref, info_ref, patch_base):
    rows = lay.frames * BLOCK
    row_slot = lax.broadcasted_iota(jnp.int32, (rows, 1), 0) // BLOCK
    col_slot = lax.broadcasted_iota(jnp.int32, (1, rows), 1) // BLOCK
    row_clip = jnp.zeros((rows, 1), jnp.int32)
    row_limit = jnp.zeros((rows, 1), jnp.int32)
    col_clip = jnp.zeros((1, rows), jnp.int32)
    for t, slot in enumerate(lay.slots()):
        clip, limit, _ = slot_scalars(lay, pos_ref, info_ref, slot)
        row_clip = jnp.where(row_slot == t, clip, row_clip)
        row_limit = jnp.where(row_slot == t, limit, row_limit)
        col_clip = jnp.where(col_slot == t, clip, col_clip)
    row_patch = lax.broadcasted_iota(jnp.int32, (rows, 1), 0) % BLOCK
    col_patch = lax.broadcasted_iota(jnp.int32, (1, rows), 1) % BLOCK
    row_key = row_clip * BLOCK + row_patch
    col_key = col_clip * BLOCK + col_patch
    row_valid = (patch_base + row_patch < row_limit).astype(jnp.int32)
    row_index = lax.broadcasted_iota(jnp.int32, (rows, rows), 0)
    col_index = lax.broadcasted_iota(jnp.int32, (rows, rows), 1)
    return (row_key == col_key) & ((row_valid > 0) | (row_index == col_index))


def head_mask(values, head, head_size):
    lane = lax.broadcasted_iota(jnp.int32, (1, values.shape[1]), 1)
    inside = (lane >= head * head_size) & (lane < (head + 1) * head_size)
    return jnp.where(inside, values, jnp.zeros_like(values))


def patch_blocks(array, block):
    part = array[:, block * BLOCK : (block + 1) * BLOCK, :]
    return part.reshape(part.shape[0] * BLOCK, part.shape[2])


def start_kernel(lay, cols, pos_ref, x_ref, g_ref, w_ref, *refs):
    pair_refs, out_refs = refs[: lay.nc], refs[lay.nc :]
    half = x_ref.shape[1] // lay.nc
    for k, ref in enumerate(pair_refs):
        first = pl.multiple_of(((pos_ref[2] // lay.ny) ^ k) * half, 16)
        ref[0, 0] = x_ref[0, pl.ds(first, half), :]
        ref[0, 1] = g_ref[0, pl.ds(first, half), :]
    model = w_ref.shape[1] // 3
    for k, out_ref in enumerate(out_refs):
        chip_x = pos_ref[3] ^ k
        if lay.halves > 1:
            want = lay.row_block(pos_ref[0], chip_x, pos_ref[1])
        else:
            want = pos_ref[0] * lay.nx + chip_x
        for v in range(lay.chips * lay.halves):

            @pl.when(want == v)
            def _(v=v, out_ref=out_ref):
                parts = [
                    w_ref[:, p * model + v * cols : p * model + (v + 1) * cols]
                    for p in range(3)
                ]
                out_ref[...] = jnp.concatenate(parts, axis=1)


def fill_weights(lay, pos_ref, w_refs, w_scr):
    order = lay.doubled(lay.bits(lay.nz)[::-1])
    block = w_scr.shape[1] // lay.nz
    rows, width = w_refs[0].shape[1], w_scr.shape[2]
    for h in range(lay.halves):
        for n, k in enumerate(order):
            ref, place = w_refs[2 * h + (2 * n) // lay.nz], n % (lay.nz // 2)
            for m in range(block // rows):
                start = pl.multiple_of((pos_ref[2] ^ k) * block + m * rows, 16)
                w_scr[h, pl.ds(start, rows), :] = ref[place, :, m * width : (m + 1) * width]


def heads_stacked(lay, values):
    head_size = values.shape[1] // lay.half_heads
    parts = [head_mask(values, head, head_size) for head in range(lay.half_heads)]
    return jnp.concatenate(parts, axis=0) if len(parts) > 1 else parts[0]


def beside(lay, weights):
    return jnp.concatenate([weights[head] for head in range(lay.half_heads)], axis=1)


def attention_weights(lay, keys_stacked, queries, allowed, scaling):
    scores = dot_t(keys_stacked, queries) * scaling
    scores = jnp.where(allowed, scores.reshape((lay.half_heads,) + allowed.shape), -jnp.inf)
    exponent = jnp.exp(scores - jnp.max(scores, axis=1, keepdims=True))
    return exponent * (1.0 / jnp.sum(exponent, axis=1, keepdims=True))


def prepare_kernel(lay, pos_ref, info_ref, *refs):
    pair_refs, (mod_ref, hid_ref, gp_ref) = refs[: 2 * lay.nc], refs[2 * lay.nc :]
    _, step_patches, model = hid_ref.shape
    patches = step_patches * pl.num_programs(0)
    patch_base = lay.unit(pos_ref[1], pos_ref[2])[2] * patches + pl.program_id(0) * step_patches
    patch = patch_base + lax.broadcasted_iota(jnp.int32, (step_patches, 1), 0)
    for t, (k, j) in enumerate(lay.slots()):
        _, limit, step = slot_scalars(lay, pos_ref, info_ref, (k, j))
        n = lay.doubled(lay.chip_bits(j)).index(k)
        ref, place = pair_refs[2 * j + (2 * n) // lay.chips], n % (lay.chips // 2)
        normed, _ = normalize(ref[place, 0].astype(F32))
        shift, scale = table_row(mod_ref, step, 0, model), table_row(mod_ref, step, 1, model)
        hid_ref[t] = (normed * (1.0 + scale) + shift).astype(BF16)
        factor = jnp.where(patch < limit, table_row(mod_ref, step, 2, model), 0.0)
        gp_ref[t] = (factor * ref[place, 1].astype(F32)).astype(BF16)


def forward_kernel(lay, pos_ref, info_ref, hid_ref, gp_ref, *refs):
    w_refs, refs = refs[: 2 * lay.halves], refs[2 * lay.halves :]
    q_ref, k_ref, v_ref, att_ref, kept_ref, sent_ref, w_scr, acc_scr, cut_scr = refs
    _, step_patches, model = hid_ref.shape
    tokens = lay.frames * step_patches
    cols = w_scr.shape[2] // 3
    scaling = 1.0 / math.sqrt(cols // lay.half_heads)
    patches = step_patches * pl.num_programs(0)
    is_first = pos_ref[1] == 0

    @pl.when(pl.program_id(0) == 0)
    def _():
        fill_weights(lay, pos_ref, w_refs, w_scr)
        acc_scr[...] = jnp.zeros_like(acc_scr)

    hidden = hid_ref[...].reshape(lay.frames * step_patches, model)
    for h in range(lay.halves):
        triple = dot(hidden, w_scr[h])
        for n, ref in enumerate((q_ref, k_ref, v_ref)):
            ref[h] = triple[:, n * cols : (n + 1) * cols].astype(BF16).reshape(ref.shape[1:])

    for b in range(step_patches // BLOCK):
        patch_base = lay.unit(pos_ref[1], pos_ref[2])[2] * patches + pl.program_id(0) * step_patches + b * BLOCK
        allowed = allowed_pairs(lay, pos_ref, info_ref, patch_base)
        outputs = []
        for h in range(lay.halves):
            queries, keys, values = (patch_blocks(ref[h], b) for ref in (q_ref, k_ref, v_ref))
            weights = attention_weights(lay, heads_stacked(lay, keys), queries, allowed, scaling)
            weights = weights.astype(BF16).reshape(-1, allowed.shape[1])
            outputs.append(t_dot(weights, heads_stacked(lay, values)))
        if lay.halves > 1:
            first = jnp.where(pos_ref[1] == 0, outputs[0], outputs[1])
            second = jnp.where(pos_ref[1] == 0, outputs[1], outputs[0])
            outputs = [jnp.concatenate([first, second], axis=1)]
        attended = outputs[0].astype(BF16)
        att_ref[:, b * BLOCK : (b + 1) * BLOCK, :] = attended.reshape(lay.frames, BLOCK, -1)

    attended = att_ref[...].reshape(tokens, -1)
    acc_scr[...] += t_dot(attended, gp_ref[...].reshape(tokens, model))

    @pl.when(pl.program_id(0) == pl.num_programs(0) - 1)
    def _():
        groups, chunk_rows, chunk_width = kept_ref.shape
        block_rows, part = acc_scr.shape[0] // lay.nc, model // groups
        order = lay.doubled(lay.bits(lay.nz)[::-1])
        first, second = acc_scr[:block_rows, :], acc_scr[block_rows:, :]
        kept = jnp.where(is_first, first, second)
        sent = jnp.where(is_first, second, first)
        for ref, rows in ((kept_ref, kept), (sent_ref, sent)):
            for d in range(groups):
                chunk = [
                    rows[m * chunk_rows : (m + 1) * chunk_rows, d * part : (d + 1) * part]
                    for m in range(chunk_width // part)
                ]
                cut_scr[d] = jnp.concatenate(chunk, axis=1) if len(chunk) > 1 else chunk[0]
            for n, k in enumerate(order):
                ref[n] = cut_scr[pos_ref[2] ^ k]


def projection_kernel(lay, pos_ref, gp_ref, att_ref, *refs):
    wo_refs, (ga_ref, *refs) = refs[: lay.nc], refs[lay.nc :]
    pr_refs, (wo_scr,) = refs[: lay.chips], refs[lay.chips :]
    _, step_patches, model = gp_ref.shape
    tokens = lay.frames * step_patches
    is_first = pos_ref[1] == 0

    @pl.when(pl.program_id(0) == 0)
    def _():
        own, other = wo_refs[0][...].astype(F32), wo_refs[1][...].astype(F32)
        both = [jnp.where(is_first, own, other), jnp.where(is_first, other, own)]
        wo_scr[...] = jnp.concatenate(both, axis=0).astype(BF16)

    grad_attn = dot_t(gp_ref[...].reshape(tokens, model), wo_scr[...])
    part = wo_scr.shape[0] // lay.halves
    for h in range(lay.halves):
        ga_ref[h] = grad_attn[:, h * part : (h + 1) * part].astype(BF16).reshape(ga_ref.shape[1:])
    attended = att_ref[...].reshape(tokens, -1)
    projected = dot(attended, wo_scr[...]).reshape(lay.chips, lay.nc, step_patches, model)
    for k in range(lay.chips):
        pr_refs[k][...] = projected[k].astype(pr_refs[k].dtype)


def backward_kernel(lay, pos_ref, info_ref, *refs):
    w_refs, refs = refs[: 2 * lay.halves], refs[2 * lay.halves :]
    q_ref, k_ref, v_ref, ga_ref, *refs = refs
    gh_refs, (w_scr, gt_scr) = refs[: lay.chips], refs[lay.chips :]
    _, frames, step_patches, cols = q_ref.shape
    model = w_scr.shape[1]
    patches = step_patches * pl.num_programs(0)
    scaling = 1.0 / math.sqrt(cols // lay.half_heads)

    @pl.when(pl.program_id(0) == 0)
    def _():
        fill_weights(lay, pos_ref, w_refs, w_scr)

    for b in range(step_patches // BLOCK):
        patch_base = lay.unit(pos_ref[1], pos_ref[2])[2] * patches + pl.program_id(0) * step_patches + b * BLOCK
        allowed = allowed_pairs(lay, pos_ref, info_ref, patch_base)
        for h in range(lay.halves):
            queries, keys, values = (patch_blocks(ref[h], b) for ref in (q_ref, k_ref, v_ref))
            grad_out = patch_blocks(ga_ref[(pos_ref[1] ^ h) if lay.halves > 1 else 0], b)
            keys = heads_stacked(lay, keys)
            weights = attention_weights(lay, keys, queries, allowed, scaling)
            grad_weights = dot_t(heads_stacked(lay, values), grad_out).reshape(weights.shape)
            grad_values = dot(beside(lay, weights.astype(BF16)), heads_stacked(lay, grad_out))
            inner = jnp.sum(weights * grad_weights, axis=1, keepdims=True)
            grad_scores = (weights * (grad_weights - inner) * scaling).astype(BF16)
            grad_queries = t_dot(grad_scores.reshape(-1, grad_scores.shape[2]), keys)
            grad_keys = dot(beside(lay, grad_scores), heads_stacked(lay, queries))
            grads = jnp.concatenate([grad_queries, grad_keys, grad_values], axis=1).astype(BF16)
            gt_scr[h, :, b * BLOCK : (b + 1) * BLOCK, :] = grads.reshape(frames, BLOCK, 3 * cols)

    rows = lay.nc * step_patches
    for k in range(lay.chips):
        total = jnp.zeros((rows, model), F32)
        for h in range(lay.halves):
            part = gt_scr[h, k * lay.nc : (k + 1) * lay.nc].reshape(rows, 3 * cols)
            total = total + dot_t(part, w_scr[h])
        gh_refs[k][...] = total.reshape(gh_refs[k].shape).astype(gh_refs[k].dtype)


def output_kernel(lay, pos_ref, info_ref, *refs):
    pair_refs, refs = refs[: lay.nc], refs[lay.nc :]
    pr_refs, refs = refs[: lay.chips], refs[lay.chips :]
    mod_ref, *out_refs = refs
    step_patches, model = out_refs[0].shape
    patches = step_patches * pl.num_programs(0)
    patch_base = lay.unit(pos_ref[1], pos_ref[2])[2] * patches + pl.program_id(0) * step_patches
    patch = patch_base + lax.broadcasted_iota(jnp.int32, (step_patches, 1), 0)
    for j in range(lay.nc):
        _, limit, step = slot_scalars(lay, pos_ref, info_ref, (0, j))
        factor = jnp.where(patch < limit, table_row(mod_ref, step, 2, model), 0.0)
        projected = pr_refs[0][j]
        for k in range(1, lay.chips):
            projected = projected + pr_refs[k][j].astype(F32)
        projected = projected.astype(BF16).astype(F32)
        out_refs[j][...] = (pair_refs[j][0, 0].astype(F32) + factor * projected).astype(BF16)


def input_grad_kernel(lay, pos_ref, info_ref, *refs):
    pair_refs, refs = refs[: lay.nc], refs[lay.nc :]
    gh_refs, refs = refs[: lay.chips], refs[lay.chips :]
    mod_ref, *out_refs = refs
    model = out_refs[0].shape[1]
    for j in range(lay.nc):
        _, _, step = slot_scalars(lay, pos_ref, info_ref, (0, j))
        grad_hidden = gh_refs[0][j]
        for k in range(1, lay.chips):
            grad_hidden = grad_hidden + gh_refs[k][j].astype(F32)
        grad_hidden = grad_hidden.astype(BF16).astype(F32)
        normed, inv_sigma = normalize(pair_refs[j][0, 0].astype(F32))
        grad_norm = grad_hidden * (1.0 + table_row(mod_ref, step, 1, model))
        first_mean = jnp.mean(grad_norm, axis=-1, keepdims=True)
        second_mean = jnp.mean(grad_norm * normed, axis=-1, keepdims=True)
        grad_x = pair_refs[j][0, 1].astype(F32) + inv_sigma * (
            grad_norm - first_mean - normed * second_mean
        )
        out_refs[j][...] = grad_x.astype(BF16)


def whole_spec(shape):
    return pl.BlockSpec(shape, lambda *_: (0,) * len(shape))


def struct(shape, dtype=BF16):
    return jax.ShapeDtypeStruct(shape, dtype)


def local(lay, frames_x, grad_y, clip_ids, clip_patches, clip_step, mod_table, w_qkv, w_out):
    y, c, z, x = (lax.axis_index(name) for name in AXES)
    _, patches, model = frames_x.shape
    half = patches // lay.nc
    chips, nc, nx = lay.chips, lay.nc, lay.nx
    head_size = model // HEADS
    halves = lay.halves
    cols = lay.half_heads * head_size
    chip_width = lay.chip_heads * head_size
    rows = w_qkv.shape[0]
    groups = lay.nz
    quarter = model // groups
    step_patches = max(BLOCK, min(half, 512 // lay.frames))
    steps = half // step_patches
    tokens = lay.frames * step_patches

    def call(kernel, name, cost, in_specs, out_specs, out_shape, scratch=(), grid=(1,), prefetch=2):
        return pl.pallas_call(
            kernel,
            grid_spec=pltpu.PrefetchScalarGridSpec(
                num_scalar_prefetch=prefetch,
                grid=grid,
                in_specs=in_specs,
                out_specs=out_specs,
                scratch_shapes=list(scratch),
            ),
            out_shape=out_shape,
            compiler_params=pltpu.CompilerParams(vmem_limit_bytes=VMEM_LIMIT),
            cost_estimate=pl.CostEstimate(
                flops=cost * tokens * steps, bytes_accessed=4 * model * tokens, transcendentals=0
            ),
            name=name,
        )

    def chip_swap(k):
        ky, kx = lay.chip_of(k)
        return lay.swap(ky=ky, kx=kx)

    def from_plane(parts):
        got = [lax.ppermute(part, AXES, lay.from_plane(k)) for k, part in enumerate(parts)]
        first = jnp.where(z // lay.ny == 0, got[0], got[1])
        second = jnp.where(z // lay.ny == 0, got[1], got[0])
        return jnp.concatenate([first, second], axis=0)[None]

    def doubling(held, bits, swap, after, first=None):
        for bit in bits[:-1]:
            got = lax.ppermute(held, AXES, swap(bit)) if first is None else first
            held, first = jnp.concatenate([held, got], axis=0), None
        held, _ = lax.optimization_barrier((held, after))
        return [held, lax.ppermute(held, AXES, swap(bits[-1]))]

    def over_chips(parts):
        got = [lax.ppermute(parts[k], AXES, chip_swap(k)) for k in range(1, chips)]
        return [parts[0]] + got

    info = jnp.concatenate([clip_ids[0], clip_patches[0], clip_step[0]])[None]
    by_core = jnp.concatenate([info, lax.ppermute(info, AXES, lay.swap(kc=1))], axis=0)
    info = [by_core] + [
        lax.ppermute(by_core, AXES, lay.swap(ky=ky)) for ky in range(1, lay.ny)
    ]
    group_y, group_c, _ = lay.unit(c, z)
    info = sum(
        jnp.where((y ^ ky == group_y) & (c ^ kc == group_c), info[ky][kc], 0)
        for ky in range(lay.ny)
        for kc in range(nc)
    )
    pos = jnp.stack([y, c, z, x]).astype(jnp.int32)
    pair_shape = (1, 2, half, model)
    outputs = call(
        functools.partial(start_kernel, lay, cols),
        "start",
        2 * model * 1000,
        [whole_spec(frames_x.shape)] * 2 + [whole_spec(w_qkv.shape)],
        [whole_spec(pair_shape)] * nc + [whole_spec((rows, 3 * cols))] * nx,
        [struct(pair_shape)] * nc + [struct((rows, 3 * cols))] * nx,
        prefetch=1,
    )(pos, frames_x, grad_y, w_qkv)
    pairs, picked = outputs[:nc], outputs[nc:]
    own = [lax.ppermute(pair, AXES, lay.to_plane(k)) for k, pair in enumerate(pairs)]
    by_x = [picked[0]] + [
        lax.ppermute(picked[kx], AXES, lay.swap(kx=kx)) for kx in range(1, nx)
    ]
    if nx == 2:
        ordered = [jnp.where(x == i, by_x[0], by_x[1]) for i in range(nx)]
    else:
        stacked = jnp.stack(by_x)
        ordered = [lax.dynamic_index_in_dim(stacked, x ^ i, 0, keepdims=False) for i in range(nx)]
    w_own = jnp.concatenate(ordered, axis=1 if rows % 16 == 0 else 0)[None]
    first = lax.ppermute(own[0], AXES, chip_swap(lay.chip_bits(0)[0]))
    own[1], first = lax.optimization_barrier((own[1], first))
    w_own, _ = lax.optimization_barrier((w_own, own[1]))
    w_pieces = doubling(w_own, lay.bits(lay.nz)[::-1], lambda kz: lay.swap(kz=kz), [])
    late_w_out, _ = lax.optimization_barrier((w_out, w_pieces))
    wo_own = lax.ppermute(late_w_out, AXES, lay.rows_to_chip())

    pairs = []
    for j in range(nc):
        after = ([], None) if j else (info, first)
        pairs += doubling(own[j], lay.chip_bits(j), chip_swap, *after)
    pairs, w_pieces = lax.optimization_barrier((pairs, w_pieces))
    if halves > 1:
        w_pieces += [lax.ppermute(piece, AXES, lay.swap(kc=1)) for piece in w_pieces]


    def spread(count, width, patches_at_once):
        return pl.BlockSpec((count, patches_at_once, width), lambda i, *_: (0, i, 0))

    def pair_spec(count, patches_at_once):
        return pl.BlockSpec((count, 2, patches_at_once, model), lambda i, *_: (0, 0, i, 0))

    few = max(BLOCK, step_patches // 2)
    few_steps = half // few
    x_spec = pl.BlockSpec((few, model), lambda i, *_: (i, 0))
    triple_spec = pl.BlockSpec((halves, lay.frames, step_patches, cols), lambda i, *_: (0, 0, i, 0))
    w_specs = [whole_spec(w_pieces[0].shape)] * (2 * halves)
    w_scratch = pltpu.VMEM((halves, model, 3 * cols), BF16)
    mod_spec = whole_spec(mod_table.shape)
    triple_shape = struct((halves, lay.frames, half, cols))
    part_specs = [spread(nc, model, step_patches)] * chips
    part_shapes = [struct((nc, half, model), F32)] + [struct((nc, half, model))] * (chips - 1)

    hidden, grad_proj = call(
        functools.partial(prepare_kernel, lay),
        "prepare",
        3 * model * 1000,
        [pair_spec(chips // 2, few)] * (2 * nc) + [mod_spec],
        [spread(lay.frames, model, few)] * 2,
        [struct((lay.frames, half, model))] * 2,
        grid=(few_steps,),
    )(pos, info, *pairs, mod_table)
    wo_own, _ = lax.optimization_barrier((wo_own, hidden))
    wo_rows = [wo_own, lax.ppermute(wo_own, AXES, lay.swap(kc=1))]

    fold = 3 if rows % 24 == 0 else 1
    piece_shape = (groups, rows // fold, quarter * fold)
    token_spec = spread(lay.frames, model, step_patches)
    att_spec = spread(lay.frames, chip_width, step_patches)
    queries, keys, values, attended, kept, sent = call(
        functools.partial(forward_kernel, lay),
        "forward",
        14 * model * 1000,
        [token_spec] * 2 + w_specs,
        [triple_spec] * 3 + [att_spec] + [whole_spec(piece_shape)] * 2,
        [triple_shape] * 3
        + [struct((lay.frames, half, chip_width))]
        + [struct(piece_shape, F32)] * 2,
        [w_scratch, pltpu.VMEM((chip_width, model), F32), pltpu.VMEM(piece_shape, F32)],
        (steps,),
    )(pos, info, hidden, grad_proj, *w_pieces)
    got = lax.ppermute(sent, AXES, lay.swap(kc=1))

    grad_attn, *projected = call(
        functools.partial(projection_kernel, lay),
        "projection",
        6 * model * 1000,
        [token_spec, att_spec] + [whole_spec(w_out.shape)] * nc,
        [triple_spec] + part_specs,
        [triple_shape] + part_shapes,
        [pltpu.VMEM((chip_width, model), BF16)],
        (steps,),
        prefetch=1,
    )(pos, grad_proj, attended, *wo_rows)
    projected = over_chips(projected)

    middle = groups // 2
    cut, away = kept[:middle] + got[:middle], kept[middle:] + got[middle:]
    grad_attn, cut, away = lax.optimization_barrier((grad_attn, cut, away))
    first_away = lax.ppermute(away, AXES, lay.swap(kz=1))

    sums = call(
        functools.partial(backward_kernel, lay),
        "backward",
        10 * model * 1000,
        w_specs + [triple_spec] * 4,
        part_specs,
        part_shapes,
        [w_scratch, pltpu.VMEM((halves, lay.frames, step_patches, 3 * cols), BF16)],
        (steps,),
    )(pos, info, *w_pieces, queries, keys, values, grad_attn)
    sums, first_away, projected = lax.optimization_barrier((sums, first_away, projected))
    grad_hidden = over_chips(sums)

    out_parts = call(
        functools.partial(output_kernel, lay),
        "output",
        20 * model * 1000,
        [pair_spec(1, few)] * nc + [spread(nc, model, few)] * chips + [mod_spec],
        [x_spec] * nc,
        [struct((half, model))] * nc,
        grid=(few_steps,),
    )(pos, info, *own, *projected, mod_table)
    out_y = from_plane(out_parts)

    grad_hidden, _ = lax.optimization_barrier((grad_hidden, out_parts))
    grad_parts = call(
        functools.partial(input_grad_kernel, lay),
        "input_grad",
        3 * model * 1000,
        [pair_spec(1, few)] * nc + [spread(nc, model, few)] * chips + [mod_spec],
        [x_spec] * nc,
        [struct((half, model))] * nc,
        grid=(few_steps,),
    )(pos, info, *own, *grad_hidden, mod_table)
    grad_x = from_plane(grad_parts)

    cut, _ = lax.optimization_barrier((cut + first_away, out_parts))
    for bit in lay.bits(lay.nz)[1:]:
        middle = middle // 2
        cut = cut[:middle] + lax.ppermute(cut[middle:], AXES, lay.swap(kz=bit))
    cut, _ = lax.optimization_barrier((cut, grad_parts))
    grad_w = lax.ppermute(cut[0], AXES, lay.to_owner())
    grad_w = jnp.concatenate(
        [grad_w[:, m * quarter : (m + 1) * quarter] for m in range(fold)], axis=0
    )
    grad_w_out = grad_w * jnp.float32(1.0 / math.sqrt(groups * lay.frames * patches))
    return out_y, grad_x, grad_w_out


def solution(mesh):
    lay = Layout(mesh)
    grid = Mesh(mesh.devices.reshape(lay.ny, lay.nc, lay.nz, lay.nx), AXES)
    rows, cols = ("z", "x"), ("y", "c")
    frame = P(AXES, None, None)
    group = P(cols, None)
    return jax.shard_map(
        functools.partial(local, lay),
        mesh=grid,
        in_specs=(frame, frame, group, group, group, P(), P(rows, None), P(rows, None)),
        out_specs=(frame, frame, P(rows, cols)),
        check_vma=False,
    )
```

```python
import functools
import math

import jax
import jax.numpy as jnp
from jax import lax
from jax.experimental import pallas as pl
from jax.experimental.pallas import tpu as pltpu
from jax.sharding import Mesh, PartitionSpec as P

HEADS = 16
CORES = 2
AXES = ("y", "c", "z", "x")
BLOCK = 16
VMEM_LIMIT = 56 * 1024 * 1024
BF16 = jnp.bfloat16
F32 = jnp.float32


def dot(left, right):
    return jnp.dot(left, right, preferred_element_type=F32)


def dot_t(left, right):
    return lax.dot_general(left, right, (((1,), (1,)), ((), ())), preferred_element_type=F32)


def t_dot(left, right):
    return lax.dot_general(left, right, (((0,), (0,)), ((), ())), preferred_element_type=F32)


def normalize(values):
    centred = values - jnp.mean(values, axis=-1, keepdims=True)
    inv_sigma = lax.rsqrt(jnp.mean(centred * centred, axis=-1, keepdims=True) + 1e-06)
    return centred * inv_sigma, inv_sigma


class Layout:
    def __init__(self, mesh):
        groups, seq = mesh.shape["dp"], mesh.shape["seq"]
        self.nc = CORES
        self.ny = groups // CORES
        self.nz = groups
        self.nx = seq // self.nz
        self.chips = self.ny * self.nx
        self.frames = seq
        self.chip_heads = HEADS // self.chips
        self.halves = 2 if self.chip_heads % 2 == 0 else 1
        self.half_heads = self.chip_heads // self.halves

    def linear(self, y, c, z, x):
        return ((y * self.nc + c) * self.nz + z) * self.nx + x

    def perm(self, move):
        pairs = []
        for y in range(self.ny):
            for c in range(self.nc):
                for z in range(self.nz):
                    for x in range(self.nx):
                        pairs.append((self.linear(y, c, z, x), self.linear(*move(y, c, z, x))))
        return pairs

    def to_plane(self, k):
        def move(y, c, z, x):
            half = (z // self.ny) ^ k
            plane = ((y // self.nc) * self.nc + c) * self.nc + half
            return (z % self.ny) ^ c, y % self.nc, plane, x

        return self.perm(move)

    def unit(self, c, z):
        return (z // (self.nc * self.nc)) * self.nc + c, (z // self.nc) % self.nc, z % self.nc

    def from_plane(self, k):
        return [(target, source) for source, target in self.to_plane(k)]

    def swap(self, ky=0, kc=0, kz=0, kx=0):
        return self.perm(lambda y, c, z, x: (y ^ ky, c ^ kc, z ^ kz, x ^ kx))

    def row_block(self, y, x, i):
        if self.halves > 1:
            return (i * self.ny + y) * self.nx + x
        return self.nc * (y * self.nx + x) + i

    def rows_to_chip(self):
        reader = {
            self.row_block(y, x, i): (y, x, i)
            for y in range(self.ny)
            for x in range(self.nx)
            for i in range(self.nc)
        }

        def move(y, c, z, x):
            chip_y, chip_x, i = reader[z * self.nx + x]
            return chip_y, i, c * self.ny + (y ^ (z & 1)), chip_x

        return self.perm(move)

    def to_owner(self):
        def move(y, c, z, x):
            s = self.row_block(y, x, c)
            return z // self.nc, z % self.nc, s // self.nx, s % self.nx

        return self.perm(move)

    def chip_of(self, k):
        return k // self.nx, k % self.nx

    def bits(self, count):
        return [1 << b for b in range(count.bit_length() - 1)]

    def chip_bits(self, j):
        bits = self.bits(self.chips)
        return bits if j % 2 == 0 else bits[::-1]

    def doubled(self, bits):
        held = [0]
        for bit in bits:
            held = held + [k ^ bit for k in held]
        return held

    def slots(self):
        return [(k, j) for k in range(self.chips) for j in range(self.nc)]


def slot_scalars(lay, pos_ref, info_ref, slot):
    k, j = slot
    ky, kx = lay.chip_of(k)
    _, group_c, half = lay.unit(pos_ref[1], pos_ref[2])
    z_frame = (half ^ j) * lay.ny + (pos_ref[0] ^ ky ^ group_c)
    frame = z_frame * lay.nx + (pos_ref[3] ^ kx)
    clip = info_ref[frame]
    clips = (info_ref.shape[0] - lay.frames) // 2
    return clip, info_ref[lay.frames + clip], info_ref[lay.frames + clips + clip]


def table_row(mod_ref, step, part, width):
    return mod_ref[pl.ds(step, 1), part * width : (part + 1) * width]


def allowed_pairs(lay, pos_ref, info_ref, patch_base):
    rows = lay.frames * BLOCK
    row_slot = lax.broadcasted_iota(jnp.int32, (rows, 1), 0) // BLOCK
    col_slot = lax.broadcasted_iota(jnp.int32, (1, rows), 1) // BLOCK
    row_clip = jnp.zeros((rows, 1), jnp.int32)
    row_limit = jnp.zeros((rows, 1), jnp.int32)
    col_clip = jnp.zeros((1, rows), jnp.int32)
    for t, slot in enumerate(lay.slots()):
        clip, limit, _ = slot_scalars(lay, pos_ref, info_ref, slot)
        row_clip = jnp.where(row_slot == t, clip, row_clip)
        row_limit = jnp.where(row_slot == t, limit, row_limit)
        col_clip = jnp.where(col_slot == t, clip, col_clip)
    row_patch = lax.broadcasted_iota(jnp.int32, (rows, 1), 0) % BLOCK
    col_patch = lax.broadcasted_iota(jnp.int32, (1, rows), 1) % BLOCK
    row_key = row_clip * BLOCK + row_patch
    col_key = col_clip * BLOCK + col_patch
    row_valid = (patch_base + row_patch < row_limit).astype(jnp.int32)
    row_index = lax.broadcasted_iota(jnp.int32, (rows, rows), 0)
    col_index = lax.broadcasted_iota(jnp.int32, (rows, rows), 1)
    return (row_key == col_key) & ((row_valid > 0) | (row_index == col_index))


def head_mask(values, head, head_size):
    lane = lax.broadcasted_iota(jnp.int32, (1, values.shape[1]), 1)
    inside = (lane >= head * head_size) & (lane < (head + 1) * head_size)
    return jnp.where(inside, values, jnp.zeros_like(values))


def patch_blocks(array, block):
    part = array[:, block * BLOCK : (block + 1) * BLOCK, :]
    return part.reshape(part.shape[0] * BLOCK, part.shape[2])


def start_kernel(lay, cols, pos_ref, x_ref, g_ref, w_ref, *refs):
    pair_refs, out_refs = refs[: lay.nc], refs[lay.nc :]
    half = x_ref.shape[1] // lay.nc
    for k, ref in enumerate(pair_refs):
        first = pl.multiple_of(((pos_ref[2] // lay.ny) ^ k) * half, 16)
        ref[0, 0] = x_ref[0, pl.ds(first, half), :]
        ref[0, 1] = g_ref[0, pl.ds(first, half), :]
    model = w_ref.shape[1] // 3
    for k, out_ref in enumerate(out_refs):
        chip_x = pos_ref[3] ^ k
        if lay.halves > 1:
            want = lay.row_block(pos_ref[0], chip_x, pos_ref[1])
        else:
            want = pos_ref[0] * lay.nx + chip_x
        for v in range(lay.chips * lay.halves):

            @pl.when(want == v)
            def _(v=v, out_ref=out_ref):
                parts = [
                    w_ref[:, p * model + v * cols : p * model + (v + 1) * cols]
                    for p in range(3)
                ]
                out_ref[...] = jnp.concatenate(parts, axis=1)


def fill_weights(lay, pos_ref, w_refs, w_scr):
    order = lay.doubled(lay.bits(lay.nz)[::-1])
    block = w_scr.shape[1] // lay.nz
    rows, width = w_refs[0].shape[1], w_scr.shape[2]
    for h in range(lay.halves):
        for n, k in enumerate(order):
            ref, place = w_refs[2 * h + (2 * n) // lay.nz], n % (lay.nz // 2)
            for m in range(block // rows):
                start = pl.multiple_of((pos_ref[2] ^ k) * block + m * rows, 16)
                w_scr[h, pl.ds(start, rows), :] = ref[place, :, m * width : (m + 1) * width]


def heads_stacked(lay, values):
    head_size = values.shape[1] // lay.half_heads
    parts = [head_mask(values, head, head_size) for head in range(lay.half_heads)]
    return jnp.concatenate(parts, axis=0) if len(parts) > 1 else parts[0]


def beside(lay, weights):
    return jnp.concatenate([weights[head] for head in range(lay.half_heads)], axis=1)


def attention_weights(lay, keys_stacked, queries, allowed, scaling):
    scores = dot_t(keys_stacked, queries) * scaling
    scores = jnp.where(allowed, scores.reshape((lay.half_heads,) + allowed.shape), -jnp.inf)
    exponent = jnp.exp(scores - jnp.max(scores, axis=1, keepdims=True))
    return exponent * (1.0 / jnp.sum(exponent, axis=1, keepdims=True))


def prepare_kernel(lay, pos_ref, info_ref, *refs):
    pair_refs, (mod_ref, hid_ref, gp_ref) = refs[: 2 * lay.nc], refs[2 * lay.nc :]
    _, step_patches, model = hid_ref.shape
    patches = step_patches * pl.num_programs(0)
    patch_base = lay.unit(pos_ref[1], pos_ref[2])[2] * patches + pl.program_id(0) * step_patches
    patch = patch_base + lax.broadcasted_iota(jnp.int32, (step_patches, 1), 0)
    for t, (k, j) in enumerate(lay.slots()):
        _, limit, step = slot_scalars(lay, pos_ref, info_ref, (k, j))
        n = lay.doubled(lay.chip_bits(j)).index(k)
        ref, place = pair_refs[2 * j + (2 * n) // lay.chips], n % (lay.chips // 2)
        normed, _ = normalize(ref[place, 0].astype(F32))
        shift, scale = table_row(mod_ref, step, 0, model), table_row(mod_ref, step, 1, model)
        hid_ref[t] = (normed * (1.0 + scale) + shift).astype(BF16)
        factor = jnp.where(patch < limit, table_row(mod_ref, step, 2, model), 0.0)
        gp_ref[t] = (factor * ref[place, 1].astype(F32)).astype(BF16)


def forward_kernel(lay, pos_ref, info_ref, hid_ref, gp_ref, *refs):
    w_refs, refs = refs[: 2 * lay.halves], refs[2 * lay.halves :]
    wo_refs, refs = refs[: lay.nc], refs[lay.nc :]
    q_ref, k_ref, v_ref, ga_ref, kept_ref, sent_ref, *refs = refs
    pr_refs, (w_scr, att_scr, wo_scr, acc_scr, cut_scr) = refs[: lay.chips], refs[lay.chips :]
    _, step_patches, model = hid_ref.shape
    tokens = lay.frames * step_patches
    cols = w_scr.shape[2] // 3
    scaling = 1.0 / math.sqrt(cols // lay.half_heads)
    patches = step_patches * pl.num_programs(0)
    is_first = pos_ref[1] == 0

    @pl.when(pl.program_id(0) == 0)
    def _():
        fill_weights(lay, pos_ref, w_refs, w_scr)
        own, other = wo_refs[0][...].astype(F32), wo_refs[1][...].astype(F32)
        both = [jnp.where(is_first, own, other), jnp.where(is_first, other, own)]
        wo_scr[...] = jnp.concatenate(both, axis=0).astype(BF16)
        acc_scr[...] = jnp.zeros_like(acc_scr)

    hidden = hid_ref[...].reshape(lay.frames * step_patches, model)
    for h in range(lay.halves):
        triple = dot(hidden, w_scr[h])
        for n, ref in enumerate((q_ref, k_ref, v_ref)):
            ref[h] = triple[:, n * cols : (n + 1) * cols].astype(BF16).reshape(ref.shape[1:])

    for b in range(step_patches // BLOCK):
        patch_base = lay.unit(pos_ref[1], pos_ref[2])[2] * patches + pl.program_id(0) * step_patches + b * BLOCK
        allowed = allowed_pairs(lay, pos_ref, info_ref, patch_base)
        outputs = []
        for h in range(lay.halves):
            queries, keys, values = (patch_blocks(ref[h], b) for ref in (q_ref, k_ref, v_ref))
            weights = attention_weights(lay, heads_stacked(lay, keys), queries, allowed, scaling)
            weights = weights.astype(BF16).reshape(-1, allowed.shape[1])
            outputs.append(t_dot(weights, heads_stacked(lay, values)))
        if lay.halves > 1:
            first = jnp.where(pos_ref[1] == 0, outputs[0], outputs[1])
            second = jnp.where(pos_ref[1] == 0, outputs[1], outputs[0])
            outputs = [jnp.concatenate([first, second], axis=1)]
        attended = outputs[0].astype(BF16)
        att_scr[:, b * BLOCK : (b + 1) * BLOCK, :] = attended.reshape(lay.frames, BLOCK, -1)

    attended = att_scr[...].reshape(tokens, -1)
    grad_proj = gp_ref[...].reshape(tokens, model)
    acc_scr[...] += t_dot(attended, grad_proj)
    grad_attn = dot_t(grad_proj, wo_scr[...])
    part = wo_scr.shape[0] // lay.halves
    for h in range(lay.halves):
        ga_ref[h] = grad_attn[:, h * part : (h + 1) * part].astype(BF16).reshape(ga_ref.shape[1:])
    projected = dot(attended, wo_scr[...]).reshape(lay.chips, lay.nc, step_patches, model)
    for k in range(lay.chips):
        pr_refs[k][...] = projected[k].astype(pr_refs[k].dtype)

    @pl.when(pl.program_id(0) == pl.num_programs(0) - 1)
    def _():
        groups, chunk_rows, chunk_width = kept_ref.shape
        block_rows, part = acc_scr.shape[0] // lay.nc, model // groups
        order = lay.doubled(lay.bits(lay.nz)[::-1])
        first, second = acc_scr[:block_rows, :], acc_scr[block_rows:, :]
        kept = jnp.where(is_first, first, second)
        sent = jnp.where(is_first, second, first)
        for ref, rows in ((kept_ref, kept), (sent_ref, sent)):
            for d in range(groups):
                chunk = [
                    rows[m * chunk_rows : (m + 1) * chunk_rows, d * part : (d + 1) * part]
                    for m in range(chunk_width // part)
                ]
                cut_scr[d] = jnp.concatenate(chunk, axis=1) if len(chunk) > 1 else chunk[0]
            for n, k in enumerate(order):
                ref[n] = cut_scr[pos_ref[2] ^ k]


def backward_kernel(lay, pos_ref, info_ref, *refs):
    w_refs, refs = refs[: 2 * lay.halves], refs[2 * lay.halves :]
    q_ref, k_ref, v_ref, ga_ref, *refs = refs
    gh_refs, (w_scr, gt_scr) = refs[: lay.chips], refs[lay.chips :]
    _, frames, step_patches, cols = q_ref.shape
    model = w_scr.shape[1]
    patches = step_patches * pl.num_programs(0)
    scaling = 1.0 / math.sqrt(cols // lay.half_heads)

    @pl.when(pl.program_id(0) == 0)
    def _():
        fill_weights(lay, pos_ref, w_refs, w_scr)

    for b in range(step_patches // BLOCK):
        patch_base = lay.unit(pos_ref[1], pos_ref[2])[2] * patches + pl.program_id(0) * step_patches + b * BLOCK
        allowed = allowed_pairs(lay, pos_ref, info_ref, patch_base)
        for h in range(lay.halves):
            queries, keys, values = (patch_blocks(ref[h], b) for ref in (q_ref, k_ref, v_ref))
            grad_out = patch_blocks(ga_ref[(pos_ref[1] ^ h) if lay.halves > 1 else 0], b)
            keys = heads_stacked(lay, keys)
            weights = attention_weights(lay, keys, queries, allowed, scaling)
            grad_weights = dot_t(heads_stacked(lay, values), grad_out).reshape(weights.shape)
            grad_values = dot(beside(lay, weights.astype(BF16)), heads_stacked(lay, grad_out))
            inner = jnp.sum(weights * grad_weights, axis=1, keepdims=True)
            grad_scores = (weights * (grad_weights - inner) * scaling).astype(BF16)
            grad_queries = t_dot(grad_scores.reshape(-1, grad_scores.shape[2]), keys)
            grad_keys = dot(beside(lay, grad_scores), heads_stacked(lay, queries))
            grads = jnp.concatenate([grad_queries, grad_keys, grad_values], axis=1).astype(BF16)
            gt_scr[h, :, b * BLOCK : (b + 1) * BLOCK, :] = grads.reshape(frames, BLOCK, 3 * cols)

    rows = lay.nc * step_patches
    for k in range(lay.chips):
        total = jnp.zeros((rows, model), F32)
        for h in range(lay.halves):
            part = gt_scr[h, k * lay.nc : (k + 1) * lay.nc].reshape(rows, 3 * cols)
            total = total + dot_t(part, w_scr[h])
        gh_refs[k][...] = total.reshape(gh_refs[k].shape).astype(gh_refs[k].dtype)


def output_kernel(lay, pos_ref, info_ref, *refs):
    pair_refs, refs = refs[: lay.nc], refs[lay.nc :]
    pr_refs, refs = refs[: lay.chips], refs[lay.chips :]
    mod_ref, *out_refs = refs
    step_patches, model = out_refs[0].shape
    patches = step_patches * pl.num_programs(0)
    patch_base = lay.unit(pos_ref[1], pos_ref[2])[2] * patches + pl.program_id(0) * step_patches
    patch = patch_base + lax.broadcasted_iota(jnp.int32, (step_patches, 1), 0)
    for j in range(lay.nc):
        _, limit, step = slot_scalars(lay, pos_ref, info_ref, (0, j))
        factor = jnp.where(patch < limit, table_row(mod_ref, step, 2, model), 0.0)
        projected = pr_refs[0][j]
        for k in range(1, lay.chips):
            projected = projected + pr_refs[k][j].astype(F32)
        projected = projected.astype(BF16).astype(F32)
        out_refs[j][...] = (pair_refs[j][0, 0].astype(F32) + factor * projected).astype(BF16)


def input_grad_kernel(lay, pos_ref, info_ref, *refs):
    pair_refs, refs = refs[: lay.nc], refs[lay.nc :]
    gh_refs, refs = refs[: lay.chips], refs[lay.chips :]
    mod_ref, *out_refs = refs
    model = out_refs[0].shape[1]
    for j in range(lay.nc):
        _, _, step = slot_scalars(lay, pos_ref, info_ref, (0, j))
        grad_hidden = gh_refs[0][j]
        for k in range(1, lay.chips):
            grad_hidden = grad_hidden + gh_refs[k][j].astype(F32)
        grad_hidden = grad_hidden.astype(BF16).astype(F32)
        normed, inv_sigma = normalize(pair_refs[j][0, 0].astype(F32))
        grad_norm = grad_hidden * (1.0 + table_row(mod_ref, step, 1, model))
        first_mean = jnp.mean(grad_norm, axis=-1, keepdims=True)
        second_mean = jnp.mean(grad_norm * normed, axis=-1, keepdims=True)
        grad_x = pair_refs[j][0, 1].astype(F32) + inv_sigma * (
            grad_norm - first_mean - normed * second_mean
        )
        out_refs[j][...] = grad_x.astype(BF16)


def whole_spec(shape):
    return pl.BlockSpec(shape, lambda *_: (0,) * len(shape))


def struct(shape, dtype=BF16):
    return jax.ShapeDtypeStruct(shape, dtype)


def local(lay, frames_x, grad_y, clip_ids, clip_patches, clip_step, mod_table, w_qkv, w_out):
    y, c, z, x = (lax.axis_index(name) for name in AXES)
    _, patches, model = frames_x.shape
    half = patches // lay.nc
    chips, nc, nx = lay.chips, lay.nc, lay.nx
    head_size = model // HEADS
    halves = lay.halves
    cols = lay.half_heads * head_size
    chip_width = lay.chip_heads * head_size
    rows = w_qkv.shape[0]
    groups = lay.nz
    quarter = model // groups
    step_patches = max(BLOCK, min(half, 512 // lay.frames))
    steps = half // step_patches
    tokens = lay.frames * step_patches

    def call(kernel, name, cost, in_specs, out_specs, out_shape, scratch=(), grid=(1,), prefetch=2):
        return pl.pallas_call(
            kernel,
            grid_spec=pltpu.PrefetchScalarGridSpec(
                num_scalar_prefetch=prefetch,
                grid=grid,
                in_specs=in_specs,
                out_specs=out_specs,
                scratch_shapes=list(scratch),
            ),
            out_shape=out_shape,
            compiler_params=pltpu.CompilerParams(vmem_limit_bytes=VMEM_LIMIT),
            cost_estimate=pl.CostEstimate(
                flops=cost * tokens * steps, bytes_accessed=4 * model * tokens, transcendentals=0
            ),
            name=name,
        )

    def chip_swap(k):
        ky, kx = lay.chip_of(k)
        return lay.swap(ky=ky, kx=kx)

    def from_plane(parts):
        got = [lax.ppermute(part, AXES, lay.from_plane(k)) for k, part in enumerate(parts)]
        first = jnp.where(z // lay.ny == 0, got[0], got[1])
        second = jnp.where(z // lay.ny == 0, got[1], got[0])
        return jnp.concatenate([first, second], axis=0)[None]

    def doubling(held, bits, swap, after, first=None):
        for bit in bits[:-1]:
            got = lax.ppermute(held, AXES, swap(bit)) if first is None else first
            held, first = jnp.concatenate([held, got], axis=0), None
        held, _ = lax.optimization_barrier((held, after))
        return [held, lax.ppermute(held, AXES, swap(bits[-1]))]

    def over_chips(parts):
        got = [lax.ppermute(parts[k], AXES, chip_swap(k)) for k in range(1, chips)]
        return [parts[0]] + got

    info = jnp.concatenate([clip_ids[0], clip_patches[0], clip_step[0]])[None]
    by_core = jnp.concatenate([info, lax.ppermute(info, AXES, lay.swap(kc=1))], axis=0)
    info = [by_core] + [
        lax.ppermute(by_core, AXES, lay.swap(ky=ky)) for ky in range(1, lay.ny)
    ]
    group_y, group_c, _ = lay.unit(c, z)
    info = sum(
        jnp.where((y ^ ky == group_y) & (c ^ kc == group_c), info[ky][kc], 0)
        for ky in range(lay.ny)
        for kc in range(nc)
    )
    pos = jnp.stack([y, c, z, x]).astype(jnp.int32)
    pair_shape = (1, 2, half, model)
    outputs = call(
        functools.partial(start_kernel, lay, cols),
        "start",
        2 * model * 1000,
        [whole_spec(frames_x.shape)] * 2 + [whole_spec(w_qkv.shape)],
        [whole_spec(pair_shape)] * nc + [whole_spec((rows, 3 * cols))] * nx,
        [struct(pair_shape)] * nc + [struct((rows, 3 * cols))] * nx,
        prefetch=1,
    )(pos, frames_x, grad_y, w_qkv)
    pairs, picked = outputs[:nc], outputs[nc:]
    own = [lax.ppermute(pair, AXES, lay.to_plane(k)) for k, pair in enumerate(pairs)]
    by_x = [picked[0]] + [
        lax.ppermute(picked[kx], AXES, lay.swap(kx=kx)) for kx in range(1, nx)
    ]
    if nx == 2:
        ordered = [jnp.where(x == i, by_x[0], by_x[1]) for i in range(nx)]
    else:
        stacked = jnp.stack(by_x)
        ordered = [lax.dynamic_index_in_dim(stacked, x ^ i, 0, keepdims=False) for i in range(nx)]
    w_own = jnp.concatenate(ordered, axis=1 if rows % 16 == 0 else 0)[None]
    first = lax.ppermute(own[0], AXES, chip_swap(lay.chip_bits(0)[0]))
    own[1], first = lax.optimization_barrier((own[1], first))
    w_own, _ = lax.optimization_barrier((w_own, own[1]))
    w_pieces = doubling(w_own, lay.bits(lay.nz)[::-1], lambda kz: lay.swap(kz=kz), [])
    late_w_out, _ = lax.optimization_barrier((w_out, own))
    wo_own = lax.ppermute(late_w_out, AXES, lay.rows_to_chip())

    pairs = []
    for j in range(nc):
        after = ([], None) if j else (info, first)
        pairs += doubling(own[j], lay.chip_bits(j), chip_swap, *after)
    pairs, w_pieces = lax.optimization_barrier((pairs, w_pieces))
    if halves > 1:
        w_pieces += [lax.ppermute(piece, AXES, lay.swap(kc=1)) for piece in w_pieces]


    def spread(count, width, patches_at_once):
        return pl.BlockSpec((count, patches_at_once, width), lambda i, *_: (0, i, 0))

    def pair_spec(count, patches_at_once):
        return pl.BlockSpec((count, 2, patches_at_once, model), lambda i, *_: (0, 0, i, 0))

    few = max(BLOCK, step_patches // 2)
    few_steps = half // few
    x_spec = pl.BlockSpec((few, model), lambda i, *_: (i, 0))
    triple_spec = pl.BlockSpec((halves, lay.frames, step_patches, cols), lambda i, *_: (0, 0, i, 0))
    w_specs = [whole_spec(w_pieces[0].shape)] * (2 * halves)
    w_scratch = pltpu.VMEM((halves, model, 3 * cols), BF16)
    mod_spec = whole_spec(mod_table.shape)
    triple_shape = struct((halves, lay.frames, half, cols))
    part_specs = [spread(nc, model, step_patches)] * chips
    part_shapes = [struct((nc, half, model), F32)] + [struct((nc, half, model))] * (chips - 1)

    hidden, grad_proj = call(
        functools.partial(prepare_kernel, lay),
        "prepare",
        3 * model * 1000,
        [pair_spec(chips // 2, few)] * (2 * nc) + [mod_spec],
        [spread(lay.frames, model, few)] * 2,
        [struct((lay.frames, half, model))] * 2,
        grid=(few_steps,),
    )(pos, info, *pairs, mod_table)
    wo_own, _ = lax.optimization_barrier((wo_own, hidden))
    wo_rows = [wo_own, lax.ppermute(wo_own, AXES, lay.swap(kc=1))]

    fold = 3 if rows % 24 == 0 else 1
    piece_shape = (groups, rows // fold, quarter * fold)
    queries, keys, values, grad_attn, kept, sent, *projected = call(
        functools.partial(forward_kernel, lay),
        "forward",
        14 * model * 1000,
        [spread(lay.frames, model, step_patches)] * 2
        + w_specs
        + [whole_spec(w_out.shape)] * nc,
        [triple_spec] * 4 + [whole_spec(piece_shape)] * 2 + part_specs,
        [triple_shape] * 4 + [struct(piece_shape, F32)] * 2 + part_shapes,
        [
            w_scratch,
            pltpu.VMEM((lay.frames, step_patches, chip_width), BF16),
            pltpu.VMEM((chip_width, model), BF16),
            pltpu.VMEM((chip_width, model), F32),
            pltpu.VMEM(piece_shape, F32),
        ],
        (steps,),
    )(pos, info, hidden, grad_proj, *w_pieces, *wo_rows)
    got = lax.ppermute(sent, AXES, lay.swap(kc=1))
    projected = over_chips(projected)

    middle = groups // 2
    cut, away = kept[:middle] + got[:middle], kept[middle:] + got[middle:]
    grad_attn, cut, away = lax.optimization_barrier((grad_attn, cut, away))
    first_away = lax.ppermute(away, AXES, lay.swap(kz=1))

    sums = call(
        functools.partial(backward_kernel, lay),
        "backward",
        10 * model * 1000,
        w_specs + [triple_spec] * 4,
        part_specs,
        part_shapes,
        [w_scratch, pltpu.VMEM((halves, lay.frames, step_patches, 3 * cols), BF16)],
        (steps,),
    )(pos, info, *w_pieces, queries, keys, values, grad_attn)
    sums, first_away, projected = lax.optimization_barrier((sums, first_away, projected))
    grad_hidden = over_chips(sums)

    out_parts = call(
        functools.partial(output_kernel, lay),
        "output",
        20 * model * 1000,
        [pair_spec(1, few)] * nc + [spread(nc, model, few)] * chips + [mod_spec],
        [x_spec] * nc,
        [struct((half, model))] * nc,
        grid=(few_steps,),
    )(pos, info, *own, *projected, mod_table)
    out_y = from_plane(out_parts)

    grad_hidden, _ = lax.optimization_barrier((grad_hidden, out_parts))
    grad_parts = call(
        functools.partial(input_grad_kernel, lay),
        "input_grad",
        3 * model * 1000,
        [pair_spec(1, few)] * nc + [spread(nc, model, few)] * chips + [mod_spec],
        [x_spec] * nc,
        [struct((half, model))] * nc,
        grid=(few_steps,),
    )(pos, info, *own, *grad_hidden, mod_table)
    grad_x = from_plane(grad_parts)

    cut, _ = lax.optimization_barrier((cut + first_away, out_parts))
    for bit in lay.bits(lay.nz)[1:]:
        middle = middle // 2
        cut = cut[:middle] + lax.ppermute(cut[middle:], AXES, lay.swap(kz=bit))
    cut, _ = lax.optimization_barrier((cut, grad_parts))
    grad_w = lax.ppermute(cut[0], AXES, lay.to_owner())
    grad_w = jnp.concatenate(
        [grad_w[:, m * quarter : (m + 1) * quarter] for m in range(fold)], axis=0
    )
    grad_w_out = grad_w * jnp.float32(1.0 / math.sqrt(groups * lay.frames * patches))
    return out_y, grad_x, grad_w_out


def solution(mesh):
    lay = Layout(mesh)
    grid = Mesh(mesh.devices.reshape(lay.ny, lay.nc, lay.nz, lay.nx), AXES)
    rows, cols = ("z", "x"), ("y", "c")
    frame = P(AXES, None, None)
    group = P(cols, None)
    return jax.shard_map(
        functools.partial(local, lay),
        mesh=grid,
        in_specs=(frame, frame, group, group, group, P(), P(rows, None), P(rows, None)),
        out_specs=(frame, frame, P(rows, cols)),
        check_vma=False,
    )
```

```python
import functools
import math

import jax
import jax.numpy as jnp
from jax import lax
from jax.experimental import pallas as pl
from jax.experimental.pallas import tpu as pltpu
from jax.sharding import Mesh, PartitionSpec as P

HEADS = 16
CORES = 2
AXES = ("y", "c", "z", "x")
BLOCK = 16
VMEM_LIMIT = 64 * 1024 * 1024 - 65536
BF16 = jnp.bfloat16
F32 = jnp.float32


def dot(left, right):
    return jnp.dot(left, right, preferred_element_type=F32)


def dot_t(left, right):
    return lax.dot_general(left, right, (((1,), (1,)), ((), ())), preferred_element_type=F32)


def t_dot(left, right):
    return lax.dot_general(left, right, (((0,), (0,)), ((), ())), preferred_element_type=F32)


def normalize(values):
    centred = values - jnp.mean(values, axis=-1, keepdims=True)
    inv_sigma = lax.rsqrt(jnp.mean(centred * centred, axis=-1, keepdims=True) + 1e-06)
    return centred * inv_sigma, inv_sigma


class Layout:
    def __init__(self, mesh):
        groups, seq = mesh.shape["dp"], mesh.shape["seq"]
        self.nc = CORES
        self.ny = groups // CORES
        self.nz = groups
        self.nx = seq // self.nz
        self.chips = self.ny * self.nx
        self.frames = seq
        self.chip_heads = HEADS // self.chips
        self.halves = 2 if self.chip_heads % 2 == 0 else 1
        self.half_heads = self.chip_heads // self.halves

    def linear(self, y, c, z, x):
        return ((y * self.nc + c) * self.nz + z) * self.nx + x

    def perm(self, move):
        pairs = []
        for y in range(self.ny):
            for c in range(self.nc):
                for z in range(self.nz):
                    for x in range(self.nx):
                        pairs.append((self.linear(y, c, z, x), self.linear(*move(y, c, z, x))))
        return pairs

    def to_plane(self, k):
        def move(y, c, z, x):
            half = (z // self.ny) ^ k
            plane = ((y // self.nc) * self.nc + c) * self.nc + half
            return (z % self.ny) ^ c, y % self.nc, plane, x

        return self.perm(move)

    def unit(self, c, z):
        return (z // (self.nc * self.nc)) * self.nc + c, (z // self.nc) % self.nc, z % self.nc

    def from_plane(self, k):
        return [(target, source) for source, target in self.to_plane(k)]

    def swap(self, ky=0, kc=0, kz=0, kx=0):
        return self.perm(lambda y, c, z, x: (y ^ ky, c ^ kc, z ^ kz, x ^ kx))

    def row_block(self, y, x, i):
        if self.halves > 1:
            return (i * self.ny + y) * self.nx + x
        return self.nc * (y * self.nx + x) + i

    def rows_to_chip(self):
        reader = {
            self.row_block(y, x, i): (y, x, i)
            for y in range(self.ny)
            for x in range(self.nx)
            for i in range(self.nc)
        }

        def move(y, c, z, x):
            chip_y, chip_x, i = reader[z * self.nx + x]
            return chip_y, i, c * self.ny + (y ^ (z & 1)), chip_x

        return self.perm(move)

    def to_owner(self):
        def move(y, c, z, x):
            s = self.row_block(y, x, c)
            return z // self.nc, z % self.nc, s // self.nx, s % self.nx

        return self.perm(move)

    def chip_of(self, k):
        return k // self.nx, k % self.nx

    def bits(self, count):
        return [1 << b for b in range(count.bit_length() - 1)]

    def chip_bits(self, j):
        bits = self.bits(self.chips)
        return bits if j % 2 == 0 else bits[::-1]

    def doubled(self, bits):
        held = [0]
        for bit in bits:
            held = held + [k ^ bit for k in held]
        return held

    def slots(self):
        return [(k, j) for k in range(self.chips) for j in range(self.nc)]


def slot_scalars(lay, pos_ref, info_ref, slot):
    k, j = slot
    ky, kx = lay.chip_of(k)
    _, group_c, half = lay.unit(pos_ref[1], pos_ref[2])
    z_frame = (half ^ j) * lay.ny + (pos_ref[0] ^ ky ^ group_c)
    frame = z_frame * lay.nx + (pos_ref[3] ^ kx)
    clip = info_ref[frame]
    clips = (info_ref.shape[0] - lay.frames) // 2
    return clip, info_ref[lay.frames + clip], info_ref[lay.frames + clips + clip]


def table_row(mod_ref, step, part, width):
    return mod_ref[pl.ds(step, 1), part * width : (part + 1) * width]


def allowed_pairs(lay, pos_ref, info_ref, patch_base):
    rows = lay.frames * BLOCK
    row_slot = lax.broadcasted_iota(jnp.int32, (rows, 1), 0) // BLOCK
    col_slot = lax.broadcasted_iota(jnp.int32, (1, rows), 1) // BLOCK
    row_clip = jnp.zeros((rows, 1), jnp.int32)
    row_limit = jnp.zeros((rows, 1), jnp.int32)
    col_clip = jnp.zeros((1, rows), jnp.int32)
    for t, slot in enumerate(lay.slots()):
        clip, limit, _ = slot_scalars(lay, pos_ref, info_ref, slot)
        row_clip = jnp.where(row_slot == t, clip, row_clip)
        row_limit = jnp.where(row_slot == t, limit, row_limit)
        col_clip = jnp.where(col_slot == t, clip, col_clip)
    row_patch = lax.broadcasted_iota(jnp.int32, (rows, 1), 0) % BLOCK
    col_patch = lax.broadcasted_iota(jnp.int32, (1, rows), 1) % BLOCK
    row_key = row_clip * BLOCK + row_patch
    col_key = col_clip * BLOCK + col_patch
    row_valid = (patch_base + row_patch < row_limit).astype(jnp.int32)
    row_index = lax.broadcasted_iota(jnp.int32, (rows, rows), 0)
    col_index = lax.broadcasted_iota(jnp.int32, (rows, rows), 1)
    return (row_key == col_key) & ((row_valid > 0) | (row_index == col_index))


def head_mask(values, head, head_size):
    lane = lax.broadcasted_iota(jnp.int32, (1, values.shape[1]), 1)
    inside = (lane >= head * head_size) & (lane < (head + 1) * head_size)
    return jnp.where(inside, values, jnp.zeros_like(values))


def patch_blocks(array, block):
    part = array[:, block * BLOCK : (block + 1) * BLOCK, :]
    return part.reshape(part.shape[0] * BLOCK, part.shape[2])


def start_kernel(lay, cols, pos_ref, x_ref, g_ref, w_ref, *refs):
    pair_refs, out_refs = refs[: lay.nc], refs[lay.nc :]
    half = x_ref.shape[1] // lay.nc
    for k, ref in enumerate(pair_refs):
        first = pl.multiple_of(((pos_ref[2] // lay.ny) ^ k) * half, 16)
        ref[0, 0] = x_ref[0, pl.ds(first, half), :]
        ref[0, 1] = g_ref[0, pl.ds(first, half), :]
    model = w_ref.shape[1] // 3
    for k, out_ref in enumerate(out_refs):
        chip_x = pos_ref[3] ^ k
        if lay.halves > 1:
            want = lay.row_block(pos_ref[0], chip_x, pos_ref[1])
        else:
            want = pos_ref[0] * lay.nx + chip_x
        for v in range(lay.chips * lay.halves):

            @pl.when(want == v)
            def _(v=v, out_ref=out_ref):
                parts = [
                    w_ref[:, p * model + v * cols : p * model + (v + 1) * cols]
                    for p in range(3)
                ]
                out_ref[...] = jnp.concatenate(parts, axis=1)


def fill_weights(lay, pos_ref, w_refs, w_scr):
    order = lay.doubled(lay.bits(lay.nz)[::-1])
    block = w_scr.shape[1] // lay.nz
    rows, width = w_refs[0].shape[1], w_scr.shape[2]
    for h in range(lay.halves):
        for n, k in enumerate(order):
            ref, place = w_refs[2 * h + (2 * n) // lay.nz], n % (lay.nz // 2)
            for m in range(block // rows):
                start = pl.multiple_of((pos_ref[2] ^ k) * block + m * rows, 16)
                w_scr[h, pl.ds(start, rows), :] = ref[place, :, m * width : (m + 1) * width]


def heads_stacked(lay, values):
    head_size = values.shape[1] // lay.half_heads
    parts = [head_mask(values, head, head_size) for head in range(lay.half_heads)]
    return jnp.concatenate(parts, axis=0) if len(parts) > 1 else parts[0]


def beside(lay, weights):
    return jnp.concatenate([weights[head] for head in range(lay.half_heads)], axis=1)


def attention_weights(lay, keys_stacked, queries, allowed, scaling):
    scores = dot_t(keys_stacked, queries) * scaling
    scores = jnp.where(allowed, scores.reshape((lay.half_heads,) + allowed.shape), -jnp.inf)
    exponent = jnp.exp(scores - jnp.max(scores, axis=1, keepdims=True))
    return exponent * (1.0 / jnp.sum(exponent, axis=1, keepdims=True))


def prepare_kernel(lay, pos_ref, info_ref, *refs):
    pair_refs, (mod_ref, hid_ref, gp_ref) = refs[: 2 * lay.nc], refs[2 * lay.nc :]
    _, step_patches, model = hid_ref.shape
    patches = step_patches * pl.num_programs(0)
    patch_base = lay.unit(pos_ref[1], pos_ref[2])[2] * patches + pl.program_id(0) * step_patches
    patch = patch_base + lax.broadcasted_iota(jnp.int32, (step_patches, 1), 0)
    for t, (k, j) in enumerate(lay.slots()):
        _, limit, step = slot_scalars(lay, pos_ref, info_ref, (k, j))
        n = lay.doubled(lay.chip_bits(j)).index(k)
        ref, place = pair_refs[2 * j + (2 * n) // lay.chips], n % (lay.chips // 2)
        normed, _ = normalize(ref[place, 0].astype(F32))
        shift, scale = table_row(mod_ref, step, 0, model), table_row(mod_ref, step, 1, model)
        hid_ref[t] = (normed * (1.0 + scale) + shift).astype(BF16)
        factor = jnp.where(patch < limit, table_row(mod_ref, step, 2, model), 0.0)
        gp_ref[t] = (factor * ref[place, 1].astype(F32)).astype(BF16)


def forward_kernel(lay, pos_ref, info_ref, hid_ref, gp_ref, *refs):
    w_refs, refs = refs[: 2 * lay.halves], refs[2 * lay.halves :]
    wo_refs, refs = refs[: lay.nc], refs[lay.nc :]
    q_ref, k_ref, v_ref, ga_ref, kept_ref, sent_ref, *refs = refs
    pr_refs, (w_scr, att_scr, wo_scr, acc_scr, cut_scr) = refs[: lay.chips], refs[lay.chips :]
    _, step_patches, model = hid_ref.shape
    tokens = lay.frames * step_patches
    cols = w_scr.shape[2] // 3
    scaling = 1.0 / math.sqrt(cols // lay.half_heads)
    patches = step_patches * pl.num_programs(0)
    is_first = pos_ref[1] == 0

    @pl.when(pl.program_id(0) == 0)
    def _():
        fill_weights(lay, pos_ref, w_refs, w_scr)
        own, other = wo_refs[0][...].astype(F32), wo_refs[1][...].astype(F32)
        both = [jnp.where(is_first, own, other), jnp.where(is_first, other, own)]
        wo_scr[...] = jnp.concatenate(both, axis=0).astype(BF16)
        acc_scr[...] = jnp.zeros_like(acc_scr)

    hidden = hid_ref[...].reshape(lay.frames * step_patches, model)
    for h in range(lay.halves):
        triple = dot(hidden, w_scr[h])
        for n, ref in enumerate((q_ref, k_ref, v_ref)):
            ref[h] = triple[:, n * cols : (n + 1) * cols].astype(BF16).reshape(ref.shape[1:])

    for b in range(step_patches // BLOCK):
        patch_base = lay.unit(pos_ref[1], pos_ref[2])[2] * patches + pl.program_id(0) * step_patches + b * BLOCK
        allowed = allowed_pairs(lay, pos_ref, info_ref, patch_base)
        outputs = []
        for h in range(lay.halves):
            queries, keys, values = (patch_blocks(ref[h], b) for ref in (q_ref, k_ref, v_ref))
            weights = attention_weights(lay, heads_stacked(lay, keys), queries, allowed, scaling)
            weights = weights.astype(BF16).reshape(-1, allowed.shape[1])
            outputs.append(t_dot(weights, heads_stacked(lay, values)))
        if lay.halves > 1:
            first = jnp.where(pos_ref[1] == 0, outputs[0], outputs[1])
            second = jnp.where(pos_ref[1] == 0, outputs[1], outputs[0])
            outputs = [jnp.concatenate([first, second], axis=1)]
        attended = outputs[0].astype(BF16)
        att_scr[:, b * BLOCK : (b + 1) * BLOCK, :] = attended.reshape(lay.frames, BLOCK, -1)

    attended = att_scr[...].reshape(tokens, -1)
    grad_proj = gp_ref[...].reshape(tokens, model)
    acc_scr[...] += t_dot(attended, grad_proj)
    grad_attn = dot_t(grad_proj, wo_scr[...])
    part = wo_scr.shape[0] // lay.halves
    for h in range(lay.halves):
        ga_ref[h] = grad_attn[:, h * part : (h + 1) * part].astype(BF16).reshape(ga_ref.shape[1:])
    projected = dot(attended, wo_scr[...]).reshape(lay.chips, lay.nc, step_patches, model)
    for k in range(lay.chips):
        pr_refs[k][...] = projected[k].astype(pr_refs[k].dtype)

    @pl.when(pl.program_id(0) == pl.num_programs(0) - 1)
    def _():
        groups, chunk_rows, chunk_width = kept_ref.shape
        block_rows, part = acc_scr.shape[0] // lay.nc, model // groups
        order = lay.doubled(lay.bits(lay.nz)[::-1])
        first, second = acc_scr[:block_rows, :], acc_scr[block_rows:, :]
        kept = jnp.where(is_first, first, second)
        sent = jnp.where(is_first, second, first)
        for ref, rows in ((kept_ref, kept), (sent_ref, sent)):
            for d in range(groups):
                chunk = [
                    rows[m * chunk_rows : (m + 1) * chunk_rows, d * part : (d + 1) * part]
                    for m in range(chunk_width // part)
                ]
                cut_scr[d] = jnp.concatenate(chunk, axis=1) if len(chunk) > 1 else chunk[0]
            for n, k in enumerate(order):
                ref[n] = cut_scr[pos_ref[2] ^ k]


def backward_kernel(lay, pos_ref, info_ref, *refs):
    w_refs, refs = refs[: 2 * lay.halves], refs[2 * lay.halves :]
    q_ref, k_ref, v_ref, ga_ref, *refs = refs
    gh_refs, (w_scr, gt_scr) = refs[: lay.chips], refs[lay.chips :]
    _, frames, step_patches, cols = q_ref.shape
    model = w_scr.shape[1]
    patches = step_patches * pl.num_programs(0)
    scaling = 1.0 / math.sqrt(cols // lay.half_heads)

    @pl.when(pl.program_id(0) == 0)
    def _():
        fill_weights(lay, pos_ref, w_refs, w_scr)

    for b in range(step_patches // BLOCK):
        patch_base = lay.unit(pos_ref[1], pos_ref[2])[2] * patches + pl.program_id(0) * step_patches + b * BLOCK
        allowed = allowed_pairs(lay, pos_ref, info_ref, patch_base)
        for h in range(lay.halves):
            queries, keys, values = (patch_blocks(ref[h], b) for ref in (q_ref, k_ref, v_ref))
            grad_out = patch_blocks(ga_ref[(pos_ref[1] ^ h) if lay.halves > 1 else 0], b)
            keys = heads_stacked(lay, keys)
            weights = attention_weights(lay, keys, queries, allowed, scaling)
            grad_weights = dot_t(heads_stacked(lay, values), grad_out).reshape(weights.shape)
            grad_values = dot(beside(lay, weights.astype(BF16)), heads_stacked(lay, grad_out))
            inner = jnp.sum(weights * grad_weights, axis=1, keepdims=True)
            grad_scores = (weights * (grad_weights - inner) * scaling).astype(BF16)
            grad_queries = t_dot(grad_scores.reshape(-1, grad_scores.shape[2]), keys)
            grad_keys = dot(beside(lay, grad_scores), heads_stacked(lay, queries))
            grads = jnp.concatenate([grad_queries, grad_keys, grad_values], axis=1).astype(BF16)
            gt_scr[h, :, b * BLOCK : (b + 1) * BLOCK, :] = grads.reshape(frames, BLOCK, 3 * cols)

    total = jnp.zeros((frames * step_patches, model), F32)
    for h in range(lay.halves):
        total = total + dot_t(gt_scr[h].reshape(frames * step_patches, 3 * cols), w_scr[h])
    total = total.reshape(lay.chips, lay.nc, step_patches, model)
    for k in range(lay.chips):
        gh_refs[k][...] = total[k].astype(gh_refs[k].dtype)


def output_kernel(lay, pos_ref, info_ref, *refs):
    pair_refs, refs = refs[: lay.nc], refs[lay.nc :]
    pr_refs, refs = refs[: lay.chips], refs[lay.chips :]
    mod_ref, *out_refs = refs
    step_patches, model = out_refs[0].shape
    patches = step_patches * pl.num_programs(0)
    patch_base = lay.unit(pos_ref[1], pos_ref[2])[2] * patches + pl.program_id(0) * step_patches
    patch = patch_base + lax.broadcasted_iota(jnp.int32, (step_patches, 1), 0)
    for j in range(lay.nc):
        _, limit, step = slot_scalars(lay, pos_ref, info_ref, (0, j))
        factor = jnp.where(patch < limit, table_row(mod_ref, step, 2, model), 0.0)
        projected = pr_refs[0][j]
        for k in range(1, lay.chips):
            projected = projected + pr_refs[k][j].astype(F32)
        projected = projected.astype(BF16).astype(F32)
        out_refs[j][...] = (pair_refs[j][0, 0].astype(F32) + factor * projected).astype(BF16)


def input_grad_kernel(lay, pos_ref, info_ref, *refs):
    pair_refs, refs = refs[: lay.nc], refs[lay.nc :]
    gh_refs, refs = refs[: lay.chips], refs[lay.chips :]
    mod_ref, *out_refs = refs
    model = out_refs[0].shape[1]
    for j in range(lay.nc):
        _, _, step = slot_scalars(lay, pos_ref, info_ref, (0, j))
        grad_hidden = gh_refs[0][j]
        for k in range(1, lay.chips):
            grad_hidden = grad_hidden + gh_refs[k][j].astype(F32)
        grad_hidden = grad_hidden.astype(BF16).astype(F32)
        normed, inv_sigma = normalize(pair_refs[j][0, 0].astype(F32))
        grad_norm = grad_hidden * (1.0 + table_row(mod_ref, step, 1, model))
        first_mean = jnp.mean(grad_norm, axis=-1, keepdims=True)
        second_mean = jnp.mean(grad_norm * normed, axis=-1, keepdims=True)
        grad_x = pair_refs[j][0, 1].astype(F32) + inv_sigma * (
            grad_norm - first_mean - normed * second_mean
        )
        out_refs[j][...] = grad_x.astype(BF16)


def whole_spec(shape):
    return pl.BlockSpec(shape, lambda *_: (0,) * len(shape))


def struct(shape, dtype=BF16):
    return jax.ShapeDtypeStruct(shape, dtype)


def local(lay, frames_x, grad_y, clip_ids, clip_patches, clip_step, mod_table, w_qkv, w_out):
    y, c, z, x = (lax.axis_index(name) for name in AXES)
    _, patches, model = frames_x.shape
    half = patches // lay.nc
    chips, nc, nx = lay.chips, lay.nc, lay.nx
    head_size = model // HEADS
    halves = lay.halves
    cols = lay.half_heads * head_size
    chip_width = lay.chip_heads * head_size
    rows = w_qkv.shape[0]
    groups = lay.nz
    quarter = model // groups
    step_patches = max(BLOCK, min(half, 512 // lay.frames))
    steps = half // step_patches
    tokens = lay.frames * step_patches

    def call(kernel, name, cost, in_specs, out_specs, out_shape, scratch=(), grid=(1,), prefetch=2):
        return pl.pallas_call(
            kernel,
            grid_spec=pltpu.PrefetchScalarGridSpec(
                num_scalar_prefetch=prefetch,
                grid=grid,
                in_specs=in_specs,
                out_specs=out_specs,
                scratch_shapes=list(scratch),
            ),
            out_shape=out_shape,
            compiler_params=pltpu.CompilerParams(vmem_limit_bytes=VMEM_LIMIT),
            cost_estimate=pl.CostEstimate(
                flops=cost * tokens * steps, bytes_accessed=4 * model * tokens, transcendentals=0
            ),
            name=name,
        )

    def chip_swap(k):
        ky, kx = lay.chip_of(k)
        return lay.swap(ky=ky, kx=kx)

    def from_plane(parts):
        got = [lax.ppermute(part, AXES, lay.from_plane(k)) for k, part in enumerate(parts)]
        first = jnp.where(z // lay.ny == 0, got[0], got[1])
        second = jnp.where(z // lay.ny == 0, got[1], got[0])
        return jnp.concatenate([first, second], axis=0)[None]

    def doubling(held, bits, swap, after, first=None):
        for bit in bits[:-1]:
            got = lax.ppermute(held, AXES, swap(bit)) if first is None else first
            held, first = jnp.concatenate([held, got], axis=0), None
        held, _ = lax.optimization_barrier((held, after))
        return [held, lax.ppermute(held, AXES, swap(bits[-1]))]

    def over_chips(parts):
        got = [lax.ppermute(parts[k], AXES, chip_swap(k)) for k in range(1, chips)]
        return [parts[0]] + got

    info = jnp.concatenate([clip_ids[0], clip_patches[0], clip_step[0]])[None]
    by_core = jnp.concatenate([info, lax.ppermute(info, AXES, lay.swap(kc=1))], axis=0)
    info = [by_core] + [
        lax.ppermute(by_core, AXES, lay.swap(ky=ky)) for ky in range(1, lay.ny)
    ]
    group_y, group_c, _ = lay.unit(c, z)
    info = sum(
        jnp.where((y ^ ky == group_y) & (c ^ kc == group_c), info[ky][kc], 0)
        for ky in range(lay.ny)
        for kc in range(nc)
    )
    pos = jnp.stack([y, c, z, x]).astype(jnp.int32)
    pair_shape = (1, 2, half, model)
    outputs = call(
        functools.partial(start_kernel, lay, cols),
        "start",
        2 * model * 1000,
        [whole_spec(frames_x.shape)] * 2 + [whole_spec(w_qkv.shape)],
        [whole_spec(pair_shape)] * nc + [whole_spec((rows, 3 * cols))] * nx,
        [struct(pair_shape)] * nc + [struct((rows, 3 * cols))] * nx,
        prefetch=1,
    )(pos, frames_x, grad_y, w_qkv)
    pairs, picked = outputs[:nc], outputs[nc:]
    own = [lax.ppermute(pair, AXES, lay.to_plane(k)) for k, pair in enumerate(pairs)]
    by_x = [picked[0]] + [
        lax.ppermute(picked[kx], AXES, lay.swap(kx=kx)) for kx in range(1, nx)
    ]
    if nx == 2:
        ordered = [jnp.where(x == i, by_x[0], by_x[1]) for i in range(nx)]
    else:
        stacked = jnp.stack(by_x)
        ordered = [lax.dynamic_index_in_dim(stacked, x ^ i, 0, keepdims=False) for i in range(nx)]
    w_own = jnp.concatenate(ordered, axis=1 if rows % 16 == 0 else 0)[None]
    first = lax.ppermute(own[0], AXES, chip_swap(lay.chip_bits(0)[0]))
    own[1], first = lax.optimization_barrier((own[1], first))
    w_own, _ = lax.optimization_barrier((w_own, own[1]))
    w_pieces = doubling(w_own, lay.bits(lay.nz)[::-1], lambda kz: lay.swap(kz=kz), [])
    late_w_out, _ = lax.optimization_barrier((w_out, own))
    wo_own = lax.ppermute(late_w_out, AXES, lay.rows_to_chip())

    pairs = []
    for j in range(nc):
        after = ([], None) if j else (info, first)
        pairs += doubling(own[j], lay.chip_bits(j), chip_swap, *after)
    pairs, w_pieces = lax.optimization_barrier((pairs, w_pieces))
    if halves > 1:
        w_pieces += [lax.ppermute(piece, AXES, lay.swap(kc=1)) for piece in w_pieces]


    def spread(count, width, patches_at_once):
        return pl.BlockSpec((count, patches_at_once, width), lambda i, *_: (0, i, 0))

    def pair_spec(count, patches_at_once):
        return pl.BlockSpec((count, 2, patches_at_once, model), lambda i, *_: (0, 0, i, 0))

    few = max(BLOCK, step_patches // 2)
    few_steps = half // few
    x_spec = pl.BlockSpec((few, model), lambda i, *_: (i, 0))
    triple_spec = pl.BlockSpec((halves, lay.frames, step_patches, cols), lambda i, *_: (0, 0, i, 0))
    w_specs = [whole_spec(w_pieces[0].shape)] * (2 * halves)
    w_scratch = pltpu.VMEM((halves, model, 3 * cols), BF16)
    mod_spec = whole_spec(mod_table.shape)
    triple_shape = struct((halves, lay.frames, half, cols))
    part_specs = [spread(nc, model, step_patches)] * chips
    part_shapes = [struct((nc, half, model), F32)] + [struct((nc, half, model))] * (chips - 1)

    hidden, grad_proj = call(
        functools.partial(prepare_kernel, lay),
        "prepare",
        3 * model * 1000,
        [pair_spec(chips // 2, BLOCK)] * (2 * nc) + [mod_spec],
        [spread(lay.frames, model, BLOCK)] * 2,
        [struct((lay.frames, half, model))] * 2,
        grid=(half // BLOCK,),
    )(pos, info, *pairs, mod_table)
    wo_own, _ = lax.optimization_barrier((wo_own, hidden))
    wo_rows = [wo_own, lax.ppermute(wo_own, AXES, lay.swap(kc=1))]

    fold = 3 if rows % 24 == 0 else 1
    piece_shape = (groups, rows // fold, quarter * fold)
    queries, keys, values, grad_attn, kept, sent, *projected = call(
        functools.partial(forward_kernel, lay),
        "forward",
        14 * model * 1000,
        [spread(lay.frames, model, step_patches)] * 2
        + w_specs
        + [whole_spec(w_out.shape)] * nc,
        [triple_spec] * 4 + [whole_spec(piece_shape)] * 2 + part_specs,
        [triple_shape] * 4 + [struct(piece_shape, F32)] * 2 + part_shapes,
        [
            w_scratch,
            pltpu.VMEM((lay.frames, step_patches, chip_width), BF16),
            pltpu.VMEM((chip_width, model), BF16),
            pltpu.VMEM((chip_width, model), F32),
            pltpu.VMEM(piece_shape, F32),
        ],
        (steps,),
    )(pos, info, hidden, grad_proj, *w_pieces, *wo_rows)
    got = lax.ppermute(sent, AXES, lay.swap(kc=1))
    projected = over_chips(projected)

    middle = groups // 2
    cut, away = kept[:middle] + got[:middle], kept[middle:] + got[middle:]
    grad_attn, cut, away = lax.optimization_barrier((grad_attn, cut, away))
    first_away = lax.ppermute(away, AXES, lay.swap(kz=1))

    sums = call(
        functools.partial(backward_kernel, lay),
        "backward",
        10 * model * 1000,
        w_specs + [triple_spec] * 4,
        part_specs,
        part_shapes,
        [w_scratch, pltpu.VMEM((halves, lay.frames, step_patches, 3 * cols), BF16)],
        (steps,),
    )(pos, info, *w_pieces, queries, keys, values, grad_attn)
    sums, first_away, projected = lax.optimization_barrier((sums, first_away, projected))
    grad_hidden = over_chips(sums)

    out_parts = call(
        functools.partial(output_kernel, lay),
        "output",
        20 * model * 1000,
        [pair_spec(1, few)] * nc + [spread(nc, model, few)] * chips + [mod_spec],
        [x_spec] * nc,
        [struct((half, model))] * nc,
        grid=(few_steps,),
    )(pos, info, *own, *projected, mod_table)
    out_y = from_plane(out_parts)

    grad_hidden, _ = lax.optimization_barrier((grad_hidden, out_parts))
    grad_parts = call(
        functools.partial(input_grad_kernel, lay),
        "input_grad",
        3 * model * 1000,
        [pair_spec(1, few)] * nc + [spread(nc, model, few)] * chips + [mod_spec],
        [x_spec] * nc,
        [struct((half, model))] * nc,
        grid=(few_steps,),
    )(pos, info, *own, *grad_hidden, mod_table)
    grad_x = from_plane(grad_parts)

    cut, _ = lax.optimization_barrier((cut + first_away, out_parts))
    for bit in lay.bits(lay.nz)[1:]:
        middle = middle // 2
        cut = cut[:middle] + lax.ppermute(cut[middle:], AXES, lay.swap(kz=bit))
    cut, _ = lax.optimization_barrier((cut, grad_parts))
    grad_w = lax.ppermute(cut[0], AXES, lay.to_owner())
    grad_w = jnp.concatenate(
        [grad_w[:, m * quarter : (m + 1) * quarter] for m in range(fold)], axis=0
    )
    grad_w_out = grad_w * jnp.float32(1.0 / math.sqrt(groups * lay.frames * patches))
    return out_y, grad_x, grad_w_out


def solution(mesh):
    lay = Layout(mesh)
    grid = Mesh(mesh.devices.reshape(lay.ny, lay.nc, lay.nz, lay.nx), AXES)
    rows, cols = ("z", "x"), ("y", "c")
    frame = P(AXES, None, None)
    group = P(cols, None)
    return jax.shard_map(
        functools.partial(local, lay),
        mesh=grid,
        in_specs=(frame, frame, group, group, group, P(), P(rows, None), P(rows, None)),
        out_specs=(frame, frame, P(rows, cols)),
        check_vma=False,
    )
```

```python
import functools
import math

import jax
import jax.numpy as jnp
from jax import lax
from jax.experimental import pallas as pl
from jax.experimental.pallas import tpu as pltpu
from jax.sharding import Mesh, PartitionSpec as P

HEADS = 16
CORES = 2
AXES = ("y", "c", "z", "x")
BLOCK = 16
VMEM_LIMIT = 56 * 1024 * 1024
BF16 = jnp.bfloat16
F32 = jnp.float32


def dot(left, right):
    return jnp.dot(left, right, preferred_element_type=F32)


def dot_t(left, right):
    return lax.dot_general(left, right, (((1,), (1,)), ((), ())), preferred_element_type=F32)


def t_dot(left, right):
    return lax.dot_general(left, right, (((0,), (0,)), ((), ())), preferred_element_type=F32)


def normalize(values):
    centred = values - jnp.mean(values, axis=-1, keepdims=True)
    inv_sigma = lax.rsqrt(jnp.mean(centred * centred, axis=-1, keepdims=True) + 1e-06)
    return centred * inv_sigma, inv_sigma


class Layout:
    def __init__(self, mesh):
        groups, seq = mesh.shape["dp"], mesh.shape["seq"]
        self.nc = CORES
        self.ny = groups // CORES
        self.nz = groups
        self.nx = seq // self.nz
        self.chips = self.ny * self.nx
        self.frames = seq
        self.chip_heads = HEADS // self.chips
        self.halves = 2 if self.chip_heads % 2 == 0 else 1
        self.half_heads = self.chip_heads // self.halves

    def linear(self, y, c, z, x):
        return ((y * self.nc + c) * self.nz + z) * self.nx + x

    def perm(self, move):
        pairs = []
        for y in range(self.ny):
            for c in range(self.nc):
                for z in range(self.nz):
                    for x in range(self.nx):
                        pairs.append((self.linear(y, c, z, x), self.linear(*move(y, c, z, x))))
        return pairs

    def to_plane(self, k):
        def move(y, c, z, x):
            half = (z // self.ny) ^ k
            plane = ((y // self.nc) * self.nc + c) * self.nc + half
            return (z % self.ny) ^ c, y % self.nc, plane, x

        return self.perm(move)

    def unit(self, c, z):
        return (z // (self.nc * self.nc)) * self.nc + c, (z // self.nc) % self.nc, z % self.nc

    def from_plane(self, k):
        return [(target, source) for source, target in self.to_plane(k)]

    def swap(self, ky=0, kc=0, kz=0, kx=0):
        return self.perm(lambda y, c, z, x: (y ^ ky, c ^ kc, z ^ kz, x ^ kx))

    def row_block(self, y, x, i):
        if self.halves > 1:
            return (i * self.ny + y) * self.nx + x
        return self.nc * (y * self.nx + x) + i

    def rows_to_chip(self):
        reader = {
            self.row_block(y, x, i): (y, x, i)
            for y in range(self.ny)
            for x in range(self.nx)
            for i in range(self.nc)
        }

        def move(y, c, z, x):
            chip_y, chip_x, i = reader[z * self.nx + x]
            return chip_y, i, c * self.ny + (y ^ (z & 1)), chip_x

        return self.perm(move)

    def to_owner(self):
        def move(y, c, z, x):
            s = self.row_block(y, x, c)
            return z // self.nc, z % self.nc, s // self.nx, s % self.nx

        return self.perm(move)

    def chip_of(self, k):
        return k // self.nx, k % self.nx

    def bits(self, count):
        return [1 << b for b in range(count.bit_length() - 1)]

    def chip_bits(self, j):
        bits = self.bits(self.chips)
        return bits if j % 2 == 0 else bits[::-1]

    def doubled(self, bits):
        held = [0]
        for bit in bits:
            held = held + [k ^ bit for k in held]
        return held

    def slots(self):
        return [(k, j) for k in range(self.chips) for j in range(self.nc)]


def slot_scalars(lay, pos_ref, info_ref, slot):
    k, j = slot
    ky, kx = lay.chip_of(k)
    _, group_c, half = lay.unit(pos_ref[1], pos_ref[2])
    z_frame = (half ^ j) * lay.ny + (pos_ref[0] ^ ky ^ group_c)
    frame = z_frame * lay.nx + (pos_ref[3] ^ kx)
    clip = info_ref[frame]
    clips = (info_ref.shape[0] - lay.frames) // 2
    return clip, info_ref[lay.frames + clip], info_ref[lay.frames + clips + clip]


def table_row(mod_ref, step, part, width):
    return mod_ref[pl.ds(step, 1), part * width : (part + 1) * width]


def allowed_pairs(lay, pos_ref, info_ref, patch_base):
    rows = lay.frames * BLOCK
    row_slot = lax.broadcasted_iota(jnp.int32, (rows, 1), 0) // BLOCK
    col_slot = lax.broadcasted_iota(jnp.int32, (1, rows), 1) // BLOCK
    row_clip = jnp.zeros((rows, 1), jnp.int32)
    row_limit = jnp.zeros((rows, 1), jnp.int32)
    col_clip = jnp.zeros((1, rows), jnp.int32)
    for t, slot in enumerate(lay.slots()):
        clip, limit, _ = slot_scalars(lay, pos_ref, info_ref, slot)
        row_clip = jnp.where(row_slot == t, clip, row_clip)
        row_limit = jnp.where(row_slot == t, limit, row_limit)
        col_clip = jnp.where(col_slot == t, clip, col_clip)
    row_patch = lax.broadcasted_iota(jnp.int32, (rows, 1), 0) % BLOCK
    col_patch = lax.broadcasted_iota(jnp.int32, (1, rows), 1) % BLOCK
    row_key = row_clip * BLOCK + row_patch
    col_key = col_clip * BLOCK + col_patch
    row_valid = (patch_base + row_patch < row_limit).astype(jnp.int32)
    row_index = lax.broadcasted_iota(jnp.int32, (rows, rows), 0)
    col_index = lax.broadcasted_iota(jnp.int32, (rows, rows), 1)
    return (row_key == col_key) & ((row_valid > 0) | (row_index == col_index))


def head_mask(values, head, head_size):
    lane = lax.broadcasted_iota(jnp.int32, (1, values.shape[1]), 1)
    inside = (lane >= head * head_size) & (lane < (head + 1) * head_size)
    return jnp.where(inside, values, jnp.zeros_like(values))


def patch_blocks(array, block):
    part = array[:, block * BLOCK : (block + 1) * BLOCK, :]
    return part.reshape(part.shape[0] * BLOCK, part.shape[2])


def start_kernel(lay, cols, pos_ref, x_ref, g_ref, w_ref, *refs):
    pair_refs, out_refs = refs[: lay.nc], refs[lay.nc :]
    half = x_ref.shape[1] // lay.nc
    for k, ref in enumerate(pair_refs):
        first = pl.multiple_of(((pos_ref[2] // lay.ny) ^ k) * half, 16)
        ref[0, 0] = x_ref[0, pl.ds(first, half), :]
        ref[0, 1] = g_ref[0, pl.ds(first, half), :]
    model = w_ref.shape[1] // 3
    for k, out_ref in enumerate(out_refs):
        chip_x = pos_ref[3] ^ k
        if lay.halves > 1:
            want = lay.row_block(pos_ref[0], chip_x, pos_ref[1])
        else:
            want = pos_ref[0] * lay.nx + chip_x
        for v in range(lay.chips * lay.halves):

            @pl.when(want == v)
            def _(v=v, out_ref=out_ref):
                parts = [
                    w_ref[:, p * model + v * cols : p * model + (v + 1) * cols]
                    for p in range(3)
                ]
                out_ref[...] = jnp.concatenate(parts, axis=1)


def fill_weights(lay, pos_ref, w_refs, w_scr):
    order = lay.doubled(lay.bits(lay.nz)[::-1])
    block = w_scr.shape[1] // lay.nz
    rows, width = w_refs[0].shape[1], w_scr.shape[2]
    for h in range(lay.halves):
        for n, k in enumerate(order):
            ref, place = w_refs[2 * h + (2 * n) // lay.nz], n % (lay.nz // 2)
            for m in range(block // rows):
                start = pl.multiple_of((pos_ref[2] ^ k) * block + m * rows, 16)
                w_scr[h, pl.ds(start, rows), :] = ref[place, :, m * width : (m + 1) * width]


def heads_stacked(lay, values):
    head_size = values.shape[1] // lay.half_heads
    parts = [head_mask(values, head, head_size) for head in range(lay.half_heads)]
    return jnp.concatenate(parts, axis=0) if len(parts) > 1 else parts[0]


def beside(lay, weights):
    return jnp.concatenate([weights[head] for head in range(lay.half_heads)], axis=1)


def attention_weights(lay, keys_stacked, queries, allowed, scaling):
    scores = dot_t(keys_stacked, queries) * scaling
    scores = jnp.where(allowed, scores.reshape((lay.half_heads,) + allowed.shape), -jnp.inf)
    exponent = jnp.exp(scores - jnp.max(scores, axis=1, keepdims=True))
    return exponent * (1.0 / jnp.sum(exponent, axis=1, keepdims=True))


def modulate(lay, pos_ref, info_ref, pair_refs, mod_ref, hid_ref, gp_ref):
    _, step_patches, model = hid_ref.shape
    patches = step_patches * pl.num_programs(0)
    patch_base = lay.unit(pos_ref[1], pos_ref[2])[2] * patches + pl.program_id(0) * step_patches
    patch = patch_base + lax.broadcasted_iota(jnp.int32, (step_patches, 1), 0)
    for t, (k, j) in enumerate(lay.slots()):
        _, limit, step = slot_scalars(lay, pos_ref, info_ref, (k, j))
        n = lay.doubled(lay.chip_bits(j)).index(k)
        ref, place = pair_refs[2 * j + (2 * n) // lay.chips], n % (lay.chips // 2)
        normed, _ = normalize(ref[place, 0].astype(F32))
        shift, scale = table_row(mod_ref, step, 0, model), table_row(mod_ref, step, 1, model)
        hid_ref[t] = (normed * (1.0 + scale) + shift).astype(BF16)
        factor = jnp.where(patch < limit, table_row(mod_ref, step, 2, model), 0.0)
        gp_ref[t] = (factor * ref[place, 1].astype(F32)).astype(BF16)


def forward_kernel(lay, pos_ref, info_ref, *refs):
    pair_refs, refs = refs[: 2 * lay.nc], refs[2 * lay.nc :]
    w_refs, refs = refs[: 2 * lay.halves], refs[2 * lay.halves :]
    wo_refs, refs = refs[: lay.nc], refs[lay.nc :]
    mod_ref, q_ref, k_ref, v_ref, ga_ref, kept_ref, sent_ref, *refs = refs
    pr_refs, refs = refs[: lay.chips], refs[lay.chips :]
    hid_ref, gp_ref, w_scr, att_scr, wo_scr, acc_scr, cut_scr = refs
    _, step_patches, model = hid_ref.shape
    tokens = lay.frames * step_patches
    cols = w_scr.shape[2] // 3
    scaling = 1.0 / math.sqrt(cols // lay.half_heads)
    patches = step_patches * pl.num_programs(0)
    is_first = pos_ref[1] == 0

    @pl.when(pl.program_id(0) == 0)
    def _():
        fill_weights(lay, pos_ref, w_refs, w_scr)
        own, other = wo_refs[0][...].astype(F32), wo_refs[1][...].astype(F32)
        both = [jnp.where(is_first, own, other), jnp.where(is_first, other, own)]
        wo_scr[...] = jnp.concatenate(both, axis=0).astype(BF16)
        acc_scr[...] = jnp.zeros_like(acc_scr)

    modulate(lay, pos_ref, info_ref, pair_refs, mod_ref, hid_ref, gp_ref)
    hidden = hid_ref[...].reshape(lay.frames * step_patches, model)
    for h in range(lay.halves):
        triple = dot(hidden, w_scr[h])
        for n, ref in enumerate((q_ref, k_ref, v_ref)):
            ref[h] = triple[:, n * cols : (n + 1) * cols].astype(BF16).reshape(ref.shape[1:])

    for b in range(step_patches // BLOCK):
        patch_base = lay.unit(pos_ref[1], pos_ref[2])[2] * patches + pl.program_id(0) * step_patches + b * BLOCK
        allowed = allowed_pairs(lay, pos_ref, info_ref, patch_base)
        outputs = []
        for h in range(lay.halves):
            queries, keys, values = (patch_blocks(ref[h], b) for ref in (q_ref, k_ref, v_ref))
            weights = attention_weights(lay, heads_stacked(lay, keys), queries, allowed, scaling)
            weights = weights.astype(BF16).reshape(-1, allowed.shape[1])
            outputs.append(t_dot(weights, heads_stacked(lay, values)))
        if lay.halves > 1:
            first = jnp.where(pos_ref[1] == 0, outputs[0], outputs[1])
            second = jnp.where(pos_ref[1] == 0, outputs[1], outputs[0])
            outputs = [jnp.concatenate([first, second], axis=1)]
        attended = outputs[0].astype(BF16)
        att_scr[:, b * BLOCK : (b + 1) * BLOCK, :] = attended.reshape(lay.frames, BLOCK, -1)

    attended = att_scr[...].reshape(tokens, -1)
    grad_proj = gp_ref[...].reshape(tokens, model)
    acc_scr[...] += t_dot(attended, grad_proj)
    grad_attn = dot_t(grad_proj, wo_scr[...])
    part = wo_scr.shape[0] // lay.halves
    for h in range(lay.halves):
        ga_ref[h] = grad_attn[:, h * part : (h + 1) * part].astype(BF16).reshape(ga_ref.shape[1:])
    projected = dot(attended, wo_scr[...]).reshape(lay.chips, lay.nc, step_patches, model)
    for k in range(lay.chips):
        pr_refs[k][...] = projected[k].astype(pr_refs[k].dtype)

    @pl.when(pl.program_id(0) == pl.num_programs(0) - 1)
    def _():
        groups, chunk_rows, chunk_width = kept_ref.shape
        block_rows, part = acc_scr.shape[0] // lay.nc, model // groups
        order = lay.doubled(lay.bits(lay.nz)[::-1])
        first, second = acc_scr[:block_rows, :], acc_scr[block_rows:, :]
        kept = jnp.where(is_first, first, second)
        sent = jnp.where(is_first, second, first)
        for ref, rows in ((kept_ref, kept), (sent_ref, sent)):
            for d in range(groups):
                chunk = [
                    rows[m * chunk_rows : (m + 1) * chunk_rows, d * part : (d + 1) * part]
                    for m in range(chunk_width // part)
                ]
                cut_scr[d] = jnp.concatenate(chunk, axis=1) if len(chunk) > 1 else chunk[0]
            for n, k in enumerate(order):
                ref[n] = cut_scr[pos_ref[2] ^ k]


def backward_kernel(lay, pos_ref, info_ref, *refs):
    w_refs, refs = refs[: 2 * lay.halves], refs[2 * lay.halves :]
    q_ref, k_ref, v_ref, ga_ref, *refs = refs
    gh_refs, (w_scr, gt_scr) = refs[: lay.chips], refs[lay.chips :]
    _, frames, step_patches, cols = q_ref.shape
    model = w_scr.shape[1]
    patches = step_patches * pl.num_programs(0)
    scaling = 1.0 / math.sqrt(cols // lay.half_heads)

    @pl.when(pl.program_id(0) == 0)
    def _():
        fill_weights(lay, pos_ref, w_refs, w_scr)

    for b in range(step_patches // BLOCK):
        patch_base = lay.unit(pos_ref[1], pos_ref[2])[2] * patches + pl.program_id(0) * step_patches + b * BLOCK
        allowed = allowed_pairs(lay, pos_ref, info_ref, patch_base)
        for h in range(lay.halves):
            queries, keys, values = (patch_blocks(ref[h], b) for ref in (q_ref, k_ref, v_ref))
            grad_out = patch_blocks(ga_ref[(pos_ref[1] ^ h) if lay.halves > 1 else 0], b)
            keys = heads_stacked(lay, keys)
            weights = attention_weights(lay, keys, queries, allowed, scaling)
            grad_weights = dot_t(heads_stacked(lay, values), grad_out).reshape(weights.shape)
            grad_values = dot(beside(lay, weights.astype(BF16)), heads_stacked(lay, grad_out))
            inner = jnp.sum(weights * grad_weights, axis=1, keepdims=True)
            grad_scores = (weights * (grad_weights - inner) * scaling).astype(BF16)
            grad_queries = t_dot(grad_scores.reshape(-1, grad_scores.shape[2]), keys)
            grad_keys = dot(beside(lay, grad_scores), heads_stacked(lay, queries))
            grads = jnp.concatenate([grad_queries, grad_keys, grad_values], axis=1).astype(BF16)
            gt_scr[h, :, b * BLOCK : (b + 1) * BLOCK, :] = grads.reshape(frames, BLOCK, 3 * cols)

    total = jnp.zeros((frames * step_patches, model), F32)
    for h in range(lay.halves):
        total = total + dot_t(gt_scr[h].reshape(frames * step_patches, 3 * cols), w_scr[h])
    total = total.reshape(lay.chips, lay.nc, step_patches, model)
    for k in range(lay.chips):
        gh_refs[k][...] = total[k].astype(gh_refs[k].dtype)


def output_kernel(lay, pos_ref, info_ref, *refs):
    pair_refs, refs = refs[: lay.nc], refs[lay.nc :]
    pr_refs, refs = refs[: lay.chips], refs[lay.chips :]
    mod_ref, *out_refs = refs
    step_patches, model = out_refs[0].shape
    patches = step_patches * pl.num_programs(0)
    patch_base = lay.unit(pos_ref[1], pos_ref[2])[2] * patches + pl.program_id(0) * step_patches
    patch = patch_base + lax.broadcasted_iota(jnp.int32, (step_patches, 1), 0)
    for j in range(lay.nc):
        _, limit, step = slot_scalars(lay, pos_ref, info_ref, (0, j))
        factor = jnp.where(patch < limit, table_row(mod_ref, step, 2, model), 0.0)
        projected = pr_refs[0][j]
        for k in range(1, lay.chips):
            projected = projected + pr_refs[k][j].astype(F32)
        projected = projected.astype(BF16).astype(F32)
        out_refs[j][...] = (pair_refs[j][0, 0].astype(F32) + factor * projected).astype(BF16)


def input_grad_kernel(lay, pos_ref, info_ref, *refs):
    pair_refs, refs = refs[: lay.nc], refs[lay.nc :]
    gh_refs, refs = refs[: lay.chips], refs[lay.chips :]
    mod_ref, *out_refs = refs
    model = out_refs[0].shape[1]
    for j in range(lay.nc):
        _, _, step = slot_scalars(lay, pos_ref, info_ref, (0, j))
        grad_hidden = gh_refs[0][j]
        for k in range(1, lay.chips):
            grad_hidden = grad_hidden + gh_refs[k][j].astype(F32)
        grad_hidden = grad_hidden.astype(BF16).astype(F32)
        normed, inv_sigma = normalize(pair_refs[j][0, 0].astype(F32))
        grad_norm = grad_hidden * (1.0 + table_row(mod_ref, step, 1, model))
        first_mean = jnp.mean(grad_norm, axis=-1, keepdims=True)
        second_mean = jnp.mean(grad_norm * normed, axis=-1, keepdims=True)
        grad_x = pair_refs[j][0, 1].astype(F32) + inv_sigma * (
            grad_norm - first_mean - normed * second_mean
        )
        out_refs[j][...] = grad_x.astype(BF16)


def whole_spec(shape):
    return pl.BlockSpec(shape, lambda *_: (0,) * len(shape))


def struct(shape, dtype=BF16):
    return jax.ShapeDtypeStruct(shape, dtype)


def local(lay, frames_x, grad_y, clip_ids, clip_patches, clip_step, mod_table, w_qkv, w_out):
    y, c, z, x = (lax.axis_index(name) for name in AXES)
    _, patches, model = frames_x.shape
    half = patches // lay.nc
    chips, nc, nx = lay.chips, lay.nc, lay.nx
    head_size = model // HEADS
    halves = lay.halves
    cols = lay.half_heads * head_size
    chip_width = lay.chip_heads * head_size
    rows = w_qkv.shape[0]
    groups = lay.nz
    quarter = model // groups
    step_patches = max(BLOCK, min(half, 512 // lay.frames))
    steps = half // step_patches
    tokens = lay.frames * step_patches

    def call(kernel, name, cost, in_specs, out_specs, out_shape, scratch=(), grid=(1,), prefetch=2):
        return pl.pallas_call(
            kernel,
            grid_spec=pltpu.PrefetchScalarGridSpec(
                num_scalar_prefetch=prefetch,
                grid=grid,
                in_specs=in_specs,
                out_specs=out_specs,
                scratch_shapes=list(scratch),
            ),
            out_shape=out_shape,
            compiler_params=pltpu.CompilerParams(vmem_limit_bytes=VMEM_LIMIT),
            cost_estimate=pl.CostEstimate(
                flops=cost * tokens * steps, bytes_accessed=4 * model * tokens, transcendentals=0
            ),
            name=name,
        )

    def chip_swap(k):
        ky, kx = lay.chip_of(k)
        return lay.swap(ky=ky, kx=kx)

    def from_plane(parts):
        got = [lax.ppermute(part, AXES, lay.from_plane(k)) for k, part in enumerate(parts)]
        first = jnp.where(z // lay.ny == 0, got[0], got[1])
        second = jnp.where(z // lay.ny == 0, got[1], got[0])
        return jnp.concatenate([first, second], axis=0)[None]

    def doubling(held, bits, swap, after, first=None):
        for bit in bits[:-1]:
            got = lax.ppermute(held, AXES, swap(bit)) if first is None else first
            held, first = jnp.concatenate([held, got], axis=0), None
        held, _ = lax.optimization_barrier((held, after))
        return [held, lax.ppermute(held, AXES, swap(bits[-1]))]

    def over_chips(parts):
        got = [lax.ppermute(parts[k], AXES, chip_swap(k)) for k in range(1, chips)]
        return [parts[0]] + got

    info = jnp.concatenate([clip_ids[0], clip_patches[0], clip_step[0]])[None]
    by_core = jnp.concatenate([info, lax.ppermute(info, AXES, lay.swap(kc=1))], axis=0)
    info = [by_core] + [
        lax.ppermute(by_core, AXES, lay.swap(ky=ky)) for ky in range(1, lay.ny)
    ]
    group_y, group_c, _ = lay.unit(c, z)
    info = sum(
        jnp.where((y ^ ky == group_y) & (c ^ kc == group_c), info[ky][kc], 0)
        for ky in range(lay.ny)
        for kc in range(nc)
    )
    pos = jnp.stack([y, c, z, x]).astype(jnp.int32)
    pair_shape = (1, 2, half, model)
    outputs = call(
        functools.partial(start_kernel, lay, cols),
        "start",
        2 * model * 1000,
        [whole_spec(frames_x.shape)] * 2 + [whole_spec(w_qkv.shape)],
        [whole_spec(pair_shape)] * nc + [whole_spec((rows, 3 * cols))] * nx,
        [struct(pair_shape)] * nc + [struct((rows, 3 * cols))] * nx,
        prefetch=1,
    )(pos, frames_x, grad_y, w_qkv)
    pairs, picked = outputs[:nc], outputs[nc:]
    own = [lax.ppermute(pair, AXES, lay.to_plane(k)) for k, pair in enumerate(pairs)]
    by_x = [picked[0]] + [
        lax.ppermute(picked[kx], AXES, lay.swap(kx=kx)) for kx in range(1, nx)
    ]
    if nx == 2:
        ordered = [jnp.where(x == i, by_x[0], by_x[1]) for i in range(nx)]
    else:
        stacked = jnp.stack(by_x)
        ordered = [lax.dynamic_index_in_dim(stacked, x ^ i, 0, keepdims=False) for i in range(nx)]
    w_own = jnp.concatenate(ordered, axis=1 if rows % 16 == 0 else 0)[None]
    first = lax.ppermute(own[0], AXES, chip_swap(lay.chip_bits(0)[0]))
    own[1], first = lax.optimization_barrier((own[1], first))
    w_own, _ = lax.optimization_barrier((w_own, own[1]))
    w_pieces = doubling(w_own, lay.bits(lay.nz)[::-1], lambda kz: lay.swap(kz=kz), [])
    late_w_out, _ = lax.optimization_barrier((w_out, own))
    wo_own = lax.ppermute(late_w_out, AXES, lay.rows_to_chip())

    pairs = []
    for j in range(nc):
        after = ([], None) if j else (info, first)
        pairs += doubling(own[j], lay.chip_bits(j), chip_swap, *after)
    pairs, w_pieces = lax.optimization_barrier((pairs, w_pieces))
    if halves > 1:
        w_pieces += [lax.ppermute(piece, AXES, lay.swap(kc=1)) for piece in w_pieces]


    def spread(count, width, patches_at_once):
        return pl.BlockSpec((count, patches_at_once, width), lambda i, *_: (0, i, 0))

    def pair_spec(count, patches_at_once):
        return pl.BlockSpec((count, 2, patches_at_once, model), lambda i, *_: (0, 0, i, 0))

    few = max(BLOCK, step_patches // 2)
    few_steps = half // few
    x_spec = pl.BlockSpec((few, model), lambda i, *_: (i, 0))
    triple_spec = pl.BlockSpec((halves, lay.frames, step_patches, cols), lambda i, *_: (0, 0, i, 0))
    w_specs = [whole_spec(w_pieces[0].shape)] * (2 * halves)
    w_scratch = pltpu.VMEM((halves, model, 3 * cols), BF16)
    mod_spec = whole_spec(mod_table.shape)
    triple_shape = struct((halves, lay.frames, half, cols))
    part_specs = [spread(nc, model, step_patches)] * chips
    part_shapes = [struct((nc, half, model), F32)] + [struct((nc, half, model))] * (chips - 1)

    wo_rows = [wo_own, lax.ppermute(wo_own, AXES, lay.swap(kc=1))]

    fold = 3 if rows % 24 == 0 else 1
    piece_shape = (groups, rows // fold, quarter * fold)
    queries, keys, values, grad_attn, kept, sent, *projected = call(
        functools.partial(forward_kernel, lay),
        "forward",
        14 * model * 1000,
        [pair_spec(chips // 2, step_patches)] * (2 * nc)
        + w_specs
        + [whole_spec(w_out.shape)] * nc
        + [mod_spec],
        [triple_spec] * 4 + [whole_spec(piece_shape)] * 2 + part_specs,
        [triple_shape] * 4 + [struct(piece_shape, F32)] * 2 + part_shapes,
        [pltpu.VMEM((lay.frames, step_patches, model), BF16)] * 2
        + [
            w_scratch,
            pltpu.VMEM((lay.frames, step_patches, chip_width), BF16),
            pltpu.VMEM((chip_width, model), BF16),
            pltpu.VMEM((chip_width, model), F32),
            pltpu.VMEM(piece_shape, F32),
        ],
        (steps,),
    )(pos, info, *pairs, *w_pieces, *wo_rows, mod_table)
    got = lax.ppermute(sent, AXES, lay.swap(kc=1))
    projected = over_chips(projected)

    middle = groups // 2
    cut, away = kept[:middle] + got[:middle], kept[middle:] + got[middle:]
    grad_attn, cut, away = lax.optimization_barrier((grad_attn, cut, away))
    first_away = lax.ppermute(away, AXES, lay.swap(kz=1))

    sums = call(
        functools.partial(backward_kernel, lay),
        "backward",
        10 * model * 1000,
        w_specs + [triple_spec] * 4,
        part_specs,
        part_shapes,
        [w_scratch, pltpu.VMEM((halves, lay.frames, step_patches, 3 * cols), BF16)],
        (steps,),
    )(pos, info, *w_pieces, queries, keys, values, grad_attn)
    sums, first_away, projected = lax.optimization_barrier((sums, first_away, projected))
    grad_hidden = over_chips(sums)

    out_parts = call(
        functools.partial(output_kernel, lay),
        "output",
        20 * model * 1000,
        [pair_spec(1, few)] * nc + [spread(nc, model, few)] * chips + [mod_spec],
        [x_spec] * nc,
        [struct((half, model))] * nc,
        grid=(few_steps,),
    )(pos, info, *own, *projected, mod_table)
    out_y = from_plane(out_parts)

    grad_hidden, _ = lax.optimization_barrier((grad_hidden, out_parts))
    grad_parts = call(
        functools.partial(input_grad_kernel, lay),
        "input_grad",
        3 * model * 1000,
        [pair_spec(1, few)] * nc + [spread(nc, model, few)] * chips + [mod_spec],
        [x_spec] * nc,
        [struct((half, model))] * nc,
        grid=(few_steps,),
    )(pos, info, *own, *grad_hidden, mod_table)
    grad_x = from_plane(grad_parts)

    cut, _ = lax.optimization_barrier((cut + first_away, out_parts))
    for bit in lay.bits(lay.nz)[1:]:
        middle = middle // 2
        cut = cut[:middle] + lax.ppermute(cut[middle:], AXES, lay.swap(kz=bit))
    cut, _ = lax.optimization_barrier((cut, grad_parts))
    grad_w = lax.ppermute(cut[0], AXES, lay.to_owner())
    grad_w = jnp.concatenate(
        [grad_w[:, m * quarter : (m + 1) * quarter] for m in range(fold)], axis=0
    )
    grad_w_out = grad_w * jnp.float32(1.0 / math.sqrt(groups * lay.frames * patches))
    return out_y, grad_x, grad_w_out


def solution(mesh):
    lay = Layout(mesh)
    grid = Mesh(mesh.devices.reshape(lay.ny, lay.nc, lay.nz, lay.nx), AXES)
    rows, cols = ("z", "x"), ("y", "c")
    frame = P(AXES, None, None)
    group = P(cols, None)
    return jax.shard_map(
        functools.partial(local, lay),
        mesh=grid,
        in_specs=(frame, frame, group, group, group, P(), P(rows, None), P(rows, None)),
        out_specs=(frame, frame, P(rows, cols)),
        check_vma=False,
    )
```

```python
import functools
import math

import jax
import jax.numpy as jnp
from jax import lax
from jax.experimental import pallas as pl
from jax.experimental.pallas import tpu as pltpu
from jax.sharding import Mesh, PartitionSpec as P

HEADS = 16
CORES = 2
AXES = ("y", "c", "z", "x")
BLOCK = 16
VMEM_LIMIT = 56 * 1024 * 1024
BF16 = jnp.bfloat16
F32 = jnp.float32


def dot(left, right):
    return jnp.dot(left, right, preferred_element_type=F32)


def dot_t(left, right):
    return lax.dot_general(left, right, (((1,), (1,)), ((), ())), preferred_element_type=F32)


def t_dot(left, right):
    return lax.dot_general(left, right, (((0,), (0,)), ((), ())), preferred_element_type=F32)


def normalize(values):
    centred = values - jnp.mean(values, axis=-1, keepdims=True)
    inv_sigma = lax.rsqrt(jnp.mean(centred * centred, axis=-1, keepdims=True) + 1e-06)
    return centred * inv_sigma, inv_sigma


class Layout:
    def __init__(self, mesh):
        groups, seq = mesh.shape["dp"], mesh.shape["seq"]
        self.nc = CORES
        self.ny = groups // CORES
        self.nz = groups
        self.nx = seq // self.nz
        self.chips = self.ny * self.nx
        self.frames = seq
        self.chip_heads = HEADS // self.chips
        self.halves = 2 if self.chip_heads % 2 == 0 else 1
        self.half_heads = self.chip_heads // self.halves

    def linear(self, y, c, z, x):
        return ((y * self.nc + c) * self.nz + z) * self.nx + x

    def perm(self, move):
        pairs = []
        for y in range(self.ny):
            for c in range(self.nc):
                for z in range(self.nz):
                    for x in range(self.nx):
                        pairs.append((self.linear(y, c, z, x), self.linear(*move(y, c, z, x))))
        return pairs

    def to_plane(self, k):
        def move(y, c, z, x):
            half = (z // self.ny) ^ k
            plane = ((y // self.nc) * self.nc + c) * self.nc + half
            return (z % self.ny) ^ c, y % self.nc, plane, x

        return self.perm(move)

    def unit(self, c, z):
        return (z // (self.nc * self.nc)) * self.nc + c, (z // self.nc) % self.nc, z % self.nc

    def from_plane(self, k):
        return [(target, source) for source, target in self.to_plane(k)]

    def swap(self, ky=0, kc=0, kz=0, kx=0):
        return self.perm(lambda y, c, z, x: (y ^ ky, c ^ kc, z ^ kz, x ^ kx))

    def row_block(self, y, x, i):
        if self.halves > 1:
            return (i * self.ny + y) * self.nx + x
        return self.nc * (y * self.nx + x) + i

    def rows_to_chip(self):
        reader = {
            self.row_block(y, x, i): (y, x, i)
            for y in range(self.ny)
            for x in range(self.nx)
            for i in range(self.nc)
        }

        def move(y, c, z, x):
            chip_y, chip_x, i = reader[z * self.nx + x]
            return chip_y, i, c * self.ny + (y ^ (z & 1)), chip_x

        return self.perm(move)

    def to_owner(self):
        def move(y, c, z, x):
            s = self.row_block(y, x, c)
            return z // self.nc, z % self.nc, s // self.nx, s % self.nx

        return self.perm(move)

    def chip_of(self, k):
        return k // self.nx, k % self.nx

    def bits(self, count):
        return [1 << b for b in range(count.bit_length() - 1)]

    def chip_bits(self, j):
        bits = self.bits(self.chips)
        return bits if j % 2 == 0 else bits[::-1]

    def doubled(self, bits):
        held = [0]
        for bit in bits:
            held = held + [k ^ bit for k in held]
        return held

    def slots(self):
        return [(k, j) for k in range(self.chips) for j in range(self.nc)]


def slot_scalars(lay, pos_ref, info_ref, slot):
    k, j = slot
    ky, kx = lay.chip_of(k)
    _, group_c, half = lay.unit(pos_ref[1], pos_ref[2])
    z_frame = (half ^ j) * lay.ny + (pos_ref[0] ^ ky ^ group_c)
    frame = z_frame * lay.nx + (pos_ref[3] ^ kx)
    clip = info_ref[frame]
    clips = (info_ref.shape[0] - lay.frames) // 2
    return clip, info_ref[lay.frames + clip], info_ref[lay.frames + clips + clip]


def table_row(mod_ref, step, part, width):
    return mod_ref[pl.ds(step, 1), part * width : (part + 1) * width]


def allowed_pairs(lay, pos_ref, info_ref, patch_base):
    rows = lay.frames * BLOCK
    row_slot = lax.broadcasted_iota(jnp.int32, (rows, 1), 0) // BLOCK
    col_slot = lax.broadcasted_iota(jnp.int32, (1, rows), 1) // BLOCK
    row_clip = jnp.zeros((rows, 1), jnp.int32)
    row_limit = jnp.zeros((rows, 1), jnp.int32)
    col_clip = jnp.zeros((1, rows), jnp.int32)
    for t, slot in enumerate(lay.slots()):
        clip, limit, _ = slot_scalars(lay, pos_ref, info_ref, slot)
        row_clip = jnp.where(row_slot == t, clip, row_clip)
        row_limit = jnp.where(row_slot == t, limit, row_limit)
        col_clip = jnp.where(col_slot == t, clip, col_clip)
    row_patch = lax.broadcasted_iota(jnp.int32, (rows, 1), 0) % BLOCK
    col_patch = lax.broadcasted_iota(jnp.int32, (1, rows), 1) % BLOCK
    row_key = row_clip * BLOCK + row_patch
    col_key = col_clip * BLOCK + col_patch
    row_valid = (patch_base + row_patch < row_limit).astype(jnp.int32)
    row_index = lax.broadcasted_iota(jnp.int32, (rows, rows), 0)
    col_index = lax.broadcasted_iota(jnp.int32, (rows, rows), 1)
    return (row_key == col_key) & ((row_valid > 0) | (row_index == col_index))


def head_mask(values, head, head_size):
    lane = lax.broadcasted_iota(jnp.int32, (1, values.shape[1]), 1)
    inside = (lane >= head * head_size) & (lane < (head + 1) * head_size)
    return jnp.where(inside, values, jnp.zeros_like(values))


def patch_blocks(array, block):
    part = array[:, block * BLOCK : (block + 1) * BLOCK, :]
    return part.reshape(part.shape[0] * BLOCK, part.shape[2])


def halves_kernel(lay, pos_ref, x_ref, g_ref, *pair_refs):
    half = x_ref.shape[1] // lay.nc
    for k, ref in enumerate(pair_refs):
        first = pl.multiple_of(((pos_ref[2] // lay.ny) ^ k) * half, 16)
        ref[0, 0] = x_ref[0, pl.ds(first, half), :]
        ref[0, 1] = g_ref[0, pl.ds(first, half), :]


def pick_kernel(lay, cols, pos_ref, w_ref, *out_refs):
    model = w_ref.shape[1] // 3
    for k, out_ref in enumerate(out_refs):
        chip_x = pos_ref[3] ^ k
        if lay.halves > 1:
            want = lay.row_block(pos_ref[0], chip_x, pos_ref[1])
        else:
            want = pos_ref[0] * lay.nx + chip_x
        for v in range(lay.chips * lay.halves):

            @pl.when(want == v)
            def _(v=v, out_ref=out_ref):
                parts = [
                    w_ref[:, p * model + v * cols : p * model + (v + 1) * cols]
                    for p in range(3)
                ]
                out_ref[...] = jnp.concatenate(parts, axis=1)


def fill_weights(lay, pos_ref, w_refs, w_scr):
    order = lay.doubled(lay.bits(lay.nz)[::-1])
    block = w_scr.shape[1] // lay.nz
    rows, width = w_refs[0].shape[1], w_scr.shape[2]
    for h in range(lay.halves):
        for n, k in enumerate(order):
            ref, place = w_refs[2 * h + (2 * n) // lay.nz], n % (lay.nz // 2)
            for m in range(block // rows):
                start = pl.multiple_of((pos_ref[2] ^ k) * block + m * rows, 16)
                w_scr[h, pl.ds(start, rows), :] = ref[place, :, m * width : (m + 1) * width]


def heads_stacked(lay, values):
    head_size = values.shape[1] // lay.half_heads
    parts = [head_mask(values, head, head_size) for head in range(lay.half_heads)]
    return jnp.concatenate(parts, axis=0) if len(parts) > 1 else parts[0]


def beside(lay, weights):
    return jnp.concatenate([weights[head] for head in range(lay.half_heads)], axis=1)


def attention_weights(lay, keys_stacked, queries, allowed, scaling):
    scores = dot_t(keys_stacked, queries) * scaling
    scores = jnp.where(allowed, scores.reshape((lay.half_heads,) + allowed.shape), -jnp.inf)
    exponent = jnp.exp(scores - jnp.max(scores, axis=1, keepdims=True))
    return exponent * (1.0 / jnp.sum(exponent, axis=1, keepdims=True))


def modulate(lay, pos_ref, info_ref, pair_refs, mod_ref, hid_ref, gp_ref):
    _, step_patches, model = hid_ref.shape
    patches = step_patches * pl.num_programs(0)
    patch_base = lay.unit(pos_ref[1], pos_ref[2])[2] * patches + pl.program_id(0) * step_patches
    patch = patch_base + lax.broadcasted_iota(jnp.int32, (step_patches, 1), 0)
    for t, (k, j) in enumerate(lay.slots()):
        _, limit, step = slot_scalars(lay, pos_ref, info_ref, (k, j))
        n = lay.doubled(lay.chip_bits(j)).index(k)
        ref, place = pair_refs[2 * j + (2 * n) // lay.chips], n % (lay.chips // 2)
        normed, _ = normalize(ref[place, 0].astype(F32))
        shift, scale = table_row(mod_ref, step, 0, model), table_row(mod_ref, step, 1, model)
        hid_ref[t] = (normed * (1.0 + scale) + shift).astype(BF16)
        factor = jnp.where(patch < limit, table_row(mod_ref, step, 2, model), 0.0)
        gp_ref[t] = (factor * ref[place, 1].astype(F32)).astype(BF16)


def forward_kernel(lay, pos_ref, info_ref, *refs):
    pair_refs, refs = refs[: 2 * lay.nc], refs[2 * lay.nc :]
    w_refs, refs = refs[: 2 * lay.halves], refs[2 * lay.halves :]
    wo_refs, refs = refs[: lay.nc], refs[lay.nc :]
    mod_ref, q_ref, k_ref, v_ref, ga_ref, kept_ref, sent_ref, *refs = refs
    pr_refs, refs = refs[: lay.chips], refs[lay.chips :]
    hid_ref, gp_ref, w_scr, att_scr, wo_scr, acc_scr, cut_scr = refs
    _, step_patches, model = hid_ref.shape
    tokens = lay.frames * step_patches
    cols = w_scr.shape[2] // 3
    scaling = 1.0 / math.sqrt(cols // lay.half_heads)
    patches = step_patches * pl.num_programs(0)
    is_first = pos_ref[1] == 0

    @pl.when(pl.program_id(0) == 0)
    def _():
        fill_weights(lay, pos_ref, w_refs, w_scr)
        own, other = wo_refs[0][...].astype(F32), wo_refs[1][...].astype(F32)
        both = [jnp.where(is_first, own, other), jnp.where(is_first, other, own)]
        wo_scr[...] = jnp.concatenate(both, axis=0).astype(BF16)
        acc_scr[...] = jnp.zeros_like(acc_scr)

    modulate(lay, pos_ref, info_ref, pair_refs, mod_ref, hid_ref, gp_ref)
    hidden = hid_ref[...].reshape(lay.frames * step_patches, model)
    for h in range(lay.halves):
        triple = dot(hidden, w_scr[h])
        for n, ref in enumerate((q_ref, k_ref, v_ref)):
            ref[h] = triple[:, n * cols : (n + 1) * cols].astype(BF16).reshape(ref.shape[1:])

    for b in range(step_patches // BLOCK):
        patch_base = lay.unit(pos_ref[1], pos_ref[2])[2] * patches + pl.program_id(0) * step_patches + b * BLOCK
        allowed = allowed_pairs(lay, pos_ref, info_ref, patch_base)
        outputs = []
        for h in range(lay.halves):
            queries, keys, values = (patch_blocks(ref[h], b) for ref in (q_ref, k_ref, v_ref))
            weights = attention_weights(lay, heads_stacked(lay, keys), queries, allowed, scaling)
            weights = weights.astype(BF16).reshape(-1, allowed.shape[1])
            outputs.append(t_dot(weights, heads_stacked(lay, values)))
        if lay.halves > 1:
            first = jnp.where(pos_ref[1] == 0, outputs[0], outputs[1])
            second = jnp.where(pos_ref[1] == 0, outputs[1], outputs[0])
            outputs = [jnp.concatenate([first, second], axis=1)]
        attended = outputs[0].astype(BF16)
        att_scr[:, b * BLOCK : (b + 1) * BLOCK, :] = attended.reshape(lay.frames, BLOCK, -1)

    attended = att_scr[...].reshape(tokens, -1)
    grad_proj = gp_ref[...].reshape(tokens, model)
    acc_scr[...] += t_dot(attended, grad_proj)
    grad_attn = dot_t(grad_proj, wo_scr[...])
    part = wo_scr.shape[0] // lay.halves
    for h in range(lay.halves):
        ga_ref[h] = grad_attn[:, h * part : (h + 1) * part].astype(BF16).reshape(ga_ref.shape[1:])
    projected = dot(attended, wo_scr[...]).reshape(lay.chips, lay.nc, step_patches, model)
    for k in range(lay.chips):
        pr_refs[k][...] = projected[k].astype(pr_refs[k].dtype)

    @pl.when(pl.program_id(0) == pl.num_programs(0) - 1)
    def _():
        groups, chunk_rows, chunk_width = kept_ref.shape
        block_rows, part = acc_scr.shape[0] // lay.nc, model // groups
        order = lay.doubled(lay.bits(lay.nz)[::-1])
        first, second = acc_scr[:block_rows, :], acc_scr[block_rows:, :]
        kept = jnp.where(is_first, first, second)
        sent = jnp.where(is_first, second, first)
        for ref, rows in ((kept_ref, kept), (sent_ref, sent)):
            for d in range(groups):
                chunk = [
                    rows[m * chunk_rows : (m + 1) * chunk_rows, d * part : (d + 1) * part]
                    for m in range(chunk_width // part)
                ]
                cut_scr[d] = jnp.concatenate(chunk, axis=1) if len(chunk) > 1 else chunk[0]
            for n, k in enumerate(order):
                ref[n] = cut_scr[pos_ref[2] ^ k]


def backward_kernel(lay, pos_ref, info_ref, *refs):
    w_refs, refs = refs[: 2 * lay.halves], refs[2 * lay.halves :]
    q_ref, k_ref, v_ref, ga_ref, *refs = refs
    gh_refs, (w_scr, gt_scr) = refs[: lay.chips], refs[lay.chips :]
    _, frames, step_patches, cols = q_ref.shape
    model = w_scr.shape[1]
    patches = step_patches * pl.num_programs(0)
    scaling = 1.0 / math.sqrt(cols // lay.half_heads)

    @pl.when(pl.program_id(0) == 0)
    def _():
        fill_weights(lay, pos_ref, w_refs, w_scr)

    for b in range(step_patches // BLOCK):
        patch_base = lay.unit(pos_ref[1], pos_ref[2])[2] * patches + pl.program_id(0) * step_patches + b * BLOCK
        allowed = allowed_pairs(lay, pos_ref, info_ref, patch_base)
        for h in range(lay.halves):
            queries, keys, values = (patch_blocks(ref[h], b) for ref in (q_ref, k_ref, v_ref))
            grad_out = patch_blocks(ga_ref[(pos_ref[1] ^ h) if lay.halves > 1 else 0], b)
            keys = heads_stacked(lay, keys)
            weights = attention_weights(lay, keys, queries, allowed, scaling)
            grad_weights = dot_t(heads_stacked(lay, values), grad_out).reshape(weights.shape)
            grad_values = dot(beside(lay, weights.astype(BF16)), heads_stacked(lay, grad_out))
            inner = jnp.sum(weights * grad_weights, axis=1, keepdims=True)
            grad_scores = (weights * (grad_weights - inner) * scaling).astype(BF16)
            grad_queries = t_dot(grad_scores.reshape(-1, grad_scores.shape[2]), keys)
            grad_keys = dot(beside(lay, grad_scores), heads_stacked(lay, queries))
            grads = jnp.concatenate([grad_queries, grad_keys, grad_values], axis=1).astype(BF16)
            gt_scr[h, :, b * BLOCK : (b + 1) * BLOCK, :] = grads.reshape(frames, BLOCK, 3 * cols)

    total = jnp.zeros((frames * step_patches, model), F32)
    for h in range(lay.halves):
        total = total + dot_t(gt_scr[h].reshape(frames * step_patches, 3 * cols), w_scr[h])
    total = total.reshape(lay.chips, lay.nc, step_patches, model)
    for k in range(lay.chips):
        gh_refs[k][...] = total[k].astype(gh_refs[k].dtype)


def output_kernel(lay, pos_ref, info_ref, *refs):
    pair_refs, refs = refs[: lay.nc], refs[lay.nc :]
    pr_refs, refs = refs[: lay.chips], refs[lay.chips :]
    mod_ref, *out_refs = refs
    step_patches, model = out_refs[0].shape
    patches = step_patches * pl.num_programs(0)
    patch_base = lay.unit(pos_ref[1], pos_ref[2])[2] * patches + pl.program_id(0) * step_patches
    patch = patch_base + lax.broadcasted_iota(jnp.int32, (step_patches, 1), 0)
    for j in range(lay.nc):
        _, limit, step = slot_scalars(lay, pos_ref, info_ref, (0, j))
        factor = jnp.where(patch < limit, table_row(mod_ref, step, 2, model), 0.0)
        projected = pr_refs[0][j]
        for k in range(1, lay.chips):
            projected = projected + pr_refs[k][j].astype(F32)
        projected = projected.astype(BF16).astype(F32)
        out_refs[j][...] = (pair_refs[j][0, 0].astype(F32) + factor * projected).astype(BF16)


def input_grad_kernel(lay, pos_ref, info_ref, *refs):
    pair_refs, refs = refs[: lay.nc], refs[lay.nc :]
    gh_refs, refs = refs[: lay.chips], refs[lay.chips :]
    mod_ref, *out_refs = refs
    model = out_refs[0].shape[1]
    for j in range(lay.nc):
        _, _, step = slot_scalars(lay, pos_ref, info_ref, (0, j))
        grad_hidden = gh_refs[0][j]
        for k in range(1, lay.chips):
            grad_hidden = grad_hidden + gh_refs[k][j].astype(F32)
        grad_hidden = grad_hidden.astype(BF16).astype(F32)
        normed, inv_sigma = normalize(pair_refs[j][0, 0].astype(F32))
        grad_norm = grad_hidden * (1.0 + table_row(mod_ref, step, 1, model))
        first_mean = jnp.mean(grad_norm, axis=-1, keepdims=True)
        second_mean = jnp.mean(grad_norm * normed, axis=-1, keepdims=True)
        grad_x = pair_refs[j][0, 1].astype(F32) + inv_sigma * (
            grad_norm - first_mean - normed * second_mean
        )
        out_refs[j][...] = grad_x.astype(BF16)


def whole_spec(shape):
    return pl.BlockSpec(shape, lambda *_: (0,) * len(shape))


def struct(shape, dtype=BF16):
    return jax.ShapeDtypeStruct(shape, dtype)


def local(lay, frames_x, grad_y, clip_ids, clip_patches, clip_step, mod_table, w_qkv, w_out):
    y, c, z, x = (lax.axis_index(name) for name in AXES)
    _, patches, model = frames_x.shape
    half = patches // lay.nc
    chips, nc, nx = lay.chips, lay.nc, lay.nx
    head_size = model // HEADS
    halves = lay.halves
    cols = lay.half_heads * head_size
    chip_width = lay.chip_heads * head_size
    rows = w_qkv.shape[0]
    groups = lay.nz
    quarter = model // groups
    step_patches = max(BLOCK, min(half, 512 // lay.frames))
    steps = half // step_patches
    tokens = lay.frames * step_patches

    def call(kernel, name, cost, in_specs, out_specs, out_shape, scratch=(), grid=(1,), prefetch=2):
        return pl.pallas_call(
            kernel,
            grid_spec=pltpu.PrefetchScalarGridSpec(
                num_scalar_prefetch=prefetch,
                grid=grid,
                in_specs=in_specs,
                out_specs=out_specs,
                scratch_shapes=list(scratch),
            ),
            out_shape=out_shape,
            compiler_params=pltpu.CompilerParams(vmem_limit_bytes=VMEM_LIMIT),
            cost_estimate=pl.CostEstimate(
                flops=cost * tokens * steps, bytes_accessed=4 * model * tokens, transcendentals=0
            ),
            name=name,
        )

    def chip_swap(k):
        ky, kx = lay.chip_of(k)
        return lay.swap(ky=ky, kx=kx)

    def from_plane(parts):
        got = [lax.ppermute(part, AXES, lay.from_plane(k)) for k, part in enumerate(parts)]
        first = jnp.where(z // lay.ny == 0, got[0], got[1])
        second = jnp.where(z // lay.ny == 0, got[1], got[0])
        return jnp.concatenate([first, second], axis=0)[None]

    def doubling(held, bits, swap, after, first=None):
        for bit in bits[:-1]:
            got = lax.ppermute(held, AXES, swap(bit)) if first is None else first
            held, first = jnp.concatenate([held, got], axis=0), None
        held, _ = lax.optimization_barrier((held, after))
        return [held, lax.ppermute(held, AXES, swap(bits[-1]))]

    def over_chips(parts):
        got = [lax.ppermute(parts[k], AXES, chip_swap(k)) for k in range(1, chips)]
        return [parts[0]] + got

    pos = jnp.stack([y, c, z, x]).astype(jnp.int32)
    pair_shape = (1, 2, half, model)
    pairs = call(
        functools.partial(halves_kernel, lay),
        "halves",
        model,
        [whole_spec(frames_x.shape)] * 2,
        [whole_spec(pair_shape)] * nc,
        [struct(pair_shape)] * nc,
        prefetch=1,
    )(pos, frames_x, grad_y)
    w_qkv, clip_ids, _ = lax.optimization_barrier((w_qkv, clip_ids, pairs))
    info = jnp.concatenate([clip_ids[0], clip_patches[0], clip_step[0]])[None]
    by_core = jnp.concatenate([info, lax.ppermute(info, AXES, lay.swap(kc=1))], axis=0)
    info = [by_core] + [
        lax.ppermute(by_core, AXES, lay.swap(ky=ky)) for ky in range(1, lay.ny)
    ]
    group_y, group_c, _ = lay.unit(c, z)
    info = sum(
        jnp.where((y ^ ky == group_y) & (c ^ kc == group_c), info[ky][kc], 0)
        for ky in range(lay.ny)
        for kc in range(nc)
    )
    picked = call(
        functools.partial(pick_kernel, lay, cols),
        "pick",
        20 * model * 1000,
        [whole_spec(w_qkv.shape)],
        [whole_spec((rows, 3 * cols))] * nx,
        [struct((rows, 3 * cols))] * nx,
        prefetch=1,
    )(pos, w_qkv)
    own = [lax.ppermute(pair, AXES, lay.to_plane(k)) for k, pair in enumerate(pairs)]
    by_x = [picked[0]] + [
        lax.ppermute(picked[kx], AXES, lay.swap(kx=kx)) for kx in range(1, nx)
    ]
    if nx == 2:
        ordered = [jnp.where(x == i, by_x[0], by_x[1]) for i in range(nx)]
    else:
        stacked = jnp.stack(by_x)
        ordered = [lax.dynamic_index_in_dim(stacked, x ^ i, 0, keepdims=False) for i in range(nx)]
    w_own = jnp.concatenate(ordered, axis=1 if rows % 16 == 0 else 0)[None]
    first = lax.ppermute(own[0], AXES, chip_swap(lay.chip_bits(0)[0]))
    own[1], first = lax.optimization_barrier((own[1], first))
    w_own, _ = lax.optimization_barrier((w_own, own[1]))
    w_pieces = doubling(w_own, lay.bits(lay.nz)[::-1], lambda kz: lay.swap(kz=kz), [])
    late_w_out, _ = lax.optimization_barrier((w_out, own))
    wo_own = lax.ppermute(late_w_out, AXES, lay.rows_to_chip())

    pairs = []
    for j in range(nc):
        after = ([], None) if j else (info, first)
        pairs += doubling(own[j], lay.chip_bits(j), chip_swap, *after)
    pairs, w_pieces = lax.optimization_barrier((pairs, w_pieces))
    if halves > 1:
        w_pieces += [lax.ppermute(piece, AXES, lay.swap(kc=1)) for piece in w_pieces]


    def spread(count, width, patches_at_once):
        return pl.BlockSpec((count, patches_at_once, width), lambda i, *_: (0, i, 0))

    def pair_spec(count, patches_at_once):
        return pl.BlockSpec((count, 2, patches_at_once, model), lambda i, *_: (0, 0, i, 0))

    few = max(BLOCK, step_patches // 2)
    few_steps = half // few
    x_spec = pl.BlockSpec((few, model), lambda i, *_: (i, 0))
    triple_spec = pl.BlockSpec((halves, lay.frames, step_patches, cols), lambda i, *_: (0, 0, i, 0))
    w_specs = [whole_spec(w_pieces[0].shape)] * (2 * halves)
    w_scratch = pltpu.VMEM((halves, model, 3 * cols), BF16)
    mod_spec = whole_spec(mod_table.shape)
    triple_shape = struct((halves, lay.frames, half, cols))
    part_specs = [spread(nc, model, step_patches)] * chips
    part_shapes = [struct((nc, half, model), F32)] + [struct((nc, half, model))] * (chips - 1)

    wo_rows = [wo_own, lax.ppermute(wo_own, AXES, lay.swap(kc=1))]

    fold = 3 if rows % 24 == 0 else 1
    piece_shape = (groups, rows // fold, quarter * fold)
    queries, keys, values, grad_attn, kept, sent, *projected = call(
        functools.partial(forward_kernel, lay),
        "forward",
        14 * model * 1000,
        [pair_spec(chips // 2, step_patches)] * (2 * nc)
        + w_specs
        + [whole_spec(w_out.shape)] * nc
        + [mod_spec],
        [triple_spec] * 4 + [whole_spec(piece_shape)] * 2 + part_specs,
        [triple_shape] * 4 + [struct(piece_shape, F32)] * 2 + part_shapes,
        [pltpu.VMEM((lay.frames, step_patches, model), BF16)] * 2
        + [
            w_scratch,
            pltpu.VMEM((lay.frames, step_patches, chip_width), BF16),
            pltpu.VMEM((chip_width, model), BF16),
            pltpu.VMEM((chip_width, model), F32),
            pltpu.VMEM(piece_shape, F32),
        ],
        (steps,),
    )(pos, info, *pairs, *w_pieces, *wo_rows, mod_table)
    got = lax.ppermute(sent, AXES, lay.swap(kc=1))
    projected = over_chips(projected)

    middle = groups // 2
    cut, away = kept[:middle] + got[:middle], kept[middle:] + got[middle:]
    grad_attn, cut, away = lax.optimization_barrier((grad_attn, cut, away))
    first_away = lax.ppermute(away, AXES, lay.swap(kz=1))

    sums = call(
        functools.partial(backward_kernel, lay),
        "backward",
        10 * model * 1000,
        w_specs + [triple_spec] * 4,
        part_specs,
        part_shapes,
        [w_scratch, pltpu.VMEM((halves, lay.frames, step_patches, 3 * cols), BF16)],
        (steps,),
    )(pos, info, *w_pieces, queries, keys, values, grad_attn)
    sums, first_away, projected = lax.optimization_barrier((sums, first_away, projected))
    grad_hidden = over_chips(sums)

    out_parts = call(
        functools.partial(output_kernel, lay),
        "output",
        20 * model * 1000,
        [pair_spec(1, few)] * nc + [spread(nc, model, few)] * chips + [mod_spec],
        [x_spec] * nc,
        [struct((half, model))] * nc,
        grid=(few_steps,),
    )(pos, info, *own, *projected, mod_table)
    out_y = from_plane(out_parts)

    cut = cut + first_away
    for bit in lay.bits(lay.nz)[1:]:
        middle = middle // 2
        cut = cut[:middle] + lax.ppermute(cut[middle:], AXES, lay.swap(kz=bit))
    grad_hidden, cut, _ = lax.optimization_barrier((grad_hidden, cut, out_parts))
    grad_parts = call(
        functools.partial(input_grad_kernel, lay),
        "input_grad",
        3 * model * 1000,
        [pair_spec(1, few)] * nc + [spread(nc, model, few)] * chips + [mod_spec],
        [x_spec] * nc,
        [struct((half, model))] * nc,
        grid=(few_steps,),
    )(pos, info, *own, *grad_hidden, mod_table)
    grad_x = from_plane(grad_parts)

    cut, _ = lax.optimization_barrier((cut, grad_parts))
    grad_w = lax.ppermute(cut[0], AXES, lay.to_owner())
    grad_w = jnp.concatenate(
        [grad_w[:, m * quarter : (m + 1) * quarter] for m in range(fold)], axis=0
    )
    grad_w_out = grad_w * jnp.float32(1.0 / math.sqrt(groups * lay.frames * patches))
    return out_y, grad_x, grad_w_out


def solution(mesh):
    lay = Layout(mesh)
    grid = Mesh(mesh.devices.reshape(lay.ny, lay.nc, lay.nz, lay.nx), AXES)
    rows, cols = ("z", "x"), ("y", "c")
    frame = P(AXES, None, None)
    group = P(cols, None)
    return jax.shard_map(
        functools.partial(local, lay),
        mesh=grid,
        in_specs=(frame, frame, group, group, group, P(), P(rows, None), P(rows, None)),
        out_specs=(frame, frame, P(rows, cols)),
        check_vma=False,
    )
```

```python
import functools
import math

import jax
import jax.numpy as jnp
from jax import lax
from jax.experimental import pallas as pl
from jax.experimental.pallas import tpu as pltpu
from jax.sharding import Mesh, PartitionSpec as P

HEADS = 16
CORES = 2
AXES = ("y", "c", "z", "x")
BLOCK = 16
VMEM_LIMIT = 56 * 1024 * 1024
BF16 = jnp.bfloat16
F32 = jnp.float32


def dot(left, right):
    return jnp.dot(left, right, preferred_element_type=F32)


def dot_t(left, right):
    return lax.dot_general(left, right, (((1,), (1,)), ((), ())), preferred_element_type=F32)


def t_dot(left, right):
    return lax.dot_general(left, right, (((0,), (0,)), ((), ())), preferred_element_type=F32)


def normalize(values):
    centred = values - jnp.mean(values, axis=-1, keepdims=True)
    inv_sigma = lax.rsqrt(jnp.mean(centred * centred, axis=-1, keepdims=True) + 1e-06)
    return centred * inv_sigma, inv_sigma


class Layout:
    def __init__(self, mesh):
        groups, seq = mesh.shape["dp"], mesh.shape["seq"]
        self.nc = CORES
        self.ny = groups // CORES
        self.nz = groups
        self.nx = seq // self.nz
        self.chips = self.ny * self.nx
        self.frames = seq
        self.chip_heads = HEADS // self.chips
        self.halves = 2 if self.chip_heads % 2 == 0 else 1
        self.half_heads = self.chip_heads // self.halves

    def linear(self, y, c, z, x):
        return ((y * self.nc + c) * self.nz + z) * self.nx + x

    def perm(self, move):
        pairs = []
        for y in range(self.ny):
            for c in range(self.nc):
                for z in range(self.nz):
                    for x in range(self.nx):
                        pairs.append((self.linear(y, c, z, x), self.linear(*move(y, c, z, x))))
        return pairs

    def to_plane(self, k):
        def move(y, c, z, x):
            half = (z // self.ny) ^ k
            plane = ((y // self.nc) * self.nc + c) * self.nc + half
            return (z % self.ny) ^ c, y % self.nc, plane, x

        return self.perm(move)

    def unit(self, c, z):
        return (z // (self.nc * self.nc)) * self.nc + c, (z // self.nc) % self.nc, z % self.nc

    def from_plane(self, k):
        return [(target, source) for source, target in self.to_plane(k)]

    def swap(self, ky=0, kc=0, kz=0, kx=0):
        return self.perm(lambda y, c, z, x: (y ^ ky, c ^ kc, z ^ kz, x ^ kx))

    def row_block(self, y, x, i):
        if self.halves > 1:
            return (i * self.ny + y) * self.nx + x
        return self.nc * (y * self.nx + x) + i

    def rows_to_chip(self):
        reader = {
            self.row_block(y, x, i): (y, x, i)
            for y in range(self.ny)
            for x in range(self.nx)
            for i in range(self.nc)
        }

        def move(y, c, z, x):
            chip_y, chip_x, i = reader[z * self.nx + x]
            return chip_y, i, c * self.ny + (y ^ (z & 1)), chip_x

        return self.perm(move)

    def to_owner(self):
        def move(y, c, z, x):
            s = self.row_block(y, x, c)
            return z // self.nc, z % self.nc, s // self.nx, s % self.nx

        return self.perm(move)

    def chip_of(self, k):
        return k // self.nx, k % self.nx

    def bits(self, count):
        return [1 << b for b in range(count.bit_length() - 1)]

    def chip_bits(self, j):
        bits = self.bits(self.chips)
        return bits if j % 2 == 0 else bits[::-1]

    def doubled(self, bits):
        held = [0]
        for bit in bits:
            held = held + [k ^ bit for k in held]
        return held

    def slots(self):
        return [(k, j) for k in range(self.chips) for j in range(self.nc)]


def slot_scalars(lay, pos_ref, info_ref, slot):
    k, j = slot
    ky, kx = lay.chip_of(k)
    _, group_c, half = lay.unit(pos_ref[1], pos_ref[2])
    z_frame = (half ^ j) * lay.ny + (pos_ref[0] ^ ky ^ group_c)
    frame = z_frame * lay.nx + (pos_ref[3] ^ kx)
    clip = info_ref[frame]
    clips = (info_ref.shape[0] - lay.frames) // 2
    return clip, info_ref[lay.frames + clip], info_ref[lay.frames + clips + clip]


def table_row(mod_ref, step, part, width):
    return mod_ref[pl.ds(step, 1), part * width : (part + 1) * width]


def allowed_pairs(lay, pos_ref, info_ref, patch_base):
    rows = lay.frames * BLOCK
    row_slot = lax.broadcasted_iota(jnp.int32, (rows, 1), 0) // BLOCK
    col_slot = lax.broadcasted_iota(jnp.int32, (1, rows), 1) // BLOCK
    row_clip = jnp.zeros((rows, 1), jnp.int32)
    row_limit = jnp.zeros((rows, 1), jnp.int32)
    col_clip = jnp.zeros((1, rows), jnp.int32)
    for t, slot in enumerate(lay.slots()):
        clip, limit, _ = slot_scalars(lay, pos_ref, info_ref, slot)
        row_clip = jnp.where(row_slot == t, clip, row_clip)
        row_limit = jnp.where(row_slot == t, limit, row_limit)
        col_clip = jnp.where(col_slot == t, clip, col_clip)
    row_patch = lax.broadcasted_iota(jnp.int32, (rows, 1), 0) % BLOCK
    col_patch = lax.broadcasted_iota(jnp.int32, (1, rows), 1) % BLOCK
    row_key = row_clip * BLOCK + row_patch
    col_key = col_clip * BLOCK + col_patch
    row_valid = (patch_base + row_patch < row_limit).astype(jnp.int32)
    row_index = lax.broadcasted_iota(jnp.int32, (rows, rows), 0)
    col_index = lax.broadcasted_iota(jnp.int32, (rows, rows), 1)
    return (row_key == col_key) & ((row_valid > 0) | (row_index == col_index))


def head_mask(values, head, head_size):
    lane = lax.broadcasted_iota(jnp.int32, (1, values.shape[1]), 1)
    inside = (lane >= head * head_size) & (lane < (head + 1) * head_size)
    return jnp.where(inside, values, jnp.zeros_like(values))


def patch_blocks(array, block):
    part = array[:, block * BLOCK : (block + 1) * BLOCK, :]
    return part.reshape(part.shape[0] * BLOCK, part.shape[2])


def start_kernel(lay, cols, pos_ref, x_ref, g_ref, w_ref, *refs):
    pair_refs, out_refs = refs[: lay.nc], refs[lay.nc :]
    half = x_ref.shape[1] // lay.nc
    for k, ref in enumerate(pair_refs):
        first = pl.multiple_of(((pos_ref[2] // lay.ny) ^ k) * half, 16)
        ref[0, 0] = x_ref[0, pl.ds(first, half), :]
        ref[0, 1] = g_ref[0, pl.ds(first, half), :]
    model = w_ref.shape[1] // 3
    for k, out_ref in enumerate(out_refs):
        chip_x = pos_ref[3] ^ k
        if lay.halves > 1:
            want = lay.row_block(pos_ref[0], chip_x, pos_ref[1])
        else:
            want = pos_ref[0] * lay.nx + chip_x
        for v in range(lay.chips * lay.halves):

            @pl.when(want == v)
            def _(v=v, out_ref=out_ref):
                parts = [
                    w_ref[:, p * model + v * cols : p * model + (v + 1) * cols]
                    for p in range(3)
                ]
                out_ref[...] = jnp.concatenate(parts, axis=1)


def fill_weights(lay, pos_ref, w_refs, w_scr):
    order = lay.doubled(lay.bits(lay.nz)[::-1])
    block = w_scr.shape[1] // lay.nz
    rows, width = w_refs[0].shape[1], w_scr.shape[2]
    for h in range(lay.halves):
        for n, k in enumerate(order):
            ref, place = w_refs[2 * h + (2 * n) // lay.nz], n % (lay.nz // 2)
            for m in range(block // rows):
                start = pl.multiple_of((pos_ref[2] ^ k) * block + m * rows, 16)
                w_scr[h, pl.ds(start, rows), :] = ref[place, :, m * width : (m + 1) * width]


def heads_stacked(lay, values):
    head_size = values.shape[1] // lay.half_heads
    parts = [head_mask(values, head, head_size) for head in range(lay.half_heads)]
    return jnp.concatenate(parts, axis=0) if len(parts) > 1 else parts[0]


def beside(lay, weights):
    return jnp.concatenate([weights[head] for head in range(lay.half_heads)], axis=1)


def attention_weights(lay, keys_stacked, queries, allowed, scaling):
    scores = dot_t(keys_stacked, queries) * scaling
    scores = jnp.where(allowed, scores.reshape((lay.half_heads,) + allowed.shape), -jnp.inf)
    exponent = jnp.exp(scores - jnp.max(scores, axis=1, keepdims=True))
    return exponent * (1.0 / jnp.sum(exponent, axis=1, keepdims=True))


def modulate(lay, pos_ref, info_ref, pair_refs, mod_ref, hid_ref, gp_ref):
    _, step_patches, model = hid_ref.shape
    patches = step_patches * pl.num_programs(0)
    patch_base = lay.unit(pos_ref[1], pos_ref[2])[2] * patches + pl.program_id(0) * step_patches
    patch = patch_base + lax.broadcasted_iota(jnp.int32, (step_patches, 1), 0)
    for t, (k, j) in enumerate(lay.slots()):
        _, limit, step = slot_scalars(lay, pos_ref, info_ref, (k, j))
        n = lay.doubled(lay.chip_bits(j)).index(k)
        ref, place = pair_refs[2 * j + (2 * n) // lay.chips], n % (lay.chips // 2)
        normed, _ = normalize(ref[place, 0].astype(F32))
        shift, scale = table_row(mod_ref, step, 0, model), table_row(mod_ref, step, 1, model)
        hid_ref[t] = (normed * (1.0 + scale) + shift).astype(BF16)
        factor = jnp.where(patch < limit, table_row(mod_ref, step, 2, model), 0.0)
        gp_ref[t] = (factor * ref[place, 1].astype(F32)).astype(BF16)


def forward_kernel(lay, pos_ref, info_ref, *refs):
    pair_refs, refs = refs[: 2 * lay.nc], refs[2 * lay.nc :]
    w_refs, refs = refs[: 2 * lay.halves], refs[2 * lay.halves :]
    wo_refs, refs = refs[: lay.nc], refs[lay.nc :]
    mod_ref, q_ref, k_ref, v_ref, ga_ref, kept_ref, sent_ref, *refs = refs
    pr_refs, refs = refs[: lay.chips], refs[lay.chips :]
    hid_ref, gp_ref, w_scr, att_scr, wo_scr, acc_scr, cut_scr = refs
    _, step_patches, model = hid_ref.shape
    tokens = lay.frames * step_patches
    cols = w_scr.shape[2] // 3
    scaling = 1.0 / math.sqrt(cols // lay.half_heads)
    patches = step_patches * pl.num_programs(0)
    is_first = pos_ref[1] == 0

    @pl.when(pl.program_id(0) == 0)
    def _():
        fill_weights(lay, pos_ref, w_refs, w_scr)
        own, other = wo_refs[0][...].astype(F32), wo_refs[1][...].astype(F32)
        both = [jnp.where(is_first, own, other), jnp.where(is_first, other, own)]
        wo_scr[...] = jnp.concatenate(both, axis=0).astype(BF16)
        acc_scr[...] = jnp.zeros_like(acc_scr)

    modulate(lay, pos_ref, info_ref, pair_refs, mod_ref, hid_ref, gp_ref)
    hidden = hid_ref[...].reshape(lay.frames * step_patches, model)
    for h in range(lay.halves):
        triple = dot(hidden, w_scr[h])
        for n, ref in enumerate((q_ref, k_ref, v_ref)):
            ref[h] = triple[:, n * cols : (n + 1) * cols].astype(BF16).reshape(ref.shape[1:])

    for b in range(step_patches // BLOCK):
        patch_base = lay.unit(pos_ref[1], pos_ref[2])[2] * patches + pl.program_id(0) * step_patches + b * BLOCK
        allowed = allowed_pairs(lay, pos_ref, info_ref, patch_base)
        outputs = []
        for h in range(lay.halves):
            queries, keys, values = (patch_blocks(ref[h], b) for ref in (q_ref, k_ref, v_ref))
            weights = attention_weights(lay, heads_stacked(lay, keys), queries, allowed, scaling)
            weights = weights.astype(BF16).reshape(-1, allowed.shape[1])
            outputs.append(t_dot(weights, heads_stacked(lay, values)))
        if lay.halves > 1:
            first = jnp.where(pos_ref[1] == 0, outputs[0], outputs[1])
            second = jnp.where(pos_ref[1] == 0, outputs[1], outputs[0])
            outputs = [jnp.concatenate([first, second], axis=1)]
        attended = outputs[0].astype(BF16)
        att_scr[:, b * BLOCK : (b + 1) * BLOCK, :] = attended.reshape(lay.frames, BLOCK, -1)

    attended = att_scr[...].reshape(tokens, -1)
    grad_proj = gp_ref[...].reshape(tokens, model)
    acc_scr[...] += t_dot(attended, grad_proj)
    grad_attn = dot_t(grad_proj, wo_scr[...])
    part = wo_scr.shape[0] // lay.halves
    for h in range(lay.halves):
        ga_ref[h] = grad_attn[:, h * part : (h + 1) * part].astype(BF16).reshape(ga_ref.shape[1:])
    projected = dot(attended, wo_scr[...]).reshape(lay.chips, lay.nc, step_patches, model)
    for k in range(lay.chips):
        pr_refs[k][...] = projected[k].astype(pr_refs[k].dtype)

    @pl.when(pl.program_id(0) == pl.num_programs(0) - 1)
    def _():
        groups, chunk_rows, chunk_width = kept_ref.shape
        block_rows, part = acc_scr.shape[0] // lay.nc, model // groups
        order = lay.doubled(lay.bits(lay.nz)[::-1])
        first, second = acc_scr[:block_rows, :], acc_scr[block_rows:, :]
        kept = jnp.where(is_first, first, second)
        sent = jnp.where(is_first, second, first)
        for ref, rows in ((kept_ref, kept), (sent_ref, sent)):
            for d in range(groups):
                chunk = [
                    rows[m * chunk_rows : (m + 1) * chunk_rows, d * part : (d + 1) * part]
                    for m in range(chunk_width // part)
                ]
                cut_scr[d] = jnp.concatenate(chunk, axis=1) if len(chunk) > 1 else chunk[0]
            for n, k in enumerate(order):
                ref[n] = cut_scr[pos_ref[2] ^ k]


def backward_kernel(lay, pos_ref, info_ref, *refs):
    w_refs, refs = refs[: 2 * lay.halves], refs[2 * lay.halves :]
    q_ref, k_ref, v_ref, ga_ref, *refs = refs
    gh_refs, (w_scr, gt_scr) = refs[: lay.chips], refs[lay.chips :]
    _, frames, step_patches, cols = q_ref.shape
    model = w_scr.shape[1]
    patches = step_patches * pl.num_programs(0)
    scaling = 1.0 / math.sqrt(cols // lay.half_heads)

    @pl.when(pl.program_id(0) == 0)
    def _():
        fill_weights(lay, pos_ref, w_refs, w_scr)

    for b in range(step_patches // BLOCK):
        patch_base = lay.unit(pos_ref[1], pos_ref[2])[2] * patches + pl.program_id(0) * step_patches + b * BLOCK
        allowed = allowed_pairs(lay, pos_ref, info_ref, patch_base)
        for h in range(lay.halves):
            queries, keys, values = (patch_blocks(ref[h], b) for ref in (q_ref, k_ref, v_ref))
            grad_out = patch_blocks(ga_ref[(pos_ref[1] ^ h) if lay.halves > 1 else 0], b)
            keys = heads_stacked(lay, keys)
            weights = attention_weights(lay, keys, queries, allowed, scaling)
            grad_weights = dot_t(heads_stacked(lay, values), grad_out).reshape(weights.shape)
            grad_values = dot(beside(lay, weights.astype(BF16)), heads_stacked(lay, grad_out))
            inner = jnp.sum(weights * grad_weights, axis=1, keepdims=True)
            grad_scores = (weights * (grad_weights - inner) * scaling).astype(BF16)
            grad_queries = t_dot(grad_scores.reshape(-1, grad_scores.shape[2]), keys)
            grad_keys = dot(beside(lay, grad_scores), heads_stacked(lay, queries))
            grads = jnp.concatenate([grad_queries, grad_keys, grad_values], axis=1).astype(BF16)
            gt_scr[h, :, b * BLOCK : (b + 1) * BLOCK, :] = grads.reshape(frames, BLOCK, 3 * cols)

    total = jnp.zeros((frames * step_patches, model), F32)
    for h in range(lay.halves):
        total = total + dot_t(gt_scr[h].reshape(frames * step_patches, 3 * cols), w_scr[h])
    total = total.reshape(lay.chips, lay.nc, step_patches, model)
    for k in range(lay.chips):
        gh_refs[k][...] = total[k].astype(gh_refs[k].dtype)


def output_kernel(lay, pos_ref, info_ref, *refs):
    pair_refs, refs = refs[: lay.nc], refs[lay.nc :]
    pr_refs, refs = refs[: lay.chips], refs[lay.chips :]
    mod_ref, *out_refs = refs
    step_patches, model = out_refs[0].shape
    patches = step_patches * pl.num_programs(0)
    patch_base = lay.unit(pos_ref[1], pos_ref[2])[2] * patches + pl.program_id(0) * step_patches
    patch = patch_base + lax.broadcasted_iota(jnp.int32, (step_patches, 1), 0)
    for j in range(lay.nc):
        _, limit, step = slot_scalars(lay, pos_ref, info_ref, (0, j))
        factor = jnp.where(patch < limit, table_row(mod_ref, step, 2, model), 0.0)
        projected = pr_refs[0][j]
        for k in range(1, lay.chips):
            projected = projected + pr_refs[k][j].astype(F32)
        projected = projected.astype(BF16).astype(F32)
        out_refs[j][...] = (pair_refs[j][0, 0].astype(F32) + factor * projected).astype(BF16)


def input_grad_kernel(lay, pos_ref, info_ref, *refs):
    pair_refs, refs = refs[: lay.nc], refs[lay.nc :]
    gh_refs, refs = refs[: lay.chips], refs[lay.chips :]
    mod_ref, *out_refs = refs
    model = out_refs[0].shape[1]
    for j in range(lay.nc):
        _, _, step = slot_scalars(lay, pos_ref, info_ref, (0, j))
        grad_hidden = gh_refs[0][j]
        for k in range(1, lay.chips):
            grad_hidden = grad_hidden + gh_refs[k][j].astype(F32)
        grad_hidden = grad_hidden.astype(BF16).astype(F32)
        normed, inv_sigma = normalize(pair_refs[j][0, 0].astype(F32))
        grad_norm = grad_hidden * (1.0 + table_row(mod_ref, step, 1, model))
        first_mean = jnp.mean(grad_norm, axis=-1, keepdims=True)
        second_mean = jnp.mean(grad_norm * normed, axis=-1, keepdims=True)
        grad_x = pair_refs[j][0, 1].astype(F32) + inv_sigma * (
            grad_norm - first_mean - normed * second_mean
        )
        out_refs[j][...] = grad_x.astype(BF16)


def whole_spec(shape):
    return pl.BlockSpec(shape, lambda *_: (0,) * len(shape))


def struct(shape, dtype=BF16):
    return jax.ShapeDtypeStruct(shape, dtype)


def local(lay, frames_x, grad_y, clip_ids, clip_patches, clip_step, mod_table, w_qkv, w_out):
    y, c, z, x = (lax.axis_index(name) for name in AXES)
    _, patches, model = frames_x.shape
    half = patches // lay.nc
    chips, nc, nx = lay.chips, lay.nc, lay.nx
    head_size = model // HEADS
    halves = lay.halves
    cols = lay.half_heads * head_size
    chip_width = lay.chip_heads * head_size
    rows = w_qkv.shape[0]
    groups = lay.nz
    quarter = model // groups
    step_patches = max(BLOCK, min(half, 512 // lay.frames))
    steps = half // step_patches
    tokens = lay.frames * step_patches

    def call(kernel, name, cost, in_specs, out_specs, out_shape, scratch=(), grid=(1,), prefetch=2):
        return pl.pallas_call(
            kernel,
            grid_spec=pltpu.PrefetchScalarGridSpec(
                num_scalar_prefetch=prefetch,
                grid=grid,
                in_specs=in_specs,
                out_specs=out_specs,
                scratch_shapes=list(scratch),
            ),
            out_shape=out_shape,
            compiler_params=pltpu.CompilerParams(vmem_limit_bytes=VMEM_LIMIT),
            cost_estimate=pl.CostEstimate(
                flops=cost * tokens * steps, bytes_accessed=4 * model * tokens, transcendentals=0
            ),
            name=name,
        )

    def chip_swap(k):
        ky, kx = lay.chip_of(k)
        return lay.swap(ky=ky, kx=kx)

    def from_plane(parts):
        got = [lax.ppermute(part, AXES, lay.from_plane(k)) for k, part in enumerate(parts)]
        first = jnp.where(z // lay.ny == 0, got[0], got[1])
        second = jnp.where(z // lay.ny == 0, got[1], got[0])
        return jnp.concatenate([first, second], axis=0)[None]

    def doubling(held, bits, swap, after, first=None):
        for bit in bits[:-1]:
            got = lax.ppermute(held, AXES, swap(bit)) if first is None else first
            held, first = jnp.concatenate([held, got], axis=0), None
        held, _ = lax.optimization_barrier((held, after))
        return [held, lax.ppermute(held, AXES, swap(bits[-1]))]

    def over_chips(parts):
        got = [lax.ppermute(parts[k], AXES, chip_swap(k)) for k in range(1, chips)]
        return [parts[0]] + got

    info = jnp.concatenate([clip_ids[0], clip_patches[0], clip_step[0]])[None]
    by_core = jnp.concatenate([info, lax.ppermute(info, AXES, lay.swap(kc=1))], axis=0)
    info = [by_core] + [
        lax.ppermute(by_core, AXES, lay.swap(ky=ky)) for ky in range(1, lay.ny)
    ]
    group_y, group_c, _ = lay.unit(c, z)
    info = sum(
        jnp.where((y ^ ky == group_y) & (c ^ kc == group_c), info[ky][kc], 0)
        for ky in range(lay.ny)
        for kc in range(nc)
    )
    pos = jnp.stack([y, c, z, x]).astype(jnp.int32)
    pair_shape = (1, 2, half, model)
    outputs = call(
        functools.partial(start_kernel, lay, cols),
        "start",
        2 * model * 1000,
        [whole_spec(frames_x.shape)] * 2 + [whole_spec(w_qkv.shape)],
        [whole_spec(pair_shape)] * nc + [whole_spec((rows, 3 * cols))] * nx,
        [struct(pair_shape)] * nc + [struct((rows, 3 * cols))] * nx,
        prefetch=1,
    )(pos, frames_x, grad_y, w_qkv)
    pairs, picked = outputs[:nc], outputs[nc:]
    own = [lax.ppermute(pair, AXES, lay.to_plane(k)) for k, pair in enumerate(pairs)]
    by_x = [picked[0]] + [
        lax.ppermute(picked[kx], AXES, lay.swap(kx=kx)) for kx in range(1, nx)
    ]
    if nx == 2:
        ordered = [jnp.where(x == i, by_x[0], by_x[1]) for i in range(nx)]
    else:
        stacked = jnp.stack(by_x)
        ordered = [lax.dynamic_index_in_dim(stacked, x ^ i, 0, keepdims=False) for i in range(nx)]
    w_own = jnp.concatenate(ordered, axis=1 if rows % 16 == 0 else 0)[None]
    first = lax.ppermute(own[0], AXES, chip_swap(lay.chip_bits(0)[0]))
    own[1], first = lax.optimization_barrier((own[1], first))
    late_w_out, _ = lax.optimization_barrier((w_out, own[0]))
    wo_own = lax.ppermute(late_w_out, AXES, lay.rows_to_chip())
    wo_rows = [wo_own, lax.ppermute(wo_own, AXES, lay.swap(kc=1))]
    w_own, _ = lax.optimization_barrier((w_own, (own[1], wo_own)))
    w_pieces = doubling(w_own, lay.bits(lay.nz)[::-1], lambda kz: lay.swap(kz=kz), [])
    pairs = []
    for j in range(nc):
        after = ([], None) if j else (info, first)
        pairs += doubling(own[j], lay.chip_bits(j), chip_swap, *after)
    early = [lax.ppermute(w_pieces[0], AXES, lay.swap(kc=1))] if halves > 1 else []
    pairs, w_pieces, early, wo_rows = lax.optimization_barrier((pairs, w_pieces, early, wo_rows))
    if halves > 1:
        w_pieces += early + [lax.ppermute(w_pieces[1], AXES, lay.swap(kc=1))]


    def spread(count, width, patches_at_once):
        return pl.BlockSpec((count, patches_at_once, width), lambda i, *_: (0, i, 0))

    def pair_spec(count, patches_at_once):
        return pl.BlockSpec((count, 2, patches_at_once, model), lambda i, *_: (0, 0, i, 0))

    few = max(BLOCK, step_patches // 2)
    few_steps = half // few
    x_spec = pl.BlockSpec((few, model), lambda i, *_: (i, 0))
    triple_spec = pl.BlockSpec((halves, lay.frames, step_patches, cols), lambda i, *_: (0, 0, i, 0))
    w_specs = [whole_spec(w_pieces[0].shape)] * (2 * halves)
    w_scratch = pltpu.VMEM((halves, model, 3 * cols), BF16)
    mod_spec = whole_spec(mod_table.shape)
    triple_shape = struct((halves, lay.frames, half, cols))
    part_specs = [spread(nc, model, step_patches)] * chips
    part_shapes = [struct((nc, half, model), F32)] + [struct((nc, half, model))] * (chips - 1)

    fold = 3 if rows % 24 == 0 else 1
    piece_shape = (groups, rows // fold, quarter * fold)
    queries, keys, values, grad_attn, kept, sent, *projected = call(
        functools.partial(forward_kernel, lay),
        "forward",
        14 * model * 1000,
        [pair_spec(chips // 2, step_patches)] * (2 * nc)
        + w_specs
        + [whole_spec(w_out.shape)] * nc
        + [mod_spec],
        [triple_spec] * 4 + [whole_spec(piece_shape)] * 2 + part_specs,
        [triple_shape] * 4 + [struct(piece_shape, F32)] * 2 + part_shapes,
        [pltpu.VMEM((lay.frames, step_patches, model), BF16)] * 2
        + [
            w_scratch,
            pltpu.VMEM((lay.frames, step_patches, chip_width), BF16),
            pltpu.VMEM((chip_width, model), BF16),
            pltpu.VMEM((chip_width, model), F32),
            pltpu.VMEM(piece_shape, F32),
        ],
        (steps,),
    )(pos, info, *pairs, *w_pieces, *wo_rows, mod_table)
    got = lax.ppermute(sent, AXES, lay.swap(kc=1))
    projected = over_chips(projected)

    middle = groups // 2
    cut, away = kept[:middle] + got[:middle], kept[middle:] + got[middle:]
    grad_attn, cut, away = lax.optimization_barrier((grad_attn, cut, away))
    first_away = lax.ppermute(away, AXES, lay.swap(kz=1))

    sums = call(
        functools.partial(backward_kernel, lay),
        "backward",
        10 * model * 1000,
        w_specs + [triple_spec] * 4,
        part_specs,
        part_shapes,
        [w_scratch, pltpu.VMEM((halves, lay.frames, step_patches, 3 * cols), BF16)],
        (steps,),
    )(pos, info, *w_pieces, queries, keys, values, grad_attn)
    sums, first_away, projected = lax.optimization_barrier((sums, first_away, projected))
    grad_hidden = over_chips(sums)

    out_parts = call(
        functools.partial(output_kernel, lay),
        "output",
        20 * model * 1000,
        [pair_spec(1, few)] * nc + [spread(nc, model, few)] * chips + [mod_spec],
        [x_spec] * nc,
        [struct((half, model))] * nc,
        grid=(few_steps,),
    )(pos, info, *own, *projected, mod_table)
    out_y = from_plane(out_parts)

    grad_hidden, _ = lax.optimization_barrier((grad_hidden, out_parts))
    grad_parts = call(
        functools.partial(input_grad_kernel, lay),
        "input_grad",
        3 * model * 1000,
        [pair_spec(1, few)] * nc + [spread(nc, model, few)] * chips + [mod_spec],
        [x_spec] * nc,
        [struct((half, model))] * nc,
        grid=(few_steps,),
    )(pos, info, *own, *grad_hidden, mod_table)
    grad_x = from_plane(grad_parts)

    cut, _ = lax.optimization_barrier((cut + first_away, out_parts))
    for bit in lay.bits(lay.nz)[1:]:
        middle = middle // 2
        cut = cut[:middle] + lax.ppermute(cut[middle:], AXES, lay.swap(kz=bit))
    cut, _ = lax.optimization_barrier((cut, grad_parts))
    grad_w = lax.ppermute(cut[0], AXES, lay.to_owner())
    grad_w = jnp.concatenate(
        [grad_w[:, m * quarter : (m + 1) * quarter] for m in range(fold)], axis=0
    )
    grad_w_out = grad_w * jnp.float32(1.0 / math.sqrt(groups * lay.frames * patches))
    return out_y, grad_x, grad_w_out


def solution(mesh):
    lay = Layout(mesh)
    grid = Mesh(mesh.devices.reshape(lay.ny, lay.nc, lay.nz, lay.nx), AXES)
    rows, cols = ("z", "x"), ("y", "c")
    frame = P(AXES, None, None)
    group = P(cols, None)
    return jax.shard_map(
        functools.partial(local, lay),
        mesh=grid,
        in_specs=(frame, frame, group, group, group, P(), P(rows, None), P(rows, None)),
        out_specs=(frame, frame, P(rows, cols)),
        check_vma=False,
    )
```

```python
import functools
import math

import jax
import jax.numpy as jnp
from jax import lax
from jax.experimental import pallas as pl
from jax.experimental.pallas import tpu as pltpu
from jax.sharding import Mesh, PartitionSpec as P

HEADS = 16
CORES = 2
AXES = ("y", "c", "z", "x")
BLOCK = 16
VMEM_LIMIT = 56 * 1024 * 1024
BF16 = jnp.bfloat16
F32 = jnp.float32


def dot(left, right):
    return jnp.dot(left, right, preferred_element_type=F32)


def dot_t(left, right):
    return lax.dot_general(left, right, (((1,), (1,)), ((), ())), preferred_element_type=F32)


def t_dot(left, right):
    return lax.dot_general(left, right, (((0,), (0,)), ((), ())), preferred_element_type=F32)


def normalize(values):
    centred = values - jnp.mean(values, axis=-1, keepdims=True)
    inv_sigma = lax.rsqrt(jnp.mean(centred * centred, axis=-1, keepdims=True) + 1e-06)
    return centred * inv_sigma, inv_sigma


class Layout:
    def __init__(self, mesh):
        groups, seq = mesh.shape["dp"], mesh.shape["seq"]
        self.nc = CORES
        self.ny = groups // CORES
        self.nz = groups
        self.nx = seq // self.nz
        self.chips = self.ny * self.nx
        self.frames = seq
        self.chip_heads = HEADS // self.chips
        self.halves = 2 if self.chip_heads % 2 == 0 else 1
        self.half_heads = self.chip_heads // self.halves

    def linear(self, y, c, z, x):
        return ((y * self.nc + c) * self.nz + z) * self.nx + x

    def perm(self, move):
        pairs = []
        for y in range(self.ny):
            for c in range(self.nc):
                for z in range(self.nz):
                    for x in range(self.nx):
                        pairs.append((self.linear(y, c, z, x), self.linear(*move(y, c, z, x))))
        return pairs

    def to_plane(self, k):
        def move(y, c, z, x):
            half = (z // self.ny) ^ k
            plane = ((y // self.nc) * self.nc + c) * self.nc + half
            return (z % self.ny) ^ c, y % self.nc, plane, x

        return self.perm(move)

    def unit(self, c, z):
        return (z // (self.nc * self.nc)) * self.nc + c, (z // self.nc) % self.nc, z % self.nc

    def from_plane(self, k):
        return [(target, source) for source, target in self.to_plane(k)]

    def swap(self, ky=0, kc=0, kz=0, kx=0):
        return self.perm(lambda y, c, z, x: (y ^ ky, c ^ kc, z ^ kz, x ^ kx))

    def row_block(self, y, x, i):
        if self.halves > 1:
            return (i * self.ny + y) * self.nx + x
        return self.nc * (y * self.nx + x) + i

    def rows_to_chip(self):
        reader = {
            self.row_block(y, x, i): (y, x, i)
            for y in range(self.ny)
            for x in range(self.nx)
            for i in range(self.nc)
        }

        def move(y, c, z, x):
            chip_y, chip_x, i = reader[z * self.nx + x]
            return chip_y, i, c * self.ny + (y ^ (z & 1)), chip_x

        return self.perm(move)

    def to_owner(self):
        def move(y, c, z, x):
            s = self.row_block(y, x, c)
            return z // self.nc, z % self.nc, s // self.nx, s % self.nx

        return self.perm(move)

    def chip_of(self, k):
        return k // self.nx, k % self.nx

    def bits(self, count):
        return [1 << b for b in range(count.bit_length() - 1)]

    def chip_bits(self, j):
        bits = self.bits(self.chips)
        return bits if j % 2 == 0 else bits[::-1]

    def doubled(self, bits):
        held = [0]
        for bit in bits:
            held = held + [k ^ bit for k in held]
        return held

    def slots(self):
        return [(k, j) for k in range(self.chips) for j in range(self.nc)]


def slot_scalars(lay, pos_ref, info_ref, slot):
    k, j = slot
    ky, kx = lay.chip_of(k)
    _, group_c, half = lay.unit(pos_ref[1], pos_ref[2])
    z_frame = (half ^ j) * lay.ny + (pos_ref[0] ^ ky ^ group_c)
    frame = z_frame * lay.nx + (pos_ref[3] ^ kx)
    clip = info_ref[frame]
    clips = (info_ref.shape[0] - lay.frames) // 2
    return clip, info_ref[lay.frames + clip], info_ref[lay.frames + clips + clip]


def table_row(mod_ref, step, part, width):
    return mod_ref[pl.ds(step, 1), part * width : (part + 1) * width]


def allowed_pairs(lay, pos_ref, info_ref, patch_base):
    rows = lay.frames * BLOCK
    row_slot = lax.broadcasted_iota(jnp.int32, (rows, 1), 0) // BLOCK
    col_slot = lax.broadcasted_iota(jnp.int32, (1, rows), 1) // BLOCK
    row_clip = jnp.zeros((rows, 1), jnp.int32)
    row_limit = jnp.zeros((rows, 1), jnp.int32)
    col_clip = jnp.zeros((1, rows), jnp.int32)
    for t, slot in enumerate(lay.slots()):
        clip, limit, _ = slot_scalars(lay, pos_ref, info_ref, slot)
        row_clip = jnp.where(row_slot == t, clip, row_clip)
        row_limit = jnp.where(row_slot == t, limit, row_limit)
        col_clip = jnp.where(col_slot == t, clip, col_clip)
    row_patch = lax.broadcasted_iota(jnp.int32, (rows, 1), 0) % BLOCK
    col_patch = lax.broadcasted_iota(jnp.int32, (1, rows), 1) % BLOCK
    row_key = row_clip * BLOCK + row_patch
    col_key = col_clip * BLOCK + col_patch
    row_valid = (patch_base + row_patch < row_limit).astype(jnp.int32)
    row_index = lax.broadcasted_iota(jnp.int32, (rows, rows), 0)
    col_index = lax.broadcasted_iota(jnp.int32, (rows, rows), 1)
    return (row_key == col_key) & ((row_valid > 0) | (row_index == col_index))


def head_mask(values, head, head_size):
    lane = lax.broadcasted_iota(jnp.int32, (1, values.shape[1]), 1)
    inside = (lane >= head * head_size) & (lane < (head + 1) * head_size)
    return jnp.where(inside, values, jnp.zeros_like(values))


def patch_blocks(array, block):
    part = array[:, block * BLOCK : (block + 1) * BLOCK, :]
    return part.reshape(part.shape[0] * BLOCK, part.shape[2])


def start_kernel(lay, cols, pos_ref, x_ref, g_ref, w_ref, *refs):
    pair_refs, out_refs = refs[: lay.nc], refs[lay.nc :]
    half = x_ref.shape[1] // lay.nc
    for k, ref in enumerate(pair_refs):
        first = pl.multiple_of(((pos_ref[2] // lay.ny) ^ k) * half, 16)
        ref[0, 0] = x_ref[0, pl.ds(first, half), :]
        ref[0, 1] = g_ref[0, pl.ds(first, half), :]
    model = w_ref.shape[1] // 3
    for k, out_ref in enumerate(out_refs):
        chip_x = pos_ref[3] ^ k
        if lay.halves > 1:
            want = lay.row_block(pos_ref[0], chip_x, pos_ref[1])
        else:
            want = pos_ref[0] * lay.nx + chip_x
        for v in range(lay.chips * lay.halves):

            @pl.when(want == v)
            def _(v=v, out_ref=out_ref):
                parts = [
                    w_ref[:, p * model + v * cols : p * model + (v + 1) * cols]
                    for p in range(3)
                ]
                out_ref[...] = jnp.concatenate(parts, axis=1)


def fill_weights(lay, pos_ref, w_refs, w_scr):
    block = w_scr.shape[1] // lay.nz
    rows, width = w_refs[0].shape[1], w_scr.shape[2]
    for h in range(lay.halves):
        for k in range(lay.nz):
            ref = w_refs[h * lay.nz + k]
            for m in range(block // rows):
                start = pl.multiple_of((pos_ref[2] ^ k) * block + m * rows, 16)
                w_scr[h, pl.ds(start, rows), :] = ref[0, :, m * width : (m + 1) * width]


def heads_stacked(lay, values):
    head_size = values.shape[1] // lay.half_heads
    parts = [head_mask(values, head, head_size) for head in range(lay.half_heads)]
    return jnp.concatenate(parts, axis=0) if len(parts) > 1 else parts[0]


def beside(lay, weights):
    return jnp.concatenate([weights[head] for head in range(lay.half_heads)], axis=1)


def attention_weights(lay, keys_stacked, queries, allowed, scaling):
    scores = dot_t(keys_stacked, queries) * scaling
    scores = jnp.where(allowed, scores.reshape((lay.half_heads,) + allowed.shape), -jnp.inf)
    exponent = jnp.exp(scores - jnp.max(scores, axis=1, keepdims=True))
    return exponent * (1.0 / jnp.sum(exponent, axis=1, keepdims=True))


def modulate(lay, pos_ref, info_ref, pair_refs, mod_ref, hid_ref, gp_ref):
    _, step_patches, model = hid_ref.shape
    patches = step_patches * pl.num_programs(0)
    patch_base = lay.unit(pos_ref[1], pos_ref[2])[2] * patches + pl.program_id(0) * step_patches
    patch = patch_base + lax.broadcasted_iota(jnp.int32, (step_patches, 1), 0)
    for t, (k, j) in enumerate(lay.slots()):
        _, limit, step = slot_scalars(lay, pos_ref, info_ref, (k, j))
        n = lay.doubled(lay.chip_bits(j)).index(k)
        ref, place = pair_refs[2 * j + (2 * n) // lay.chips], n % (lay.chips // 2)
        normed, _ = normalize(ref[place, 0].astype(F32))
        shift, scale = table_row(mod_ref, step, 0, model), table_row(mod_ref, step, 1, model)
        hid_ref[t] = (normed * (1.0 + scale) + shift).astype(BF16)
        factor = jnp.where(patch < limit, table_row(mod_ref, step, 2, model), 0.0)
        gp_ref[t] = (factor * ref[place, 1].astype(F32)).astype(BF16)


def forward_kernel(lay, pos_ref, info_ref, *refs):
    pair_refs, refs = refs[: 2 * lay.nc], refs[2 * lay.nc :]
    w_refs, refs = refs[: lay.halves * lay.nz], refs[lay.halves * lay.nz :]
    wo_refs, refs = refs[: lay.nc], refs[lay.nc :]
    mod_ref, q_ref, k_ref, v_ref, ga_ref, kept_ref, sent_ref, *refs = refs
    pr_refs, refs = refs[: lay.chips], refs[lay.chips :]
    hid_ref, gp_ref, w_scr, att_scr, wo_scr, acc_scr, cut_scr = refs
    _, step_patches, model = hid_ref.shape
    tokens = lay.frames * step_patches
    cols = w_scr.shape[2] // 3
    scaling = 1.0 / math.sqrt(cols // lay.half_heads)
    patches = step_patches * pl.num_programs(0)
    is_first = pos_ref[1] == 0

    @pl.when(pl.program_id(0) == 0)
    def _():
        fill_weights(lay, pos_ref, w_refs, w_scr)
        own, other = wo_refs[0][...].astype(F32), wo_refs[1][...].astype(F32)
        both = [jnp.where(is_first, own, other), jnp.where(is_first, other, own)]
        wo_scr[...] = jnp.concatenate(both, axis=0).astype(BF16)
        acc_scr[...] = jnp.zeros_like(acc_scr)

    modulate(lay, pos_ref, info_ref, pair_refs, mod_ref, hid_ref, gp_ref)
    hidden = hid_ref[...].reshape(lay.frames * step_patches, model)
    for h in range(lay.halves):
        triple = dot(hidden, w_scr[h])
        for n, ref in enumerate((q_ref, k_ref, v_ref)):
            ref[h] = triple[:, n * cols : (n + 1) * cols].astype(BF16).reshape(ref.shape[1:])

    for b in range(step_patches // BLOCK):
        patch_base = lay.unit(pos_ref[1], pos_ref[2])[2] * patches + pl.program_id(0) * step_patches + b * BLOCK
        allowed = allowed_pairs(lay, pos_ref, info_ref, patch_base)
        outputs = []
        for h in range(lay.halves):
            queries, keys, values = (patch_blocks(ref[h], b) for ref in (q_ref, k_ref, v_ref))
            weights = attention_weights(lay, heads_stacked(lay, keys), queries, allowed, scaling)
            weights = weights.astype(BF16).reshape(-1, allowed.shape[1])
            outputs.append(t_dot(weights, heads_stacked(lay, values)))
        if lay.halves > 1:
            first = jnp.where(pos_ref[1] == 0, outputs[0], outputs[1])
            second = jnp.where(pos_ref[1] == 0, outputs[1], outputs[0])
            outputs = [jnp.concatenate([first, second], axis=1)]
        attended = outputs[0].astype(BF16)
        att_scr[:, b * BLOCK : (b + 1) * BLOCK, :] = attended.reshape(lay.frames, BLOCK, -1)

    attended = att_scr[...].reshape(tokens, -1)
    grad_proj = gp_ref[...].reshape(tokens, model)
    acc_scr[...] += t_dot(attended, grad_proj)
    grad_attn = dot_t(grad_proj, wo_scr[...])
    part = wo_scr.shape[0] // lay.halves
    for h in range(lay.halves):
        ga_ref[h] = grad_attn[:, h * part : (h + 1) * part].astype(BF16).reshape(ga_ref.shape[1:])
    projected = dot(attended, wo_scr[...]).reshape(lay.chips, lay.nc, step_patches, model)
    for k in range(lay.chips):
        pr_refs[k][...] = projected[k].astype(pr_refs[k].dtype)

    @pl.when(pl.program_id(0) == pl.num_programs(0) - 1)
    def _():
        groups, chunk_rows, chunk_width = kept_ref.shape
        block_rows, part = acc_scr.shape[0] // lay.nc, model // groups
        order = lay.doubled(lay.bits(lay.nz)[::-1])
        first, second = acc_scr[:block_rows, :], acc_scr[block_rows:, :]
        kept = jnp.where(is_first, first, second)
        sent = jnp.where(is_first, second, first)
        for ref, rows in ((kept_ref, kept), (sent_ref, sent)):
            for d in range(groups):
                chunk = [
                    rows[m * chunk_rows : (m + 1) * chunk_rows, d * part : (d + 1) * part]
                    for m in range(chunk_width // part)
                ]
                cut_scr[d] = jnp.concatenate(chunk, axis=1) if len(chunk) > 1 else chunk[0]
            for n, k in enumerate(order):
                ref[n] = cut_scr[pos_ref[2] ^ k]


def backward_kernel(lay, pos_ref, info_ref, *refs):
    w_refs, refs = refs[: lay.halves * lay.nz], refs[lay.halves * lay.nz :]
    q_ref, k_ref, v_ref, ga_ref, *refs = refs
    gh_refs, (w_scr, gt_scr) = refs[: lay.chips], refs[lay.chips :]
    _, frames, step_patches, cols = q_ref.shape
    model = w_scr.shape[1]
    patches = step_patches * pl.num_programs(0)
    scaling = 1.0 / math.sqrt(cols // lay.half_heads)

    @pl.when(pl.program_id(0) == 0)
    def _():
        fill_weights(lay, pos_ref, w_refs, w_scr)

    for b in range(step_patches // BLOCK):
        patch_base = lay.unit(pos_ref[1], pos_ref[2])[2] * patches + pl.program_id(0) * step_patches + b * BLOCK
        allowed = allowed_pairs(lay, pos_ref, info_ref, patch_base)
        for h in range(lay.halves):
            queries, keys, values = (patch_blocks(ref[h], b) for ref in (q_ref, k_ref, v_ref))
            grad_out = patch_blocks(ga_ref[(pos_ref[1] ^ h) if lay.halves > 1 else 0], b)
            keys = heads_stacked(lay, keys)
            weights = attention_weights(lay, keys, queries, allowed, scaling)
            grad_weights = dot_t(heads_stacked(lay, values), grad_out).reshape(weights.shape)
            grad_values = dot(beside(lay, weights.astype(BF16)), heads_stacked(lay, grad_out))
            inner = jnp.sum(weights * grad_weights, axis=1, keepdims=True)
            grad_scores = (weights * (grad_weights - inner) * scaling).astype(BF16)
            grad_queries = t_dot(grad_scores.reshape(-1, grad_scores.shape[2]), keys)
            grad_keys = dot(beside(lay, grad_scores), heads_stacked(lay, queries))
            grads = jnp.concatenate([grad_queries, grad_keys, grad_values], axis=1).astype(BF16)
            gt_scr[h, :, b * BLOCK : (b + 1) * BLOCK, :] = grads.reshape(frames, BLOCK, 3 * cols)

    total = jnp.zeros((frames * step_patches, model), F32)
    for h in range(lay.halves):
        total = total + dot_t(gt_scr[h].reshape(frames * step_patches, 3 * cols), w_scr[h])
    total = total.reshape(lay.chips, lay.nc, step_patches, model)
    for k in range(lay.chips):
        gh_refs[k][...] = total[k].astype(gh_refs[k].dtype)


def output_kernel(lay, pos_ref, info_ref, *refs):
    pair_refs, refs = refs[: lay.nc], refs[lay.nc :]
    pr_refs, refs = refs[: lay.chips], refs[lay.chips :]
    mod_ref, *out_refs = refs
    step_patches, model = out_refs[0].shape
    patches = step_patches * pl.num_programs(0)
    patch_base = lay.unit(pos_ref[1], pos_ref[2])[2] * patches + pl.program_id(0) * step_patches
    patch = patch_base + lax.broadcasted_iota(jnp.int32, (step_patches, 1), 0)
    for j in range(lay.nc):
        _, limit, step = slot_scalars(lay, pos_ref, info_ref, (0, j))
        factor = jnp.where(patch < limit, table_row(mod_ref, step, 2, model), 0.0)
        projected = pr_refs[0][j]
        for k in range(1, lay.chips):
            projected = projected + pr_refs[k][j].astype(F32)
        projected = projected.astype(BF16).astype(F32)
        out_refs[j][...] = (pair_refs[j][0, 0].astype(F32) + factor * projected).astype(BF16)


def input_grad_kernel(lay, pos_ref, info_ref, *refs):
    pair_refs, refs = refs[: lay.nc], refs[lay.nc :]
    gh_refs, refs = refs[: lay.chips], refs[lay.chips :]
    mod_ref, *out_refs = refs
    model = out_refs[0].shape[1]
    for j in range(lay.nc):
        _, _, step = slot_scalars(lay, pos_ref, info_ref, (0, j))
        grad_hidden = gh_refs[0][j]
        for k in range(1, lay.chips):
            grad_hidden = grad_hidden + gh_refs[k][j].astype(F32)
        grad_hidden = grad_hidden.astype(BF16).astype(F32)
        normed, inv_sigma = normalize(pair_refs[j][0, 0].astype(F32))
        grad_norm = grad_hidden * (1.0 + table_row(mod_ref, step, 1, model))
        first_mean = jnp.mean(grad_norm, axis=-1, keepdims=True)
        second_mean = jnp.mean(grad_norm * normed, axis=-1, keepdims=True)
        grad_x = pair_refs[j][0, 1].astype(F32) + inv_sigma * (
            grad_norm - first_mean - normed * second_mean
        )
        out_refs[j][...] = grad_x.astype(BF16)


def whole_spec(shape):
    return pl.BlockSpec(shape, lambda *_: (0,) * len(shape))


def struct(shape, dtype=BF16):
    return jax.ShapeDtypeStruct(shape, dtype)


def local(lay, frames_x, grad_y, clip_ids, clip_patches, clip_step, mod_table, w_qkv, w_out):
    y, c, z, x = (lax.axis_index(name) for name in AXES)
    _, patches, model = frames_x.shape
    half = patches // lay.nc
    chips, nc, nx = lay.chips, lay.nc, lay.nx
    head_size = model // HEADS
    halves = lay.halves
    cols = lay.half_heads * head_size
    chip_width = lay.chip_heads * head_size
    rows = w_qkv.shape[0]
    groups = lay.nz
    quarter = model // groups
    step_patches = max(BLOCK, min(half, 512 // lay.frames))
    steps = half // step_patches
    tokens = lay.frames * step_patches

    def call(kernel, name, cost, in_specs, out_specs, out_shape, scratch=(), grid=(1,), prefetch=2):
        return pl.pallas_call(
            kernel,
            grid_spec=pltpu.PrefetchScalarGridSpec(
                num_scalar_prefetch=prefetch,
                grid=grid,
                in_specs=in_specs,
                out_specs=out_specs,
                scratch_shapes=list(scratch),
            ),
            out_shape=out_shape,
            compiler_params=pltpu.CompilerParams(vmem_limit_bytes=VMEM_LIMIT),
            cost_estimate=pl.CostEstimate(
                flops=cost * tokens * steps, bytes_accessed=4 * model * tokens, transcendentals=0
            ),
            name=name,
        )

    def chip_swap(k):
        ky, kx = lay.chip_of(k)
        return lay.swap(ky=ky, kx=kx)

    def from_plane(parts):
        got = [lax.ppermute(part, AXES, lay.from_plane(k)) for k, part in enumerate(parts)]
        first = jnp.where(z // lay.ny == 0, got[0], got[1])
        second = jnp.where(z // lay.ny == 0, got[1], got[0])
        return jnp.concatenate([first, second], axis=0)[None]

    def doubling(held, bits, swap, after, first=None):
        for bit in bits[:-1]:
            got = lax.ppermute(held, AXES, swap(bit)) if first is None else first
            held, first = jnp.concatenate([held, got], axis=0), None
        held, _ = lax.optimization_barrier((held, after))
        return [held, lax.ppermute(held, AXES, swap(bits[-1]))]

    def over_chips(parts):
        got = [lax.ppermute(parts[k], AXES, chip_swap(k)) for k in range(1, chips)]
        return [parts[0]] + got

    info = jnp.concatenate([clip_ids[0], clip_patches[0], clip_step[0]])[None]
    by_core = jnp.concatenate([info, lax.ppermute(info, AXES, lay.swap(kc=1))], axis=0)
    info = [by_core] + [
        lax.ppermute(by_core, AXES, lay.swap(ky=ky)) for ky in range(1, lay.ny)
    ]
    group_y, group_c, _ = lay.unit(c, z)
    info = sum(
        jnp.where((y ^ ky == group_y) & (c ^ kc == group_c), info[ky][kc], 0)
        for ky in range(lay.ny)
        for kc in range(nc)
    )
    pos = jnp.stack([y, c, z, x]).astype(jnp.int32)
    pair_shape = (1, 2, half, model)
    outputs = call(
        functools.partial(start_kernel, lay, cols),
        "start",
        2 * model * 1000,
        [whole_spec(frames_x.shape)] * 2 + [whole_spec(w_qkv.shape)],
        [whole_spec(pair_shape)] * nc + [whole_spec((rows, 3 * cols))] * nx,
        [struct(pair_shape)] * nc + [struct((rows, 3 * cols))] * nx,
        prefetch=1,
    )(pos, frames_x, grad_y, w_qkv)
    pairs, picked = outputs[:nc], outputs[nc:]
    own = [lax.ppermute(pair, AXES, lay.to_plane(k)) for k, pair in enumerate(pairs)]
    by_x = [picked[0]] + [
        lax.ppermute(picked[kx], AXES, lay.swap(kx=kx)) for kx in range(1, nx)
    ]
    if nx == 2:
        ordered = [jnp.where(x == i, by_x[0], by_x[1]) for i in range(nx)]
    else:
        stacked = jnp.stack(by_x)
        ordered = [lax.dynamic_index_in_dim(stacked, x ^ i, 0, keepdims=False) for i in range(nx)]
    w_own = jnp.concatenate(ordered, axis=1 if rows % 16 == 0 else 0)[None]
    first = lax.ppermute(own[0], AXES, chip_swap(lay.chip_bits(0)[0]))
    own[1], first = lax.optimization_barrier((own[1], first))
    late_w_out, _ = lax.optimization_barrier((w_out, own[0]))
    wo_own = lax.ppermute(late_w_out, AXES, lay.rows_to_chip())
    wo_rows = [wo_own, lax.ppermute(wo_own, AXES, lay.swap(kc=1))]
    w_own, _ = lax.optimization_barrier((w_own, (own[1], wo_own)))
    by_z = {0: w_own}
    for bit in lay.bits(lay.nz):
        by_z[bit] = lax.ppermute(w_own, AXES, lay.swap(kz=bit))
    for k in range(1, lay.nz):
        if k not in by_z:
            forwarded = jnp.where(z < lay.nz, by_z[k ^ (k & -k)], w_own)
            by_z[k] = lax.ppermute(forwarded, AXES, lay.swap(kz=k & -k))
    w_pieces = [by_z[k] for k in range(lay.nz)]

    pairs = []
    for j in range(nc):
        after = ([], None) if j else (info, first)
        pairs += doubling(own[j], lay.chip_bits(j), chip_swap, *after)
    early = [lax.ppermute(piece, AXES, lay.swap(kc=1)) for piece in w_pieces[:2]]
    early = early if halves > 1 else []
    pairs, w_pieces, early, wo_rows = lax.optimization_barrier((pairs, w_pieces, early, wo_rows))
    if halves > 1:
        w_pieces += early + [lax.ppermute(piece, AXES, lay.swap(kc=1)) for piece in w_pieces[2:]]


    def spread(count, width, patches_at_once):
        return pl.BlockSpec((count, patches_at_once, width), lambda i, *_: (0, i, 0))

    def pair_spec(count, patches_at_once):
        return pl.BlockSpec((count, 2, patches_at_once, model), lambda i, *_: (0, 0, i, 0))

    few = max(BLOCK, step_patches // 2)
    few_steps = half // few
    x_spec = pl.BlockSpec((few, model), lambda i, *_: (i, 0))
    triple_spec = pl.BlockSpec((halves, lay.frames, step_patches, cols), lambda i, *_: (0, 0, i, 0))
    w_specs = [whole_spec(w_own.shape)] * (halves * lay.nz)
    w_scratch = pltpu.VMEM((halves, model, 3 * cols), BF16)
    mod_spec = whole_spec(mod_table.shape)
    triple_shape = struct((halves, lay.frames, half, cols))
    part_specs = [spread(nc, model, step_patches)] * chips
    part_shapes = [struct((nc, half, model), F32)] + [struct((nc, half, model))] * (chips - 1)

    fold = 3 if rows % 24 == 0 else 1
    piece_shape = (groups, rows // fold, quarter * fold)
    queries, keys, values, grad_attn, kept, sent, *projected = call(
        functools.partial(forward_kernel, lay),
        "forward",
        14 * model * 1000,
        [pair_spec(chips // 2, step_patches)] * (2 * nc)
        + w_specs
        + [whole_spec(w_out.shape)] * nc
        + [mod_spec],
        [triple_spec] * 4 + [whole_spec(piece_shape)] * 2 + part_specs,
        [triple_shape] * 4 + [struct(piece_shape, F32)] * 2 + part_shapes,
        [pltpu.VMEM((lay.frames, step_patches, model), BF16)] * 2
        + [
            w_scratch,
            pltpu.VMEM((lay.frames, step_patches, chip_width), BF16),
            pltpu.VMEM((chip_width, model), BF16),
            pltpu.VMEM((chip_width, model), F32),
            pltpu.VMEM(piece_shape, F32),
        ],
        (steps,),
    )(pos, info, *pairs, *w_pieces, *wo_rows, mod_table)
    got = lax.ppermute(sent, AXES, lay.swap(kc=1))
    projected = over_chips(projected)

    middle = groups // 2
    cut, away = kept[:middle] + got[:middle], kept[middle:] + got[middle:]
    grad_attn, cut, away = lax.optimization_barrier((grad_attn, cut, away))
    first_away = lax.ppermute(away, AXES, lay.swap(kz=1))

    sums = call(
        functools.partial(backward_kernel, lay),
        "backward",
        10 * model * 1000,
        w_specs + [triple_spec] * 4,
        part_specs,
        part_shapes,
        [w_scratch, pltpu.VMEM((halves, lay.frames, step_patches, 3 * cols), BF16)],
        (steps,),
    )(pos, info, *w_pieces, queries, keys, values, grad_attn)
    sums, first_away, projected = lax.optimization_barrier((sums, first_away, projected))
    grad_hidden = over_chips(sums)

    out_parts = call(
        functools.partial(output_kernel, lay),
        "output",
        20 * model * 1000,
        [pair_spec(1, few)] * nc + [spread(nc, model, few)] * chips + [mod_spec],
        [x_spec] * nc,
        [struct((half, model))] * nc,
        grid=(few_steps,),
    )(pos, info, *own, *projected, mod_table)
    out_y = from_plane(out_parts)

    grad_hidden, _ = lax.optimization_barrier((grad_hidden, out_parts))
    grad_parts = call(
        functools.partial(input_grad_kernel, lay),
        "input_grad",
        3 * model * 1000,
        [pair_spec(1, few)] * nc + [spread(nc, model, few)] * chips + [mod_spec],
        [x_spec] * nc,
        [struct((half, model))] * nc,
        grid=(few_steps,),
    )(pos, info, *own, *grad_hidden, mod_table)
    grad_x = from_plane(grad_parts)

    cut, _ = lax.optimization_barrier((cut + first_away, out_parts))
    for bit in lay.bits(lay.nz)[1:]:
        middle = middle // 2
        cut = cut[:middle] + lax.ppermute(cut[middle:], AXES, lay.swap(kz=bit))
    cut, _ = lax.optimization_barrier((cut, grad_parts))
    grad_w = lax.ppermute(cut[0], AXES, lay.to_owner())
    grad_w = jnp.concatenate(
        [grad_w[:, m * quarter : (m + 1) * quarter] for m in range(fold)], axis=0
    )
    grad_w_out = grad_w * jnp.float32(1.0 / math.sqrt(groups * lay.frames * patches))
    return out_y, grad_x, grad_w_out


def solution(mesh):
    lay = Layout(mesh)
    grid = Mesh(mesh.devices.reshape(lay.ny, lay.nc, lay.nz, lay.nx), AXES)
    rows, cols = ("z", "x"), ("y", "c")
    frame = P(AXES, None, None)
    group = P(cols, None)
    return jax.shard_map(
        functools.partial(local, lay),
        mesh=grid,
        in_specs=(frame, frame, group, group, group, P(), P(rows, None), P(rows, None)),
        out_specs=(frame, frame, P(rows, cols)),
        check_vma=False,
    )
```

```python
import functools
import math

import jax
import jax.numpy as jnp
from jax import lax
from jax.experimental import pallas as pl
from jax.experimental.pallas import tpu as pltpu
from jax.sharding import Mesh, PartitionSpec as P

HEADS = 16
CORES = 2
AXES = ("y", "c", "z", "x")
BLOCK = 16
VMEM_LIMIT = 56 * 1024 * 1024
BF16 = jnp.bfloat16
F32 = jnp.float32


def dot(left, right):
    return jnp.dot(left, right, preferred_element_type=F32)


def dot_t(left, right):
    return lax.dot_general(left, right, (((1,), (1,)), ((), ())), preferred_element_type=F32)


def t_dot(left, right):
    return lax.dot_general(left, right, (((0,), (0,)), ((), ())), preferred_element_type=F32)


def normalize(values):
    centred = values - jnp.mean(values, axis=-1, keepdims=True)
    inv_sigma = lax.rsqrt(jnp.mean(centred * centred, axis=-1, keepdims=True) + 1e-06)
    return centred * inv_sigma, inv_sigma


class Layout:
    def __init__(self, mesh):
        groups, seq = mesh.shape["dp"], mesh.shape["seq"]
        self.nc = CORES
        self.ny = groups // CORES
        self.nz = groups
        self.nx = seq // self.nz
        self.chips = self.ny * self.nx
        self.frames = seq
        self.chip_heads = HEADS // self.chips
        self.halves = 2 if self.chip_heads % 2 == 0 else 1
        self.half_heads = self.chip_heads // self.halves

    def linear(self, y, c, z, x):
        return ((y * self.nc + c) * self.nz + z) * self.nx + x

    def perm(self, move):
        pairs = []
        for y in range(self.ny):
            for c in range(self.nc):
                for z in range(self.nz):
                    for x in range(self.nx):
                        pairs.append((self.linear(y, c, z, x), self.linear(*move(y, c, z, x))))
        return pairs

    def to_plane(self, k):
        def move(y, c, z, x):
            half = (z // self.ny) ^ k
            plane = ((y // self.nc) * self.nc + c) * self.nc + half
            return (z % self.ny) ^ c, y % self.nc, plane, x

        return self.perm(move)

    def unit(self, c, z):
        return (z // (self.nc * self.nc)) * self.nc + c, (z // self.nc) % self.nc, z % self.nc

    def from_plane(self, k):
        return [(target, source) for source, target in self.to_plane(k)]

    def swap(self, ky=0, kc=0, kz=0, kx=0):
        return self.perm(lambda y, c, z, x: (y ^ ky, c ^ kc, z ^ kz, x ^ kx))

    def row_block(self, y, x, i):
        if self.halves > 1:
            return (i * self.ny + y) * self.nx + x
        return self.nc * (y * self.nx + x) + i

    def rows_to_chip(self):
        reader = {
            self.row_block(y, x, i): (y, x, i)
            for y in range(self.ny)
            for x in range(self.nx)
            for i in range(self.nc)
        }

        def move(y, c, z, x):
            chip_y, chip_x, i = reader[z * self.nx + x]
            return chip_y, i, c * self.ny + (y ^ (z & 1)), chip_x

        return self.perm(move)

    def to_owner(self):
        def move(y, c, z, x):
            s = self.row_block(y, x, c)
            return z // self.nc, z % self.nc, s // self.nx, s % self.nx

        return self.perm(move)

    def chip_of(self, k):
        return k // self.nx, k % self.nx

    def bits(self, count):
        return [1 << b for b in range(count.bit_length() - 1)]

    def chip_bits(self, j):
        bits = self.bits(self.chips)
        return bits if j % 2 == 0 else bits[::-1]

    def doubled(self, bits):
        held = [0]
        for bit in bits:
            held = held + [k ^ bit for k in held]
        return held

    def slots(self):
        return [(k, j) for k in range(self.chips) for j in range(self.nc)]


def slot_scalars(lay, pos_ref, info_ref, slot):
    k, j = slot
    ky, kx = lay.chip_of(k)
    _, group_c, half = lay.unit(pos_ref[1], pos_ref[2])
    z_frame = (half ^ j) * lay.ny + (pos_ref[0] ^ ky ^ group_c)
    frame = z_frame * lay.nx + (pos_ref[3] ^ kx)
    clip = info_ref[frame]
    clips = (info_ref.shape[0] - lay.frames) // 2
    return clip, info_ref[lay.frames + clip], info_ref[lay.frames + clips + clip]


def table_row(mod_ref, step, part, width):
    return mod_ref[pl.ds(step, 1), part * width : (part + 1) * width]


def allowed_pairs(lay, pos_ref, info_ref, patch_base):
    rows = lay.frames * BLOCK
    row_slot = lax.broadcasted_iota(jnp.int32, (rows, 1), 0) // BLOCK
    col_slot = lax.broadcasted_iota(jnp.int32, (1, rows), 1) // BLOCK
    row_clip = jnp.zeros((rows, 1), jnp.int32)
    row_limit = jnp.zeros((rows, 1), jnp.int32)
    col_clip = jnp.zeros((1, rows), jnp.int32)
    for t, slot in enumerate(lay.slots()):
        clip, limit, _ = slot_scalars(lay, pos_ref, info_ref, slot)
        row_clip = jnp.where(row_slot == t, clip, row_clip)
        row_limit = jnp.where(row_slot == t, limit, row_limit)
        col_clip = jnp.where(col_slot == t, clip, col_clip)
    row_patch = lax.broadcasted_iota(jnp.int32, (rows, 1), 0) % BLOCK
    col_patch = lax.broadcasted_iota(jnp.int32, (1, rows), 1) % BLOCK
    row_key = row_clip * BLOCK + row_patch
    col_key = col_clip * BLOCK + col_patch
    row_valid = (patch_base + row_patch < row_limit).astype(jnp.int32)
    row_index = lax.broadcasted_iota(jnp.int32, (rows, rows), 0)
    col_index = lax.broadcasted_iota(jnp.int32, (rows, rows), 1)
    return (row_key == col_key) & ((row_valid > 0) | (row_index == col_index))


def head_mask(values, head, head_size):
    lane = lax.broadcasted_iota(jnp.int32, (1, values.shape[1]), 1)
    inside = (lane >= head * head_size) & (lane < (head + 1) * head_size)
    return jnp.where(inside, values, jnp.zeros_like(values))


def patch_blocks(array, block):
    part = array[:, block * BLOCK : (block + 1) * BLOCK, :]
    return part.reshape(part.shape[0] * BLOCK, part.shape[2])


def start_kernel(lay, cols, pos_ref, x_ref, g_ref, w_ref, *refs):
    pair_refs, out_refs = refs[: lay.nc], refs[lay.nc :]
    half = x_ref.shape[1] // lay.nc
    for k, ref in enumerate(pair_refs):
        first = pl.multiple_of(((pos_ref[2] // lay.ny) ^ k) * half, 16)
        ref[0, 0] = x_ref[0, pl.ds(first, half), :]
        ref[0, 1] = g_ref[0, pl.ds(first, half), :]
    model = w_ref.shape[1] // 3
    for k, out_ref in enumerate(out_refs):
        chip_x = pos_ref[3] ^ k
        if lay.halves > 1:
            want = lay.row_block(pos_ref[0], chip_x, pos_ref[1])
        else:
            want = pos_ref[0] * lay.nx + chip_x
        for v in range(lay.chips * lay.halves):

            @pl.when(want == v)
            def _(v=v, out_ref=out_ref):
                parts = [
                    w_ref[:, p * model + v * cols : p * model + (v + 1) * cols]
                    for p in range(3)
                ]
                out_ref[...] = jnp.concatenate(parts, axis=1)


def fill_weights(lay, pos_ref, w_refs, w_scr):
    block = w_scr.shape[1] // lay.nz
    rows, width = w_refs[0].shape[1], w_scr.shape[2]
    for h in range(lay.halves):
        for k in range(lay.nz):
            ref = w_refs[h * lay.nz + k]
            for m in range(block // rows):
                start = pl.multiple_of((pos_ref[2] ^ k) * block + m * rows, 16)
                w_scr[h, pl.ds(start, rows), :] = ref[0, :, m * width : (m + 1) * width]


def heads_stacked(lay, values):
    head_size = values.shape[1] // lay.half_heads
    parts = [head_mask(values, head, head_size) for head in range(lay.half_heads)]
    return jnp.concatenate(parts, axis=0) if len(parts) > 1 else parts[0]


def beside(lay, weights):
    return jnp.concatenate([weights[head] for head in range(lay.half_heads)], axis=1)


def attention_weights(lay, keys_stacked, queries, allowed, scaling):
    scores = dot_t(keys_stacked, queries) * scaling
    scores = jnp.where(allowed, scores.reshape((lay.half_heads,) + allowed.shape), -jnp.inf)
    exponent = jnp.exp(scores - jnp.max(scores, axis=1, keepdims=True))
    return exponent * (1.0 / jnp.sum(exponent, axis=1, keepdims=True))


def modulate(lay, pos_ref, info_ref, pair_refs, mod_ref, hid_ref, gp_ref):
    _, step_patches, model = hid_ref.shape
    patches = step_patches * pl.num_programs(0)
    patch_base = lay.unit(pos_ref[1], pos_ref[2])[2] * patches + pl.program_id(0) * step_patches
    patch = patch_base + lax.broadcasted_iota(jnp.int32, (step_patches, 1), 0)
    for t, (k, j) in enumerate(lay.slots()):
        _, limit, step = slot_scalars(lay, pos_ref, info_ref, (k, j))
        n = lay.doubled(lay.chip_bits(j)).index(k)
        ref, place = pair_refs[2 * j + (2 * n) // lay.chips], n % (lay.chips // 2)
        normed, _ = normalize(ref[place, 0].astype(F32))
        shift, scale = table_row(mod_ref, step, 0, model), table_row(mod_ref, step, 1, model)
        hid_ref[t] = (normed * (1.0 + scale) + shift).astype(BF16)
        factor = jnp.where(patch < limit, table_row(mod_ref, step, 2, model), 0.0)
        gp_ref[t] = (factor * ref[place, 1].astype(F32)).astype(BF16)


def forward_kernel(lay, pos_ref, info_ref, *refs):
    pair_refs, refs = refs[: 2 * lay.nc], refs[2 * lay.nc :]
    w_refs, refs = refs[: lay.halves * lay.nz], refs[lay.halves * lay.nz :]
    wo_refs, refs = refs[: lay.nc], refs[lay.nc :]
    mod_ref, q_ref, k_ref, v_ref, ga_ref, kept_ref, sent_ref, *refs = refs
    pr_refs, refs = refs[: lay.chips], refs[lay.chips :]
    hid_ref, gp_ref, w_scr, att_scr, wo_scr, acc_scr, cut_scr = refs
    _, step_patches, model = hid_ref.shape
    tokens = lay.frames * step_patches
    cols = w_scr.shape[2] // 3
    scaling = 1.0 / math.sqrt(cols // lay.half_heads)
    patches = step_patches * pl.num_programs(0)
    is_first = pos_ref[1] == 0

    @pl.when(pl.program_id(0) == 0)
    def _():
        fill_weights(lay, pos_ref, w_refs, w_scr)
        own, other = wo_refs[0][...].astype(F32), wo_refs[1][...].astype(F32)
        both = [jnp.where(is_first, own, other), jnp.where(is_first, other, own)]
        wo_scr[...] = jnp.concatenate(both, axis=0).astype(BF16)
        acc_scr[...] = jnp.zeros_like(acc_scr)

    modulate(lay, pos_ref, info_ref, pair_refs, mod_ref, hid_ref, gp_ref)
    hidden = hid_ref[...].reshape(lay.frames * step_patches, model)
    for h in range(lay.halves):
        triple = dot(hidden, w_scr[h])
        for n, ref in enumerate((q_ref, k_ref, v_ref)):
            ref[h] = triple[:, n * cols : (n + 1) * cols].astype(BF16).reshape(ref.shape[1:])

    for b in range(step_patches // BLOCK):
        patch_base = lay.unit(pos_ref[1], pos_ref[2])[2] * patches + pl.program_id(0) * step_patches + b * BLOCK
        allowed = allowed_pairs(lay, pos_ref, info_ref, patch_base)
        outputs = []
        for h in range(lay.halves):
            queries, keys, values = (patch_blocks(ref[h], b) for ref in (q_ref, k_ref, v_ref))
            weights = attention_weights(lay, heads_stacked(lay, keys), queries, allowed, scaling)
            weights = weights.astype(BF16).reshape(-1, allowed.shape[1])
            outputs.append(t_dot(weights, heads_stacked(lay, values)))
        if lay.halves > 1:
            first = jnp.where(pos_ref[1] == 0, outputs[0], outputs[1])
            second = jnp.where(pos_ref[1] == 0, outputs[1], outputs[0])
            outputs = [jnp.concatenate([first, second], axis=1)]
        attended = outputs[0].astype(BF16)
        att_scr[:, b * BLOCK : (b + 1) * BLOCK, :] = attended.reshape(lay.frames, BLOCK, -1)

    attended = att_scr[...].reshape(tokens, -1)
    grad_proj = gp_ref[...].reshape(tokens, model)
    acc_scr[...] += t_dot(attended, grad_proj)
    grad_attn = dot_t(grad_proj, wo_scr[...])
    part = wo_scr.shape[0] // lay.halves
    for h in range(lay.halves):
        ga_ref[h] = grad_attn[:, h * part : (h + 1) * part].astype(BF16).reshape(ga_ref.shape[1:])
    projected = dot(attended, wo_scr[...]).reshape(lay.chips, lay.nc, step_patches, model)
    for k in range(lay.chips):
        pr_refs[k][...] = projected[k].astype(pr_refs[k].dtype)

    @pl.when(pl.program_id(0) == pl.num_programs(0) - 1)
    def _():
        groups, chunk_rows, chunk_width = kept_ref.shape
        block_rows, part = acc_scr.shape[0] // lay.nc, model // groups
        order = lay.doubled(lay.bits(lay.nz)[::-1])
        first, second = acc_scr[:block_rows, :], acc_scr[block_rows:, :]
        kept = jnp.where(is_first, first, second)
        sent = jnp.where(is_first, second, first)
        for ref, rows in ((kept_ref, kept), (sent_ref, sent)):
            for d in range(groups):
                chunk = [
                    rows[m * chunk_rows : (m + 1) * chunk_rows, d * part : (d + 1) * part]
                    for m in range(chunk_width // part)
                ]
                cut_scr[d] = jnp.concatenate(chunk, axis=1) if len(chunk) > 1 else chunk[0]
            for n, k in enumerate(order):
                ref[n] = cut_scr[pos_ref[2] ^ k]


def backward_kernel(lay, pos_ref, info_ref, *refs):
    w_refs, refs = refs[: lay.halves * lay.nz], refs[lay.halves * lay.nz :]
    q_ref, k_ref, v_ref, ga_ref, *refs = refs
    gh_refs, (w_scr, gt_scr) = refs[: lay.chips], refs[lay.chips :]
    _, frames, step_patches, cols = q_ref.shape
    model = w_scr.shape[1]
    patches = step_patches * pl.num_programs(0)
    scaling = 1.0 / math.sqrt(cols // lay.half_heads)

    @pl.when(pl.program_id(0) == 0)
    def _():
        fill_weights(lay, pos_ref, w_refs, w_scr)

    for b in range(step_patches // BLOCK):
        patch_base = lay.unit(pos_ref[1], pos_ref[2])[2] * patches + pl.program_id(0) * step_patches + b * BLOCK
        allowed = allowed_pairs(lay, pos_ref, info_ref, patch_base)
        for h in range(lay.halves):
            queries, keys, values = (patch_blocks(ref[h], b) for ref in (q_ref, k_ref, v_ref))
            grad_out = patch_blocks(ga_ref[(pos_ref[1] ^ h) if lay.halves > 1 else 0], b)
            keys = heads_stacked(lay, keys)
            weights = attention_weights(lay, keys, queries, allowed, scaling)
            grad_weights = dot_t(heads_stacked(lay, values), grad_out).reshape(weights.shape)
            grad_values = dot(beside(lay, weights.astype(BF16)), heads_stacked(lay, grad_out))
            inner = jnp.sum(weights * grad_weights, axis=1, keepdims=True)
            grad_scores = (weights * (grad_weights - inner) * scaling).astype(BF16)
            grad_queries = t_dot(grad_scores.reshape(-1, grad_scores.shape[2]), keys)
            grad_keys = dot(beside(lay, grad_scores), heads_stacked(lay, queries))
            grads = jnp.concatenate([grad_queries, grad_keys, grad_values], axis=1).astype(BF16)
            gt_scr[h, :, b * BLOCK : (b + 1) * BLOCK, :] = grads.reshape(frames, BLOCK, 3 * cols)

    total = jnp.zeros((frames * step_patches, model), F32)
    for h in range(lay.halves):
        total = total + dot_t(gt_scr[h].reshape(frames * step_patches, 3 * cols), w_scr[h])
    total = total.reshape(lay.chips, lay.nc, step_patches, model)
    for k in range(lay.chips):
        gh_refs[k][...] = total[k].astype(gh_refs[k].dtype)


def output_kernel(lay, pos_ref, info_ref, *refs):
    pair_refs, refs = refs[: lay.nc], refs[lay.nc :]
    pr_refs, refs = refs[: lay.chips], refs[lay.chips :]
    mod_ref, *out_refs = refs
    step_patches, model = out_refs[0].shape
    patches = step_patches * pl.num_programs(0)
    patch_base = lay.unit(pos_ref[1], pos_ref[2])[2] * patches + pl.program_id(0) * step_patches
    patch = patch_base + lax.broadcasted_iota(jnp.int32, (step_patches, 1), 0)
    for j in range(lay.nc):
        _, limit, step = slot_scalars(lay, pos_ref, info_ref, (0, j))
        factor = jnp.where(patch < limit, table_row(mod_ref, step, 2, model), 0.0)
        projected = pr_refs[0][j]
        for k in range(1, lay.chips):
            projected = projected + pr_refs[k][j].astype(F32)
        projected = projected.astype(BF16).astype(F32)
        out_refs[j][...] = (pair_refs[j][0, 0].astype(F32) + factor * projected).astype(BF16)


def input_grad_kernel(lay, pos_ref, info_ref, *refs):
    pair_refs, refs = refs[: lay.nc], refs[lay.nc :]
    gh_refs, refs = refs[: lay.chips], refs[lay.chips :]
    mod_ref, *out_refs = refs
    model = out_refs[0].shape[1]
    for j in range(lay.nc):
        _, _, step = slot_scalars(lay, pos_ref, info_ref, (0, j))
        grad_hidden = gh_refs[0][j]
        for k in range(1, lay.chips):
            grad_hidden = grad_hidden + gh_refs[k][j].astype(F32)
        grad_hidden = grad_hidden.astype(BF16).astype(F32)
        normed, inv_sigma = normalize(pair_refs[j][0, 0].astype(F32))
        grad_norm = grad_hidden * (1.0 + table_row(mod_ref, step, 1, model))
        first_mean = jnp.mean(grad_norm, axis=-1, keepdims=True)
        second_mean = jnp.mean(grad_norm * normed, axis=-1, keepdims=True)
        grad_x = pair_refs[j][0, 1].astype(F32) + inv_sigma * (
            grad_norm - first_mean - normed * second_mean
        )
        out_refs[j][...] = grad_x.astype(BF16)


def whole_spec(shape):
    return pl.BlockSpec(shape, lambda *_: (0,) * len(shape))


def struct(shape, dtype=BF16):
    return jax.ShapeDtypeStruct(shape, dtype)


def local(lay, frames_x, grad_y, clip_ids, clip_patches, clip_step, mod_table, w_qkv, w_out):
    y, c, z, x = (lax.axis_index(name) for name in AXES)
    _, patches, model = frames_x.shape
    half = patches // lay.nc
    chips, nc, nx = lay.chips, lay.nc, lay.nx
    head_size = model // HEADS
    halves = lay.halves
    cols = lay.half_heads * head_size
    chip_width = lay.chip_heads * head_size
    rows = w_qkv.shape[0]
    groups = lay.nz
    quarter = model // groups
    step_patches = max(BLOCK, min(half, 512 // lay.frames))
    steps = half // step_patches
    tokens = lay.frames * step_patches

    def call(kernel, name, cost, in_specs, out_specs, out_shape, scratch=(), grid=(1,), prefetch=2):
        return pl.pallas_call(
            kernel,
            grid_spec=pltpu.PrefetchScalarGridSpec(
                num_scalar_prefetch=prefetch,
                grid=grid,
                in_specs=in_specs,
                out_specs=out_specs,
                scratch_shapes=list(scratch),
            ),
            out_shape=out_shape,
            compiler_params=pltpu.CompilerParams(vmem_limit_bytes=VMEM_LIMIT),
            cost_estimate=pl.CostEstimate(
                flops=cost * tokens * steps, bytes_accessed=4 * model * tokens, transcendentals=0
            ),
            name=name,
        )

    def chip_swap(k):
        ky, kx = lay.chip_of(k)
        return lay.swap(ky=ky, kx=kx)

    def from_plane(parts):
        got = [lax.ppermute(part, AXES, lay.from_plane(k)) for k, part in enumerate(parts)]
        first = jnp.where(z // lay.ny == 0, got[0], got[1])
        second = jnp.where(z // lay.ny == 0, got[1], got[0])
        return jnp.concatenate([first, second], axis=0)[None]

    def doubling(held, bits, swap, after, first=None):
        for bit in bits[:-1]:
            got = lax.ppermute(held, AXES, swap(bit)) if first is None else first
            held, first = jnp.concatenate([held, got], axis=0), None
        held, _ = lax.optimization_barrier((held, after))
        return [held, lax.ppermute(held, AXES, swap(bits[-1]))]

    def over_chips(parts):
        got = [lax.ppermute(parts[k], AXES, chip_swap(k)) for k in range(1, chips)]
        return [parts[0]] + got

    info = jnp.concatenate([clip_ids[0], clip_patches[0], clip_step[0]])[None]
    by_core = jnp.concatenate([info, lax.ppermute(info, AXES, lay.swap(kc=1))], axis=0)
    info = [by_core] + [
        lax.ppermute(by_core, AXES, lay.swap(ky=ky)) for ky in range(1, lay.ny)
    ]
    group_y, group_c, _ = lay.unit(c, z)
    info = sum(
        jnp.where((y ^ ky == group_y) & (c ^ kc == group_c), info[ky][kc], 0)
        for ky in range(lay.ny)
        for kc in range(nc)
    )
    pos = jnp.stack([y, c, z, x]).astype(jnp.int32)
    pair_shape = (1, 2, half, model)
    outputs = call(
        functools.partial(start_kernel, lay, cols),
        "start",
        2 * model * 1000,
        [whole_spec(frames_x.shape)] * 2 + [whole_spec(w_qkv.shape)],
        [whole_spec(pair_shape)] * nc + [whole_spec((rows, 3 * cols))] * nx,
        [struct(pair_shape)] * nc + [struct((rows, 3 * cols))] * nx,
        prefetch=1,
    )(pos, frames_x, grad_y, w_qkv)
    pairs, picked = outputs[:nc], outputs[nc:]
    own = [lax.ppermute(pair, AXES, lay.to_plane(k)) for k, pair in enumerate(pairs)]
    by_x = [picked[0]] + [
        lax.ppermute(picked[kx], AXES, lay.swap(kx=kx)) for kx in range(1, nx)
    ]
    if nx == 2:
        ordered = [jnp.where(x == i, by_x[0], by_x[1]) for i in range(nx)]
    else:
        stacked = jnp.stack(by_x)
        ordered = [lax.dynamic_index_in_dim(stacked, x ^ i, 0, keepdims=False) for i in range(nx)]
    w_own = jnp.concatenate(ordered, axis=1 if rows % 16 == 0 else 0)[None]
    first = lax.ppermute(own[0], AXES, chip_swap(lay.chip_bits(0)[0]))
    own[1], first = lax.optimization_barrier((own[1], first))
    late_w_out, _ = lax.optimization_barrier((w_out, own[0]))
    wo_own = lax.ppermute(late_w_out, AXES, lay.rows_to_chip())
    wo_rows = [wo_own, lax.ppermute(wo_own, AXES, lay.swap(kc=1))]
    w_own, _ = lax.optimization_barrier((w_own, (own[1], wo_own)))
    by_z = {0: w_own}
    for bit in lay.bits(lay.nz):
        by_z[bit] = lax.ppermute(w_own, AXES, lay.swap(kz=bit))
    for k in range(1, lay.nz):
        if k not in by_z:
            forwarded = jnp.where(z < lay.nz, by_z[k ^ (k & -k)], w_own)
            by_z[k] = lax.ppermute(forwarded, AXES, lay.swap(kz=k & -k))
    w_pieces = [by_z[k] for k in range(lay.nz)]

    pairs = []
    for j in range(nc):
        after = ([], None) if j else (info, first)
        pairs += doubling(own[j], lay.chip_bits(j), chip_swap, *after)
    near = jnp.where(z < lay.nz, w_pieces[1], w_own)
    early = [lax.ppermute(piece, AXES, lay.swap(kc=1)) for piece in (w_own, near)]
    early = early if halves > 1 else []
    pairs, w_pieces, early, wo_rows = lax.optimization_barrier((pairs, w_pieces, early, wo_rows))
    if halves > 1:
        w_pieces += early + [lax.ppermute(piece, AXES, lay.swap(kc=1)) for piece in w_pieces[2:]]


    def spread(count, width, patches_at_once):
        return pl.BlockSpec((count, patches_at_once, width), lambda i, *_: (0, i, 0))

    def pair_spec(count, patches_at_once):
        return pl.BlockSpec((count, 2, patches_at_once, model), lambda i, *_: (0, 0, i, 0))

    few = max(BLOCK, step_patches // 2)
    few_steps = half // few
    x_spec = pl.BlockSpec((few, model), lambda i, *_: (i, 0))
    triple_spec = pl.BlockSpec((halves, lay.frames, step_patches, cols), lambda i, *_: (0, 0, i, 0))
    w_specs = [whole_spec(w_own.shape)] * (halves * lay.nz)
    w_scratch = pltpu.VMEM((halves, model, 3 * cols), BF16)
    mod_spec = whole_spec(mod_table.shape)
    triple_shape = struct((halves, lay.frames, half, cols))
    part_specs = [spread(nc, model, step_patches)] * chips
    part_shapes = [struct((nc, half, model), F32)] + [struct((nc, half, model))] * (chips - 1)

    fold = 3 if rows % 24 == 0 else 1
    piece_shape = (groups, rows // fold, quarter * fold)
    queries, keys, values, grad_attn, kept, sent, *projected = call(
        functools.partial(forward_kernel, lay),
        "forward",
        14 * model * 1000,
        [pair_spec(chips // 2, step_patches)] * (2 * nc)
        + w_specs
        + [whole_spec(w_out.shape)] * nc
        + [mod_spec],
        [triple_spec] * 4 + [whole_spec(piece_shape)] * 2 + part_specs,
        [triple_shape] * 4 + [struct(piece_shape, F32)] * 2 + part_shapes,
        [pltpu.VMEM((lay.frames, step_patches, model), BF16)] * 2
        + [
            w_scratch,
            pltpu.VMEM((lay.frames, step_patches, chip_width), BF16),
            pltpu.VMEM((chip_width, model), BF16),
            pltpu.VMEM((chip_width, model), F32),
            pltpu.VMEM(piece_shape, F32),
        ],
        (steps,),
    )(pos, info, *pairs, *w_pieces, *wo_rows, mod_table)
    got = lax.ppermute(sent, AXES, lay.swap(kc=1))
    projected = over_chips(projected)

    middle = groups // 2
    cut, away = kept[:middle] + got[:middle], kept[middle:] + got[middle:]
    grad_attn, cut, away = lax.optimization_barrier((grad_attn, cut, away))
    first_away = lax.ppermute(away, AXES, lay.swap(kz=1))

    sums = call(
        functools.partial(backward_kernel, lay),
        "backward",
        10 * model * 1000,
        w_specs + [triple_spec] * 4,
        part_specs,
        part_shapes,
        [w_scratch, pltpu.VMEM((halves, lay.frames, step_patches, 3 * cols), BF16)],
        (steps,),
    )(pos, info, *w_pieces, queries, keys, values, grad_attn)
    sums, first_away, projected = lax.optimization_barrier((sums, first_away, projected))
    grad_hidden = over_chips(sums)

    out_parts = call(
        functools.partial(output_kernel, lay),
        "output",
        20 * model * 1000,
        [pair_spec(1, few)] * nc + [spread(nc, model, few)] * chips + [mod_spec],
        [x_spec] * nc,
        [struct((half, model))] * nc,
        grid=(few_steps,),
    )(pos, info, *own, *projected, mod_table)
    out_y = from_plane(out_parts)

    grad_hidden, _ = lax.optimization_barrier((grad_hidden, out_parts))
    grad_parts = call(
        functools.partial(input_grad_kernel, lay),
        "input_grad",
        3 * model * 1000,
        [pair_spec(1, few)] * nc + [spread(nc, model, few)] * chips + [mod_spec],
        [x_spec] * nc,
        [struct((half, model))] * nc,
        grid=(few_steps,),
    )(pos, info, *own, *grad_hidden, mod_table)
    grad_x = from_plane(grad_parts)

    cut, _ = lax.optimization_barrier((cut + first_away, out_parts))
    for bit in lay.bits(lay.nz)[1:]:
        middle = middle // 2
        cut = cut[:middle] + lax.ppermute(cut[middle:], AXES, lay.swap(kz=bit))
    cut, _ = lax.optimization_barrier((cut, grad_parts))
    grad_w = lax.ppermute(cut[0], AXES, lay.to_owner())
    grad_w = jnp.concatenate(
        [grad_w[:, m * quarter : (m + 1) * quarter] for m in range(fold)], axis=0
    )
    grad_w_out = grad_w * jnp.float32(1.0 / math.sqrt(groups * lay.frames * patches))
    return out_y, grad_x, grad_w_out


def solution(mesh):
    lay = Layout(mesh)
    grid = Mesh(mesh.devices.reshape(lay.ny, lay.nc, lay.nz, lay.nx), AXES)
    rows, cols = ("z", "x"), ("y", "c")
    frame = P(AXES, None, None)
    group = P(cols, None)
    return jax.shard_map(
        functools.partial(local, lay),
        mesh=grid,
        in_specs=(frame, frame, group, group, group, P(), P(rows, None), P(rows, None)),
        out_specs=(frame, frame, P(rows, cols)),
        check_vma=False,
    )
```

```python
import functools
import math

import jax
import jax.numpy as jnp
from jax import lax
from jax.experimental import pallas as pl
from jax.experimental.pallas import tpu as pltpu
from jax.sharding import Mesh, PartitionSpec as P

HEADS = 16
CORES = 2
AXES = ("y", "c", "z", "x")
BLOCK = 16
VMEM_LIMIT = 56 * 1024 * 1024
BF16 = jnp.bfloat16
F32 = jnp.float32


def dot(left, right):
    return jnp.dot(left, right, preferred_element_type=F32)


def dot_t(left, right):
    return lax.dot_general(left, right, (((1,), (1,)), ((), ())), preferred_element_type=F32)


def t_dot(left, right):
    return lax.dot_general(left, right, (((0,), (0,)), ((), ())), preferred_element_type=F32)


def normalize(values):
    centred = values - jnp.mean(values, axis=-1, keepdims=True)
    inv_sigma = lax.rsqrt(jnp.mean(centred * centred, axis=-1, keepdims=True) + 1e-06)
    return centred * inv_sigma, inv_sigma


class Layout:
    def __init__(self, mesh):
        groups, seq = mesh.shape["dp"], mesh.shape["seq"]
        self.nc = CORES
        self.ny = groups // CORES
        self.nz = groups
        self.nx = seq // self.nz
        self.chips = self.ny * self.nx
        self.frames = seq
        self.chip_heads = HEADS // self.chips
        self.halves = 2 if self.chip_heads % 2 == 0 else 1
        self.half_heads = self.chip_heads // self.halves

    def linear(self, y, c, z, x):
        return ((y * self.nc + c) * self.nz + z) * self.nx + x

    def perm(self, move):
        pairs = []
        for y in range(self.ny):
            for c in range(self.nc):
                for z in range(self.nz):
                    for x in range(self.nx):
                        pairs.append((self.linear(y, c, z, x), self.linear(*move(y, c, z, x))))
        return pairs

    def to_plane(self, k):
        def move(y, c, z, x):
            half = (z // self.ny) ^ k
            plane = ((y // self.nc) * self.nc + c) * self.nc + half
            return (z % self.ny) ^ c, y % self.nc, plane, x

        return self.perm(move)

    def unit(self, c, z):
        return (z // (self.nc * self.nc)) * self.nc + c, (z // self.nc) % self.nc, z % self.nc

    def from_plane(self, k):
        return [(target, source) for source, target in self.to_plane(k)]

    def swap(self, ky=0, kc=0, kz=0, kx=0):
        return self.perm(lambda y, c, z, x: (y ^ ky, c ^ kc, z ^ kz, x ^ kx))

    def row_block(self, y, x, i):
        if self.halves > 1:
            return (i * self.ny + y) * self.nx + x
        return self.nc * (y * self.nx + x) + i

    def rows_to_chip(self):
        reader = {
            self.row_block(y, x, i): (y, x, i)
            for y in range(self.ny)
            for x in range(self.nx)
            for i in range(self.nc)
        }

        def move(y, c, z, x):
            chip_y, chip_x, i = reader[z * self.nx + x]
            return chip_y, i, c * self.ny + (y ^ (z & 1)), chip_x

        return self.perm(move)

    def to_owner(self):
        def move(y, c, z, x):
            s = self.row_block(y, x, c)
            return z // self.nc, z % self.nc, s // self.nx, s % self.nx

        return self.perm(move)

    def chip_of(self, k):
        return k // self.nx, k % self.nx

    def bits(self, count):
        return [1 << b for b in range(count.bit_length() - 1)]

    def chip_bits(self, j):
        bits = self.bits(self.chips)
        return bits if j % 2 == 0 else bits[::-1]

    def doubled(self, bits):
        held = [0]
        for bit in bits:
            held = held + [k ^ bit for k in held]
        return held

    def slots(self):
        return [(k, j) for k in range(self.chips) for j in range(self.nc)]


def slot_scalars(lay, pos_ref, info_ref, slot):
    k, j = slot
    ky, kx = lay.chip_of(k)
    _, group_c, half = lay.unit(pos_ref[1], pos_ref[2])
    z_frame = (half ^ j) * lay.ny + (pos_ref[0] ^ ky ^ group_c)
    frame = z_frame * lay.nx + (pos_ref[3] ^ kx)
    clip = info_ref[frame]
    clips = (info_ref.shape[0] - lay.frames) // 2
    return clip, info_ref[lay.frames + clip], info_ref[lay.frames + clips + clip]


def table_row(mod_ref, step, part, width):
    return mod_ref[pl.ds(step, 1), part * width : (part + 1) * width]


def allowed_pairs(lay, pos_ref, info_ref, patch_base):
    rows = lay.frames * BLOCK
    row_slot = lax.broadcasted_iota(jnp.int32, (rows, 1), 0) // BLOCK
    col_slot = lax.broadcasted_iota(jnp.int32, (1, rows), 1) // BLOCK
    row_clip = jnp.zeros((rows, 1), jnp.int32)
    row_limit = jnp.zeros((rows, 1), jnp.int32)
    col_clip = jnp.zeros((1, rows), jnp.int32)
    for t, slot in enumerate(lay.slots()):
        clip, limit, _ = slot_scalars(lay, pos_ref, info_ref, slot)
        row_clip = jnp.where(row_slot == t, clip, row_clip)
        row_limit = jnp.where(row_slot == t, limit, row_limit)
        col_clip = jnp.where(col_slot == t, clip, col_clip)
    row_patch = lax.broadcasted_iota(jnp.int32, (rows, 1), 0) % BLOCK
    col_patch = lax.broadcasted_iota(jnp.int32, (1, rows), 1) % BLOCK
    row_key = row_clip * BLOCK + row_patch
    col_key = col_clip * BLOCK + col_patch
    row_valid = (patch_base + row_patch < row_limit).astype(jnp.int32)
    row_index = lax.broadcasted_iota(jnp.int32, (rows, rows), 0)
    col_index = lax.broadcasted_iota(jnp.int32, (rows, rows), 1)
    return (row_key == col_key) & ((row_valid > 0) | (row_index == col_index))


def head_mask(values, head, head_size):
    lane = lax.broadcasted_iota(jnp.int32, (1, values.shape[1]), 1)
    inside = (lane >= head * head_size) & (lane < (head + 1) * head_size)
    return jnp.where(inside, values, jnp.zeros_like(values))


def patch_blocks(array, block):
    part = array[:, block * BLOCK : (block + 1) * BLOCK, :]
    return part.reshape(part.shape[0] * BLOCK, part.shape[2])


def start_kernel(lay, cols, pos_ref, x_ref, g_ref, w_ref, *refs):
    pair_refs, out_refs = refs[: lay.nc], refs[lay.nc :]
    half = x_ref.shape[1] // lay.nc
    for k, ref in enumerate(pair_refs):
        first = pl.multiple_of(((pos_ref[2] // lay.ny) ^ k) * half, 16)
        ref[0, 0] = x_ref[0, pl.ds(first, half), :]
        ref[0, 1] = g_ref[0, pl.ds(first, half), :]
    model = w_ref.shape[1] // 3
    for k, out_ref in enumerate(out_refs):
        chip_x = pos_ref[3] ^ k
        if lay.halves > 1:
            want = lay.row_block(pos_ref[0], chip_x, pos_ref[1])
        else:
            want = pos_ref[0] * lay.nx + chip_x
        for v in range(lay.chips * lay.halves):

            @pl.when(want == v)
            def _(v=v, out_ref=out_ref):
                parts = [
                    w_ref[:, p * model + v * cols : p * model + (v + 1) * cols]
                    for p in range(3)
                ]
                out_ref[...] = jnp.concatenate(parts, axis=1)


def fill_weights(lay, pos_ref, w_refs, w_scr):
    block = w_scr.shape[1] // lay.nz
    rows, width = w_refs[0].shape[1], w_scr.shape[2]
    for h in range(lay.halves):
        for k in range(lay.nz):
            ref = w_refs[h * lay.nz + k]
            for m in range(block // rows):
                start = pl.multiple_of((pos_ref[2] ^ k) * block + m * rows, 16)
                w_scr[h, pl.ds(start, rows), :] = ref[0, :, m * width : (m + 1) * width]


def heads_stacked(lay, values):
    head_size = values.shape[1] // lay.half_heads
    parts = [head_mask(values, head, head_size) for head in range(lay.half_heads)]
    return jnp.concatenate(parts, axis=0) if len(parts) > 1 else parts[0]


def beside(lay, weights):
    return jnp.concatenate([weights[head] for head in range(lay.half_heads)], axis=1)


def attention_weights(lay, keys_stacked, queries, allowed, scaling):
    scores = dot_t(keys_stacked, queries) * scaling
    scores = jnp.where(allowed, scores.reshape((lay.half_heads,) + allowed.shape), -jnp.inf)
    exponent = jnp.exp(scores - jnp.max(scores, axis=1, keepdims=True))
    return exponent * (1.0 / jnp.sum(exponent, axis=1, keepdims=True))


def modulate(lay, pos_ref, info_ref, pair_refs, mod_ref, hid_ref, gp_ref):
    _, step_patches, model = hid_ref.shape
    patches = step_patches * pl.num_programs(0)
    patch_base = lay.unit(pos_ref[1], pos_ref[2])[2] * patches + pl.program_id(0) * step_patches
    patch = patch_base + lax.broadcasted_iota(jnp.int32, (step_patches, 1), 0)
    for t, (k, j) in enumerate(lay.slots()):
        _, limit, step = slot_scalars(lay, pos_ref, info_ref, (k, j))
        n = lay.doubled(lay.chip_bits(j)).index(k)
        ref, place = pair_refs[2 * j + (2 * n) // lay.chips], n % (lay.chips // 2)
        normed, _ = normalize(ref[place, 0].astype(F32))
        shift, scale = table_row(mod_ref, step, 0, model), table_row(mod_ref, step, 1, model)
        hid_ref[t] = (normed * (1.0 + scale) + shift).astype(BF16)
        factor = jnp.where(patch < limit, table_row(mod_ref, step, 2, model), 0.0)
        gp_ref[t] = (factor * ref[place, 1].astype(F32)).astype(BF16)


def forward_kernel(lay, pos_ref, info_ref, *refs):
    pair_refs, refs = refs[: 2 * lay.nc], refs[2 * lay.nc :]
    w_refs, refs = refs[: lay.halves * lay.nz], refs[lay.halves * lay.nz :]
    wo_refs, refs = refs[: lay.nc], refs[lay.nc :]
    mod_ref, q_ref, k_ref, v_ref, ga_ref, kept_ref, sent_ref, *refs = refs
    pr_refs, refs = refs[: lay.chips], refs[lay.chips :]
    hid_ref, gp_ref, w_scr, att_scr, wo_scr, acc_scr, cut_scr = refs
    _, step_patches, model = hid_ref.shape
    tokens = lay.frames * step_patches
    cols = w_scr.shape[2] // 3
    scaling = 1.0 / math.sqrt(cols // lay.half_heads)
    patches = step_patches * pl.num_programs(0)
    is_first = pos_ref[1] == 0

    @pl.when(pl.program_id(0) == 0)
    def _():
        fill_weights(lay, pos_ref, w_refs, w_scr)
        own, other = wo_refs[0][...].astype(F32), wo_refs[1][...].astype(F32)
        both = [jnp.where(is_first, own, other), jnp.where(is_first, other, own)]
        wo_scr[...] = jnp.concatenate(both, axis=0).astype(BF16)
        acc_scr[...] = jnp.zeros_like(acc_scr)

    modulate(lay, pos_ref, info_ref, pair_refs, mod_ref, hid_ref, gp_ref)
    hidden = hid_ref[...].reshape(lay.frames * step_patches, model)
    for h in range(lay.halves):
        triple = dot(hidden, w_scr[h])
        for n, ref in enumerate((q_ref, k_ref, v_ref)):
            ref[h] = triple[:, n * cols : (n + 1) * cols].astype(BF16).reshape(ref.shape[1:])

    for b in range(step_patches // BLOCK):
        patch_base = lay.unit(pos_ref[1], pos_ref[2])[2] * patches + pl.program_id(0) * step_patches + b * BLOCK
        allowed = allowed_pairs(lay, pos_ref, info_ref, patch_base)
        outputs = []
        for h in range(lay.halves):
            queries, keys, values = (patch_blocks(ref[h], b) for ref in (q_ref, k_ref, v_ref))
            weights = attention_weights(lay, heads_stacked(lay, keys), queries, allowed, scaling)
            weights = weights.astype(BF16).reshape(-1, allowed.shape[1])
            outputs.append(t_dot(weights, heads_stacked(lay, values)))
        if lay.halves > 1:
            first = jnp.where(pos_ref[1] == 0, outputs[0], outputs[1])
            second = jnp.where(pos_ref[1] == 0, outputs[1], outputs[0])
            outputs = [jnp.concatenate([first, second], axis=1)]
        attended = outputs[0].astype(BF16)
        att_scr[:, b * BLOCK : (b + 1) * BLOCK, :] = attended.reshape(lay.frames, BLOCK, -1)

    attended = att_scr[...].reshape(tokens, -1)
    grad_proj = gp_ref[...].reshape(tokens, model)
    acc_scr[...] += t_dot(attended, grad_proj)
    grad_attn = dot_t(grad_proj, wo_scr[...])
    part = wo_scr.shape[0] // lay.halves
    for h in range(lay.halves):
        ga_ref[h] = grad_attn[:, h * part : (h + 1) * part].astype(BF16).reshape(ga_ref.shape[1:])
    projected = dot(attended, wo_scr[...]).reshape(lay.chips, lay.nc, step_patches, model)
    for k in range(lay.chips):
        pr_refs[k][...] = projected[k].astype(pr_refs[k].dtype)

    @pl.when(pl.program_id(0) == pl.num_programs(0) - 1)
    def _():
        groups, chunk_rows, chunk_width = kept_ref.shape
        block_rows, part = acc_scr.shape[0] // lay.nc, model // groups
        order = lay.doubled(lay.bits(lay.nz)[::-1])
        first, second = acc_scr[:block_rows, :], acc_scr[block_rows:, :]
        kept = jnp.where(is_first, first, second)
        sent = jnp.where(is_first, second, first)
        for ref, rows in ((kept_ref, kept), (sent_ref, sent)):
            for d in range(groups):
                chunk = [
                    rows[m * chunk_rows : (m + 1) * chunk_rows, d * part : (d + 1) * part]
                    for m in range(chunk_width // part)
                ]
                cut_scr[d] = jnp.concatenate(chunk, axis=1) if len(chunk) > 1 else chunk[0]
            for n, k in enumerate(order):
                ref[n] = cut_scr[pos_ref[2] ^ k]


def backward_kernel(lay, pos_ref, info_ref, *refs):
    w_refs, refs = refs[: lay.halves * lay.nz], refs[lay.halves * lay.nz :]
    q_ref, k_ref, v_ref, ga_ref, *refs = refs
    gh_refs, (w_scr, gt_scr) = refs[: lay.chips], refs[lay.chips :]
    _, frames, step_patches, cols = q_ref.shape
    model = w_scr.shape[1]
    patches = step_patches * pl.num_programs(0)
    scaling = 1.0 / math.sqrt(cols // lay.half_heads)

    @pl.when(pl.program_id(0) == 0)
    def _():
        fill_weights(lay, pos_ref, w_refs, w_scr)

    for b in range(step_patches // BLOCK):
        patch_base = lay.unit(pos_ref[1], pos_ref[2])[2] * patches + pl.program_id(0) * step_patches + b * BLOCK
        allowed = allowed_pairs(lay, pos_ref, info_ref, patch_base)
        for h in range(lay.halves):
            queries, keys, values = (patch_blocks(ref[h], b) for ref in (q_ref, k_ref, v_ref))
            grad_out = patch_blocks(ga_ref[(pos_ref[1] ^ h) if lay.halves > 1 else 0], b)
            keys = heads_stacked(lay, keys)
            weights = attention_weights(lay, keys, queries, allowed, scaling)
            grad_weights = dot_t(heads_stacked(lay, values), grad_out).reshape(weights.shape)
            grad_values = dot(beside(lay, weights.astype(BF16)), heads_stacked(lay, grad_out))
            inner = jnp.sum(weights * grad_weights, axis=1, keepdims=True)
            grad_scores = (weights * (grad_weights - inner) * scaling).astype(BF16)
            grad_queries = t_dot(grad_scores.reshape(-1, grad_scores.shape[2]), keys)
            grad_keys = dot(beside(lay, grad_scores), heads_stacked(lay, queries))
            grads = jnp.concatenate([grad_queries, grad_keys, grad_values], axis=1).astype(BF16)
            gt_scr[h, :, b * BLOCK : (b + 1) * BLOCK, :] = grads.reshape(frames, BLOCK, 3 * cols)

    total = jnp.zeros((frames * step_patches, model), F32)
    for h in range(lay.halves):
        total = total + dot_t(gt_scr[h].reshape(frames * step_patches, 3 * cols), w_scr[h])
    total = total.reshape(lay.chips, lay.nc, step_patches, model)
    for k in range(lay.chips):
        gh_refs[k][...] = total[k].astype(gh_refs[k].dtype)


def output_kernel(lay, pos_ref, info_ref, *refs):
    pair_refs, refs = refs[: lay.nc], refs[lay.nc :]
    pr_refs, refs = refs[: lay.chips], refs[lay.chips :]
    mod_ref, *out_refs = refs
    step_patches, model = out_refs[0].shape
    patches = step_patches * pl.num_programs(0)
    patch_base = lay.unit(pos_ref[1], pos_ref[2])[2] * patches + pl.program_id(0) * step_patches
    patch = patch_base + lax.broadcasted_iota(jnp.int32, (step_patches, 1), 0)
    for j in range(lay.nc):
        _, limit, step = slot_scalars(lay, pos_ref, info_ref, (0, j))
        factor = jnp.where(patch < limit, table_row(mod_ref, step, 2, model), 0.0)
        projected = pr_refs[0][j]
        for k in range(1, lay.chips):
            projected = projected + pr_refs[k][j].astype(F32)
        projected = projected.astype(BF16).astype(F32)
        out_refs[j][...] = (pair_refs[j][0, 0].astype(F32) + factor * projected).astype(BF16)


def input_grad_kernel(lay, pos_ref, info_ref, *refs):
    pair_refs, refs = refs[: lay.nc], refs[lay.nc :]
    gh_refs, refs = refs[: lay.chips], refs[lay.chips :]
    mod_ref, *out_refs = refs
    model = out_refs[0].shape[1]
    for j in range(lay.nc):
        _, _, step = slot_scalars(lay, pos_ref, info_ref, (0, j))
        grad_hidden = gh_refs[0][j]
        for k in range(1, lay.chips):
            grad_hidden = grad_hidden + gh_refs[k][j].astype(F32)
        grad_hidden = grad_hidden.astype(BF16).astype(F32)
        normed, inv_sigma = normalize(pair_refs[j][0, 0].astype(F32))
        grad_norm = grad_hidden * (1.0 + table_row(mod_ref, step, 1, model))
        first_mean = jnp.mean(grad_norm, axis=-1, keepdims=True)
        second_mean = jnp.mean(grad_norm * normed, axis=-1, keepdims=True)
        grad_x = pair_refs[j][0, 1].astype(F32) + inv_sigma * (
            grad_norm - first_mean - normed * second_mean
        )
        out_refs[j][...] = grad_x.astype(BF16)


def whole_spec(shape):
    return pl.BlockSpec(shape, lambda *_: (0,) * len(shape))


def struct(shape, dtype=BF16):
    return jax.ShapeDtypeStruct(shape, dtype)


def local(lay, frames_x, grad_y, clip_ids, clip_patches, clip_step, mod_table, w_qkv, w_out):
    y, c, z, x = (lax.axis_index(name) for name in AXES)
    _, patches, model = frames_x.shape
    half = patches // lay.nc
    chips, nc, nx = lay.chips, lay.nc, lay.nx
    head_size = model // HEADS
    halves = lay.halves
    cols = lay.half_heads * head_size
    chip_width = lay.chip_heads * head_size
    rows = w_qkv.shape[0]
    groups = lay.nz
    quarter = model // groups
    step_patches = max(BLOCK, min(half, 512 // lay.frames))
    steps = half // step_patches
    tokens = lay.frames * step_patches

    def call(kernel, name, cost, in_specs, out_specs, out_shape, scratch=(), grid=(1,), prefetch=2):
        return pl.pallas_call(
            kernel,
            grid_spec=pltpu.PrefetchScalarGridSpec(
                num_scalar_prefetch=prefetch,
                grid=grid,
                in_specs=in_specs,
                out_specs=out_specs,
                scratch_shapes=list(scratch),
            ),
            out_shape=out_shape,
            compiler_params=pltpu.CompilerParams(vmem_limit_bytes=VMEM_LIMIT),
            cost_estimate=pl.CostEstimate(
                flops=cost * tokens * steps, bytes_accessed=4 * model * tokens, transcendentals=0
            ),
            name=name,
        )

    def chip_swap(k):
        ky, kx = lay.chip_of(k)
        return lay.swap(ky=ky, kx=kx)

    def from_plane(parts):
        got = [lax.ppermute(part, AXES, lay.from_plane(k)) for k, part in enumerate(parts)]
        first = jnp.where(z // lay.ny == 0, got[0], got[1])
        second = jnp.where(z // lay.ny == 0, got[1], got[0])
        return jnp.concatenate([first, second], axis=0)[None]

    def doubling(held, bits, swap, after, first=None):
        for bit in bits[:-1]:
            got = lax.ppermute(held, AXES, swap(bit)) if first is None else first
            held, first = jnp.concatenate([held, got], axis=0), None
        held, _ = lax.optimization_barrier((held, after))
        return [held, lax.ppermute(held, AXES, swap(bits[-1]))]

    def over_chips(parts):
        got = [lax.ppermute(parts[k], AXES, chip_swap(k)) for k in range(1, chips)]
        return [parts[0]] + got

    info = jnp.concatenate([clip_ids[0], clip_patches[0], clip_step[0]])[None]
    by_core = jnp.concatenate([info, lax.ppermute(info, AXES, lay.swap(kc=1))], axis=0)
    info = [by_core] + [
        lax.ppermute(by_core, AXES, lay.swap(ky=ky)) for ky in range(1, lay.ny)
    ]
    group_y, group_c, _ = lay.unit(c, z)
    info = sum(
        jnp.where((y ^ ky == group_y) & (c ^ kc == group_c), info[ky][kc], 0)
        for ky in range(lay.ny)
        for kc in range(nc)
    )
    pos = jnp.stack([y, c, z, x]).astype(jnp.int32)
    pair_shape = (1, 2, half, model)
    outputs = call(
        functools.partial(start_kernel, lay, cols),
        "start",
        2 * model * 1000,
        [whole_spec(frames_x.shape)] * 2 + [whole_spec(w_qkv.shape)],
        [whole_spec(pair_shape)] * nc + [whole_spec((rows, 3 * cols))] * nx,
        [struct(pair_shape)] * nc + [struct((rows, 3 * cols))] * nx,
        prefetch=1,
    )(pos, frames_x, grad_y, w_qkv)
    pairs, picked = outputs[:nc], outputs[nc:]
    own = [lax.ppermute(pair, AXES, lay.to_plane(k)) for k, pair in enumerate(pairs)]
    by_x = [picked[0]] + [
        lax.ppermute(picked[kx], AXES, lay.swap(kx=kx)) for kx in range(1, nx)
    ]
    if nx == 2:
        ordered = [jnp.where(x == i, by_x[0], by_x[1]) for i in range(nx)]
    else:
        stacked = jnp.stack(by_x)
        ordered = [lax.dynamic_index_in_dim(stacked, x ^ i, 0, keepdims=False) for i in range(nx)]
    w_own = jnp.concatenate(ordered, axis=1 if rows % 16 == 0 else 0)[None]
    first = lax.ppermute(own[0], AXES, chip_swap(lay.chip_bits(0)[0]))
    own[1], first = lax.optimization_barrier((own[1], first))
    late_w_out, _ = lax.optimization_barrier((w_out, own[0]))
    wo_own = lax.ppermute(late_w_out, AXES, lay.rows_to_chip())
    wo_rows = [wo_own, lax.ppermute(wo_own, AXES, lay.swap(kc=1))]
    w_own, _ = lax.optimization_barrier((w_own, (own[1], wo_own)))
    by_z = {0: w_own}
    for bit in lay.bits(lay.nz):
        by_z[bit] = lax.ppermute(w_own, AXES, lay.swap(kz=bit))
    for k in range(1, lay.nz):
        if k not in by_z:
            forwarded = jnp.where(z < lay.nz, by_z[k ^ (k & -k)], w_own)
            by_z[k] = lax.ppermute(forwarded, AXES, lay.swap(kz=k & -k))
    w_pieces = [by_z[k] for k in range(lay.nz)]

    pairs = []
    for j in range(nc):
        after = ([], None) if j else (info, first)
        pairs += doubling(own[j], lay.chip_bits(j), chip_swap, *after)
    near = jnp.where(z < lay.nz, w_pieces[1], w_own)
    early = [lax.ppermute(piece, AXES, lay.swap(kc=1)) for piece in (w_own, near)]
    early = early if halves > 1 else []
    pairs, w_pieces, early, wo_rows = lax.optimization_barrier((pairs, w_pieces, early, wo_rows))
    if halves > 1:
        w_pieces += early + [lax.ppermute(piece, AXES, lay.swap(kc=1)) for piece in w_pieces[2:]]


    def spread(count, width, patches_at_once):
        return pl.BlockSpec((count, patches_at_once, width), lambda i, *_: (0, i, 0))

    def pair_spec(count, patches_at_once):
        return pl.BlockSpec((count, 2, patches_at_once, model), lambda i, *_: (0, 0, i, 0))

    few = max(BLOCK, step_patches // 2)
    few_steps = half // few
    x_spec = pl.BlockSpec((few, model), lambda i, *_: (i, 0))
    triple_spec = pl.BlockSpec((halves, lay.frames, step_patches, cols), lambda i, *_: (0, 0, i, 0))
    w_specs = [whole_spec(w_own.shape)] * (halves * lay.nz)
    w_scratch = pltpu.VMEM((halves, model, 3 * cols), BF16)
    mod_spec = whole_spec(mod_table.shape)
    triple_shape = struct((halves, lay.frames, half, cols))
    part_specs = [spread(nc, model, step_patches)] * chips
    part_shapes = [struct((nc, half, model), F32)] + [struct((nc, half, model))] * (chips - 1)

    fold = 3 if rows % 24 == 0 else 1
    piece_shape = (groups, rows // fold, quarter * fold)
    queries, keys, values, grad_attn, kept, sent, *projected = call(
        functools.partial(forward_kernel, lay),
        "forward",
        14 * model * 1000,
        [pair_spec(chips // 2, step_patches)] * (2 * nc)
        + w_specs
        + [whole_spec(w_out.shape)] * nc
        + [mod_spec],
        [triple_spec] * 4 + [whole_spec(piece_shape)] * 2 + part_specs,
        [triple_shape] * 4 + [struct(piece_shape, F32)] * 2 + part_shapes,
        [pltpu.VMEM((lay.frames, step_patches, model), BF16)] * 2
        + [
            w_scratch,
            pltpu.VMEM((lay.frames, step_patches, chip_width), BF16),
            pltpu.VMEM((chip_width, model), BF16),
            pltpu.VMEM((chip_width, model), F32),
            pltpu.VMEM(piece_shape, F32),
        ],
        (steps,),
    )(pos, info, *pairs, *w_pieces, *wo_rows, mod_table)
    got = lax.ppermute(sent, AXES, lay.swap(kc=1))
    projected = over_chips(projected)

    middle = groups // 2
    cut, away = kept[:middle] + got[:middle], kept[middle:] + got[middle:]
    grad_attn, cut, away = lax.optimization_barrier((grad_attn, cut, away))
    first_away = lax.ppermute(away, AXES, lay.swap(kz=1))

    sums = call(
        functools.partial(backward_kernel, lay),
        "backward",
        10 * model * 1000,
        w_specs + [triple_spec] * 4,
        part_specs,
        part_shapes,
        [w_scratch, pltpu.VMEM((halves, lay.frames, step_patches, 3 * cols), BF16)],
        (steps,),
    )(pos, info, *w_pieces, queries, keys, values, grad_attn)
    sums, first_away, projected[1] = lax.optimization_barrier((sums, first_away, projected[1]))
    projected, _ = lax.optimization_barrier((projected, sums))
    grad_hidden = over_chips(sums)

    out_parts = call(
        functools.partial(output_kernel, lay),
        "output",
        20 * model * 1000,
        [pair_spec(1, few)] * nc + [spread(nc, model, few)] * chips + [mod_spec],
        [x_spec] * nc,
        [struct((half, model))] * nc,
        grid=(few_steps,),
    )(pos, info, *own, *projected, mod_table)
    out_y = from_plane(out_parts)

    grad_hidden, _ = lax.optimization_barrier((grad_hidden, out_parts))
    grad_parts = call(
        functools.partial(input_grad_kernel, lay),
        "input_grad",
        3 * model * 1000,
        [pair_spec(1, few)] * nc + [spread(nc, model, few)] * chips + [mod_spec],
        [x_spec] * nc,
        [struct((half, model))] * nc,
        grid=(few_steps,),
    )(pos, info, *own, *grad_hidden, mod_table)
    grad_x = from_plane(grad_parts)

    cut, _ = lax.optimization_barrier((cut + first_away, out_parts))
    for bit in lay.bits(lay.nz)[1:]:
        middle = middle // 2
        cut = cut[:middle] + lax.ppermute(cut[middle:], AXES, lay.swap(kz=bit))
    cut, _ = lax.optimization_barrier((cut, grad_parts))
    grad_w = lax.ppermute(cut[0], AXES, lay.to_owner())
    grad_w = jnp.concatenate(
        [grad_w[:, m * quarter : (m + 1) * quarter] for m in range(fold)], axis=0
    )
    grad_w_out = grad_w * jnp.float32(1.0 / math.sqrt(groups * lay.frames * patches))
    return out_y, grad_x, grad_w_out


def solution(mesh):
    lay = Layout(mesh)
    grid = Mesh(mesh.devices.reshape(lay.ny, lay.nc, lay.nz, lay.nx), AXES)
    rows, cols = ("z", "x"), ("y", "c")
    frame = P(AXES, None, None)
    group = P(cols, None)
    return jax.shard_map(
        functools.partial(local, lay),
        mesh=grid,
        in_specs=(frame, frame, group, group, group, P(), P(rows, None), P(rows, None)),
        out_specs=(frame, frame, P(rows, cols)),
        check_vma=False,
    )
```

```python
import functools
import math

import jax
import jax.numpy as jnp
from jax import lax
from jax.experimental import pallas as pl
from jax.experimental.pallas import tpu as pltpu
from jax.sharding import Mesh, PartitionSpec as P

HEADS = 16
CORES = 2
AXES = ("y", "c", "z", "x")
BLOCK = 16
VMEM_LIMIT = 56 * 1024 * 1024
BF16 = jnp.bfloat16
F32 = jnp.float32


def dot(left, right):
    return jnp.dot(left, right, preferred_element_type=F32)


def dot_t(left, right):
    return lax.dot_general(left, right, (((1,), (1,)), ((), ())), preferred_element_type=F32)


def t_dot(left, right):
    return lax.dot_general(left, right, (((0,), (0,)), ((), ())), preferred_element_type=F32)


def normalize(values):
    centred = values - jnp.mean(values, axis=-1, keepdims=True)
    inv_sigma = lax.rsqrt(jnp.mean(centred * centred, axis=-1, keepdims=True) + 1e-06)
    return centred * inv_sigma, inv_sigma


class Layout:
    def __init__(self, mesh):
        groups, seq = mesh.shape["dp"], mesh.shape["seq"]
        self.nc = CORES
        self.ny = groups // CORES
        self.nz = groups
        self.nx = seq // self.nz
        self.chips = self.ny * self.nx
        self.frames = seq
        self.chip_heads = HEADS // self.chips
        self.halves = 2 if self.chip_heads % 2 == 0 else 1
        self.half_heads = self.chip_heads // self.halves

    def linear(self, y, c, z, x):
        return ((y * self.nc + c) * self.nz + z) * self.nx + x

    def perm(self, move):
        pairs = []
        for y in range(self.ny):
            for c in range(self.nc):
                for z in range(self.nz):
                    for x in range(self.nx):
                        pairs.append((self.linear(y, c, z, x), self.linear(*move(y, c, z, x))))
        return pairs

    def to_plane(self, k):
        def move(y, c, z, x):
            half = (z // self.ny) ^ k
            plane = ((y // self.nc) * self.nc + c) * self.nc + half
            return (z % self.ny) ^ c, y % self.nc, plane, x

        return self.perm(move)

    def unit(self, c, z):
        return (z // (self.nc * self.nc)) * self.nc + c, (z // self.nc) % self.nc, z % self.nc

    def from_plane(self, k):
        return [(target, source) for source, target in self.to_plane(k)]

    def swap(self, ky=0, kc=0, kz=0, kx=0):
        return self.perm(lambda y, c, z, x: (y ^ ky, c ^ kc, z ^ kz, x ^ kx))

    def row_block(self, y, x, i):
        if self.halves > 1:
            return (i * self.ny + y) * self.nx + x
        return self.nc * (y * self.nx + x) + i

    def rows_to_chip(self):
        reader = {
            self.row_block(y, x, i): (y, x, i)
            for y in range(self.ny)
            for x in range(self.nx)
            for i in range(self.nc)
        }

        def move(y, c, z, x):
            chip_y, chip_x, i = reader[z * self.nx + x]
            return chip_y, i, c * self.ny + (y ^ (z & 1)), chip_x

        return self.perm(move)

    def to_owner(self):
        def move(y, c, z, x):
            s = self.row_block(y, x, c)
            return z // self.nc, z % self.nc, s // self.nx, s % self.nx

        return self.perm(move)

    def chip_of(self, k):
        return k // self.nx, k % self.nx

    def bits(self, count):
        return [1 << b for b in range(count.bit_length() - 1)]

    def chip_bits(self, j):
        bits = self.bits(self.chips)
        return bits if j % 2 == 0 else bits[::-1]

    def doubled(self, bits):
        held = [0]
        for bit in bits:
            held = held + [k ^ bit for k in held]
        return held

    def slots(self):
        return [(k, j) for k in range(self.chips) for j in range(self.nc)]


def slot_scalars(lay, pos_ref, info_ref, slot):
    k, j = slot
    ky, kx = lay.chip_of(k)
    _, group_c, half = lay.unit(pos_ref[1], pos_ref[2])
    z_frame = (half ^ j) * lay.ny + (pos_ref[0] ^ ky ^ group_c)
    frame = z_frame * lay.nx + (pos_ref[3] ^ kx)
    clip = info_ref[frame]
    clips = (info_ref.shape[0] - lay.frames) // 2
    return clip, info_ref[lay.frames + clip], info_ref[lay.frames + clips + clip]


def table_row(mod_ref, step, part, width):
    return mod_ref[pl.ds(step, 1), part * width : (part + 1) * width]


def allowed_pairs(lay, pos_ref, info_ref, patch_base):
    rows = lay.frames * BLOCK
    row_slot = lax.broadcasted_iota(jnp.int32, (rows, 1), 0) // BLOCK
    col_slot = lax.broadcasted_iota(jnp.int32, (1, rows), 1) // BLOCK
    row_clip = jnp.zeros((rows, 1), jnp.int32)
    row_limit = jnp.zeros((rows, 1), jnp.int32)
    col_clip = jnp.zeros((1, rows), jnp.int32)
    for t, slot in enumerate(lay.slots()):
        clip, limit, _ = slot_scalars(lay, pos_ref, info_ref, slot)
        row_clip = jnp.where(row_slot == t, clip, row_clip)
        row_limit = jnp.where(row_slot == t, limit, row_limit)
        col_clip = jnp.where(col_slot == t, clip, col_clip)
    row_patch = lax.broadcasted_iota(jnp.int32, (rows, 1), 0) % BLOCK
    col_patch = lax.broadcasted_iota(jnp.int32, (1, rows), 1) % BLOCK
    row_key = row_clip * BLOCK + row_patch
    col_key = col_clip * BLOCK + col_patch
    row_valid = (patch_base + row_patch < row_limit).astype(jnp.int32)
    row_index = lax.broadcasted_iota(jnp.int32, (rows, rows), 0)
    col_index = lax.broadcasted_iota(jnp.int32, (rows, rows), 1)
    return (row_key == col_key) & ((row_valid > 0) | (row_index == col_index))


def head_mask(values, head, head_size):
    lane = lax.broadcasted_iota(jnp.int32, (1, values.shape[1]), 1)
    inside = (lane >= head * head_size) & (lane < (head + 1) * head_size)
    return jnp.where(inside, values, jnp.zeros_like(values))


def patch_blocks(array, block):
    part = array[:, block * BLOCK : (block + 1) * BLOCK, :]
    return part.reshape(part.shape[0] * BLOCK, part.shape[2])


def start_kernel(lay, cols, pos_ref, x_ref, g_ref, w_ref, *refs):
    pair_refs, out_refs = refs[: lay.nc], refs[lay.nc :]
    half = x_ref.shape[1] // lay.nc
    for k, ref in enumerate(pair_refs):
        first = pl.multiple_of(((pos_ref[2] // lay.ny) ^ k) * half, 16)
        ref[0, 0] = x_ref[0, pl.ds(first, half), :]
        ref[0, 1] = g_ref[0, pl.ds(first, half), :]
    model = w_ref.shape[1] // 3
    for k, out_ref in enumerate(out_refs):
        chip_x = pos_ref[3] ^ k
        if lay.halves > 1:
            want = lay.row_block(pos_ref[0], chip_x, pos_ref[1])
        else:
            want = pos_ref[0] * lay.nx + chip_x
        for v in range(lay.chips * lay.halves):

            @pl.when(want == v)
            def _(v=v, out_ref=out_ref):
                parts = [
                    w_ref[:, p * model + v * cols : p * model + (v + 1) * cols]
                    for p in range(3)
                ]
                out_ref[...] = jnp.concatenate(parts, axis=1)


def fill_weights(lay, pos_ref, w_refs, w_scr):
    block = w_scr.shape[1] // lay.nz
    rows, width = w_refs[0].shape[1], w_scr.shape[2]
    for h in range(lay.halves):
        for k in range(lay.nz):
            ref = w_refs[h * lay.nz + k]
            for m in range(block // rows):
                start = pl.multiple_of((pos_ref[2] ^ k) * block + m * rows, 16)
                w_scr[h, pl.ds(start, rows), :] = ref[0, :, m * width : (m + 1) * width]


def heads_stacked(lay, values):
    head_size = values.shape[1] // lay.half_heads
    parts = [head_mask(values, head, head_size) for head in range(lay.half_heads)]
    return jnp.concatenate(parts, axis=0) if len(parts) > 1 else parts[0]


def beside(lay, weights):
    return jnp.concatenate([weights[head] for head in range(lay.half_heads)], axis=1)


def attention_weights(lay, keys_stacked, queries, allowed, scaling):
    scores = dot_t(keys_stacked, queries) * scaling
    scores = jnp.where(allowed, scores.reshape((lay.half_heads,) + allowed.shape), -jnp.inf)
    exponent = jnp.exp(scores - jnp.max(scores, axis=1, keepdims=True))
    return exponent * (1.0 / jnp.sum(exponent, axis=1, keepdims=True))


def modulate(lay, pos_ref, info_ref, pair_refs, mod_ref, hid_ref, gp_ref):
    _, step_patches, model = hid_ref.shape
    patches = step_patches * pl.num_programs(0)
    patch_base = lay.unit(pos_ref[1], pos_ref[2])[2] * patches + pl.program_id(0) * step_patches
    patch = patch_base + lax.broadcasted_iota(jnp.int32, (step_patches, 1), 0)
    for t, (k, j) in enumerate(lay.slots()):
        _, limit, step = slot_scalars(lay, pos_ref, info_ref, (k, j))
        n = lay.doubled(lay.chip_bits(j)).index(k)
        ref, place = pair_refs[2 * j + (2 * n) // lay.chips], n % (lay.chips // 2)
        normed, _ = normalize(ref[place, 0].astype(F32))
        shift, scale = table_row(mod_ref, step, 0, model), table_row(mod_ref, step, 1, model)
        hid_ref[t] = (normed * (1.0 + scale) + shift).astype(BF16)
        factor = jnp.where(patch < limit, table_row(mod_ref, step, 2, model), 0.0)
        gp_ref[t] = (factor * ref[place, 1].astype(F32)).astype(BF16)


def forward_kernel(lay, pos_ref, info_ref, *refs):
    pair_refs, refs = refs[: 2 * lay.nc], refs[2 * lay.nc :]
    w_refs, refs = refs[: lay.halves * lay.nz], refs[lay.halves * lay.nz :]
    wo_refs, refs = refs[: lay.nc], refs[lay.nc :]
    mod_ref, q_ref, k_ref, v_ref, ga_ref, kept_ref, sent_ref, *refs = refs
    pr_refs, refs = refs[: lay.chips], refs[lay.chips :]
    hid_ref, gp_ref, w_scr, att_scr, wo_scr, acc_scr, cut_scr = refs
    _, step_patches, model = hid_ref.shape
    tokens = lay.frames * step_patches
    cols = w_scr.shape[2] // 3
    scaling = 1.0 / math.sqrt(cols // lay.half_heads)
    patches = step_patches * pl.num_programs(0)
    is_first = pos_ref[1] == 0

    @pl.when(pl.program_id(0) == 0)
    def _():
        fill_weights(lay, pos_ref, w_refs, w_scr)
        own, other = wo_refs[0][...].astype(F32), wo_refs[1][...].astype(F32)
        both = [jnp.where(is_first, own, other), jnp.where(is_first, other, own)]
        wo_scr[...] = jnp.concatenate(both, axis=0).astype(BF16)
        acc_scr[...] = jnp.zeros_like(acc_scr)

    modulate(lay, pos_ref, info_ref, pair_refs, mod_ref, hid_ref, gp_ref)
    hidden = hid_ref[...].reshape(lay.frames * step_patches, model)
    for h in range(lay.halves):
        triple = dot(hidden, w_scr[h])
        for n, ref in enumerate((q_ref, k_ref, v_ref)):
            ref[h] = triple[:, n * cols : (n + 1) * cols].astype(BF16).reshape(ref.shape[1:])

    for b in range(step_patches // BLOCK):
        patch_base = lay.unit(pos_ref[1], pos_ref[2])[2] * patches + pl.program_id(0) * step_patches + b * BLOCK
        allowed = allowed_pairs(lay, pos_ref, info_ref, patch_base)
        outputs = []
        for h in range(lay.halves):
            queries, keys, values = (patch_blocks(ref[h], b) for ref in (q_ref, k_ref, v_ref))
            weights = attention_weights(lay, heads_stacked(lay, keys), queries, allowed, scaling)
            weights = weights.astype(BF16).reshape(-1, allowed.shape[1])
            outputs.append(t_dot(weights, heads_stacked(lay, values)))
        if lay.halves > 1:
            first = jnp.where(pos_ref[1] == 0, outputs[0], outputs[1])
            second = jnp.where(pos_ref[1] == 0, outputs[1], outputs[0])
            outputs = [jnp.concatenate([first, second], axis=1)]
        attended = outputs[0].astype(BF16)
        att_scr[:, b * BLOCK : (b + 1) * BLOCK, :] = attended.reshape(lay.frames, BLOCK, -1)

    attended = att_scr[...].reshape(tokens, -1)
    grad_proj = gp_ref[...].reshape(tokens, model)
    acc_scr[...] += t_dot(attended, grad_proj)
    grad_attn = dot_t(grad_proj, wo_scr[...])
    part = wo_scr.shape[0] // lay.halves
    for h in range(lay.halves):
        ga_ref[h] = grad_attn[:, h * part : (h + 1) * part].astype(BF16).reshape(ga_ref.shape[1:])
    projected = dot(attended, wo_scr[...]).reshape(lay.chips, lay.nc, step_patches, model)
    for k in range(lay.chips):
        pr_refs[k][...] = projected[k].astype(pr_refs[k].dtype)

    @pl.when(pl.program_id(0) == pl.num_programs(0) - 1)
    def _():
        groups, chunk_rows, chunk_width = kept_ref.shape
        block_rows, part = acc_scr.shape[0] // lay.nc, model // groups
        order = lay.doubled(lay.bits(lay.nz)[::-1])
        first, second = acc_scr[:block_rows, :], acc_scr[block_rows:, :]
        kept = jnp.where(is_first, first, second)
        sent = jnp.where(is_first, second, first)
        for ref, rows in ((kept_ref, kept), (sent_ref, sent)):
            for d in range(groups):
                chunk = [
                    rows[m * chunk_rows : (m + 1) * chunk_rows, d * part : (d + 1) * part]
                    for m in range(chunk_width // part)
                ]
                cut_scr[d] = jnp.concatenate(chunk, axis=1) if len(chunk) > 1 else chunk[0]
            for n, k in enumerate(order):
                ref[n] = cut_scr[pos_ref[2] ^ k]


def backward_kernel(lay, pos_ref, info_ref, *refs):
    w_refs, refs = refs[: lay.halves * lay.nz], refs[lay.halves * lay.nz :]
    q_ref, k_ref, v_ref, ga_ref, *refs = refs
    gh_refs, (w_scr, gt_scr) = refs[: lay.chips], refs[lay.chips :]
    _, frames, step_patches, cols = q_ref.shape
    model = w_scr.shape[1]
    patches = step_patches * pl.num_programs(0)
    scaling = 1.0 / math.sqrt(cols // lay.half_heads)

    @pl.when(pl.program_id(0) == 0)
    def _():
        fill_weights(lay, pos_ref, w_refs, w_scr)

    for b in range(step_patches // BLOCK):
        patch_base = lay.unit(pos_ref[1], pos_ref[2])[2] * patches + pl.program_id(0) * step_patches + b * BLOCK
        allowed = allowed_pairs(lay, pos_ref, info_ref, patch_base)
        for h in range(lay.halves):
            queries, keys, values = (patch_blocks(ref[h], b) for ref in (q_ref, k_ref, v_ref))
            grad_out = patch_blocks(ga_ref[(pos_ref[1] ^ h) if lay.halves > 1 else 0], b)
            keys = heads_stacked(lay, keys)
            weights = attention_weights(lay, keys, queries, allowed, scaling)
            grad_weights = dot_t(heads_stacked(lay, values), grad_out).reshape(weights.shape)
            grad_values = dot(beside(lay, weights.astype(BF16)), heads_stacked(lay, grad_out))
            inner = jnp.sum(weights * grad_weights, axis=1, keepdims=True)
            grad_scores = (weights * (grad_weights - inner) * scaling).astype(BF16)
            grad_queries = t_dot(grad_scores.reshape(-1, grad_scores.shape[2]), keys)
            grad_keys = dot(beside(lay, grad_scores), heads_stacked(lay, queries))
            grads = jnp.concatenate([grad_queries, grad_keys, grad_values], axis=1).astype(BF16)
            gt_scr[h, :, b * BLOCK : (b + 1) * BLOCK, :] = grads.reshape(frames, BLOCK, 3 * cols)

    total = jnp.zeros((frames * step_patches, model), F32)
    for h in range(lay.halves):
        total = total + dot_t(gt_scr[h].reshape(frames * step_patches, 3 * cols), w_scr[h])
    total = total.reshape(lay.chips, lay.nc, step_patches, model)
    for k in range(lay.chips):
        gh_refs[k][...] = total[k].astype(gh_refs[k].dtype)


def output_kernel(lay, pos_ref, info_ref, *refs):
    pair_refs, refs = refs[: lay.nc], refs[lay.nc :]
    pr_refs, refs = refs[: lay.chips], refs[lay.chips :]
    mod_ref, *out_refs = refs
    step_patches, model = out_refs[0].shape
    patches = step_patches * pl.num_programs(0)
    patch_base = lay.unit(pos_ref[1], pos_ref[2])[2] * patches + pl.program_id(0) * step_patches
    patch = patch_base + lax.broadcasted_iota(jnp.int32, (step_patches, 1), 0)
    for j in range(lay.nc):
        _, limit, step = slot_scalars(lay, pos_ref, info_ref, (0, j))
        factor = jnp.where(patch < limit, table_row(mod_ref, step, 2, model), 0.0)
        projected = pr_refs[0][j]
        for k in range(1, lay.chips):
            projected = projected + pr_refs[k][j].astype(F32)
        projected = projected.astype(BF16).astype(F32)
        out_refs[j][...] = (pair_refs[j][0, 0].astype(F32) + factor * projected).astype(BF16)


def input_grad_kernel(lay, pos_ref, info_ref, *refs):
    pair_refs, refs = refs[: lay.nc], refs[lay.nc :]
    gh_refs, refs = refs[: lay.chips], refs[lay.chips :]
    mod_ref, *out_refs = refs
    model = out_refs[0].shape[1]
    for j in range(lay.nc):
        _, _, step = slot_scalars(lay, pos_ref, info_ref, (0, j))
        grad_hidden = gh_refs[0][j]
        for k in range(1, lay.chips):
            grad_hidden = grad_hidden + gh_refs[k][j].astype(F32)
        grad_hidden = grad_hidden.astype(BF16).astype(F32)
        normed, inv_sigma = normalize(pair_refs[j][0, 0].astype(F32))
        grad_norm = grad_hidden * (1.0 + table_row(mod_ref, step, 1, model))
        first_mean = jnp.mean(grad_norm, axis=-1, keepdims=True)
        second_mean = jnp.mean(grad_norm * normed, axis=-1, keepdims=True)
        grad_x = pair_refs[j][0, 1].astype(F32) + inv_sigma * (
            grad_norm - first_mean - normed * second_mean
        )
        out_refs[j][...] = grad_x.astype(BF16)


def whole_spec(shape):
    return pl.BlockSpec(shape, lambda *_: (0,) * len(shape))


def struct(shape, dtype=BF16):
    return jax.ShapeDtypeStruct(shape, dtype)


def local(lay, frames_x, grad_y, clip_ids, clip_patches, clip_step, mod_table, w_qkv, w_out):
    y, c, z, x = (lax.axis_index(name) for name in AXES)
    _, patches, model = frames_x.shape
    half = patches // lay.nc
    chips, nc, nx = lay.chips, lay.nc, lay.nx
    head_size = model // HEADS
    halves = lay.halves
    cols = lay.half_heads * head_size
    chip_width = lay.chip_heads * head_size
    rows = w_qkv.shape[0]
    groups = lay.nz
    quarter = model // groups
    step_patches = max(BLOCK, min(half, 512 // lay.frames))
    steps = half // step_patches
    tokens = lay.frames * step_patches

    def call(kernel, name, cost, in_specs, out_specs, out_shape, scratch=(), grid=(1,), prefetch=2):
        return pl.pallas_call(
            kernel,
            grid_spec=pltpu.PrefetchScalarGridSpec(
                num_scalar_prefetch=prefetch,
                grid=grid,
                in_specs=in_specs,
                out_specs=out_specs,
                scratch_shapes=list(scratch),
            ),
            out_shape=out_shape,
            compiler_params=pltpu.CompilerParams(vmem_limit_bytes=VMEM_LIMIT),
            cost_estimate=pl.CostEstimate(
                flops=cost * tokens * steps, bytes_accessed=4 * model * tokens, transcendentals=0
            ),
            name=name,
        )

    def chip_swap(k):
        ky, kx = lay.chip_of(k)
        return lay.swap(ky=ky, kx=kx)

    def from_plane(parts):
        got = [lax.ppermute(part, AXES, lay.from_plane(k)) for k, part in enumerate(parts)]
        first = jnp.where(z // lay.ny == 0, got[0], got[1])
        second = jnp.where(z // lay.ny == 0, got[1], got[0])
        return jnp.concatenate([first, second], axis=0)[None]

    def doubling(held, bits, swap, after, first=None):
        for bit in bits[:-1]:
            got = lax.ppermute(held, AXES, swap(bit)) if first is None else first
            held, first = jnp.concatenate([held, got], axis=0), None
        held, _ = lax.optimization_barrier((held, after))
        return [held, lax.ppermute(held, AXES, swap(bits[-1]))]

    def over_chips(parts):
        got = [lax.ppermute(parts[k], AXES, chip_swap(k)) for k in range(1, chips)]
        return [parts[0]] + got

    info = jnp.concatenate([clip_ids[0], clip_patches[0], clip_step[0]])[None]
    by_core = jnp.concatenate([info, lax.ppermute(info, AXES, lay.swap(kc=1))], axis=0)
    info = [by_core] + [
        lax.ppermute(by_core, AXES, lay.swap(ky=ky)) for ky in range(1, lay.ny)
    ]
    group_y, group_c, _ = lay.unit(c, z)
    info = sum(
        jnp.where((y ^ ky == group_y) & (c ^ kc == group_c), info[ky][kc], 0)
        for ky in range(lay.ny)
        for kc in range(nc)
    )
    pos = jnp.stack([y, c, z, x]).astype(jnp.int32)
    pair_shape = (1, 2, half, model)
    outputs = call(
        functools.partial(start_kernel, lay, cols),
        "start",
        2 * model * 1000,
        [whole_spec(frames_x.shape)] * 2 + [whole_spec(w_qkv.shape)],
        [whole_spec(pair_shape)] * nc + [whole_spec((rows, 3 * cols))] * nx,
        [struct(pair_shape)] * nc + [struct((rows, 3 * cols))] * nx,
        prefetch=1,
    )(pos, frames_x, grad_y, w_qkv)
    pairs, picked = outputs[:nc], outputs[nc:]
    own = [lax.ppermute(pair, AXES, lay.to_plane(k)) for k, pair in enumerate(pairs)]
    by_x = [picked[0]] + [
        lax.ppermute(picked[kx], AXES, lay.swap(kx=kx)) for kx in range(1, nx)
    ]
    if nx == 2:
        ordered = [jnp.where(x == i, by_x[0], by_x[1]) for i in range(nx)]
    else:
        stacked = jnp.stack(by_x)
        ordered = [lax.dynamic_index_in_dim(stacked, x ^ i, 0, keepdims=False) for i in range(nx)]
    w_own = jnp.concatenate(ordered, axis=1 if rows % 16 == 0 else 0)[None]
    first = lax.ppermute(own[0], AXES, chip_swap(lay.chip_bits(0)[0]))
    own[1], first = lax.optimization_barrier((own[1], first))
    late_w_out, _ = lax.optimization_barrier((w_out, own[0]))
    wo_own = lax.ppermute(late_w_out, AXES, lay.rows_to_chip())
    wo_rows = [wo_own, lax.ppermute(wo_own, AXES, lay.swap(kc=1))]
    w_own, _ = lax.optimization_barrier((w_own, (own[1], wo_own)))
    by_z = {0: w_own}
    for bit in lay.bits(lay.nz):
        by_z[bit] = lax.ppermute(w_own, AXES, lay.swap(kz=bit))
    for k in range(1, lay.nz):
        if k not in by_z:
            forwarded = jnp.where(z < lay.nz, by_z[k ^ (k & -k)], w_own)
            by_z[k] = lax.ppermute(forwarded, AXES, lay.swap(kz=k & -k))
    w_pieces = [by_z[k] for k in range(lay.nz)]

    pairs = []
    for j in range(nc):
        after = ([], None) if j else (info, first)
        pairs += doubling(own[j], lay.chip_bits(j), chip_swap, *after)
    near = jnp.where(z < lay.nz, w_pieces[1], w_own)
    early = [lax.ppermute(piece, AXES, lay.swap(kc=1)) for piece in (w_own, near)]
    early = early if halves > 1 else []
    pairs, w_pieces, early, wo_rows = lax.optimization_barrier((pairs, w_pieces, early, wo_rows))
    if halves > 1:
        w_pieces += early + [lax.ppermute(piece, AXES, lay.swap(kc=1)) for piece in w_pieces[2:]]


    def spread(count, width, patches_at_once):
        return pl.BlockSpec((count, patches_at_once, width), lambda i, *_: (0, i, 0))

    def pair_spec(count, patches_at_once):
        return pl.BlockSpec((count, 2, patches_at_once, model), lambda i, *_: (0, 0, i, 0))

    few = max(BLOCK, step_patches // 2)
    few_steps = half // few
    x_spec = pl.BlockSpec((few, model), lambda i, *_: (i, 0))
    triple_spec = pl.BlockSpec((halves, lay.frames, step_patches, cols), lambda i, *_: (0, 0, i, 0))
    w_specs = [whole_spec(w_own.shape)] * (halves * lay.nz)
    w_scratch = pltpu.VMEM((halves, model, 3 * cols), BF16)
    mod_spec = whole_spec(mod_table.shape)
    triple_shape = struct((halves, lay.frames, half, cols))
    part_specs = [spread(nc, model, step_patches)] * chips
    part_shapes = [struct((nc, half, model), F32)] + [struct((nc, half, model))] * (chips - 1)

    fold = 3 if rows % 24 == 0 else 1
    piece_shape = (groups, rows // fold, quarter * fold)
    queries, keys, values, grad_attn, kept, sent, *projected = call(
        functools.partial(forward_kernel, lay),
        "forward",
        14 * model * 1000,
        [pair_spec(chips // 2, step_patches)] * (2 * nc)
        + w_specs
        + [whole_spec(w_out.shape)] * nc
        + [mod_spec],
        [triple_spec] * 4 + [whole_spec(piece_shape)] * 2 + part_specs,
        [triple_shape] * 4 + [struct(piece_shape, F32)] * 2 + part_shapes,
        [pltpu.VMEM((lay.frames, step_patches, model), BF16)] * 2
        + [
            w_scratch,
            pltpu.VMEM((lay.frames, step_patches, chip_width), BF16),
            pltpu.VMEM((chip_width, model), BF16),
            pltpu.VMEM((chip_width, model), F32),
            pltpu.VMEM(piece_shape, F32),
        ],
        (steps,),
    )(pos, info, *pairs, *w_pieces, *wo_rows, mod_table)
    got = lax.ppermute(sent, AXES, lay.swap(kc=1))
    projected = over_chips(projected)

    middle = groups // 2
    grad_attn, away = lax.optimization_barrier((grad_attn, kept[middle:] + got[middle:]))
    first_away = lax.ppermute(away, AXES, lay.swap(kz=1))

    sums = call(
        functools.partial(backward_kernel, lay),
        "backward",
        10 * model * 1000,
        w_specs + [triple_spec] * 4,
        part_specs,
        part_shapes,
        [w_scratch, pltpu.VMEM((halves, lay.frames, step_patches, 3 * cols), BF16)],
        (steps,),
    )(pos, info, *w_pieces, queries, keys, values, grad_attn)
    sums, first_away, projected[1] = lax.optimization_barrier((sums, first_away, projected[1]))
    projected, _ = lax.optimization_barrier((projected, sums))
    grad_hidden = over_chips(sums)

    out_parts = call(
        functools.partial(output_kernel, lay),
        "output",
        20 * model * 1000,
        [pair_spec(1, few)] * nc + [spread(nc, model, few)] * chips + [mod_spec],
        [x_spec] * nc,
        [struct((half, model))] * nc,
        grid=(few_steps,),
    )(pos, info, *own, *projected, mod_table)
    out_y = from_plane(out_parts)

    grad_hidden, _ = lax.optimization_barrier((grad_hidden, out_parts))
    grad_parts = call(
        functools.partial(input_grad_kernel, lay),
        "input_grad",
        3 * model * 1000,
        [pair_spec(1, few)] * nc + [spread(nc, model, few)] * chips + [mod_spec],
        [x_spec] * nc,
        [struct((half, model))] * nc,
        grid=(few_steps,),
    )(pos, info, *own, *grad_hidden, mod_table)
    grad_x = from_plane(grad_parts)

    cut = kept[:middle] + got[:middle] + first_away
    cut, _ = lax.optimization_barrier((cut, out_parts))
    for bit in lay.bits(lay.nz)[1:]:
        middle = middle // 2
        cut = cut[:middle] + lax.ppermute(cut[middle:], AXES, lay.swap(kz=bit))
    cut, _ = lax.optimization_barrier((cut, grad_parts))
    grad_w = lax.ppermute(cut[0], AXES, lay.to_owner())
    grad_w = jnp.concatenate(
        [grad_w[:, m * quarter : (m + 1) * quarter] for m in range(fold)], axis=0
    )
    grad_w_out = grad_w * jnp.float32(1.0 / math.sqrt(groups * lay.frames * patches))
    return out_y, grad_x, grad_w_out


def solution(mesh):
    lay = Layout(mesh)
    grid = Mesh(mesh.devices.reshape(lay.ny, lay.nc, lay.nz, lay.nx), AXES)
    rows, cols = ("z", "x"), ("y", "c")
    frame = P(AXES, None, None)
    group = P(cols, None)
    return jax.shard_map(
        functools.partial(local, lay),
        mesh=grid,
        in_specs=(frame, frame, group, group, group, P(), P(rows, None), P(rows, None)),
        out_specs=(frame, frame, P(rows, cols)),
        check_vma=False,
    )
```

```python
import functools
import math

import jax
import jax.numpy as jnp
from jax import lax
from jax.experimental import pallas as pl
from jax.experimental.pallas import tpu as pltpu
from jax.sharding import Mesh, PartitionSpec as P

HEADS = 16
CORES = 2
AXES = ("y", "c", "z", "x")
BLOCK = 16
VMEM_LIMIT = 56 * 1024 * 1024
BF16 = jnp.bfloat16
F32 = jnp.float32


def dot(left, right):
    return jnp.dot(left, right, preferred_element_type=F32)


def dot_t(left, right):
    return lax.dot_general(left, right, (((1,), (1,)), ((), ())), preferred_element_type=F32)


def t_dot(left, right):
    return lax.dot_general(left, right, (((0,), (0,)), ((), ())), preferred_element_type=F32)


def normalize(values):
    centred = values - jnp.mean(values, axis=-1, keepdims=True)
    inv_sigma = lax.rsqrt(jnp.mean(centred * centred, axis=-1, keepdims=True) + 1e-06)
    return centred * inv_sigma, inv_sigma


class Layout:
    def __init__(self, mesh):
        groups, seq = mesh.shape["dp"], mesh.shape["seq"]
        self.nc = CORES
        self.ny = groups // CORES
        self.nz = groups
        self.nx = seq // self.nz
        self.chips = self.ny * self.nx
        self.frames = seq
        self.chip_heads = HEADS // self.chips
        self.halves = 2 if self.chip_heads % 2 == 0 else 1
        self.half_heads = self.chip_heads // self.halves

    def linear(self, y, c, z, x):
        return ((y * self.nc + c) * self.nz + z) * self.nx + x

    def perm(self, move):
        pairs = []
        for y in range(self.ny):
            for c in range(self.nc):
                for z in range(self.nz):
                    for x in range(self.nx):
                        pairs.append((self.linear(y, c, z, x), self.linear(*move(y, c, z, x))))
        return pairs

    def to_plane(self, k):
        def move(y, c, z, x):
            half = (z // self.ny) ^ k
            plane = ((y // self.nc) * self.nc + c) * self.nc + half
            return (z % self.ny) ^ c, y % self.nc, plane, x

        return self.perm(move)

    def unit(self, c, z):
        return (z // (self.nc * self.nc)) * self.nc + c, (z // self.nc) % self.nc, z % self.nc

    def from_plane(self, k):
        return [(target, source) for source, target in self.to_plane(k)]

    def swap(self, ky=0, kc=0, kz=0, kx=0):
        return self.perm(lambda y, c, z, x: (y ^ ky, c ^ kc, z ^ kz, x ^ kx))

    def row_block(self, y, x, i):
        if self.halves > 1:
            return (i * self.ny + y) * self.nx + x
        return self.nc * (y * self.nx + x) + i

    def rows_to_chip(self):
        reader = {
            self.row_block(y, x, i): (y, x, i)
            for y in range(self.ny)
            for x in range(self.nx)
            for i in range(self.nc)
        }

        def move(y, c, z, x):
            chip_y, chip_x, i = reader[z * self.nx + x]
            return chip_y, i, c * self.ny + (y ^ (z & 1)), chip_x

        return self.perm(move)

    def to_owner(self):
        def move(y, c, z, x):
            s = self.row_block(y, x, c)
            return z // self.nc, z % self.nc, s // self.nx, s % self.nx

        return self.perm(move)

    def chip_of(self, k):
        return k // self.nx, k % self.nx

    def bits(self, count):
        return [1 << b for b in range(count.bit_length() - 1)]

    def chip_bits(self, j):
        bits = self.bits(self.chips)
        return bits if j % 2 == 0 else bits[::-1]

    def doubled(self, bits):
        held = [0]
        for bit in bits:
            held = held + [k ^ bit for k in held]
        return held

    def slots(self):
        return [(k, j) for k in range(self.chips) for j in range(self.nc)]


def slot_scalars(lay, pos_ref, info_ref, slot):
    k, j = slot
    ky, kx = lay.chip_of(k)
    _, group_c, half = lay.unit(pos_ref[1], pos_ref[2])
    z_frame = (half ^ j) * lay.ny + (pos_ref[0] ^ ky ^ group_c)
    frame = z_frame * lay.nx + (pos_ref[3] ^ kx)
    clip = info_ref[frame]
    clips = (info_ref.shape[0] - lay.frames) // 2
    return clip, info_ref[lay.frames + clip], info_ref[lay.frames + clips + clip]


def table_row(mod_ref, step, part, width):
    return mod_ref[pl.ds(step, 1), part * width : (part + 1) * width]


def allowed_pairs(lay, pos_ref, info_ref, patch_base):
    rows = lay.frames * BLOCK
    row_slot = lax.broadcasted_iota(jnp.int32, (rows, 1), 0) // BLOCK
    col_slot = lax.broadcasted_iota(jnp.int32, (1, rows), 1) // BLOCK
    row_clip = jnp.zeros((rows, 1), jnp.int32)
    row_limit = jnp.zeros((rows, 1), jnp.int32)
    col_clip = jnp.zeros((1, rows), jnp.int32)
    for t, slot in enumerate(lay.slots()):
        clip, limit, _ = slot_scalars(lay, pos_ref, info_ref, slot)
        row_clip = jnp.where(row_slot == t, clip, row_clip)
        row_limit = jnp.where(row_slot == t, limit, row_limit)
        col_clip = jnp.where(col_slot == t, clip, col_clip)
    row_patch = lax.broadcasted_iota(jnp.int32, (rows, 1), 0) % BLOCK
    col_patch = lax.broadcasted_iota(jnp.int32, (1, rows), 1) % BLOCK
    row_key = row_clip * BLOCK + row_patch
    col_key = col_clip * BLOCK + col_patch
    row_valid = (patch_base + row_patch < row_limit).astype(jnp.int32)
    row_index = lax.broadcasted_iota(jnp.int32, (rows, rows), 0)
    col_index = lax.broadcasted_iota(jnp.int32, (rows, rows), 1)
    return (row_key == col_key) & ((row_valid > 0) | (row_index == col_index))


def head_mask(values, head, head_size):
    lane = lax.broadcasted_iota(jnp.int32, (1, values.shape[1]), 1)
    inside = (lane >= head * head_size) & (lane < (head + 1) * head_size)
    return jnp.where(inside, values, jnp.zeros_like(values))


def patch_blocks(array, block):
    part = array[:, block * BLOCK : (block + 1) * BLOCK, :]
    return part.reshape(part.shape[0] * BLOCK, part.shape[2])


def start_kernel(lay, cols, pos_ref, x_ref, g_ref, w_ref, *refs):
    pair_refs, out_refs = refs[: lay.nc], refs[lay.nc :]
    half = x_ref.shape[1] // lay.nc
    for k, ref in enumerate(pair_refs):
        first = pl.multiple_of(((pos_ref[2] // lay.ny) ^ k) * half, 16)
        ref[0, 0] = x_ref[0, pl.ds(first, half), :]
        ref[0, 1] = g_ref[0, pl.ds(first, half), :]
    model = w_ref.shape[1] // 3
    for k, out_ref in enumerate(out_refs):
        chip_x = pos_ref[3] ^ k
        if lay.halves > 1:
            want = lay.row_block(pos_ref[0], chip_x, pos_ref[1])
        else:
            want = pos_ref[0] * lay.nx + chip_x
        for v in range(lay.chips * lay.halves):

            @pl.when(want == v)
            def _(v=v, out_ref=out_ref):
                parts = [
                    w_ref[:, p * model + v * cols : p * model + (v + 1) * cols]
                    for p in range(3)
                ]
                out_ref[...] = jnp.concatenate(parts, axis=1)


def fill_weights(lay, pos_ref, w_refs, w_scr):
    block = w_scr.shape[1] // lay.nz
    rows, width = w_refs[0].shape[1], w_scr.shape[2]
    for h in range(lay.halves):
        for k in range(lay.nz):
            ref = w_refs[h * lay.nz + k]
            for m in range(block // rows):
                start = pl.multiple_of((pos_ref[2] ^ k) * block + m * rows, 16)
                w_scr[h, pl.ds(start, rows), :] = ref[0, :, m * width : (m + 1) * width]


def heads_stacked(lay, values):
    head_size = values.shape[1] // lay.half_heads
    parts = [head_mask(values, head, head_size) for head in range(lay.half_heads)]
    return jnp.concatenate(parts, axis=0) if len(parts) > 1 else parts[0]


def beside(lay, weights):
    return jnp.concatenate([weights[head] for head in range(lay.half_heads)], axis=1)


def attention_weights(lay, keys_stacked, queries, allowed, scaling):
    scores = dot_t(keys_stacked, queries) * scaling
    scores = jnp.where(allowed, scores.reshape((lay.half_heads,) + allowed.shape), -jnp.inf)
    exponent = jnp.exp(scores - jnp.max(scores, axis=1, keepdims=True))
    return exponent * (1.0 / jnp.sum(exponent, axis=1, keepdims=True))


def modulate(lay, pos_ref, info_ref, pair_refs, mod_ref, hid_ref, gp_ref):
    _, step_patches, model = hid_ref.shape
    patches = step_patches * pl.num_programs(0)
    patch_base = lay.unit(pos_ref[1], pos_ref[2])[2] * patches + pl.program_id(0) * step_patches
    patch = patch_base + lax.broadcasted_iota(jnp.int32, (step_patches, 1), 0)
    for t, (k, j) in enumerate(lay.slots()):
        _, limit, step = slot_scalars(lay, pos_ref, info_ref, (k, j))
        n = lay.doubled(lay.chip_bits(j)).index(k)
        ref, place = pair_refs[2 * j + (2 * n) // lay.chips], n % (lay.chips // 2)
        normed, _ = normalize(ref[place, 0].astype(F32))
        shift, scale = table_row(mod_ref, step, 0, model), table_row(mod_ref, step, 1, model)
        hid_ref[t] = (normed * (1.0 + scale) + shift).astype(BF16)
        factor = jnp.where(patch < limit, table_row(mod_ref, step, 2, model), 0.0)
        gp_ref[t] = (factor * ref[place, 1].astype(F32)).astype(BF16)


def forward_kernel(lay, pos_ref, info_ref, *refs):
    pair_refs, refs = refs[: 2 * lay.nc], refs[2 * lay.nc :]
    w_refs, refs = refs[: lay.halves * lay.nz], refs[lay.halves * lay.nz :]
    wo_refs, refs = refs[: lay.nc], refs[lay.nc :]
    mod_ref, q_ref, k_ref, v_ref, ga_ref, kept_ref, sent_ref, *refs = refs
    pr_refs, refs = refs[: lay.chips], refs[lay.chips :]
    hid_ref, gp_ref, w_scr, att_scr, wo_scr, acc_scr, cut_scr = refs
    _, step_patches, model = hid_ref.shape
    tokens = lay.frames * step_patches
    cols = w_scr.shape[2] // 3
    scaling = 1.0 / math.sqrt(cols // lay.half_heads)
    patches = step_patches * pl.num_programs(0)
    is_first = pos_ref[1] == 0

    @pl.when(pl.program_id(0) == 0)
    def _():
        fill_weights(lay, pos_ref, w_refs, w_scr)
        own, other = wo_refs[0][...].astype(F32), wo_refs[1][...].astype(F32)
        both = [jnp.where(is_first, own, other), jnp.where(is_first, other, own)]
        wo_scr[...] = jnp.concatenate(both, axis=0).astype(BF16)
        acc_scr[...] = jnp.zeros_like(acc_scr)

    modulate(lay, pos_ref, info_ref, pair_refs, mod_ref, hid_ref, gp_ref)
    hidden = hid_ref[...].reshape(lay.frames * step_patches, model)
    for h in range(lay.halves):
        triple = dot(hidden, w_scr[h])
        for n, ref in enumerate((q_ref, k_ref, v_ref)):
            ref[h] = triple[:, n * cols : (n + 1) * cols].astype(BF16).reshape(ref.shape[1:])

    for b in range(step_patches // BLOCK):
        patch_base = lay.unit(pos_ref[1], pos_ref[2])[2] * patches + pl.program_id(0) * step_patches + b * BLOCK
        allowed = allowed_pairs(lay, pos_ref, info_ref, patch_base)
        outputs = []
        for h in range(lay.halves):
            queries, keys, values = (patch_blocks(ref[h], b) for ref in (q_ref, k_ref, v_ref))
            weights = attention_weights(lay, heads_stacked(lay, keys), queries, allowed, scaling)
            weights = weights.astype(BF16).reshape(-1, allowed.shape[1])
            outputs.append(t_dot(weights, heads_stacked(lay, values)))
        if lay.halves > 1:
            first = jnp.where(pos_ref[1] == 0, outputs[0], outputs[1])
            second = jnp.where(pos_ref[1] == 0, outputs[1], outputs[0])
            outputs = [jnp.concatenate([first, second], axis=1)]
        attended = outputs[0].astype(BF16)
        att_scr[:, b * BLOCK : (b + 1) * BLOCK, :] = attended.reshape(lay.frames, BLOCK, -1)

    attended = att_scr[...].reshape(tokens, -1)
    grad_proj = gp_ref[...].reshape(tokens, model)
    acc_scr[...] += t_dot(attended, grad_proj)
    grad_attn = dot_t(grad_proj, wo_scr[...])
    part = wo_scr.shape[0] // lay.halves
    for h in range(lay.halves):
        ga_ref[h] = grad_attn[:, h * part : (h + 1) * part].astype(BF16).reshape(ga_ref.shape[1:])
    projected = dot(attended, wo_scr[...]).reshape(lay.chips, lay.nc, step_patches, model)
    for k in range(lay.chips):
        pr_refs[k][...] = projected[k].astype(pr_refs[k].dtype)

    @pl.when(pl.program_id(0) == pl.num_programs(0) - 1)
    def _():
        groups, chunk_rows, chunk_width = kept_ref.shape
        block_rows, part = acc_scr.shape[0] // lay.nc, model // groups
        order = lay.doubled(lay.bits(lay.nz)[::-1])
        first, second = acc_scr[:block_rows, :], acc_scr[block_rows:, :]
        kept = jnp.where(is_first, first, second)
        sent = jnp.where(is_first, second, first)
        for ref, rows in ((kept_ref, kept), (sent_ref, sent)):
            for d in range(groups):
                chunk = [
                    rows[m * chunk_rows : (m + 1) * chunk_rows, d * part : (d + 1) * part]
                    for m in range(chunk_width // part)
                ]
                cut_scr[d] = jnp.concatenate(chunk, axis=1) if len(chunk) > 1 else chunk[0]
            for n, k in enumerate(order):
                ref[n] = cut_scr[pos_ref[2] ^ k]


def backward_kernel(lay, pos_ref, info_ref, *refs):
    w_refs, refs = refs[: lay.halves * lay.nz], refs[lay.halves * lay.nz :]
    q_ref, k_ref, v_ref, ga_ref, *refs = refs
    gh_refs, (w_scr, gt_scr) = refs[: lay.chips], refs[lay.chips :]
    _, frames, step_patches, cols = q_ref.shape
    model = w_scr.shape[1]
    patches = step_patches * pl.num_programs(0)
    scaling = 1.0 / math.sqrt(cols // lay.half_heads)

    @pl.when(pl.program_id(0) == 0)
    def _():
        fill_weights(lay, pos_ref, w_refs, w_scr)

    for b in range(step_patches // BLOCK):
        patch_base = lay.unit(pos_ref[1], pos_ref[2])[2] * patches + pl.program_id(0) * step_patches + b * BLOCK
        allowed = allowed_pairs(lay, pos_ref, info_ref, patch_base)
        for h in range(lay.halves):
            queries, keys, values = (patch_blocks(ref[h], b) for ref in (q_ref, k_ref, v_ref))
            grad_out = patch_blocks(ga_ref[(pos_ref[1] ^ h) if lay.halves > 1 else 0], b)
            keys = heads_stacked(lay, keys)
            weights = attention_weights(lay, keys, queries, allowed, scaling)
            grad_weights = dot_t(heads_stacked(lay, values), grad_out).reshape(weights.shape)
            grad_values = dot(beside(lay, weights.astype(BF16)), heads_stacked(lay, grad_out))
            inner = jnp.sum(weights * grad_weights, axis=1, keepdims=True)
            grad_scores = (weights * (grad_weights - inner) * scaling).astype(BF16)
            grad_queries = t_dot(grad_scores.reshape(-1, grad_scores.shape[2]), keys)
            grad_keys = dot(beside(lay, grad_scores), heads_stacked(lay, queries))
            grads = jnp.concatenate([grad_queries, grad_keys, grad_values], axis=1).astype(BF16)
            gt_scr[h, :, b * BLOCK : (b + 1) * BLOCK, :] = grads.reshape(frames, BLOCK, 3 * cols)

    total = jnp.zeros((frames * step_patches, model), F32)
    for h in range(lay.halves):
        total = total + dot_t(gt_scr[h].reshape(frames * step_patches, 3 * cols), w_scr[h])
    total = total.reshape(lay.chips, lay.nc, step_patches, model)
    for k in range(lay.chips):
        gh_refs[k][...] = total[k].astype(gh_refs[k].dtype)


def output_kernel(lay, pos_ref, info_ref, *refs):
    pair_refs, refs = refs[: lay.nc], refs[lay.nc :]
    pr_refs, refs = refs[: lay.chips], refs[lay.chips :]
    mod_ref, *out_refs = refs
    step_patches, model = out_refs[0].shape
    patches = step_patches * pl.num_programs(0)
    patch_base = lay.unit(pos_ref[1], pos_ref[2])[2] * patches + pl.program_id(0) * step_patches
    patch = patch_base + lax.broadcasted_iota(jnp.int32, (step_patches, 1), 0)
    for j in range(lay.nc):
        _, limit, step = slot_scalars(lay, pos_ref, info_ref, (0, j))
        factor = jnp.where(patch < limit, table_row(mod_ref, step, 2, model), 0.0)
        projected = pr_refs[0][j]
        for k in range(1, lay.chips):
            projected = projected + pr_refs[k][j].astype(F32)
        projected = projected.astype(BF16).astype(F32)
        out_refs[j][...] = (pair_refs[j][0, 0].astype(F32) + factor * projected).astype(BF16)


def input_grad_kernel(lay, pos_ref, info_ref, *refs):
    pair_refs, refs = refs[: lay.nc], refs[lay.nc :]
    gh_refs, refs = refs[: lay.chips], refs[lay.chips :]
    mod_ref, *out_refs = refs
    model = out_refs[0].shape[1]
    for j in range(lay.nc):
        _, _, step = slot_scalars(lay, pos_ref, info_ref, (0, j))
        grad_hidden = gh_refs[0][j]
        for k in range(1, lay.chips):
            grad_hidden = grad_hidden + gh_refs[k][j].astype(F32)
        grad_hidden = grad_hidden.astype(BF16).astype(F32)
        normed, inv_sigma = normalize(pair_refs[j][0, 0].astype(F32))
        grad_norm = grad_hidden * (1.0 + table_row(mod_ref, step, 1, model))
        first_mean = jnp.mean(grad_norm, axis=-1, keepdims=True)
        second_mean = jnp.mean(grad_norm * normed, axis=-1, keepdims=True)
        grad_x = pair_refs[j][0, 1].astype(F32) + inv_sigma * (
            grad_norm - first_mean - normed * second_mean
        )
        out_refs[j][...] = grad_x.astype(BF16)


def whole_spec(shape):
    return pl.BlockSpec(shape, lambda *_: (0,) * len(shape))


def struct(shape, dtype=BF16):
    return jax.ShapeDtypeStruct(shape, dtype)


def local(lay, frames_x, grad_y, clip_ids, clip_patches, clip_step, mod_table, w_qkv, w_out):
    y, c, z, x = (lax.axis_index(name) for name in AXES)
    _, patches, model = frames_x.shape
    half = patches // lay.nc
    chips, nc, nx = lay.chips, lay.nc, lay.nx
    head_size = model // HEADS
    halves = lay.halves
    cols = lay.half_heads * head_size
    chip_width = lay.chip_heads * head_size
    rows = w_qkv.shape[0]
    groups = lay.nz
    quarter = model // groups
    step_patches = max(BLOCK, min(half, 512 // lay.frames))
    steps = half // step_patches
    tokens = lay.frames * step_patches

    def call(kernel, name, cost, in_specs, out_specs, out_shape, scratch=(), grid=(1,), prefetch=2):
        return pl.pallas_call(
            kernel,
            grid_spec=pltpu.PrefetchScalarGridSpec(
                num_scalar_prefetch=prefetch,
                grid=grid,
                in_specs=in_specs,
                out_specs=out_specs,
                scratch_shapes=list(scratch),
            ),
            out_shape=out_shape,
            compiler_params=pltpu.CompilerParams(vmem_limit_bytes=VMEM_LIMIT),
            cost_estimate=pl.CostEstimate(
                flops=cost * tokens * steps, bytes_accessed=4 * model * tokens, transcendentals=0
            ),
            name=name,
        )

    def chip_swap(k):
        ky, kx = lay.chip_of(k)
        return lay.swap(ky=ky, kx=kx)

    def from_plane(parts):
        got = [lax.ppermute(part, AXES, lay.from_plane(k)) for k, part in enumerate(parts)]
        first = jnp.where(z // lay.ny == 0, got[0], got[1])
        second = jnp.where(z // lay.ny == 0, got[1], got[0])
        return jnp.concatenate([first, second], axis=0)[None]

    def doubling(held, bits, swap, after, first=None):
        for bit in bits[:-1]:
            got = lax.ppermute(held, AXES, swap(bit)) if first is None else first
            held, first = jnp.concatenate([held, got], axis=0), None
        held, _ = lax.optimization_barrier((held, after))
        return [held, lax.ppermute(held, AXES, swap(bits[-1]))]

    def over_chips(parts):
        got = [lax.ppermute(parts[k], AXES, chip_swap(k)) for k in range(1, chips)]
        return [parts[0]] + got

    pos = jnp.stack([y, c, z, x]).astype(jnp.int32)
    pair_shape = (1, 2, half, model)
    outputs = call(
        functools.partial(start_kernel, lay, cols),
        "start",
        2 * model * 1000,
        [whole_spec(frames_x.shape)] * 2 + [whole_spec(w_qkv.shape)],
        [whole_spec(pair_shape)] * nc + [whole_spec((rows, 3 * cols))] * nx,
        [struct(pair_shape)] * nc + [struct((rows, 3 * cols))] * nx,
        prefetch=1,
    )(pos, frames_x, grad_y, w_qkv)
    pairs, picked = outputs[:nc], outputs[nc:]
    own = [lax.ppermute(pair, AXES, lay.to_plane(k)) for k, pair in enumerate(pairs)]
    clip_ids, own[0] = lax.optimization_barrier((clip_ids, own[0]))
    info = jnp.concatenate([clip_ids[0], clip_patches[0], clip_step[0]])[None]
    by_core = jnp.concatenate([info, lax.ppermute(info, AXES, lay.swap(kc=1))], axis=0)
    info = [by_core] + [
        lax.ppermute(by_core, AXES, lay.swap(ky=ky)) for ky in range(1, lay.ny)
    ]
    group_y, group_c, _ = lay.unit(c, z)
    info = sum(
        jnp.where((y ^ ky == group_y) & (c ^ kc == group_c), info[ky][kc], 0)
        for ky in range(lay.ny)
        for kc in range(nc)
    )
    by_x = [picked[0]] + [
        lax.ppermute(picked[kx], AXES, lay.swap(kx=kx)) for kx in range(1, nx)
    ]
    if nx == 2:
        ordered = [jnp.where(x == i, by_x[0], by_x[1]) for i in range(nx)]
    else:
        stacked = jnp.stack(by_x)
        ordered = [lax.dynamic_index_in_dim(stacked, x ^ i, 0, keepdims=False) for i in range(nx)]
    w_own = jnp.concatenate(ordered, axis=1 if rows % 16 == 0 else 0)[None]
    first = lax.ppermute(own[0], AXES, chip_swap(lay.chip_bits(0)[0]))
    own[1], first = lax.optimization_barrier((own[1], first))
    late_w_out, _ = lax.optimization_barrier((w_out, own[0]))
    wo_own = lax.ppermute(late_w_out, AXES, lay.rows_to_chip())
    wo_rows = [wo_own, lax.ppermute(wo_own, AXES, lay.swap(kc=1))]
    w_own, _ = lax.optimization_barrier((w_own, (own[1], wo_own)))
    by_z = {0: w_own}
    for bit in lay.bits(lay.nz):
        by_z[bit] = lax.ppermute(w_own, AXES, lay.swap(kz=bit))
    for k in range(1, lay.nz):
        if k not in by_z:
            forwarded = jnp.where(z < lay.nz, by_z[k ^ (k & -k)], w_own)
            by_z[k] = lax.ppermute(forwarded, AXES, lay.swap(kz=k & -k))
    w_pieces = [by_z[k] for k in range(lay.nz)]

    pairs = []
    for j in range(nc):
        after = ([], None) if j else (info, first)
        pairs += doubling(own[j], lay.chip_bits(j), chip_swap, *after)
    near = jnp.where(z < lay.nz, w_pieces[1], w_own)
    early = [lax.ppermute(piece, AXES, lay.swap(kc=1)) for piece in (w_own, near)]
    early = early if halves > 1 else []
    pairs, w_pieces, early, wo_rows = lax.optimization_barrier((pairs, w_pieces, early, wo_rows))
    if halves > 1:
        w_pieces += early + [lax.ppermute(piece, AXES, lay.swap(kc=1)) for piece in w_pieces[2:]]


    def spread(count, width, patches_at_once):
        return pl.BlockSpec((count, patches_at_once, width), lambda i, *_: (0, i, 0))

    def pair_spec(count, patches_at_once):
        return pl.BlockSpec((count, 2, patches_at_once, model), lambda i, *_: (0, 0, i, 0))

    few = max(BLOCK, step_patches // 2)
    few_steps = half // few
    x_spec = pl.BlockSpec((few, model), lambda i, *_: (i, 0))
    triple_spec = pl.BlockSpec((halves, lay.frames, step_patches, cols), lambda i, *_: (0, 0, i, 0))
    w_specs = [whole_spec(w_own.shape)] * (halves * lay.nz)
    w_scratch = pltpu.VMEM((halves, model, 3 * cols), BF16)
    mod_spec = whole_spec(mod_table.shape)
    triple_shape = struct((halves, lay.frames, half, cols))
    part_specs = [spread(nc, model, step_patches)] * chips
    part_shapes = [struct((nc, half, model), F32)] + [struct((nc, half, model))] * (chips - 1)

    fold = 3 if rows % 24 == 0 else 1
    piece_shape = (groups, rows // fold, quarter * fold)
    queries, keys, values, grad_attn, kept, sent, *projected = call(
        functools.partial(forward_kernel, lay),
        "forward",
        14 * model * 1000,
        [pair_spec(chips // 2, step_patches)] * (2 * nc)
        + w_specs
        + [whole_spec(w_out.shape)] * nc
        + [mod_spec],
        [triple_spec] * 4 + [whole_spec(piece_shape)] * 2 + part_specs,
        [triple_shape] * 4 + [struct(piece_shape, F32)] * 2 + part_shapes,
        [pltpu.VMEM((lay.frames, step_patches, model), BF16)] * 2
        + [
            w_scratch,
            pltpu.VMEM((lay.frames, step_patches, chip_width), BF16),
            pltpu.VMEM((chip_width, model), BF16),
            pltpu.VMEM((chip_width, model), F32),
            pltpu.VMEM(piece_shape, F32),
        ],
        (steps,),
    )(pos, info, *pairs, *w_pieces, *wo_rows, mod_table)
    got = lax.ppermute(sent, AXES, lay.swap(kc=1))
    projected = over_chips(projected)

    middle = groups // 2
    grad_attn, away = lax.optimization_barrier((grad_attn, kept[middle:] + got[middle:]))
    first_away = lax.ppermute(away, AXES, lay.swap(kz=1))

    sums = call(
        functools.partial(backward_kernel, lay),
        "backward",
        10 * model * 1000,
        w_specs + [triple_spec] * 4,
        part_specs,
        part_shapes,
        [w_scratch, pltpu.VMEM((halves, lay.frames, step_patches, 3 * cols), BF16)],
        (steps,),
    )(pos, info, *w_pieces, queries, keys, values, grad_attn)
    sums, first_away, projected[1] = lax.optimization_barrier((sums, first_away, projected[1]))
    projected, _ = lax.optimization_barrier((projected, sums))
    grad_hidden = over_chips(sums)

    out_parts = call(
        functools.partial(output_kernel, lay),
        "output",
        20 * model * 1000,
        [pair_spec(1, few)] * nc + [spread(nc, model, few)] * chips + [mod_spec],
        [x_spec] * nc,
        [struct((half, model))] * nc,
        grid=(few_steps,),
    )(pos, info, *own, *projected, mod_table)
    out_y = from_plane(out_parts)

    grad_hidden, _ = lax.optimization_barrier((grad_hidden, out_parts))
    grad_parts = call(
        functools.partial(input_grad_kernel, lay),
        "input_grad",
        3 * model * 1000,
        [pair_spec(1, few)] * nc + [spread(nc, model, few)] * chips + [mod_spec],
        [x_spec] * nc,
        [struct((half, model))] * nc,
        grid=(few_steps,),
    )(pos, info, *own, *grad_hidden, mod_table)
    grad_x = from_plane(grad_parts)

    cut = kept[:middle] + got[:middle] + first_away
    cut, _ = lax.optimization_barrier((cut, out_parts))
    for bit in lay.bits(lay.nz)[1:]:
        middle = middle // 2
        cut = cut[:middle] + lax.ppermute(cut[middle:], AXES, lay.swap(kz=bit))
    cut, _ = lax.optimization_barrier((cut, grad_parts))
    grad_w = lax.ppermute(cut[0], AXES, lay.to_owner())
    grad_w = jnp.concatenate(
        [grad_w[:, m * quarter : (m + 1) * quarter] for m in range(fold)], axis=0
    )
    grad_w_out = grad_w * jnp.float32(1.0 / math.sqrt(groups * lay.frames * patches))
    return out_y, grad_x, grad_w_out


def solution(mesh):
    lay = Layout(mesh)
    grid = Mesh(mesh.devices.reshape(lay.ny, lay.nc, lay.nz, lay.nx), AXES)
    rows, cols = ("z", "x"), ("y", "c")
    frame = P(AXES, None, None)
    group = P(cols, None)
    return jax.shard_map(
        functools.partial(local, lay),
        mesh=grid,
        in_specs=(frame, frame, group, group, group, P(), P(rows, None), P(rows, None)),
        out_specs=(frame, frame, P(rows, cols)),
        check_vma=False,
    )
```
